32 devices in a mesh: lat: 4 (over y, core), lon: 8 (over z, x).
Axes of the slice: x: 2, y: 2, z: 4, core: 2. Of those that a mesh axis runs over, the one named last changes fastest.
Arguments:
- tracers: float32 [2, 4, 64, 2048], P(None, None, 'lat', 'lon'), may hold values from -6 to 6
- cotangent: float32 [2, 4, 64, 2048], P(None, None, 'lat', 'lon'), may hold values from -6 to 6
- land_mask: int32 [4, 64, 2048], P(None, 'lat', 'lon'), may hold values 0 or 1
- diffusion: float32 [3, 4, 64, 2048], P(None, None, 'lat', 'lon'), may hold values from 0.01 to 0.1
- velocity: float32 [2, 4, 64, 2048], P(None, None, 'lat', 'lon'), may hold values from -0.1 to 0.1
- weights: float32 [32, 128, 128], replicated, may hold values from -0.1875 to 0.1875
- atm_state: float32 [2, 4, 2048, 128], P(None, 'lat', 'lon'), may hold values from -6 to 6
- margins: int32 [3, 4, 8, 8, 64], P(None, 'lat', 'lon'), may hold values from -1 to 255, as said below
Outputs:
- final_tracers: float32 [2, 4, 64, 2048], P(None, None, 'lat', 'lon')
- adjoint_tracers: float32 [2, 4, 64, 2048], P(None, None, 'lat', 'lon')
- atm_gradient: float32 [2, 4, 2048, 128], P(None, 'lat', 'lon')
The draws below stay inside these ranges and needn't reach their ends.
Inputs may be any that keep to these rules, and one draw needn't show every extreme that they name: margins[0, i, j, k, s] is a top-level block of ocean tile (i, k), or -1 where slot s from longitude tile j to longitude tile k in latitude row i is empty; margins[1] is an atmosphere block of tile (i, j) and margins[2] a weight block in every slot. Live slots lie anywhere among the 64. In each latitude row one receiving tile has all 64 slots live from every sender.
All inputs are finite; a program needn't handle non-finite values. No bound on the sum of `land_mask` on one device may be relied on, other than what follows from the above.
Results may differ from the reference program's by a relative error of at most 0.0003.
Values sent between devices are 32-bit elements; how exact they have to be, the bound alone decides.
No kernel may reach another device: no remote copies, remote signals or barrier semaphores. Data moves between devices by JAX's collectives and lax.ppermute only.
A program may use at most 64 MiB of HBM per device.

```python
import math
import jax
import jax.numpy as jnp
from jax import lax

LEV = 4
CLAT = 16
CLON = 256
BLOCK = 128
ATM_DEV = 256
CAP = 64
WBLOCKS = 32
STEPS = 4
LATS = 64
LONS = 2048
ATM_ROW = 2048
OCN_BLK = 32
N_LAT = 4
N_LON = 8


def draw_margins(key, part):
    keys = jax.random.split(key, 6)
    full_dest = jax.random.randint(keys[0], (N_LAT,), 0, N_LON)
    counts = jax.random.randint(keys[1], (N_LAT, N_LON, N_LON), 1, CAP // 2 + 1)
    dest_ids = jnp.arange(N_LON)[None, None, :]
    counts = jnp.where(dest_ids == full_dest[:, None, None], CAP, counts)
    scores = jax.random.randint(keys[2], (N_LAT, N_LON, N_LON, CAP), 0, 1 << 20) * CAP + jnp.arange(CAP)
    order = jnp.argsort(scores, axis=-1)
    ranks = jnp.argsort(order, axis=-1)
    live_slot = ranks < counts[..., None]
    ocean = jnp.where(live_slot, jax.random.randint(keys[3], (N_LAT, N_LON, N_LON, CAP), 0, OCN_BLK), -1)
    atmosphere = jax.random.randint(keys[4], (N_LAT, N_LON, N_LON, CAP), 0, ATM_DEV)
    table = jax.random.randint(keys[5], (N_LAT, N_LON, N_LON, CAP), 0, WBLOCKS)
    return jnp.stack([ocean, atmosphere, table]).astype(jnp.int32)


def place_ends(values, rng, least, top_value):
    index_at = [jax.random.randint(jax.random.fold_in(rng, axis), (), 0, length) for axis, length in enumerate(values.shape)]
    widest = values.shape.index(max(values.shape))
    neighbour = index_at[:widest] + [(index_at[widest] + 1) % values.shape[widest]] + index_at[widest + 1:]
    return values.at[tuple(index_at)].set(least).at[tuple(neighbour)].set(top_value)


def levels(own_key, extent, pieces, least, largest):
    gain, own = 1.0, jax.random.fold_in(own_key, 6)
    for axis_at, shards_of in pieces:
        heights = jnp.exp(jax.random.uniform(jax.random.fold_in(own, axis_at), (shards_of,), jnp.float32, least / len(pieces), largest / len(pieces)))
        gain = gain * jnp.repeat(heights, extent[axis_at] // shards_of).reshape([-1 if axis == axis_at else 1 for axis in range(len(extent))])
    return gain


def bell_draw(rng, shape, scale, limit, cuts=(), dtype=jnp.bfloat16):
    array = jax.random.normal(rng, shape, jnp.float32) * scale
    if len(cuts) > 0:
        array = levels(rng, shape, cuts, -0.22, 0.18) * array
    return jnp.clip(array, min=-limit, max=limit).astype(dtype)


def setup_inputs(seed: int = 0) -> dict:
    streams_of = jax.random.split(jax.random.key(seed), 9)
    return {
        "tracers": bell_draw(streams_of[0], (2, LEV, LATS, LONS), 1.0, 6.0, ((2, 4), (3, 8)), jnp.float32),
        "cotangent": bell_draw(streams_of[1], (2, LEV, LATS, LONS), 1.0, 6.0, ((2, 4), (3, 8)), jnp.float32),
        "land_mask": place_ends((jax.random.randint(streams_of[2], (LEV, LATS, LONS), 0, 5) < 4).astype(jnp.int32), jax.random.fold_in(streams_of[2], 1), 0, 1),
        "diffusion": jnp.clip(jnp.exp(math.log(0.1) - 2.3025851 * jax.random.uniform(streams_of[3], (3, LEV, LATS, LONS), jnp.float32) ** levels(streams_of[3], (3, LEV, LATS, LONS), ((2, 4), (3, 8)), -0.2, 0.2)), 0.01, 0.1),
        "velocity": jnp.clip(jax.random.uniform(streams_of[4], (2, LEV, LATS, LONS), jnp.float32, -0.1, 0.1) * levels(streams_of[4], (2, LEV, LATS, LONS), ((2, 4), (3, 8)), -0.4, 0.0), -0.1, 0.1),
        "weights": bell_draw(streams_of[5], (WBLOCKS, BLOCK, BLOCK), (8 * BLOCK) ** -0.5, 0.1875, (), jnp.float32),
        "atm_state": bell_draw(streams_of[6], (2, N_LAT, ATM_ROW, BLOCK), 1.0, 6.0, ((1, 4), (2, 8)), jnp.float32),
        "margins": draw_margins(jax.random.fold_in(streams_of[8], 71), 0),
    }


def face_terms(land_mask, diffusion, velocity):
    ocean_mask = land_mask.astype(jnp.float32)
    mask_east = jnp.roll(ocean_mask, -1, axis=2)
    mask_north = jnp.concatenate([ocean_mask[:, 1:], jnp.zeros_like(ocean_mask[:, :1])], axis=1)
    east_k = diffusion[0] * ocean_mask * mask_east
    east_v = velocity[0] * ocean_mask * mask_east
    north_k = diffusion[1] * ocean_mask * mask_north
    north_v = velocity[1] * ocean_mask * mask_north
    below_k = diffusion[2][:-1] * ocean_mask[:-1] * ocean_mask[1:]
    coeffs = (jnp.maximum(east_v, 0.0) + east_k, jnp.minimum(east_v, 0.0) - east_k, jnp.maximum(north_v, 0.0) + north_k, jnp.minimum(north_v, 0.0) - north_k, below_k)
    return (coeffs, ocean_mask)

def advance(quantity, coeffs):
    east_a, east_b, north_a, north_b, below_k = coeffs
    east_flux = east_a * quantity + east_b * jnp.roll(quantity, -1, axis=3)
    zero_row = jnp.zeros_like(quantity[:, :, :1])
    north_flux = north_a * quantity + north_b * jnp.concatenate([quantity[:, :, 1:], zero_row], axis=2)
    below_flux = below_k * (quantity[:, :-1] - quantity[:, 1:])
    zero_level = jnp.zeros_like(quantity[:, :1])
    return quantity - (east_flux - jnp.roll(east_flux, 1, axis=3)) - (north_flux - jnp.concatenate([zero_row, north_flux[:, :, :-1]], axis=2)) - (jnp.concatenate([below_flux, zero_level], axis=1) - jnp.concatenate([zero_level, below_flux], axis=1))

def slot_forcing(atm_state, weights, margins):

    def one_row(row_data):
        atm_row, slot_lists = row_data
        products = jnp.einsum('wpq,faq->wafp', weights, atm_row, precision=lax.Precision.HIGHEST)
        flat_table = products.reshape(WBLOCKS * ATM_ROW, 2 * BLOCK)
        source = jnp.arange(N_LON).astype(jnp.int32)[:, None, None]
        dest_ids = jnp.arange(N_LON).astype(jnp.int32)[None, :, None]
        table_rows = (slot_lists[2] * ATM_ROW + source * ATM_DEV + slot_lists[1]).astype(jnp.int32)
        values = jnp.take(flat_table, table_rows.reshape(-1), axis=0)
        target = jnp.where(slot_lists[0] >= 0, dest_ids * OCN_BLK + slot_lists[0], N_LON * OCN_BLK).astype(jnp.int32)
        block_sums = jax.ops.segment_sum(values, target.reshape(-1), num_segments=N_LON * OCN_BLK + 1)
        return block_sums[:-1]
    return lax.map(one_row, (atm_state.transpose(1, 0, 2, 3), margins.transpose(1, 0, 2, 3, 4)))

def slot_gradient(surface_blocks, weights, margins):

    def one_row(row_data):
        blocks_row, slot_lists = row_data
        source = jnp.arange(N_LON).astype(jnp.int32)[:, None, None]
        dest_ids = jnp.arange(N_LON).astype(jnp.int32)[None, :, None]
        live_slot = slot_lists[0] >= 0
        pick_rows = jnp.where(live_slot, dest_ids * OCN_BLK + slot_lists[0], 0).astype(jnp.int32)
        values = jnp.take(blocks_row, pick_rows.reshape(-1), axis=0) * live_slot.reshape(-1, 1).astype(jnp.float32)
        table_rows = (slot_lists[2] * ATM_ROW + source * ATM_DEV + slot_lists[1]).astype(jnp.int32)
        gathered = jax.ops.segment_sum(values, table_rows.reshape(-1), num_segments=WBLOCKS * ATM_ROW)
        gathered = gathered.reshape(WBLOCKS, ATM_ROW, 2, BLOCK)
        return jnp.einsum('wpq,wafp->faq', weights, gathered, precision=lax.Precision.HIGHEST)
    result = lax.map(one_row, (surface_blocks, margins.transpose(1, 0, 2, 3, 4)))
    return result.transpose(1, 0, 2, 3)

def blocks_to_field(blocks):
    shaped = blocks.reshape(N_LAT, N_LON, CLAT, CLON // BLOCK, 2, BLOCK)
    return shaped.transpose(4, 0, 2, 1, 3, 5).reshape(2, LATS, LONS)

def field_to_blocks(surface):
    shaped = surface.reshape(2, N_LAT, CLAT, N_LON, CLON // BLOCK, BLOCK)
    return shaped.transpose(1, 3, 2, 4, 0, 5).reshape(N_LAT, N_LON * OCN_BLK, 2 * BLOCK)

def reference(tracers, cotangent, land_mask, diffusion, velocity, weights, atm_state, margins):
    coeffs, ocean_mask = face_terms(land_mask, diffusion, velocity)
    surface = blocks_to_field(slot_forcing(atm_state, weights, margins)) * ocean_mask[0]
    force_full = jnp.concatenate([surface[:, None], jnp.zeros((2, LEV - 1, LATS, LONS), jnp.float32)], axis=1)
    quantity = tracers
    for step_index in range(STEPS):
        quantity = advance(quantity, coeffs) + force_full
    adjoint_map = jax.vjp(lambda inner: advance(inner, coeffs), jnp.zeros_like(cotangent))[1]
    adjoint = cotangent
    surface_sum = jnp.zeros_like(cotangent[:, 0])
    for step_index in range(STEPS):
        surface_sum = surface_sum + adjoint[:, 0]
        adjoint = adjoint_map(adjoint)[0]
    surface_adjoint = surface_sum * ocean_mask[0]
    gradient = slot_gradient(field_to_blocks(surface_adjoint), weights, margins)
    return (quantity, adjoint, gradient)
```

```python
import jax
import jax.numpy as jnp
from jax import lax
from jax.experimental import pallas as pl
from jax.experimental.pallas import tpu as pltpu
from jax.sharding import PartitionSpec as P

BLOCK = 128
STEPS = 4
HALO = STEPS
PER_LANES = BLOCK // HALO
GROUP = 4
f32 = jnp.float32
bf16 = jnp.bfloat16
VMEM_LIMIT = 48 * 1024 * 1024


def call(body, outs, scratch=(), flops=0, name=None):
    return pl.pallas_call(
        body,
        out_shape=[jax.ShapeDtypeStruct(s, f32) for s in outs],
        scratch_shapes=list(scratch),
        compiler_params=pltpu.CompilerParams(vmem_limit_bytes=VMEM_LIMIT),
        cost_estimate=pl.CostEstimate(flops=flops, bytes_accessed=1 << 20, transcendentals=0),
        name=name,
    )


def lanes(shape):
    return lax.broadcasted_iota(jnp.int32, shape, len(shape) - 1)


def rows(shape):
    return lax.broadcasted_iota(jnp.int32, shape, len(shape) - 2)


def turn(x, shift, axis):
    shift %= x.shape[axis]
    return pltpu.roll(x, shift, axis) if shift else x


def tile_fields(tracers, cotangent, land_mask, diffusion, velocity):
    levels = land_mask.shape[0]
    mask = [land_mask[level].astype(f32) for level in range(levels)]
    out = [tracers[f, level] for f in range(2) for level in range(levels)]
    out += [cotangent[f, level] for f in range(2) for level in range(levels)]
    out += [diffusion[0, level] * mask[level] for level in range(levels)]
    out += [velocity[0, level] * mask[level] for level in range(levels)]
    out += [diffusion[1, level] * mask[level] for level in range(levels)]
    out += [velocity[1, level] * mask[level] for level in range(levels)]
    out += [diffusion[2, level] * mask[level] * mask[level + 1] for level in range(levels - 1)]
    return out


def pack_columns(tracers, cotangent, land_mask, diffusion, velocity, to_west, to_east):
    fields = tile_fields(tracers, cotangent, land_mask, diffusion, velocity)
    shape = to_west.shape[1:]
    lane = lanes(shape)
    west = [jnp.zeros(shape, f32) for _ in range(to_west.shape[0])]
    east = [jnp.zeros(shape, f32) for _ in range(to_west.shape[0])]
    for i, field in enumerate(fields):
        part, at = divmod(i, PER_LANES)
        at *= HALO
        here = (lane >= at) & (lane < at + HALO)
        west[part] = jnp.where(here, turn(field[:, :BLOCK], at, 1), west[part])
        east[part] = jnp.where(here, turn(field[:, -BLOCK:], at + HALO, 1), east[part])
    for part in range(to_west.shape[0]):
        to_west[part] = west[part]
        to_east[part] = east[part]


def pack_rows(
    tracers, cotangent, land_mask, diffusion, velocity, from_west, from_east, side, to_north, to_south
):
    fields = tile_fields(tracers, cotangent, land_mask, diffusion, velocity)
    count = len(fields)
    half = to_north.shape[0]
    shape = from_west.shape[1:]
    lane = lanes(shape)
    tile_lat = shape[0]
    wide = []
    for i, field in enumerate(fields):
        part, at = divmod(i, PER_LANES)
        at *= HALO
        columns = jnp.where(
            lane < HALO,
            turn(from_east[part], -at, 1),
            jnp.where(lane >= BLOCK - HALO, turn(from_west[part], -at - HALO, 1), 0.0),
        )
        side[i] = columns
        wide.append(jnp.concatenate([field, columns], axis=1))
    row = rows((8, wide[0].shape[1]))
    for i in range(half):
        first = wide[i]
        second = wide[i + half] if i + half < count else jnp.zeros_like(first)
        to_north[i] = jnp.where(row < HALO, turn(first[tile_lat - 8 :], HALO, 0), second[tile_lat - 8 :])
        to_south[i] = jnp.where(row < HALO, first[:8], turn(second[:8], HALO, 0))


def widen(fields, side, from_north, from_south, wide):
    half = from_north.shape[0]
    tile_lat, tile_lon = fields[0].shape
    row = rows((8, from_north.shape[2]))
    for i, field in enumerate(fields):
        wide[i, :tile_lat, :tile_lon] = field
        wide[i, :tile_lat, tile_lon:] = side[i]
        if i < half:
            north, south = from_north[i], turn(from_south[i], HALO, 0)
        else:
            north, south = turn(from_north[i - half], HALO, 0), from_south[i - half]
        wide[i, tile_lat:, :] = jnp.where(row < HALO, north, south)


def eastward(x):
    return turn(x, -1, 1)


def westward(x):
    return turn(x, 1, 1)


def northward(x):
    return turn(x, -1, 0)


def southward(x):
    return turn(x, 1, 0)


def run_adjoint(
    tracers,
    cotangent,
    land_mask,
    diffusion,
    velocity,
    side,
    from_north,
    from_south,
    adjoint_out,
    blocks,
    coeffs,
    start,
    wide,
    state,
):
    levels, tile_lat, tile_lon = land_mask.shape
    fields = tile_fields(tracers, cotangent, land_mask, diffusion, velocity)
    widen(fields, side, from_north, from_south, wide)
    base = 4 * levels
    for f in range(2):
        for level in range(levels):
            start[f, level] = wide[f * levels + level]
    mask0 = None
    for level in range(levels):
        east_d, east_u = wide[base + level], wide[base + levels + level]
        north_d, north_u = wide[base + 2 * levels + level], wide[base + 3 * levels + level]
        mask = (east_d > 0.0).astype(f32)
        mask0 = mask if mask0 is None else mask0
        mask_e, mask_n = eastward(mask), northward(mask)
        east_k, east_v = east_d * mask_e, east_u * mask_e
        north_k, north_v = north_d * mask_n, north_u * mask_n
        coeffs[0, level] = jnp.maximum(east_v, 0.0) + east_k
        coeffs[1, level] = jnp.minimum(east_v, 0.0) - east_k
        coeffs[2, level] = jnp.maximum(north_v, 0.0) + north_k
        coeffs[3, level] = jnp.minimum(north_v, 0.0) - north_k
        coeffs[4, level] = wide[base + 4 * levels + level] if level < levels - 1 else jnp.zeros_like(mask)
        coeffs[5, level] = mask
    for f in range(2):
        surface = jnp.zeros((tile_lat, tile_lon), f32)
        for step in range(STEPS):
            above = None
            for level in range(levels):
                source = wide.at[(2 + f) * levels + level] if step == 0 else state.at[(step - 1) % 2, level]
                lam = source[...]
                if level == 0:
                    surface = surface + lam[:tile_lat, :tile_lon]
                step_x = eastward(lam) - lam
                step_y = northward(lam) - lam
                out = lam + coeffs[0, level] * step_x + westward(coeffs[1, level] * step_x)
                out = out + coeffs[2, level] * step_y + southward(coeffs[3, level] * step_y)
                if level < levels - 1:
                    if step == 0:
                        lower = wide[(2 + f) * levels + level + 1]
                    else:
                        lower = state[(step - 1) % 2, level + 1]
                    vertical = coeffs[4, level] * (lower - lam)
                    out = out + vertical
                if above is not None:
                    out = out - above
                above = vertical if level < levels - 1 else None
                if step == STEPS - 1:
                    adjoint_out[f, level] = out[:tile_lat, :tile_lon]
                else:
                    state[step % 2, level] = out
        surface = surface * mask0[:tile_lat, :tile_lon]
        halves = tile_lon // BLOCK
        for h in range(halves):
            at = (f * halves + h) * tile_lat
            blocks[at : at + tile_lat] = surface[:, h * BLOCK : (h + 1) * BLOCK]


def sum_forcing(received, forcing, to_north, to_south):
    tile_lat = forcing.shape[1]
    halves = forcing.shape[2] // BLOCK - 1
    total = received[0]
    for j in range(1, received.shape[0]):
        total = total + received[j]
    lane = lanes((tile_lat, BLOCK))
    packed = total[2 * halves * tile_lat :]
    for f in range(2):
        for h in range(halves):
            at = (f * halves + h) * tile_lat
            forcing[f, :, h * BLOCK : (h + 1) * BLOCK] = total[at : at + tile_lat]
        near = (lane < HALO) | (lane >= BLOCK - HALO)
        if f == 0:
            edge = packed
        else:
            edge = jnp.where(lane < HALO, turn(packed, -HALO, 1), turn(packed, HALO, 1))
        forcing[f, :, halves * BLOCK :] = jnp.where(near, edge, 0.0)
    row = rows((8, forcing.shape[2]))
    to_north[...] = jnp.where(row < HALO, turn(forcing[0, tile_lat - 8 :], HALO, 0), forcing[1, tile_lat - 8 :])
    to_south[...] = jnp.where(row < HALO, forcing[0, :8], turn(forcing[1, :8], HALO, 0))


def run_forward(coeffs, start, forcing, from_north, from_south, final, state):
    levels = coeffs.shape[1]
    tile_lat, tile_lon = final.shape[2:]
    row = rows((8, forcing.shape[2]))
    mask = None
    for f in range(2):
        if f == 0:
            north, south = from_north[...], turn(from_south[...], HALO, 0)
        else:
            north, south = turn(from_north[...], HALO, 0), from_south[...]
        force = jnp.concatenate([forcing[f], jnp.where(row < HALO, north, south)], axis=0)
        force = force * coeffs[5, 0]
        for step in range(STEPS):
            above = None
            for level in range(levels):
                read = (lambda n: start[f, n]) if step == 0 else (lambda n: state[(step - 1) % 2, n])
                theta = read(level)
                east_flux = coeffs[0, level] * theta + coeffs[1, level] * eastward(theta)
                north_flux = coeffs[2, level] * theta + coeffs[3, level] * northward(theta)
                out = theta - (east_flux - westward(east_flux)) - (north_flux - southward(north_flux))
                if level < levels - 1:
                    vertical = coeffs[4, level] * (theta - read(level + 1))
                    out = out - vertical
                if above is not None:
                    out = out + above
                above = vertical if level < levels - 1 else None
                if level == 0:
                    out = out + force
                if step == STEPS - 1:
                    final[f, level] = out[:tile_lat, :tile_lon]
                else:
                    state[step % 2, level] = out


def split(x):
    high = x.astype(bf16)
    return high, (x - high.astype(f32)).astype(bf16)


def as_column(ids):
    n = ids.shape[1]
    shape = (n, n)
    return jnp.sum(
        jnp.where(rows(shape) == lanes(shape), jnp.broadcast_to(ids.astype(f32), shape), 0.0),
        axis=1,
        keepdims=True,
    )


def one_hot(where):
    return jnp.where(where, 1.0, 0.0).astype(bf16)


def apply_weights(weights, vectors, picks, total, transposed):
    blocks = weights.shape[0]
    slots = vectors.shape[0]
    total[...] = jnp.zeros_like(total)

    def group(g, carry):
        left, right = [[], []], []
        for u in range(GROUP):
            w = g * GROUP + u
            here = picks[...] == lax.convert_element_type(w.astype(f32), bf16)
            here = jnp.concatenate([here, here], axis=1)
            for f in range(2):
                own = vectors[:, f * 2 * BLOCK : (f + 1) * 2 * BLOCK]
                left[f].append(jnp.where(here, own, jnp.zeros_like(own)))
            high, low = split(weights[w])
            if transposed:
                both = jnp.concatenate([high, low], axis=1)
                right.append(jnp.concatenate([both, both], axis=0))
            else:
                both = jnp.concatenate([high, low], axis=0)
                right.append(jnp.concatenate([both, both], axis=1))
        right = jnp.concatenate(right, axis=0 if transposed else 1)
        contract = (((1,), (0 if transposed else 1,)), ((), ()))
        for f in range(2):
            product = lax.dot_general(
                jnp.concatenate(left[f], axis=1), right, contract, preferred_element_type=f32
            )
            total[f] += product
        return carry

    lax.fori_loop(0, blocks // GROUP, group, 0)


def slot_columns(ids, out_dtype=f32):
    return jnp.concatenate([as_column(ids[k : k + 1, :]) for k in range(ids.shape[0])], axis=0)


def weigh(atm_state, margins, weights, payload, vectors, picks, total):
    lon_count, cap = margins.shape[3:]
    slots = lon_count * cap
    atm = atm_state.shape[2]
    tile_lat = payload.shape[1] // 5
    ocean, atm_ids, block_ids = (margins[n, 0, 0] for n in range(3))
    picks[...] = jnp.broadcast_to(slot_columns(block_ids), (slots, BLOCK)).astype(bf16)
    parts = [part for f in range(2) for part in split(atm_state[f, 0])]
    table = jnp.concatenate(parts, axis=1)
    pick = one_hot(slot_columns(atm_ids).astype(jnp.int32) == lanes((slots, atm)))
    vectors[...] = jnp.dot(pick, table, preferred_element_type=f32).astype(bf16)
    apply_weights(weights, vectors, picks, total, False)
    ocean_blocks = 2 * tile_lat
    order = rows((ocean_blocks, cap))
    order = (order % tile_lat) * 2 + order // tile_lat
    lane = lanes((tile_lat, BLOCK))
    sums = []
    for k in range(lon_count):
        place = one_hot(jnp.broadcast_to(ocean[k : k + 1, :], (ocean_blocks, cap)) == order)
        parts = []
        for f in range(2):
            value = total[f, k * cap : (k + 1) * cap]
            parts += split(value[:, :BLOCK] + value[:, BLOCK:])
        product = jnp.dot(place, jnp.concatenate(parts, axis=1), preferred_element_type=f32)
        sums.append(
            [product[:, 2 * f * BLOCK : (2 * f + 1) * BLOCK] + product[:, (2 * f + 1) * BLOCK : (2 * f + 2) * BLOCK]
             for f in range(2)]
        )
        for f in range(2):
            payload[k, f * ocean_blocks : (f + 1) * ocean_blocks] = sums[k][f]
    for k in range(lon_count):
        after, before = sums[(k + 1) % lon_count], sums[(k - 1) % lon_count]
        edge = jnp.zeros((tile_lat, BLOCK), f32)
        for f in range(2):
            at = f * HALO
            edge = jnp.where((lane >= at) & (lane < at + HALO), turn(after[f][:tile_lat], at, 1), edge)
            end = BLOCK - at
            edge = jnp.where((lane >= end - HALO) & (lane < end), turn(before[f][tile_lat:], -at, 1), edge)
        payload[k, 2 * ocean_blocks :] = edge


def unweigh(gathered, margins, weights, gradient, vectors, picks, total):
    lon_count, cap = margins.shape[3:]
    slots = lon_count * cap
    atm = gradient.shape[2]
    ocean_blocks = gathered.shape[1] // 2
    tile_lat = ocean_blocks // 2
    ocean, atm_ids, block_ids = (margins[n, 0, 0] for n in range(3))
    picks[...] = jnp.broadcast_to(slot_columns(block_ids), (slots, BLOCK)).astype(bf16)
    order = lanes((cap, ocean_blocks))
    order = (order % tile_lat) * 2 + order // tile_lat
    for k in range(lon_count):
        pick = one_hot(as_column(ocean[k : k + 1, :]).astype(jnp.int32) == order)
        parts = [
            part for f in range(2) for part in split(gathered[k, f * ocean_blocks : (f + 1) * ocean_blocks])
        ]
        vectors[k * cap : (k + 1) * cap] = jnp.dot(
            pick, jnp.concatenate(parts, axis=1), preferred_element_type=f32
        ).astype(bf16)
    apply_weights(weights, vectors, picks, total, True)
    place = jnp.concatenate(
        [
            one_hot(jnp.broadcast_to(atm_ids[k : k + 1, :], (atm, cap)) == rows((atm, cap)))
            for k in range(lon_count)
        ],
        axis=1,
    )
    parts = [part for f in range(2) for part in split(total[f, :, :BLOCK] + total[f, :, BLOCK:])]
    product = jnp.dot(place, jnp.concatenate(parts, axis=1), preferred_element_type=f32)
    for f in range(2):
        at = 2 * f * BLOCK
        gradient[f, 0] = product[:, at : at + BLOCK] + product[:, at + BLOCK : at + 2 * BLOCK]


def on_device(tracers, cotangent, land_mask, diffusion, velocity, weights, atm_state, margins):
    levels, tile_lat, tile_lon = land_mask.shape
    lon_count, lat_count = lax.axis_size("lon"), lax.axis_size("lat")
    slots = lon_count * margins.shape[4]
    halves = tile_lon // BLOCK
    wide_lat, wide_lon = tile_lat + 8, tile_lon + BLOCK
    count = 9 * levels - 1
    parts = -(-count // PER_LANES)
    pairs = -(-count // 2)
    to_next = [(i, (i + 1) % lon_count) for i in range(lon_count)]
    to_prev = [(j, i) for i, j in to_next]
    up = [(i, i + 1) for i in range(lat_count - 1)]
    down = [(j, i) for i, j in up]
    inputs = (tracers, cotangent, land_mask, diffusion, velocity)

    message = (parts, tile_lat, BLOCK)
    to_west, to_east = call(pack_columns, [message, message], name="pack_columns")(*inputs)
    from_east = lax.ppermute(to_west, "lon", to_prev)
    from_west = lax.ppermute(to_east, "lon", to_next)

    coupling_scratch = [
        pltpu.VMEM((slots, 4 * BLOCK), bf16),
        pltpu.VMEM((slots, BLOCK), bf16),
        pltpu.VMEM((2, slots, 2 * BLOCK), f32),
    ]
    coupling_flops = 4 * slots * weights.shape[0] * 4 * BLOCK * BLOCK * 2
    payload_rows = (2 * halves + 1) * tile_lat
    (payload,) = call(
        weigh, [(lon_count, payload_rows, BLOCK)], coupling_scratch, coupling_flops, name="weigh"
    )(atm_state, margins, weights)
    received = lax.all_to_all(payload, "lon", split_axis=0, concat_axis=0, tiled=True)

    message = (pairs, 8, wide_lon)
    side, to_north, to_south = call(
        pack_rows, [(count, tile_lat, BLOCK), message, message], name="pack_rows"
    )(*inputs, from_west, from_east)
    from_south = lax.ppermute(to_north, "lat", up)
    from_north = lax.ppermute(to_south, "lat", down)

    wide = (wide_lat, wide_lon)
    adjoint, blocks, coeffs, start = call(
        run_adjoint,
        [
            cotangent.shape,
            (2 * halves * tile_lat, BLOCK),
            (6, levels, *wide),
            (2, levels, *wide),
        ],
        [pltpu.VMEM((count, *wide), f32), pltpu.VMEM((2, levels, *wide), f32)],
        name="run_adjoint",
    )(*inputs, side, from_north, from_south)
    gathered = lax.all_gather(blocks, "lon", axis=0)

    forcing, to_north, to_south = call(
        sum_forcing, [(2, tile_lat, wide_lon), (8, wide_lon), (8, wide_lon)], name="sum_forcing"
    )(received)
    force_south = lax.ppermute(to_north, "lat", up)
    force_north = lax.ppermute(to_south, "lat", down)
    (final,) = call(
        run_forward, [tracers.shape], [pltpu.VMEM((2, levels, *wide), f32)], name="run_forward"
    )(coeffs, start, forcing, force_north, force_south)

    (gradient,) = call(
        unweigh, [atm_state.shape], coupling_scratch, coupling_flops, name="unweigh"
    )(gathered, margins, weights)
    return (final, adjoint, gradient)


def solution(mesh):
    return jax.shard_map(
        on_device,
        mesh=mesh,
        in_specs=(
            P(None, None, "lat", "lon"),
            P(None, None, "lat", "lon"),
            P(None, "lat", "lon"),
            P(None, None, "lat", "lon"),
            P(None, None, "lat", "lon"),
            P(),
            P(None, "lat", "lon", None),
            P(None, "lat", "lon", None, None),
        ),
        out_specs=(
            P(None, None, "lat", "lon"),
            P(None, None, "lat", "lon"),
            P(None, "lat", "lon", None),
        ),
        check_vma=False,
    )
```

```python
import jax
import jax.numpy as jnp
from jax import lax
from jax.experimental import pallas as pl
from jax.experimental.pallas import tpu as pltpu
from jax.sharding import PartitionSpec as P

BLOCK = 128
STEPS = 4
HALO = STEPS
PER_LANES = BLOCK // HALO
GROUP = 4
f32 = jnp.float32
bf16 = jnp.bfloat16
VMEM_LIMIT = 48 * 1024 * 1024


def call(body, outs, scratch=(), flops=0, name=None, inputs=0, far=()):
    outs = [s if isinstance(s, jax.ShapeDtypeStruct) else jax.ShapeDtypeStruct(s, f32) for s in outs]
    near = pl.BlockSpec(memory_space=pltpu.VMEM)
    return pl.pallas_call(
        body,
        out_shape=outs,
        in_specs=[pl.BlockSpec(memory_space=pl.ANY) if n in far else near for n in range(inputs)],
        out_specs=[near] * len(outs),
        scratch_shapes=list(scratch),
        compiler_params=pltpu.CompilerParams(vmem_limit_bytes=VMEM_LIMIT),
        cost_estimate=pl.CostEstimate(flops=flops, bytes_accessed=1 << 20, transcendentals=0),
        name=name,
    )


def lanes(shape):
    return lax.broadcasted_iota(jnp.int32, shape, len(shape) - 1)


def rows(shape):
    return lax.broadcasted_iota(jnp.int32, shape, len(shape) - 2)


def turn(x, shift, axis):
    shift %= x.shape[axis]
    return pltpu.roll(x, shift, axis) if shift else x


def tile_fields(tracers, cotangent, land_mask, diffusion, velocity):
    levels = land_mask.shape[0]
    mask = [land_mask[level].astype(f32) for level in range(levels)]
    out = [tracers[f, level] for f in range(2) for level in range(levels)]
    out += [cotangent[f, level] for f in range(2) for level in range(levels)]
    out += [diffusion[0, level] * mask[level] for level in range(levels)]
    out += [velocity[0, level] * mask[level] for level in range(levels)]
    out += [diffusion[1, level] * mask[level] for level in range(levels)]
    out += [velocity[1, level] * mask[level] for level in range(levels)]
    out += [diffusion[2, level] * mask[level] * mask[level + 1] for level in range(levels - 1)]
    return out


def pack_columns(tracers, cotangent, land_mask, diffusion, velocity, to_west, to_east):
    fields = tile_fields(tracers, cotangent, land_mask, diffusion, velocity)
    shape = to_west.shape[1:]
    lane = lanes(shape)
    west = [jnp.zeros(shape, f32) for _ in range(to_west.shape[0])]
    east = [jnp.zeros(shape, f32) for _ in range(to_west.shape[0])]
    for i, field in enumerate(fields):
        part, at = divmod(i, PER_LANES)
        at *= HALO
        here = (lane >= at) & (lane < at + HALO)
        west[part] = jnp.where(here, turn(field[:, :BLOCK], at, 1), west[part])
        east[part] = jnp.where(here, turn(field[:, -BLOCK:], at + HALO, 1), east[part])
    for part in range(to_west.shape[0]):
        to_west[part] = west[part]
        to_east[part] = east[part]


def pack_rows(
    tracers, cotangent, land_mask, diffusion, velocity, from_west, from_east, side, to_north, to_south
):
    fields = tile_fields(tracers, cotangent, land_mask, diffusion, velocity)
    count = len(fields)
    half = to_north.shape[0]
    shape = from_west.shape[1:]
    lane = lanes(shape)
    tile_lat = shape[0]
    wide = []
    for i, field in enumerate(fields):
        part, at = divmod(i, PER_LANES)
        at *= HALO
        columns = jnp.where(
            lane < HALO,
            turn(from_east[part], -at, 1),
            jnp.where(lane >= BLOCK - HALO, turn(from_west[part], -at - HALO, 1), 0.0),
        )
        side[i] = columns
        wide.append(jnp.concatenate([field, columns], axis=1))
    row = rows((8, wide[0].shape[1]))
    for i in range(half):
        first = wide[i]
        second = wide[i + half] if i + half < count else jnp.zeros_like(first)
        to_north[i] = jnp.where(row < HALO, turn(first[tile_lat - 8 :], HALO, 0), second[tile_lat - 8 :])
        to_south[i] = jnp.where(row < HALO, first[:8], turn(second[:8], HALO, 0))


def widen(fields, side, from_north, from_south, wide):
    half = from_north.shape[0]
    tile_lat, tile_lon = fields[0].shape
    row = rows((8, from_north.shape[2]))
    for i, field in enumerate(fields):
        wide[i, :tile_lat, :tile_lon] = field
        wide[i, :tile_lat, tile_lon:] = side[i]
        if i < half:
            north, south = from_north[i], turn(from_south[i], HALO, 0)
        else:
            north, south = turn(from_north[i - half], HALO, 0), from_south[i - half]
        wide[i, tile_lat:, :] = jnp.where(row < HALO, north, south)


def eastward(x):
    return turn(x, -1, 1)


def westward(x):
    return turn(x, 1, 1)


def northward(x):
    return turn(x, -1, 0)


def southward(x):
    return turn(x, 1, 0)


def run_adjoint(
    tracers,
    cotangent,
    land_mask,
    diffusion,
    velocity,
    side,
    from_north,
    from_south,
    adjoint_out,
    blocks,
    coeffs,
    start,
    wide,
    state,
):
    levels, tile_lat, tile_lon = land_mask.shape
    fields = tile_fields(tracers, cotangent, land_mask, diffusion, velocity)
    widen(fields, side, from_north, from_south, wide)
    base = 4 * levels
    for f in range(2):
        for level in range(levels):
            start[f, level] = wide[f * levels + level]
    mask0 = None
    for level in range(levels):
        east_d, east_u = wide[base + level], wide[base + levels + level]
        north_d, north_u = wide[base + 2 * levels + level], wide[base + 3 * levels + level]
        mask = (east_d > 0.0).astype(f32)
        mask0 = mask if mask0 is None else mask0
        mask_e, mask_n = eastward(mask), northward(mask)
        east_k, east_v = east_d * mask_e, east_u * mask_e
        north_k, north_v = north_d * mask_n, north_u * mask_n
        coeffs[0, level] = jnp.maximum(east_v, 0.0) + east_k
        coeffs[1, level] = jnp.minimum(east_v, 0.0) - east_k
        coeffs[2, level] = jnp.maximum(north_v, 0.0) + north_k
        coeffs[3, level] = jnp.minimum(north_v, 0.0) - north_k
        coeffs[4, level] = wide[base + 4 * levels + level] if level < levels - 1 else jnp.zeros_like(mask)
        coeffs[5, level] = mask
    for f in range(2):
        surface = jnp.zeros((tile_lat, tile_lon), f32)
        for step in range(STEPS):
            above = None
            for level in range(levels):
                source = wide.at[(2 + f) * levels + level] if step == 0 else state.at[(step - 1) % 2, level]
                lam = source[...]
                if level == 0:
                    surface = surface + lam[:tile_lat, :tile_lon]
                step_x = eastward(lam) - lam
                step_y = northward(lam) - lam
                out = lam + coeffs[0, level] * step_x + westward(coeffs[1, level] * step_x)
                out = out + coeffs[2, level] * step_y + southward(coeffs[3, level] * step_y)
                if level < levels - 1:
                    if step == 0:
                        lower = wide[(2 + f) * levels + level + 1]
                    else:
                        lower = state[(step - 1) % 2, level + 1]
                    vertical = coeffs[4, level] * (lower - lam)
                    out = out + vertical
                if above is not None:
                    out = out - above
                above = vertical if level < levels - 1 else None
                if step == STEPS - 1:
                    adjoint_out[f, level] = out[:tile_lat, :tile_lon]
                else:
                    state[step % 2, level] = out
        surface = surface * mask0[:tile_lat, :tile_lon]
        halves = tile_lon // BLOCK
        for h in range(halves):
            at = (f * halves + h) * tile_lat
            for k in range(blocks.shape[0]):
                blocks[k, at : at + tile_lat] = surface[:, h * BLOCK : (h + 1) * BLOCK]


def sum_forcing(received, forcing, to_north, to_south):
    tile_lat = forcing.shape[1]
    halves = forcing.shape[2] // BLOCK - 1
    total = received[0]
    for j in range(1, received.shape[0]):
        total = total + received[j]
    lane = lanes((tile_lat, BLOCK))
    packed = total[2 * halves * tile_lat :]
    for f in range(2):
        for h in range(halves):
            at = (f * halves + h) * tile_lat
            forcing[f, :, h * BLOCK : (h + 1) * BLOCK] = total[at : at + tile_lat]
        near = (lane < HALO) | (lane >= BLOCK - HALO)
        if f == 0:
            edge = packed
        else:
            edge = jnp.where(lane < HALO, turn(packed, -HALO, 1), turn(packed, HALO, 1))
        forcing[f, :, halves * BLOCK :] = jnp.where(near, edge, 0.0)
    row = rows((8, forcing.shape[2]))
    to_north[...] = jnp.where(row < HALO, turn(forcing[0, tile_lat - 8 :], HALO, 0), forcing[1, tile_lat - 8 :])
    to_south[...] = jnp.where(row < HALO, forcing[0, :8], turn(forcing[1, :8], HALO, 0))


def run_forward(coeffs, start, forcing, from_north, from_south, final, state):
    levels = coeffs.shape[1]
    tile_lat, tile_lon = final.shape[2:]
    row = rows((8, forcing.shape[2]))
    mask = None
    for f in range(2):
        if f == 0:
            north, south = from_north[...], turn(from_south[...], HALO, 0)
        else:
            north, south = turn(from_north[...], HALO, 0), from_south[...]
        force = jnp.concatenate([forcing[f], jnp.where(row < HALO, north, south)], axis=0)
        force = force * coeffs[5, 0]
        for step in range(STEPS):
            above = None
            for level in range(levels):
                read = (lambda n: start[f, n]) if step == 0 else (lambda n: state[(step - 1) % 2, n])
                theta = read(level)
                east_flux = coeffs[0, level] * theta + coeffs[1, level] * eastward(theta)
                north_flux = coeffs[2, level] * theta + coeffs[3, level] * northward(theta)
                out = theta - (east_flux - westward(east_flux)) - (north_flux - southward(north_flux))
                if level < levels - 1:
                    vertical = coeffs[4, level] * (theta - read(level + 1))
                    out = out - vertical
                if above is not None:
                    out = out + above
                above = vertical if level < levels - 1 else None
                if level == 0:
                    out = out + force
                if step == STEPS - 1:
                    final[f, level] = out[:tile_lat, :tile_lon]
                else:
                    state[step % 2, level] = out


def split(x):
    high = x.astype(bf16)
    return high, (x - high.astype(f32)).astype(bf16)


def as_column(ids):
    n = ids.shape[1]
    shape = (n, n)
    return jnp.sum(
        jnp.where(rows(shape) == lanes(shape), jnp.broadcast_to(ids.astype(f32), shape), 0.0),
        axis=1,
        keepdims=True,
    )


def one_hot(where):
    return jnp.where(where, 1.0, 0.0).astype(bf16)


def fetch_group(weights, first, held, arrived, g):
    return pltpu.make_async_copy(
        weights.at[pl.ds((first + g) * GROUP, GROUP)], held.at[g], arrived.at[g]
    )


def fetch_weights(weights, first, held, arrived):
    for g in range(held.shape[0]):
        fetch_group(weights, first, held, arrived, g).start()


def apply_weights(weights, first, held, arrived, vectors, picks, total, transposed):
    def group(g, carry):
        left, right = [[], []], []
        fetch_group(weights, first, held, arrived, g).wait()
        for u in range(GROUP):
            w = (first + g) * GROUP + u
            here = picks[...] == lax.convert_element_type(w.astype(f32), bf16)
            here = jnp.concatenate([here, here], axis=1)
            for f in range(2):
                own = vectors[:, f * 2 * BLOCK : (f + 1) * 2 * BLOCK]
                left[f].append(jnp.where(here, own, jnp.zeros_like(own)))
            high, low = split(held[g, u])
            if transposed:
                both = jnp.concatenate([high, low], axis=1)
                right.append(jnp.concatenate([both, both], axis=0))
            else:
                both = jnp.concatenate([high, low], axis=0)
                right.append(jnp.concatenate([both, both], axis=1))
        right = jnp.concatenate(right, axis=0 if transposed else 1)
        contract = (((1,), (0 if transposed else 1,)), ((), ()))
        for f in range(2):
            product = lax.dot_general(
                jnp.concatenate(left[f], axis=1), right, contract, preferred_element_type=f32
            )
            total[f] += product
        return carry

    lax.fori_loop(0, held.shape[0], group, 0)


def slot_columns(ids, out_dtype=f32):
    return jnp.concatenate([as_column(ids[k : k + 1, :]) for k in range(ids.shape[0])], axis=0)


def weigh_first(atm_state, margins, weights, after, vectors, picks, total, held, arrived):
    lon_count, cap = margins.shape[3:]
    slots = lon_count * cap
    atm = atm_state.shape[2]
    fetch_weights(weights, 0, held, arrived)
    atm_ids, block_ids = (margins[n, 0, 0] for n in (1, 2))
    picks[...] = jnp.broadcast_to(slot_columns(block_ids), (slots, BLOCK)).astype(bf16)
    parts = [part for f in range(2) for part in split(atm_state[f, 0])]
    table = jnp.concatenate(parts, axis=1)
    pick = one_hot(slot_columns(atm_ids).astype(jnp.int32) == lanes((slots, atm)))
    vectors[...] = jnp.dot(pick, table, preferred_element_type=f32).astype(bf16)
    total[...] = jnp.zeros_like(total)
    apply_weights(weights, 0, held, arrived, vectors, picks, total, False)


def weigh_rest(vectors, picks, begun, margins, weights, after, payload, total, held, arrived):
    lon_count, cap = margins.shape[3:]
    tile_lat = payload.shape[1] // 5
    first = weights.shape[0] // GROUP - held.shape[0]
    fetch_weights(weights, first, held, arrived)
    ocean = margins[0, 0, 0]
    total[...] = begun[...]
    apply_weights(weights, first, held, arrived, vectors, picks, total, False)
    ocean_blocks = 2 * tile_lat
    order = rows((ocean_blocks, cap))
    order = (order % tile_lat) * 2 + order // tile_lat
    lane = lanes((tile_lat, BLOCK))
    sums = []
    for k in range(lon_count):
        place = one_hot(jnp.broadcast_to(ocean[k : k + 1, :], (ocean_blocks, cap)) == order)
        parts = []
        for f in range(2):
            value = total[f, k * cap : (k + 1) * cap]
            parts += split(value[:, :BLOCK] + value[:, BLOCK:])
        product = jnp.dot(place, jnp.concatenate(parts, axis=1), preferred_element_type=f32)
        sums.append(
            [product[:, 2 * f * BLOCK : (2 * f + 1) * BLOCK] + product[:, (2 * f + 1) * BLOCK : (2 * f + 2) * BLOCK]
             for f in range(2)]
        )
        for f in range(2):
            payload[k, f * ocean_blocks : (f + 1) * ocean_blocks] = sums[k][f]
    for k in range(lon_count):
        after, before = sums[(k + 1) % lon_count], sums[(k - 1) % lon_count]
        edge = jnp.zeros((tile_lat, BLOCK), f32)
        for f in range(2):
            at = f * HALO
            edge = jnp.where((lane >= at) & (lane < at + HALO), turn(after[f][:tile_lat], at, 1), edge)
            end = BLOCK - at
            edge = jnp.where((lane >= end - HALO) & (lane < end), turn(before[f][tile_lat:], -at, 1), edge)
        payload[k, 2 * ocean_blocks :] = edge


def unweigh(gathered, margins, weights, gradient, vectors, picks, total, held, arrived):
    fetch_weights(weights, 0, held, arrived)
    lon_count, cap = margins.shape[3:]
    slots = lon_count * cap
    atm = gradient.shape[2]
    ocean_blocks = gathered.shape[1] // 2
    tile_lat = ocean_blocks // 2
    ocean, atm_ids, block_ids = (margins[n, 0, 0] for n in range(3))
    picks[...] = jnp.broadcast_to(slot_columns(block_ids), (slots, BLOCK)).astype(bf16)
    order = lanes((cap, ocean_blocks))
    order = (order % tile_lat) * 2 + order // tile_lat
    for k in range(lon_count):
        pick = one_hot(as_column(ocean[k : k + 1, :]).astype(jnp.int32) == order)
        parts = [
            part for f in range(2) for part in split(gathered[k, f * ocean_blocks : (f + 1) * ocean_blocks])
        ]
        vectors[k * cap : (k + 1) * cap] = jnp.dot(
            pick, jnp.concatenate(parts, axis=1), preferred_element_type=f32
        ).astype(bf16)
    total[...] = jnp.zeros_like(total)
    apply_weights(weights, 0, held, arrived, vectors, picks, total, True)
    place = jnp.concatenate(
        [
            one_hot(jnp.broadcast_to(atm_ids[k : k + 1, :], (atm, cap)) == rows((atm, cap)))
            for k in range(lon_count)
        ],
        axis=1,
    )
    parts = [part for f in range(2) for part in split(total[f, :, :BLOCK] + total[f, :, BLOCK:])]
    product = jnp.dot(place, jnp.concatenate(parts, axis=1), preferred_element_type=f32)
    for f in range(2):
        at = 2 * f * BLOCK
        gradient[f, 0] = product[:, at : at + BLOCK] + product[:, at + BLOCK : at + 2 * BLOCK]


def on_device(tracers, cotangent, land_mask, diffusion, velocity, weights, atm_state, margins):
    levels, tile_lat, tile_lon = land_mask.shape
    lon_count, lat_count = lax.axis_size("lon"), lax.axis_size("lat")
    slots = lon_count * margins.shape[4]
    halves = tile_lon // BLOCK
    wide_lat, wide_lon = tile_lat + 8, tile_lon + BLOCK
    count = 9 * levels - 1
    parts = -(-count // PER_LANES)
    pairs = -(-count // 2)
    to_next = [(i, (i + 1) % lon_count) for i in range(lon_count)]
    to_prev = [(j, i) for i, j in to_next]
    up = [(i, i + 1) for i in range(lat_count - 1)]
    down = [(j, i) for i, j in up]
    inputs = (tracers, cotangent, land_mask, diffusion, velocity)

    message = (parts, tile_lat, BLOCK)
    to_west, to_east = call(pack_columns, [message, message], name="pack_columns", inputs=5)(*inputs)
    from_east = lax.ppermute(to_west, "lon", to_prev)
    from_west = lax.ppermute(to_east, "lon", to_next)

    groups = weights.shape[0] // GROUP
    vectors = jax.ShapeDtypeStruct((slots, 4 * BLOCK), bf16)
    picks = jax.ShapeDtypeStruct((slots, BLOCK), bf16)
    total = jax.ShapeDtypeStruct((2, slots, 2 * BLOCK), f32)

    def held(n):
        return [pltpu.VMEM((n, GROUP, BLOCK, BLOCK), f32), pltpu.SemaphoreType.DMA((n,))]

    def in_vmem(s):
        return pltpu.VMEM(s.shape, s.dtype)

    coupling_flops = 4 * slots * weights.shape[0] * 4 * BLOCK * BLOCK * 2
    begun = call(
        weigh_first,
        [vectors, picks, total],
        held(groups // 2),
        coupling_flops // 2,
        name="weigh_first",
        inputs=4,
        far=(2, 3),
    )(atm_state, margins, weights, to_west)

    message = (pairs, 8, wide_lon)
    side, to_north, to_south = call(
        pack_rows, [(count, tile_lat, BLOCK), message, message], name="pack_rows", inputs=7
    )(*inputs, from_west, from_east)
    from_south = lax.ppermute(to_north, "lat", up)
    from_north = lax.ppermute(to_south, "lat", down)

    payload_rows = (2 * halves + 1) * tile_lat
    (payload,) = call(
        weigh_rest,
        [(lon_count, payload_rows, BLOCK)],
        [in_vmem(total), *held(groups - groups // 2)],
        coupling_flops // 2,
        name="weigh_rest",
        inputs=6,
        far=(4, 5),
    )(*begun, margins, weights, to_north)
    received = lax.all_to_all(payload, "lon", split_axis=0, concat_axis=0, tiled=True)

    wide = (wide_lat, wide_lon)
    adjoint, blocks, coeffs, start = call(
        run_adjoint,
        [
            cotangent.shape,
            (lon_count, 2 * halves * tile_lat, BLOCK),
            (6, levels, *wide),
            (2, levels, *wide),
        ],
        [pltpu.VMEM((count, *wide), f32), pltpu.VMEM((2, levels, *wide), f32)],
        name="run_adjoint",
        inputs=8,
    )(*inputs, side, from_north, from_south)
    gathered = lax.all_to_all(blocks, "lon", split_axis=0, concat_axis=0, tiled=True)

    forcing, to_north, to_south = call(
        sum_forcing,
        [(2, tile_lat, wide_lon), (8, wide_lon), (8, wide_lon)],
        name="sum_forcing",
        inputs=1,
    )(received)
    force_south = lax.ppermute(to_north, "lat", up)
    force_north = lax.ppermute(to_south, "lat", down)
    (final,) = call(
        run_forward,
        [tracers.shape],
        [pltpu.VMEM((2, levels, *wide), f32)],
        name="run_forward",
        inputs=5,
    )(coeffs, start, forcing, force_north, force_south)

    (gradient,) = call(
        unweigh,
        [atm_state.shape],
        [in_vmem(vectors), in_vmem(picks), in_vmem(total), *held(groups)],
        coupling_flops,
        name="unweigh",
        inputs=3,
        far=(2,),
    )(gathered, margins, weights)
    return (final, adjoint, gradient)


def solution(mesh):
    return jax.shard_map(
        on_device,
        mesh=mesh,
        in_specs=(
            P(None, None, "lat", "lon"),
            P(None, None, "lat", "lon"),
            P(None, "lat", "lon"),
            P(None, None, "lat", "lon"),
            P(None, None, "lat", "lon"),
            P(),
            P(None, "lat", "lon", None),
            P(None, "lat", "lon", None, None),
        ),
        out_specs=(
            P(None, None, "lat", "lon"),
            P(None, None, "lat", "lon"),
            P(None, "lat", "lon", None),
        ),
        check_vma=False,
    )
```

```python
import functools

import jax
import jax.numpy as jnp
from jax import lax
from jax.experimental import pallas as pl
from jax.experimental.pallas import tpu as pltpu
from jax.sharding import PartitionSpec as P

BLOCK = 128
STEPS = 4
HALO = STEPS
PER_LANES = BLOCK // HALO
GROUP = 4
f32 = jnp.float32
bf16 = jnp.bfloat16
VMEM_LIMIT = 48 * 1024 * 1024


def call(body, outs, scratch=(), flops=0, name=None, inputs=0, far=()):
    outs = [s if isinstance(s, jax.ShapeDtypeStruct) else jax.ShapeDtypeStruct(s, f32) for s in outs]
    near = pl.BlockSpec(memory_space=pltpu.VMEM)
    kernel = pl.pallas_call(
        body,
        out_shape=outs,
        in_specs=[pl.BlockSpec(memory_space=pltpu.HBM) if n in far else near for n in range(inputs)],
        out_specs=[near] * len(outs),
        scratch_shapes=list(scratch),
        compiler_params=pltpu.CompilerParams(vmem_limit_bytes=VMEM_LIMIT),
        cost_estimate=pl.CostEstimate(flops=flops, bytes_accessed=1 << 20, transcendentals=0),
        name=name,
    )

    def run(*args):
        return kernel(
            *(pltpu.with_memory_space_constraint(x, pltpu.HBM) if n in far else x for n, x in enumerate(args))
        )

    return run


def lanes(shape):
    return lax.broadcasted_iota(jnp.int32, shape, len(shape) - 1)


def rows(shape):
    return lax.broadcasted_iota(jnp.int32, shape, len(shape) - 2)


def turn(x, shift, axis):
    shift %= x.shape[axis]
    return pltpu.roll(x, shift, axis) if shift else x


def tile_fields(tracers, cotangent, land_mask, diffusion, velocity):
    levels = land_mask.shape[0]
    mask = [land_mask[level].astype(f32) for level in range(levels)]
    out = [tracers[f, level] for f in range(2) for level in range(levels)]
    out += [cotangent[f, level] for f in range(2) for level in range(levels)]
    out += [diffusion[0, level] * mask[level] for level in range(levels)]
    out += [velocity[0, level] * mask[level] for level in range(levels)]
    out += [diffusion[1, level] * mask[level] for level in range(levels)]
    out += [velocity[1, level] * mask[level] for level in range(levels)]
    out += [diffusion[2, level] * mask[level] * mask[level + 1] for level in range(levels - 1)]
    return out


def fetch(pairs, arrived):
    copies = [pltpu.make_async_copy(src, dst, arrived.at[n]) for n, (src, dst) in enumerate(pairs)]
    for copy in copies:
        copy.start()
    return copies


def pack_columns(*refs):
    inputs, (fields, to_west, to_east), scratch = refs[:5], refs[5:8], refs[8:]
    for copy in fetch(zip(inputs, scratch[:5]), scratch[5]):
        copy.wait()
    shape = to_west.shape[1:]
    lane = lanes(shape)
    west = [jnp.zeros(shape, f32) for _ in range(to_west.shape[0])]
    east = [jnp.zeros(shape, f32) for _ in range(to_west.shape[0])]
    for i, field in enumerate(tile_fields(*scratch[:5])):
        fields[i] = field
        part, at = divmod(i, PER_LANES)
        at *= HALO
        here = (lane >= at) & (lane < at + HALO)
        west[part] = jnp.where(here, turn(field[:, :BLOCK], at, 1), west[part])
        east[part] = jnp.where(here, turn(field[:, -BLOCK:], at + HALO, 1), east[part])
    for part in range(to_west.shape[0]):
        to_west[part] = west[part]
        to_east[part] = east[part]


def unpack_columns(from_west, from_east, i):
    part, at = divmod(i, PER_LANES)
    at *= HALO
    lane = lanes(from_west[part].shape)
    east = turn(from_east[part], -at, 1)
    west = turn(from_west[part], -at - HALO, 1)
    return jnp.where(lane < HALO, east, jnp.where(lane >= BLOCK - HALO, west, 0.0))


def row_sources(fields, from_west, from_east, sums):
    out = [(fields, (i, slice(None), slice(h * BLOCK, (h + 1) * BLOCK)))
           for i in range(fields.shape[0]) for h in range(fields.shape[2] // BLOCK)]
    for columns in (from_west, from_east):
        out += [(columns, (part,)) for part in range(columns.shape[0])]
    return out + [(sums, (k, part)) for k in range(sums.shape[0]) for part in range(sums.shape[1])]


def pack_rows(fields, from_west, from_east, sums, to_north, to_south):
    sources = [ref[at] for ref, at in row_sources(fields, from_west, from_east, sums)]
    half = to_north.shape[0]
    row = rows((8, BLOCK))
    for i in range(half):
        first = sources[i]
        second = sources[i + half] if i + half < len(sources) else jnp.zeros_like(first)
        to_north[i] = jnp.where(row < HALO, turn(first[-8:], HALO, 0), second[-8:])
        to_south[i] = jnp.where(row < HALO, first[:8], turn(second[:8], HALO, 0))


def edge_rows(from_north, from_south, i):
    half = from_north.shape[0]
    if i < half:
        north, south = from_north[i], turn(from_south[i], HALO, 0)
    else:
        north, south = turn(from_north[i - half], HALO, 0), from_south[i - half]
    return jnp.where(rows((8, BLOCK)) < HALO, north, south)


def widen(fields, from_west, from_east, from_north, from_south, wide):
    count, tile_lat, tile_lon = fields.shape
    halves = tile_lon // BLOCK
    parts = from_west.shape[0]
    corners = [edge_rows(from_north, from_south, count * halves + n) for n in range(2 * parts)]
    for i in range(count):
        wide[i, :tile_lat, :tile_lon] = fields[i]
        wide[i, :tile_lat, tile_lon:] = unpack_columns(from_west, from_east, i)
        for h in range(halves):
            wide[i, tile_lat:, h * BLOCK : (h + 1) * BLOCK] = edge_rows(from_north, from_south, i * halves + h)
        wide[i, tile_lat:, tile_lon:] = unpack_columns(corners[:parts], corners[parts:], i)


def place_sums(first, sums, from_north, from_south, payload):
    lon_count, parts, tile_lat = sums.shape[:3]
    for k in range(lon_count):
        for part in range(parts):
            payload[k, part, :tile_lat] = sums[k, part]
            payload[k, part, tile_lat:] = edge_rows(from_north, from_south, first + k * parts + part)


def eastward(x):
    return turn(x, -1, 1)


def westward(x):
    return turn(x, 1, 1)


def northward(x):
    return turn(x, -1, 0)


def southward(x):
    return turn(x, 1, 0)


def run_adjoint(
    fields, from_west, from_east, from_north, from_south, adjoint_out, blocks, coeffs, start, wide, state
):
    levels = adjoint_out.shape[1]
    tile_lat, tile_lon = fields.shape[1:]
    widen(fields, from_west, from_east, from_north, from_south, wide)
    base = 4 * levels
    for f in range(2):
        for level in range(levels):
            start[f, level] = wide[f * levels + level]
    mask0 = None
    for level in range(levels):
        east_d, east_u = wide[base + level], wide[base + levels + level]
        north_d, north_u = wide[base + 2 * levels + level], wide[base + 3 * levels + level]
        mask = (east_d > 0.0).astype(f32)
        mask0 = mask if mask0 is None else mask0
        mask_e, mask_n = eastward(mask), northward(mask)
        east_k, east_v = east_d * mask_e, east_u * mask_e
        north_k, north_v = north_d * mask_n, north_u * mask_n
        coeffs[0, level] = jnp.maximum(east_v, 0.0) + east_k
        coeffs[1, level] = jnp.minimum(east_v, 0.0) - east_k
        coeffs[2, level] = jnp.maximum(north_v, 0.0) + north_k
        coeffs[3, level] = jnp.minimum(north_v, 0.0) - north_k
        coeffs[4, level] = wide[base + 4 * levels + level] if level < levels - 1 else jnp.zeros_like(mask)
        coeffs[5, level] = mask
    for f in range(2):
        surface = jnp.zeros((tile_lat, tile_lon), f32)
        for step in range(STEPS):
            above = None
            for level in range(levels):
                source = wide.at[(2 + f) * levels + level] if step == 0 else state.at[(step - 1) % 2, level]
                lam = source[...]
                if level == 0:
                    surface = surface + lam[:tile_lat, :tile_lon]
                step_x = eastward(lam) - lam
                step_y = northward(lam) - lam
                out = lam + coeffs[0, level] * step_x + westward(coeffs[1, level] * step_x)
                out = out + coeffs[2, level] * step_y + southward(coeffs[3, level] * step_y)
                if level < levels - 1:
                    if step == 0:
                        lower = wide[(2 + f) * levels + level + 1]
                    else:
                        lower = state[(step - 1) % 2, level + 1]
                    vertical = coeffs[4, level] * (lower - lam)
                    out = out + vertical
                if above is not None:
                    out = out - above
                above = vertical if level < levels - 1 else None
                if step == STEPS - 1:
                    adjoint_out[f, level] = out[:tile_lat, :tile_lon]
                else:
                    state[step % 2, level] = out
        surface = surface * mask0[:tile_lat, :tile_lon]
        halves = tile_lon // BLOCK
        for h in range(halves):
            at = (f * halves + h) * tile_lat
            for k in range(blocks.shape[0]):
                blocks[k, at : at + tile_lat] = surface[:, h * BLOCK : (h + 1) * BLOCK]


def run_forward(coeffs, start, received, final, state):
    levels = coeffs.shape[1]
    tile_lat, tile_lon = final.shape[2:]
    halves = tile_lon // BLOCK
    total = [
        sum((received[j, part] for j in range(1, received.shape[0])), received[0, part])
        for part in range(received.shape[1])
    ]
    lane = lanes(total[0].shape)
    for f in range(2):
        edge = total[2 * halves]
        if f == 1:
            edge = jnp.where(lane < HALO, turn(edge, -HALO, 1), turn(edge, HALO, 1))
        edge = jnp.where((lane < HALO) | (lane >= BLOCK - HALO), edge, 0.0)
        force = jnp.concatenate([*total[f * halves : (f + 1) * halves], edge], axis=1)
        force = force * coeffs[5, 0]
        for step in range(STEPS):
            above = None
            for level in range(levels):
                read = (lambda n: start[f, n]) if step == 0 else (lambda n: state[(step - 1) % 2, n])
                theta = read(level)
                east_flux = coeffs[0, level] * theta + coeffs[1, level] * eastward(theta)
                north_flux = coeffs[2, level] * theta + coeffs[3, level] * northward(theta)
                out = theta - (east_flux - westward(east_flux)) - (north_flux - southward(north_flux))
                if level < levels - 1:
                    vertical = coeffs[4, level] * (theta - read(level + 1))
                    out = out - vertical
                if above is not None:
                    out = out + above
                above = vertical if level < levels - 1 else None
                if level == 0:
                    out = out + force
                if step == STEPS - 1:
                    final[f, level] = out[:tile_lat, :tile_lon]
                else:
                    state[step % 2, level] = out


def split(x):
    high = x.astype(bf16)
    return high, (x - high.astype(f32)).astype(bf16)


def as_column(ids):
    n = ids.shape[1]
    shape = (n, n)
    return jnp.sum(
        jnp.where(rows(shape) == lanes(shape), jnp.broadcast_to(ids.astype(f32), shape), 0.0),
        axis=1,
        keepdims=True,
    )


def one_hot(where):
    return jnp.where(where, 1.0, 0.0).astype(bf16)


def fetch_group(weights, first, held, arrived, g):
    return pltpu.make_async_copy(
        weights.at[pl.ds((first + g) * GROUP, GROUP)], held.at[g], arrived.at[g]
    )


def fetch_weights(weights, first, held, arrived):
    for g in range(held.shape[0]):
        fetch_group(weights, first, held, arrived, g).start()


def apply_weights(weights, first, held, arrived, vectors, picks, total, transposed):
    def group(g, carry):
        left, right = [[], []], []
        fetch_group(weights, first, held, arrived, g).wait()
        for u in range(GROUP):
            w = (first + g) * GROUP + u
            here = picks[...] == lax.convert_element_type(w.astype(f32), bf16)
            here = jnp.concatenate([here, here], axis=1)
            for f in range(2):
                own = vectors[:, f * 2 * BLOCK : (f + 1) * 2 * BLOCK]
                left[f].append(jnp.where(here, own, jnp.zeros_like(own)))
            high, low = split(held[g, u])
            if transposed:
                both = jnp.concatenate([high, low], axis=1)
                right.append(jnp.concatenate([both, both], axis=0))
            else:
                both = jnp.concatenate([high, low], axis=0)
                right.append(jnp.concatenate([both, both], axis=1))
        right = jnp.concatenate(right, axis=0 if transposed else 1)
        contract = (((1,), (0 if transposed else 1,)), ((), ()))
        for f in range(2):
            product = lax.dot_general(
                jnp.concatenate(left[f], axis=1), right, contract, preferred_element_type=f32
            )
            total[f] += product
        return carry

    lax.fori_loop(0, held.shape[0], group, 0)


def slot_columns(ids, out_dtype=f32):
    return jnp.concatenate([as_column(ids[k : k + 1, :]) for k in range(ids.shape[0])], axis=0)


def weigh(
    atm_state, margins, weights, after, sums, vectors, picks, total, held, arrived, atm_near, ids, near
):
    lon_count, cap = margins.shape[3:]
    slots = lon_count * cap
    atm = atm_state.shape[2]
    tile_lat = sums.shape[2]
    copies = fetch([(margins, ids), (atm_state, atm_near)], near)
    fetch_weights(weights, 0, held, arrived)
    for copy in copies:
        copy.wait()
    ocean, atm_ids, block_ids = (ids[n, 0, 0] for n in range(3))
    picks[...] = jnp.broadcast_to(slot_columns(block_ids), (slots, BLOCK)).astype(bf16)
    parts = [part for f in range(2) for part in split(atm_near[f, 0])]
    table = jnp.concatenate(parts, axis=1)
    pick = one_hot(slot_columns(atm_ids).astype(jnp.int32) == lanes((slots, atm)))
    vectors[...] = jnp.dot(pick, table, preferred_element_type=f32).astype(bf16)
    total[...] = jnp.zeros_like(total)
    apply_weights(weights, 0, held, arrived, vectors, picks, total, False)
    ocean_blocks = 2 * tile_lat
    order = rows((ocean_blocks, cap))
    order = (order % tile_lat) * 2 + order // tile_lat
    lane = lanes((tile_lat, BLOCK))
    products = []
    for k in range(lon_count):
        place = one_hot(jnp.broadcast_to(ocean[k : k + 1, :], (ocean_blocks, cap)) == order)
        parts = []
        for f in range(2):
            value = total[f, k * cap : (k + 1) * cap]
            parts += split(value[:, :BLOCK] + value[:, BLOCK:])
        product = jnp.dot(place, jnp.concatenate(parts, axis=1), preferred_element_type=f32)
        products.append(
            [product[:, 2 * f * BLOCK : (2 * f + 1) * BLOCK] + product[:, (2 * f + 1) * BLOCK : (2 * f + 2) * BLOCK]
             for f in range(2)]
        )
        for f in range(2):
            for h in range(2):
                sums[k, 2 * f + h] = products[k][f][h * tile_lat : (h + 1) * tile_lat]
    for k in range(lon_count):
        after, before = products[(k + 1) % lon_count], products[(k - 1) % lon_count]
        edge = jnp.zeros((tile_lat, BLOCK), f32)
        for f in range(2):
            at = f * HALO
            edge = jnp.where((lane >= at) & (lane < at + HALO), turn(after[f][:tile_lat], at, 1), edge)
            end = BLOCK - at
            edge = jnp.where((lane >= end - HALO) & (lane < end), turn(before[f][tile_lat:], -at, 1), edge)
        sums[k, 4] = edge


def unweigh(gathered, margins, weights, gradient, vectors, picks, total, held, arrived, ids, near):
    lon_count, cap = margins.shape[3:]
    slots = lon_count * cap
    atm = gradient.shape[2]
    ocean_blocks = gathered.shape[1] // 2
    tile_lat = ocean_blocks // 2
    copies = fetch([(margins, ids)], near)
    fetch_weights(weights, 0, held, arrived)
    for copy in copies:
        copy.wait()
    ocean, atm_ids, block_ids = (ids[n, 0, 0] for n in range(3))
    picks[...] = jnp.broadcast_to(slot_columns(block_ids), (slots, BLOCK)).astype(bf16)
    order = lanes((cap, ocean_blocks))
    order = (order % tile_lat) * 2 + order // tile_lat
    for k in range(lon_count):
        pick = one_hot(as_column(ocean[k : k + 1, :]).astype(jnp.int32) == order)
        parts = [
            part for f in range(2) for part in split(gathered[k, f * ocean_blocks : (f + 1) * ocean_blocks])
        ]
        vectors[k * cap : (k + 1) * cap] = jnp.dot(
            pick, jnp.concatenate(parts, axis=1), preferred_element_type=f32
        ).astype(bf16)
    total[...] = jnp.zeros_like(total)
    apply_weights(weights, 0, held, arrived, vectors, picks, total, True)
    place = jnp.concatenate(
        [
            one_hot(jnp.broadcast_to(atm_ids[k : k + 1, :], (atm, cap)) == rows((atm, cap)))
            for k in range(lon_count)
        ],
        axis=1,
    )
    parts = [part for f in range(2) for part in split(total[f, :, :BLOCK] + total[f, :, BLOCK:])]
    product = jnp.dot(place, jnp.concatenate(parts, axis=1), preferred_element_type=f32)
    for f in range(2):
        at = 2 * f * BLOCK
        gradient[f, 0] = product[:, at : at + BLOCK] + product[:, at + BLOCK : at + 2 * BLOCK]


def on_device(tracers, cotangent, land_mask, diffusion, velocity, weights, atm_state, margins):
    levels, tile_lat, tile_lon = land_mask.shape
    lon_count, lat_count = lax.axis_size("lon"), lax.axis_size("lat")
    slots = lon_count * margins.shape[4]
    halves = tile_lon // BLOCK
    count = 9 * levels - 1
    parts = -(-count // PER_LANES)
    to_next = [(i, (i + 1) % lon_count) for i in range(lon_count)]
    to_prev = [(j, i) for i, j in to_next]
    up = [(i, i + 1) for i in range(lat_count - 1)]
    down = [(j, i) for i, j in up]
    inputs = (tracers, cotangent, land_mask, diffusion, velocity)

    def in_vmem(s):
        return pltpu.VMEM(s.shape, s.dtype)

    message = (parts, tile_lat, BLOCK)
    fields, to_west, to_east = call(
        pack_columns,
        [(count, tile_lat, tile_lon), message, message],
        [*map(in_vmem, inputs), pltpu.SemaphoreType.DMA((5,))],
        name="pack_columns",
        inputs=5,
        far=range(5),
    )(*inputs)
    from_east = lax.ppermute(to_west, "lon", to_prev)
    from_west = lax.ppermute(to_east, "lon", to_next)

    groups = weights.shape[0] // GROUP
    coupling_scratch = [
        pltpu.VMEM((slots, 4 * BLOCK), bf16),
        pltpu.VMEM((slots, BLOCK), bf16),
        pltpu.VMEM((2, slots, 2 * BLOCK), f32),
        pltpu.VMEM((groups, GROUP, BLOCK, BLOCK), f32),
        pltpu.SemaphoreType.DMA((groups,)),
    ]
    coupling_flops = 4 * slots * weights.shape[0] * 4 * BLOCK * BLOCK * 2
    sum_parts = 2 * halves + 1
    (sums,) = call(
        weigh,
        [(lon_count, sum_parts, tile_lat, BLOCK)],
        [*coupling_scratch, in_vmem(atm_state), in_vmem(margins), pltpu.SemaphoreType.DMA((2,))],
        coupling_flops,
        name="weigh",
        inputs=4,
        far=range(3),
    )(atm_state, margins, weights, to_west)

    sources = count * halves + 2 * parts + lon_count * sum_parts
    message = (-(-sources // 2), 8, BLOCK)
    to_north, to_south = call(pack_rows, [message, message], name="pack_rows", inputs=4)(
        fields, from_west, from_east, sums
    )
    from_south = lax.ppermute(to_north, "lat", up)
    from_north = lax.ppermute(to_south, "lat", down)

    (payload,) = call(
        functools.partial(place_sums, sources - lon_count * sum_parts),
        [(lon_count, sum_parts, tile_lat + 8, BLOCK)],
        name="place_sums",
        inputs=3,
    )(sums, from_north, from_south)
    received = lax.all_to_all(payload, "lon", split_axis=0, concat_axis=0, tiled=True)

    wide = (tile_lat + 8, tile_lon + BLOCK)
    adjoint, blocks, coeffs, start = call(
        run_adjoint,
        [
            cotangent.shape,
            (lon_count, 2 * halves * tile_lat, BLOCK),
            (6, levels, *wide),
            (2, levels, *wide),
        ],
        [pltpu.VMEM((count, *wide), f32), pltpu.VMEM((2, levels, *wide), f32)],
        name="run_adjoint",
        inputs=5,
    )(fields, from_west, from_east, from_north, from_south)
    gathered = lax.all_to_all(blocks, "lon", split_axis=0, concat_axis=0, tiled=True)

    (final,) = call(
        run_forward,
        [tracers.shape],
        [pltpu.VMEM((2, levels, *wide), f32)],
        name="run_forward",
        inputs=3,
    )(coeffs, start, received)

    (gradient,) = call(
        unweigh,
        [atm_state.shape],
        [*coupling_scratch, in_vmem(margins), pltpu.SemaphoreType.DMA((1,))],
        coupling_flops,
        name="unweigh",
        inputs=3,
        far=(1, 2),
    )(gathered, margins, weights)
    return (final, adjoint, gradient)


def solution(mesh):
    return jax.shard_map(
        on_device,
        mesh=mesh,
        in_specs=(
            P(None, None, "lat", "lon"),
            P(None, None, "lat", "lon"),
            P(None, "lat", "lon"),
            P(None, None, "lat", "lon"),
            P(None, None, "lat", "lon"),
            P(),
            P(None, "lat", "lon", None),
            P(None, "lat", "lon", None, None),
        ),
        out_specs=(
            P(None, None, "lat", "lon"),
            P(None, None, "lat", "lon"),
            P(None, "lat", "lon", None),
        ),
        check_vma=False,
    )
```

```python
import jax
import jax.numpy as jnp
from jax import lax
from jax.experimental import pallas as pl
from jax.experimental.pallas import tpu as pltpu
from jax.sharding import PartitionSpec as P

BLOCK = 128
STEPS = 4
HALO = STEPS
PER_LANES = BLOCK // HALO
GROUP = 4
f32 = jnp.float32
bf16 = jnp.bfloat16
VMEM_LIMIT = 48 * 1024 * 1024


def call(body, outs, scratch=(), flops=0, name=None, inputs=0, far=()):
    outs = [s if isinstance(s, jax.ShapeDtypeStruct) else jax.ShapeDtypeStruct(s, f32) for s in outs]
    near = pl.BlockSpec(memory_space=pltpu.VMEM)
    kernel = pl.pallas_call(
        body,
        out_shape=outs,
        in_specs=[pl.BlockSpec(memory_space=pltpu.HBM) if n in far else near for n in range(inputs)],
        out_specs=[near] * len(outs),
        scratch_shapes=list(scratch),
        compiler_params=pltpu.CompilerParams(vmem_limit_bytes=VMEM_LIMIT),
        cost_estimate=pl.CostEstimate(flops=flops, bytes_accessed=1 << 20, transcendentals=0),
        name=name,
    )

    def run(*args):
        return kernel(
            *(pltpu.with_memory_space_constraint(x, pltpu.HBM) if n in far else x for n, x in enumerate(args))
        )

    return run


def lanes(shape):
    return lax.broadcasted_iota(jnp.int32, shape, len(shape) - 1)


def rows(shape):
    return lax.broadcasted_iota(jnp.int32, shape, len(shape) - 2)


def turn(x, shift, axis):
    shift %= x.shape[axis]
    return pltpu.roll(x, shift, axis) if shift else x


def tile_fields(tracers, cotangent, land_mask, diffusion, velocity):
    levels = land_mask.shape[0]
    mask = [land_mask[level].astype(f32) for level in range(levels)]
    out = [tracers[f, level] for f in range(2) for level in range(levels)]
    out += [cotangent[f, level] for f in range(2) for level in range(levels)]
    out += [diffusion[0, level] * mask[level] for level in range(levels)]
    out += [velocity[0, level] * mask[level] for level in range(levels)]
    out += [diffusion[1, level] * mask[level] for level in range(levels)]
    out += [velocity[1, level] * mask[level] for level in range(levels)]
    out += [diffusion[2, level] * mask[level] * mask[level + 1] for level in range(levels - 1)]
    return out


def fetch(pairs, arrived):
    copies = [pltpu.make_async_copy(src, dst, arrived.at[n]) for n, (src, dst) in enumerate(pairs)]
    for copy in copies:
        copy.start()
    return copies


def pack_columns(*refs):
    inputs, (fields, to_west, to_east), scratch = refs[:5], refs[5:8], refs[8:]
    for copy in fetch(zip(inputs, scratch[:5]), scratch[5]):
        copy.wait()
    shape = to_west.shape[1:]
    lane = lanes(shape)
    west = [jnp.zeros(shape, f32) for _ in range(to_west.shape[0])]
    east = [jnp.zeros(shape, f32) for _ in range(to_west.shape[0])]
    for i, field in enumerate(tile_fields(*scratch[:5])):
        fields[i] = field
        part, at = divmod(i, PER_LANES)
        at *= HALO
        here = (lane >= at) & (lane < at + HALO)
        west[part] = jnp.where(here, turn(field[:, :BLOCK], at, 1), west[part])
        east[part] = jnp.where(here, turn(field[:, -BLOCK:], at + HALO, 1), east[part])
    for part in range(to_west.shape[0]):
        to_west[part] = west[part]
        to_east[part] = east[part]


def unpack_columns(from_west, from_east, i):
    part, at = divmod(i, PER_LANES)
    at *= HALO
    lane = lanes(from_west[part].shape)
    east = turn(from_east[part], -at, 1)
    west = turn(from_west[part], -at - HALO, 1)
    return jnp.where(lane < HALO, east, jnp.where(lane >= BLOCK - HALO, west, 0.0))


def row_sources(fields, from_west, from_east):
    out = [(fields, (i, slice(None), slice(h * BLOCK, (h + 1) * BLOCK)))
           for i in range(fields.shape[0]) for h in range(fields.shape[2] // BLOCK)]
    for columns in (from_west, from_east):
        out += [(columns, (part,)) for part in range(columns.shape[0])]
    return out


def pack_rows(fields, from_west, from_east, to_north, to_south):
    sources = [ref[at] for ref, at in row_sources(fields, from_west, from_east)]
    half = to_north.shape[0]
    row = rows((8, BLOCK))
    for i in range(half):
        first = sources[i]
        second = sources[i + half] if i + half < len(sources) else jnp.zeros_like(first)
        to_north[i] = jnp.where(row < HALO, turn(first[-8:], HALO, 0), second[-8:])
        to_south[i] = jnp.where(row < HALO, first[:8], turn(second[:8], HALO, 0))


def edge_rows(from_north, from_south, i):
    half = from_north.shape[0]
    if i < half:
        north, south = from_north[i], turn(from_south[i], HALO, 0)
    else:
        north, south = turn(from_north[i - half], HALO, 0), from_south[i - half]
    return jnp.where(rows((8, BLOCK)) < HALO, north, south)


def widen(fields, from_west, from_east, from_north, from_south, wide):
    count, tile_lat, tile_lon = fields.shape
    halves = tile_lon // BLOCK
    parts = from_west.shape[0]
    corners = [edge_rows(from_north, from_south, count * halves + n) for n in range(2 * parts)]
    for i in range(count):
        wide[i, :tile_lat, :tile_lon] = fields[i]
        wide[i, :tile_lat, tile_lon:] = unpack_columns(from_west, from_east, i)
        for h in range(halves):
            wide[i, tile_lat:, h * BLOCK : (h + 1) * BLOCK] = edge_rows(from_north, from_south, i * halves + h)
        wide[i, tile_lat:, tile_lon:] = unpack_columns(corners[:parts], corners[parts:], i)


def eastward(x):
    return turn(x, -1, 1)


def westward(x):
    return turn(x, 1, 1)


def northward(x):
    return turn(x, -1, 0)


def southward(x):
    return turn(x, 1, 0)


def run_adjoint(
    fields, from_west, from_east, from_north, from_south, adjoint_out, blocks, coeffs, start, wide, state
):
    levels = adjoint_out.shape[1]
    tile_lat, tile_lon = fields.shape[1:]
    widen(fields, from_west, from_east, from_north, from_south, wide)
    base = 4 * levels
    for f in range(2):
        for level in range(levels):
            start[f, level] = wide[f * levels + level]
    mask0 = None
    for level in range(levels):
        east_d, east_u = wide[base + level], wide[base + levels + level]
        north_d, north_u = wide[base + 2 * levels + level], wide[base + 3 * levels + level]
        mask = (east_d > 0.0).astype(f32)
        mask0 = mask if mask0 is None else mask0
        mask_e, mask_n = eastward(mask), northward(mask)
        east_k, east_v = east_d * mask_e, east_u * mask_e
        north_k, north_v = north_d * mask_n, north_u * mask_n
        coeffs[0, level] = jnp.maximum(east_v, 0.0) + east_k
        coeffs[1, level] = jnp.minimum(east_v, 0.0) - east_k
        coeffs[2, level] = jnp.maximum(north_v, 0.0) + north_k
        coeffs[3, level] = jnp.minimum(north_v, 0.0) - north_k
        coeffs[4, level] = wide[base + 4 * levels + level] if level < levels - 1 else jnp.zeros_like(mask)
        coeffs[5, level] = mask
    for f in range(2):
        surface = jnp.zeros((tile_lat, tile_lon), f32)
        for step in range(STEPS):
            above = None
            for level in range(levels):
                source = wide.at[(2 + f) * levels + level] if step == 0 else state.at[(step - 1) % 2, level]
                lam = source[...]
                if level == 0:
                    surface = surface + lam[:tile_lat, :tile_lon]
                step_x = eastward(lam) - lam
                step_y = northward(lam) - lam
                out = lam + coeffs[0, level] * step_x + westward(coeffs[1, level] * step_x)
                out = out + coeffs[2, level] * step_y + southward(coeffs[3, level] * step_y)
                if level < levels - 1:
                    if step == 0:
                        lower = wide[(2 + f) * levels + level + 1]
                    else:
                        lower = state[(step - 1) % 2, level + 1]
                    vertical = coeffs[4, level] * (lower - lam)
                    out = out + vertical
                if above is not None:
                    out = out - above
                above = vertical if level < levels - 1 else None
                if step == STEPS - 1:
                    adjoint_out[f, level] = out[:tile_lat, :tile_lon]
                else:
                    state[step % 2, level] = out
        surface = surface * mask0[:tile_lat, :tile_lon]
        halves = tile_lon // BLOCK
        for h in range(halves):
            at = (f * halves + h) * tile_lat
            for k in range(blocks.shape[0]):
                blocks[k, at : at + tile_lat] = surface[:, h * BLOCK : (h + 1) * BLOCK]


def sum_forcing(received, forcing, to_north, to_south):
    tile_lat = forcing.shape[1]
    halves = forcing.shape[2] // BLOCK - 1
    total = [
        sum((received[j, part] for j in range(1, received.shape[0])), received[0, part])
        for part in range(received.shape[1])
    ]
    lane = lanes((tile_lat, BLOCK))
    packed = total[2 * halves]
    for f in range(2):
        for h in range(halves):
            forcing[f, :, h * BLOCK : (h + 1) * BLOCK] = total[f * halves + h]
        near = (lane < HALO) | (lane >= BLOCK - HALO)
        if f == 0:
            edge = packed
        else:
            edge = jnp.where(lane < HALO, turn(packed, -HALO, 1), turn(packed, HALO, 1))
        forcing[f, :, halves * BLOCK :] = jnp.where(near, edge, 0.0)
    row = rows((8, forcing.shape[2]))
    to_north[...] = jnp.where(row < HALO, turn(forcing[0, tile_lat - 8 :], HALO, 0), forcing[1, tile_lat - 8 :])
    to_south[...] = jnp.where(row < HALO, forcing[0, :8], turn(forcing[1, :8], HALO, 0))


def run_forward(coeffs, start, forcing, from_north, from_south, final, state):
    levels = coeffs.shape[1]
    tile_lat, tile_lon = final.shape[2:]
    row = rows((8, forcing.shape[2]))
    mask = None
    for f in range(2):
        if f == 0:
            north, south = from_north[...], turn(from_south[...], HALO, 0)
        else:
            north, south = turn(from_north[...], HALO, 0), from_south[...]
        force = jnp.concatenate([forcing[f], jnp.where(row < HALO, north, south)], axis=0)
        force = force * coeffs[5, 0]
        for step in range(STEPS):
            above = None
            for level in range(levels):
                read = (lambda n: start[f, n]) if step == 0 else (lambda n: state[(step - 1) % 2, n])
                theta = read(level)
                east_flux = coeffs[0, level] * theta + coeffs[1, level] * eastward(theta)
                north_flux = coeffs[2, level] * theta + coeffs[3, level] * northward(theta)
                out = theta - (east_flux - westward(east_flux)) - (north_flux - southward(north_flux))
                if level < levels - 1:
                    vertical = coeffs[4, level] * (theta - read(level + 1))
                    out = out - vertical
                if above is not None:
                    out = out + above
                above = vertical if level < levels - 1 else None
                if level == 0:
                    out = out + force
                if step == STEPS - 1:
                    final[f, level] = out[:tile_lat, :tile_lon]
                else:
                    state[step % 2, level] = out


def split(x):
    high = x.astype(bf16)
    return high, (x - high.astype(f32)).astype(bf16)


def weight_copies(weights, held, arrived):
    for g in range(held.shape[0]):
        yield pltpu.make_async_copy(weights.at[pl.ds(g * GROUP, GROUP)], held.at[g], arrived.at[g])


def fetch_weights(weights, held, arrived):
    for copy in weight_copies(weights, held, arrived):
        copy.start()


def wait_weights(weights, held, arrived):
    for copy in weight_copies(weights, held, arrived):
        copy.wait()


def one_hot(where):
    return jnp.where(where, 1.0, 0.0).astype(bf16)


def places(slots, blocks):
    return 8 * (-(-2 * slots // (8 * blocks)) + 1)


def as_row(ids):
    return jnp.concatenate([ids[k : k + 1, :] for k in range(ids.shape[0])], axis=1)


def rank_slots(block_row, blocks):
    slots = block_row.shape[1]
    mine = rows((blocks, slots)) == block_row
    upper = one_hot(rows((slots, slots)) < lanes((slots, slots)))
    before = jnp.dot(one_hot(mine), upper, preferred_element_type=f32)
    return jnp.sum(jnp.where(mine, before, 0.0), axis=0, keepdims=True)


def couple(weights_near, ready, table, keys, block_row, rank, gather_first, transposed, result, scratch):
    code, size = keys
    column, vectors, products = scratch
    slots = block_row.shape[1]
    blocks = weights_near.shape[0] * weights_near.shape[1]
    capacity = places(slots, blocks)
    total_rows = column.shape[0]
    result[...] = jnp.zeros_like(result)
    rounds = jnp.max(rank).astype(jnp.int32) // capacity + 1

    def one_round(r, carry):
        place = rank.astype(jnp.int32) - r * capacity
        place = jnp.where((place >= 0) & (place < capacity), block_row * capacity + place, -1)
        eye = rows((BLOCK, BLOCK)) == lanes((BLOCK, BLOCK))
        place_hot = []
        for at in range(0, total_rows, BLOCK):
            here = rows((BLOCK, slots)) + at == place
            found = jnp.sum(jnp.where(here, code + 1.0, 0.0), axis=1, keepdims=True) - 1.0
            found = jnp.broadcast_to(found, (BLOCK, BLOCK))
            first = jnp.floor((found + 0.5) * (1.0 / size))
            second = found - first * size
            gather, put = (first, second) if gather_first else (second, first)
            width = table.shape[0]
            gather = jnp.concatenate([gather] * (width // BLOCK), axis=1)
            hot = one_hot(gather == lanes((BLOCK, width)).astype(f32))
            vectors[at : at + BLOCK] = jnp.dot(hot, table, preferred_element_type=f32)
            put = jnp.sum(jnp.where(eye, put, 0.0), axis=0, keepdims=True)
            place_hot.append(one_hot(rows((result.shape[0], BLOCK)).astype(f32) == put))
        pl.when(r == 0)(ready)

        def group(g, carry):
            for u in range(GROUP):
                at = pl.multiple_of((g * GROUP + u) * capacity, 8)
                own = vectors[pl.ds(at, capacity)]
                left = jnp.concatenate([own[:, n * BLOCK : (n + 1) * BLOCK] for n in range(4)], axis=0)
                high, low = split(weights_near[g, u])
                right = jnp.concatenate([high, low], axis=1 if transposed else 0)
                contract = (((1,), (0 if transposed else 1,)), ((), ()))
                product = lax.dot_general(left.astype(bf16), right, contract, preferred_element_type=f32)
                for f in range(2):
                    high_part = product[f * capacity : (f + 1) * capacity]
                    low_part = product[(f + 2) * capacity : (f + 3) * capacity, :BLOCK]
                    products[pl.ds(at, capacity), f * BLOCK : (f + 1) * BLOCK] = (
                        high_part[:, BLOCK:] + low_part
                    ) + high_part[:, :BLOCK]
            return carry

        lax.fori_loop(0, weights_near.shape[0], group, 0)
        summed = jnp.dot(
            jnp.concatenate(place_hot, axis=1),
            jnp.concatenate(split(products[...]), axis=1),
            preferred_element_type=f32,
        )
        result[...] += summed[:, : 2 * BLOCK] + summed[:, 2 * BLOCK :]
        return carry

    lax.fori_loop(0, rounds, one_round, 0)


def slot_keys(ids, tile_lat, atm):
    lon_count, cap = ids.shape[3:]
    ocean, atm_ids, block_ids = (ids[n, 0, 0] for n in range(3))
    order = (ocean & 1) * tile_lat + (ocean >> 1) + rows((lon_count, cap)) * (2 * tile_lat)
    order = jnp.where(ocean >= 0, order, lon_count * 2 * tile_lat)
    return as_row((order * atm + atm_ids).astype(f32)), as_row(block_ids)


def weigh(atm_state, margins, weights, after, sums, rank_out, result, *scratch):
    scratch, (held, arrived, atm_near, ids, near) = scratch[:3], scratch[3:]
    lon_count = margins.shape[3]
    atm = atm_state.shape[2]
    tile_lat = sums.shape[2]
    copies = fetch([(margins, ids), (atm_state, atm_near)], near)
    fetch_weights(weights, held, arrived)
    for copy in copies:
        copy.wait()
    code, block_row = slot_keys(ids, tile_lat, atm)
    rank = rank_slots(block_row, weights.shape[0])
    rank_out[...] = rank
    parts = [split(atm_near[f, 0]) for f in range(2)]
    table = jnp.concatenate([parts[f][n] for n in range(2) for f in range(2)], axis=1)
    couple(
        held,
        lambda: wait_weights(weights, held, arrived),
        table,
        (code, atm),
        block_row,
        rank,
        False,
        False,
        result,
        scratch,
    )
    lane = lanes((tile_lat, BLOCK))

    def block_sums(k, f, h):
        at = (2 * k + h) * tile_lat
        return result[at : at + tile_lat, f * BLOCK : (f + 1) * BLOCK]

    for k in range(lon_count):
        edge = jnp.zeros((tile_lat, BLOCK), f32)
        for f in range(2):
            for h in range(2):
                sums[k, 2 * f + h] = block_sums(k, f, h)
            at = f * HALO
            after = turn(block_sums((k + 1) % lon_count, f, 0), at, 1)
            before = turn(block_sums((k - 1) % lon_count, f, 1), -at, 1)
            edge = jnp.where((lane >= at) & (lane < at + HALO), after, edge)
            end = BLOCK - at
            edge = jnp.where((lane >= end - HALO) & (lane < end), before, edge)
        sums[k, 4] = edge


def unweigh(gathered, rank, margins, weights, gradient, result, *scratch):
    scratch, (held, arrived, ids, near) = scratch[:3], scratch[3:]
    atm = gradient.shape[2]
    lon_count, ocean_blocks = gathered.shape[0], gathered.shape[1] // 2
    copies = fetch([(margins, ids)], near)
    fetch_weights(weights, held, arrived)
    for copy in copies:
        copy.wait()
    code, block_row = slot_keys(ids, ocean_blocks // 2, atm)
    parts = [
        split(
            jnp.concatenate(
                [gathered[k, f * ocean_blocks : (f + 1) * ocean_blocks] for k in range(lon_count)], axis=0
            )
        )
        for f in range(2)
    ]
    table = jnp.concatenate([parts[f][n] for n in range(2) for f in range(2)], axis=1)
    couple(
        held,
        lambda: wait_weights(weights, held, arrived),
        table,
        (code, atm),
        block_row,
        rank[...],
        True,
        True,
        result,
        scratch,
    )
    for f in range(2):
        gradient[f, 0] = result[:, f * BLOCK : (f + 1) * BLOCK]


def on_device(tracers, cotangent, land_mask, diffusion, velocity, weights, atm_state, margins):
    levels, tile_lat, tile_lon = land_mask.shape
    lon_count, lat_count = lax.axis_size("lon"), lax.axis_size("lat")
    slots = lon_count * margins.shape[4]
    halves = tile_lon // BLOCK
    count = 9 * levels - 1
    parts = -(-count // PER_LANES)
    to_next = [(i, (i + 1) % lon_count) for i in range(lon_count)]
    to_prev = [(j, i) for i, j in to_next]
    up = [(i, i + 1) for i in range(lat_count - 1)]
    down = [(j, i) for i, j in up]
    inputs = (tracers, cotangent, land_mask, diffusion, velocity)

    def in_vmem(s):
        return pltpu.VMEM(s.shape, s.dtype)

    message = (parts, tile_lat, BLOCK)
    fields, to_west, to_east = call(
        pack_columns,
        [(count, tile_lat, tile_lon), message, message],
        [*map(in_vmem, inputs), pltpu.SemaphoreType.DMA((5,))],
        name="pack_columns",
        inputs=5,
        far=range(5),
    )(*inputs)
    from_east = lax.ppermute(to_west, "lon", to_prev)
    from_west = lax.ppermute(to_east, "lon", to_next)

    blocks_of, atm = weights.shape[0], atm_state.shape[2]
    groups = blocks_of // GROUP
    sum_parts = 2 * halves + 1
    ocean_blocks = lon_count * halves * tile_lat
    held_rows = -(-places(slots, blocks_of) * blocks_of // BLOCK) * BLOCK

    def coupling_scratch(result_rows):
        return [
            pltpu.VMEM((result_rows, 2 * BLOCK), f32),
            pltpu.VMEM((held_rows, BLOCK), f32),
            pltpu.VMEM((held_rows, 4 * BLOCK), f32),
            pltpu.VMEM((held_rows, 2 * BLOCK), f32),
            pltpu.VMEM((groups, GROUP, BLOCK, BLOCK), f32),
            pltpu.SemaphoreType.DMA((groups,)),
        ]

    coupling_flops = 4 * slots * blocks_of * 2 * BLOCK * BLOCK * 2
    sums, rank = call(
        weigh,
        [(lon_count, sum_parts, tile_lat, BLOCK), (1, slots)],
        [*coupling_scratch(ocean_blocks), in_vmem(atm_state), in_vmem(margins), pltpu.SemaphoreType.DMA((2,))],
        coupling_flops,
        name="weigh",
        inputs=4,
        far=range(3),
    )(atm_state, margins, weights, to_west)
    received = lax.all_to_all(sums, "lon", split_axis=0, concat_axis=0, tiled=True)

    sources = count * halves + 2 * parts
    message = (-(-sources // 2), 8, BLOCK)
    to_north, to_south = call(pack_rows, [message, message], name="pack_rows", inputs=3)(
        fields, from_west, from_east
    )
    from_south = lax.ppermute(to_north, "lat", up)
    from_north = lax.ppermute(to_south, "lat", down)

    wide = (tile_lat + 8, tile_lon + BLOCK)
    adjoint, blocks, coeffs, start = call(
        run_adjoint,
        [
            cotangent.shape,
            (lon_count, 2 * halves * tile_lat, BLOCK),
            (6, levels, *wide),
            (2, levels, *wide),
        ],
        [pltpu.VMEM((count, *wide), f32), pltpu.VMEM((2, levels, *wide), f32)],
        name="run_adjoint",
        inputs=5,
    )(fields, from_west, from_east, from_north, from_south)
    gathered = lax.all_to_all(blocks, "lon", split_axis=0, concat_axis=0, tiled=True)

    message = (8, tile_lon + BLOCK)
    forcing, to_north, to_south = call(
        sum_forcing, [(2, tile_lat, tile_lon + BLOCK), message, message], name="sum_forcing", inputs=1
    )(received)
    force_south = lax.ppermute(to_north, "lat", up)
    force_north = lax.ppermute(to_south, "lat", down)
    (final,) = call(
        run_forward,
        [tracers.shape],
        [pltpu.VMEM((2, levels, *wide), f32)],
        name="run_forward",
        inputs=5,
    )(coeffs, start, forcing, force_north, force_south)

    (gradient,) = call(
        unweigh,
        [atm_state.shape],
        [*coupling_scratch(atm), in_vmem(margins), pltpu.SemaphoreType.DMA((1,))],
        coupling_flops,
        name="unweigh",
        inputs=4,
        far=(2, 3),
    )(gathered, rank, margins, weights)
    return (final, adjoint, gradient)


def solution(mesh):
    return jax.shard_map(
        on_device,
        mesh=mesh,
        in_specs=(
            P(None, None, "lat", "lon"),
            P(None, None, "lat", "lon"),
            P(None, "lat", "lon"),
            P(None, None, "lat", "lon"),
            P(None, None, "lat", "lon"),
            P(),
            P(None, "lat", "lon", None),
            P(None, "lat", "lon", None, None),
        ),
        out_specs=(
            P(None, None, "lat", "lon"),
            P(None, None, "lat", "lon"),
            P(None, "lat", "lon", None),
        ),
        check_vma=False,
    )
```

```python
import jax
import jax.numpy as jnp
from jax import lax
from jax.experimental import pallas as pl
from jax.experimental.pallas import tpu as pltpu
from jax.sharding import PartitionSpec as P

BLOCK = 128
STEPS = 4
HALO = STEPS
PER_LANES = BLOCK // HALO
GROUP = 8
f32 = jnp.float32
bf16 = jnp.bfloat16
VMEM_LIMIT = 48 * 1024 * 1024


def call(body, outs, scratch=(), flops=0, name=None, inputs=0, far=(), aliases=None):
    outs = [s if isinstance(s, jax.ShapeDtypeStruct) else jax.ShapeDtypeStruct(s, f32) for s in outs]
    near = pl.BlockSpec(memory_space=pltpu.VMEM)
    aliases = aliases or {}
    kernel = pl.pallas_call(
        body,
        out_shape=outs,
        in_specs=[
            pl.BlockSpec(memory_space=pl.ANY)
            if n in aliases
            else pl.BlockSpec(memory_space=pltpu.HBM)
            if n in far
            else near
            for n in range(inputs)
        ],
        out_specs=[
            pl.BlockSpec(memory_space=pl.ANY) if n in aliases.values() else near for n in range(len(outs))
        ],
        input_output_aliases=aliases,
        scratch_shapes=list(scratch),
        compiler_params=pltpu.CompilerParams(vmem_limit_bytes=VMEM_LIMIT),
        cost_estimate=pl.CostEstimate(flops=flops, bytes_accessed=1 << 20, transcendentals=0),
        name=name,
    )

    def run(*args):
        return kernel(
            *(pltpu.with_memory_space_constraint(x, pltpu.HBM) if n in far else x for n, x in enumerate(args))
        )

    return run


def lanes(shape):
    return lax.broadcasted_iota(jnp.int32, shape, len(shape) - 1)


def rows(shape):
    return lax.broadcasted_iota(jnp.int32, shape, len(shape) - 2)


def turn(x, shift, axis):
    shift %= x.shape[axis]
    return pltpu.roll(x, shift, axis) if shift else x


def tile_fields(tracers, cotangent, land_mask, diffusion, velocity):
    levels = land_mask.shape[0]
    mask = [land_mask[level].astype(f32) for level in range(levels)]
    out = [tracers[f, level] for f in range(2) for level in range(levels)]
    out += [cotangent[f, level] for f in range(2) for level in range(levels)]
    out += [diffusion[0, level] * mask[level] for level in range(levels)]
    out += [velocity[0, level] * mask[level] for level in range(levels)]
    out += [diffusion[1, level] * mask[level] for level in range(levels)]
    out += [velocity[1, level] * mask[level] for level in range(levels)]
    out += [diffusion[2, level] * mask[level] * mask[level + 1] for level in range(levels - 1)]
    return out


def fetch(pairs, arrived):
    copies = [pltpu.make_async_copy(src, dst, arrived.at[n]) for n, (src, dst) in enumerate(pairs)]
    for copy in copies:
        copy.start()
    return copies


def pack_columns(*refs):
    inputs, (fields, to_west, to_east), scratch = refs[:7], refs[7:10], refs[12:]
    copies = fetch(zip(inputs, [*scratch[:5], *refs[10:12]]), scratch[5])
    for copy in copies[:5]:
        copy.wait()
    shape = to_west.shape[1:]
    lane = lanes(shape)
    west = [jnp.zeros(shape, f32) for _ in range(to_west.shape[0])]
    east = [jnp.zeros(shape, f32) for _ in range(to_west.shape[0])]
    for i, field in enumerate(tile_fields(*scratch[:5])):
        fields[i] = field
        part, at = divmod(i, PER_LANES)
        at *= HALO
        here = (lane >= at) & (lane < at + HALO)
        west[part] = jnp.where(here, turn(field[:, :BLOCK], at, 1), west[part])
        east[part] = jnp.where(here, turn(field[:, -BLOCK:], at + HALO, 1), east[part])
    for part in range(to_west.shape[0]):
        to_west[part] = west[part]
        to_east[part] = east[part]
    for copy in copies[5:]:
        copy.wait()


def unpack_columns(from_west, from_east, i):
    part, at = divmod(i, PER_LANES)
    at *= HALO
    lane = lanes(from_west[part].shape)
    east = turn(from_east[part], -at, 1)
    west = turn(from_west[part], -at - HALO, 1)
    return jnp.where(lane < HALO, east, jnp.where(lane >= BLOCK - HALO, west, 0.0))


def row_sources(fields, from_west, from_east):
    out = [(fields, (i, slice(None), slice(h * BLOCK, (h + 1) * BLOCK)))
           for i in range(fields.shape[0]) for h in range(fields.shape[2] // BLOCK)]
    for columns in (from_west, from_east):
        out += [(columns, (part,)) for part in range(columns.shape[0])]
    return out


def pack_rows(fields, from_west, from_east, sums, to_north, to_south, same_sums):
    sources = [ref[at] for ref, at in row_sources(fields, from_west, from_east)]
    half = to_north.shape[0]
    row = rows((8, BLOCK))
    for i in range(half):
        first = sources[i]
        second = sources[i + half] if i + half < len(sources) else jnp.zeros_like(first)
        to_north[i] = jnp.where(row < HALO, turn(first[-8:], HALO, 0), second[-8:])
        to_south[i] = jnp.where(row < HALO, first[:8], turn(second[:8], HALO, 0))


def edge_rows(from_north, from_south, i):
    half = from_north.shape[0]
    if i < half:
        north, south = from_north[i], turn(from_south[i], HALO, 0)
    else:
        north, south = turn(from_north[i - half], HALO, 0), from_south[i - half]
    return jnp.where(rows((8, BLOCK)) < HALO, north, south)


def widen(fields, from_west, from_east, from_north, from_south, wide):
    count, tile_lat, tile_lon = fields.shape
    halves = tile_lon // BLOCK
    parts = from_west.shape[0]
    corners = [edge_rows(from_north, from_south, count * halves + n) for n in range(2 * parts)]
    for i in range(count):
        wide[i, :tile_lat, :tile_lon] = fields[i]
        wide[i, :tile_lat, tile_lon:] = unpack_columns(from_west, from_east, i)
        for h in range(halves):
            wide[i, tile_lat:, h * BLOCK : (h + 1) * BLOCK] = edge_rows(from_north, from_south, i * halves + h)
        wide[i, tile_lat:, tile_lon:] = unpack_columns(corners[:parts], corners[parts:], i)


def eastward(x):
    return turn(x, -1, 1)


def westward(x):
    return turn(x, 1, 1)


def northward(x):
    return turn(x, -1, 0)


def southward(x):
    return turn(x, 1, 0)


def run_adjoint(
    fields, from_west, from_east, from_north, from_south, adjoint_out, blocks, coeffs, start, wide, state
):
    levels = adjoint_out.shape[1]
    tile_lat, tile_lon = fields.shape[1:]
    widen(fields, from_west, from_east, from_north, from_south, wide)
    base = 4 * levels
    for f in range(2):
        for level in range(levels):
            start[f, level] = wide[f * levels + level]
    mask0 = None
    for level in range(levels):
        east_d, east_u = wide[base + level], wide[base + levels + level]
        north_d, north_u = wide[base + 2 * levels + level], wide[base + 3 * levels + level]
        mask = (east_d > 0.0).astype(f32)
        mask0 = mask if mask0 is None else mask0
        mask_e, mask_n = eastward(mask), northward(mask)
        east_k, east_v = east_d * mask_e, east_u * mask_e
        north_k, north_v = north_d * mask_n, north_u * mask_n
        coeffs[0, level] = jnp.maximum(east_v, 0.0) + east_k
        coeffs[1, level] = jnp.minimum(east_v, 0.0) - east_k
        coeffs[2, level] = jnp.maximum(north_v, 0.0) + north_k
        coeffs[3, level] = jnp.minimum(north_v, 0.0) - north_k
        coeffs[4, level] = wide[base + 4 * levels + level] if level < levels - 1 else jnp.zeros_like(mask)
        coeffs[5, level] = mask
    for f in range(2):
        surface = jnp.zeros((tile_lat, tile_lon), f32)
        for step in range(STEPS):
            above = None
            for level in range(levels):
                source = wide.at[(2 + f) * levels + level] if step == 0 else state.at[(step - 1) % 2, level]
                lam = source[...]
                if level == 0:
                    surface = surface + lam[:tile_lat, :tile_lon]
                step_x = eastward(lam) - lam
                step_y = northward(lam) - lam
                out = lam + coeffs[0, level] * step_x + westward(coeffs[1, level] * step_x)
                out = out + coeffs[2, level] * step_y + southward(coeffs[3, level] * step_y)
                if level < levels - 1:
                    if step == 0:
                        lower = wide[(2 + f) * levels + level + 1]
                    else:
                        lower = state[(step - 1) % 2, level + 1]
                    vertical = coeffs[4, level] * (lower - lam)
                    out = out + vertical
                if above is not None:
                    out = out - above
                above = vertical if level < levels - 1 else None
                if step == STEPS - 1:
                    adjoint_out[f, level] = out[:tile_lat, :tile_lon]
                else:
                    state[step % 2, level] = out
        surface = surface * mask0[:tile_lat, :tile_lon]
        halves = tile_lon // BLOCK
        for h in range(halves):
            at = (f * halves + h) * tile_lat
            for k in range(blocks.shape[0]):
                blocks[k, at : at + tile_lat] = surface[:, h * BLOCK : (h + 1) * BLOCK]


def sum_forcing(received, forcing, to_north, to_south):
    tile_lat = forcing.shape[1]
    halves = forcing.shape[2] // BLOCK - 1
    total = [
        sum((received[j, part] for j in range(1, received.shape[0])), received[0, part])
        for part in range(received.shape[1])
    ]
    lane = lanes((tile_lat, BLOCK))
    packed = total[2 * halves]
    for f in range(2):
        for h in range(halves):
            forcing[f, :, h * BLOCK : (h + 1) * BLOCK] = total[f * halves + h]
        near = (lane < HALO) | (lane >= BLOCK - HALO)
        if f == 0:
            edge = packed
        else:
            edge = jnp.where(lane < HALO, turn(packed, -HALO, 1), turn(packed, HALO, 1))
        forcing[f, :, halves * BLOCK :] = jnp.where(near, edge, 0.0)
    row = rows((8, forcing.shape[2]))
    to_north[...] = jnp.where(row < HALO, turn(forcing[0, tile_lat - 8 :], HALO, 0), forcing[1, tile_lat - 8 :])
    to_south[...] = jnp.where(row < HALO, forcing[0, :8], turn(forcing[1, :8], HALO, 0))


def run_forward(coeffs, start, forcing, from_north, from_south, final, state):
    levels = coeffs.shape[1]
    tile_lat, tile_lon = final.shape[2:]
    row = rows((8, forcing.shape[2]))
    mask = None
    for f in range(2):
        if f == 0:
            north, south = from_north[...], turn(from_south[...], HALO, 0)
        else:
            north, south = turn(from_north[...], HALO, 0), from_south[...]
        force = jnp.concatenate([forcing[f], jnp.where(row < HALO, north, south)], axis=0)
        force = force * coeffs[5, 0]
        for step in range(STEPS):
            above = None
            for level in range(levels):
                read = (lambda n: start[f, n]) if step == 0 else (lambda n: state[(step - 1) % 2, n])
                theta = read(level)
                east_flux = coeffs[0, level] * theta + coeffs[1, level] * eastward(theta)
                north_flux = coeffs[2, level] * theta + coeffs[3, level] * northward(theta)
                out = theta - (east_flux - westward(east_flux)) - (north_flux - southward(north_flux))
                if level < levels - 1:
                    vertical = coeffs[4, level] * (theta - read(level + 1))
                    out = out - vertical
                if above is not None:
                    out = out + above
                above = vertical if level < levels - 1 else None
                if level == 0:
                    out = out + force
                if step == STEPS - 1:
                    final[f, level] = out[:tile_lat, :tile_lon]
                else:
                    state[step % 2, level] = out


def split(x):
    high = x.astype(bf16)
    return high, (x - high.astype(f32)).astype(bf16)


def weight_copies(weights, held, arrived):
    for g in range(held.shape[0]):
        yield pltpu.make_async_copy(weights.at[pl.ds(g * GROUP, GROUP)], held.at[g], arrived.at[g])


def fetch_weights(weights, held, arrived):
    for copy in weight_copies(weights, held, arrived):
        copy.start()


def wait_weights(weights, held, arrived):
    for copy in weight_copies(weights, held, arrived):
        copy.wait()


def one_hot(where):
    return jnp.where(where, 1.0, 0.0).astype(bf16)


def places(slots, blocks):
    return 8 * (-(-2 * slots // (8 * blocks)) + 1)


def as_row(ids):
    return jnp.concatenate([ids[k : k + 1, :] for k in range(ids.shape[0])], axis=1)


def rank_slots(block_row, blocks):
    slots = block_row.shape[1]
    mine = rows((blocks, slots)) == block_row
    upper = one_hot(rows((slots, slots)) < lanes((slots, slots)))
    before = jnp.dot(one_hot(mine), upper, preferred_element_type=f32)
    return jnp.sum(jnp.where(mine, before, 0.0), axis=0, keepdims=True)


def find_slots(r, code, block_row, rank, capacity, column):
    slots = block_row.shape[1]
    place = rank.astype(jnp.int32) - r * capacity
    place = jnp.where((place >= 0) & (place < capacity), block_row * capacity + place, -1)
    for at in range(0, column.shape[0], BLOCK):
        here = rows((BLOCK, slots)) + at == place
        found = jnp.sum(jnp.where(here, code + 1.0, 0.0), axis=1, keepdims=True) - 1.0
        column[at : at + BLOCK] = jnp.broadcast_to(found, (BLOCK, BLOCK))


def couple(weights_near, table, size, capacity, rounds, prepare, column, gather_first, transposed, result, scratch):
    vectors, products = scratch
    total_rows = column.shape[0]
    result[...] = jnp.zeros_like(result)

    def one_round(r, carry):
        prepare(r)
        eye = rows((BLOCK, BLOCK)) == lanes((BLOCK, BLOCK))
        place_hot = []
        for at in range(0, total_rows, BLOCK):
            found = column[at : at + BLOCK]
            first = jnp.floor((found + 0.5) * (1.0 / size))
            second = found - first * size
            gather, put = (first, second) if gather_first else (second, first)
            width = table.shape[0]
            gather = jnp.concatenate([gather] * (width // BLOCK), axis=1)
            hot = one_hot(gather == lanes((BLOCK, width)).astype(f32))
            vectors[at : at + BLOCK] = jnp.dot(hot, table, preferred_element_type=f32)
            put = jnp.sum(jnp.where(eye, put, 0.0), axis=0, keepdims=True)
            place_hot.append(one_hot(rows((result.shape[0], BLOCK)).astype(f32) == put))

        def group(g, carry):
            for u in range(GROUP):
                at = pl.multiple_of((g * GROUP + u) * capacity, 8)
                own = vectors[pl.ds(at, capacity)]
                left = jnp.concatenate([own[:, n * BLOCK : (n + 1) * BLOCK] for n in range(4)], axis=0)
                high, low = split(weights_near[g, u])
                right = jnp.concatenate([high, low], axis=1 if transposed else 0)
                contract = (((1,), (0 if transposed else 1,)), ((), ()))
                product = lax.dot_general(left.astype(bf16), right, contract, preferred_element_type=f32)
                for f in range(2):
                    high_part = product[f * capacity : (f + 1) * capacity]
                    low_part = product[(f + 2) * capacity : (f + 3) * capacity, :BLOCK]
                    products[pl.ds(at, capacity), f * BLOCK : (f + 1) * BLOCK] = (
                        high_part[:, BLOCK:] + low_part
                    ) + high_part[:, :BLOCK]
            return carry

        lax.fori_loop(0, weights_near.shape[0], group, 0)
        summed = jnp.dot(
            jnp.concatenate(place_hot, axis=1),
            jnp.concatenate(split(products[...]), axis=1),
            preferred_element_type=f32,
        )
        result[...] += summed[:, : 2 * BLOCK] + summed[:, 2 * BLOCK :]
        return carry

    lax.fori_loop(0, rounds, one_round, 0)


def slot_keys(ids, tile_lat, atm):
    lon_count, cap = ids.shape[3:]
    ocean, atm_ids, block_ids = (ids[n, 0, 0] for n in range(3))
    order = (ocean & 1) * tile_lat + (ocean >> 1) + rows((lon_count, cap)) * (2 * tile_lat)
    order = jnp.where(ocean >= 0, order, lon_count * 2 * tile_lat)
    return as_row((order * atm + atm_ids).astype(f32)), as_row(block_ids)


def weigh(atm_near, margins, weights, after, sums, found, keys, result, *scratch):
    scratch, (held, arrived) = scratch[:2], scratch[2:]
    fetch_weights(weights, held, arrived)
    lon_count = margins.shape[3]
    atm = atm_near.shape[2]
    blocks = weights.shape[0]
    tile_lat = sums.shape[2]
    code, block_row = slot_keys(margins, tile_lat, atm)
    rank = rank_slots(block_row, blocks)
    keys[0:1] = code
    keys[1:2] = block_row.astype(f32)
    keys[2:3] = rank
    capacity = places(code.shape[1], blocks)
    rounds = jnp.max(rank).astype(jnp.int32) // capacity + 1
    parts = [split(atm_near[f, 0]) for f in range(2)]
    table = jnp.concatenate([parts[f][n] for n in range(2) for f in range(2)], axis=1)

    def prepare(r):
        find_slots(rounds - 1 - r, code, block_row, rank, capacity, found)
        pl.when(r == 0)(lambda: wait_weights(weights, held, arrived))

    couple(held, table, atm, capacity, rounds, prepare, found, False, False, result, scratch)
    lane = lanes((tile_lat, BLOCK))

    def block_sums(k, f, h):
        at = (2 * k + h) * tile_lat
        return result[at : at + tile_lat, f * BLOCK : (f + 1) * BLOCK]

    for k in range(lon_count):
        edge = jnp.zeros((tile_lat, BLOCK), f32)
        for f in range(2):
            for h in range(2):
                sums[k, 2 * f + h] = block_sums(k, f, h)
            at = f * HALO
            after = turn(block_sums((k + 1) % lon_count, f, 0), at, 1)
            before = turn(block_sums((k - 1) % lon_count, f, 1), -at, 1)
            edge = jnp.where((lane >= at) & (lane < at + HALO), after, edge)
            end = BLOCK - at
            edge = jnp.where((lane >= end - HALO) & (lane < end), before, edge)
        sums[k, 4] = edge


def unweigh(gathered, found, keys, weights, gradient, result, column, *scratch):
    scratch, (held, arrived) = scratch[:2], scratch[2:]
    fetch_weights(weights, held, arrived)
    atm = gradient.shape[2]
    blocks = weights.shape[0]
    lon_count, ocean_blocks = gathered.shape[0], gathered.shape[1] // 2
    capacity = places(keys.shape[1], blocks)
    rounds = jnp.max(keys[2:3]).astype(jnp.int32) // capacity + 1
    parts = [
        split(
            jnp.concatenate(
                [gathered[k, f * ocean_blocks : (f + 1) * ocean_blocks] for k in range(lon_count)], axis=0
            )
        )
        for f in range(2)
    ]
    table = jnp.concatenate([parts[f][n] for n in range(2) for f in range(2)], axis=1)

    def prepare(r):
        @pl.when(r == 0)
        def _():
            column[...] = found[...]
            wait_weights(weights, held, arrived)

        @pl.when(r > 0)
        def _():
            find_slots(r, keys[0:1], keys[1:2].astype(jnp.int32), keys[2:3], capacity, column)

    couple(held, table, atm, capacity, rounds, prepare, column, True, True, result, scratch)
    for f in range(2):
        gradient[f, 0] = result[:, f * BLOCK : (f + 1) * BLOCK]


def on_device(tracers, cotangent, land_mask, diffusion, velocity, weights, atm_state, margins):
    levels, tile_lat, tile_lon = land_mask.shape
    lon_count, lat_count = lax.axis_size("lon"), lax.axis_size("lat")
    slots = lon_count * margins.shape[4]
    halves = tile_lon // BLOCK
    count = 9 * levels - 1
    parts = -(-count // PER_LANES)
    to_next = [(i, (i + 1) % lon_count) for i in range(lon_count)]
    to_prev = [(j, i) for i, j in to_next]
    up = [(i, i + 1) for i in range(lat_count - 1)]
    down = [(j, i) for i, j in up]
    inputs = (tracers, cotangent, land_mask, diffusion, velocity)

    def in_vmem(s):
        return pltpu.VMEM(s.shape, s.dtype)

    message = (parts, tile_lat, BLOCK)
    fields, to_west, to_east, atm_near, margins_near = call(
        pack_columns,
        [
            (count, tile_lat, tile_lon),
            message,
            message,
            atm_state.shape,
            jax.ShapeDtypeStruct(margins.shape, margins.dtype),
        ],
        [*map(in_vmem, inputs), pltpu.SemaphoreType.DMA((7,))],
        name="pack_columns",
        inputs=7,
        far=range(7),
    )(*inputs, atm_state, margins)
    from_east = lax.ppermute(to_west, "lon", to_prev)
    from_west = lax.ppermute(to_east, "lon", to_next)

    blocks_of, atm = weights.shape[0], atm_state.shape[2]
    groups = blocks_of // GROUP
    sum_parts = 2 * halves + 1
    ocean_blocks = lon_count * halves * tile_lat
    held_rows = -(-places(slots, blocks_of) * blocks_of // BLOCK) * BLOCK

    def coupling_scratch(result_rows):
        return [
            pltpu.VMEM((result_rows, 2 * BLOCK), f32),
            pltpu.VMEM((held_rows, 4 * BLOCK), f32),
            pltpu.VMEM((held_rows, 2 * BLOCK), f32),
            pltpu.VMEM((groups, GROUP, BLOCK, BLOCK), f32),
            pltpu.SemaphoreType.DMA((groups,)),
        ]

    coupling_flops = 4 * slots * blocks_of * 2 * BLOCK * BLOCK * 2
    sums, found, keys = call(
        weigh,
        [(lon_count, sum_parts, tile_lat, BLOCK), (held_rows, BLOCK), (8, slots)],
        coupling_scratch(ocean_blocks),
        coupling_flops,
        name="weigh",
        inputs=4,
        far=(2,),
    )(atm_near, margins_near, weights, to_west)

    sources = count * halves + 2 * parts
    message = (-(-sources // 2), 8, BLOCK)
    to_north, to_south, sums = call(
        pack_rows, [message, message, sums.shape], name="pack_rows", inputs=4, aliases={3: 2}
    )(fields, from_west, from_east, sums)
    received = lax.all_to_all(sums, "lon", split_axis=0, concat_axis=0, tiled=True)
    from_south = lax.ppermute(to_north, "lat", up)
    from_north = lax.ppermute(to_south, "lat", down)

    wide = (tile_lat + 8, tile_lon + BLOCK)
    adjoint, blocks, coeffs, start = call(
        run_adjoint,
        [
            cotangent.shape,
            (lon_count, 2 * halves * tile_lat, BLOCK),
            (6, levels, *wide),
            (2, levels, *wide),
        ],
        [pltpu.VMEM((count, *wide), f32), pltpu.VMEM((2, levels, *wide), f32)],
        name="run_adjoint",
        inputs=5,
    )(fields, from_west, from_east, from_north, from_south)
    gathered = lax.all_to_all(blocks, "lon", split_axis=0, concat_axis=0, tiled=True)

    message = (8, tile_lon + BLOCK)
    forcing, to_north, to_south = call(
        sum_forcing, [(2, tile_lat, tile_lon + BLOCK), message, message], name="sum_forcing", inputs=1
    )(received)
    force_south = lax.ppermute(to_north, "lat", up)
    force_north = lax.ppermute(to_south, "lat", down)
    (final,) = call(
        run_forward,
        [tracers.shape],
        [pltpu.VMEM((2, levels, *wide), f32)],
        name="run_forward",
        inputs=5,
    )(coeffs, start, forcing, force_north, force_south)

    (gradient,) = call(
        unweigh,
        [atm_state.shape],
        [coupling_scratch(atm)[0], in_vmem(found), *coupling_scratch(atm)[1:]],
        coupling_flops,
        name="unweigh",
        inputs=4,
        far=(3,),
    )(gathered, found, keys, weights)
    return (final, adjoint, gradient)


def solution(mesh):
    return jax.shard_map(
        on_device,
        mesh=mesh,
        in_specs=(
            P(None, None, "lat", "lon"),
            P(None, None, "lat", "lon"),
            P(None, "lat", "lon"),
            P(None, None, "lat", "lon"),
            P(None, None, "lat", "lon"),
            P(),
            P(None, "lat", "lon", None),
            P(None, "lat", "lon", None, None),
        ),
        out_specs=(
            P(None, None, "lat", "lon"),
            P(None, None, "lat", "lon"),
            P(None, "lat", "lon", None),
        ),
        check_vma=False,
    )
```

```python
import jax
import jax.numpy as jnp
from jax import lax
from jax.experimental import pallas as pl
from jax.experimental.pallas import tpu as pltpu
from jax.sharding import PartitionSpec as P

BLOCK = 128
STEPS = 4
HALO = STEPS
PER_LANES = BLOCK // HALO
GROUP = 8
f32 = jnp.float32
bf16 = jnp.bfloat16
VMEM_LIMIT = 32 * 1024 * 1024


def call(body, outs, scratch=(), flops=0, name=None, inputs=0, far=(), far_outs=(), aliases=None):
    outs = [s if isinstance(s, jax.ShapeDtypeStruct) else jax.ShapeDtypeStruct(s, f32) for s in outs]
    near = pl.BlockSpec(memory_space=pltpu.VMEM)
    aliases = aliases or {}
    kernel = pl.pallas_call(
        body,
        out_shape=outs,
        in_specs=[
            pl.BlockSpec(memory_space=pl.ANY)
            if n in aliases
            else pl.BlockSpec(memory_space=pltpu.HBM)
            if n in far
            else near
            for n in range(inputs)
        ],
        out_specs=[
            pl.BlockSpec(memory_space=pl.ANY) if n in aliases.values() or n in far_outs else near
            for n in range(len(outs))
        ],
        input_output_aliases=aliases,
        scratch_shapes=list(scratch),
        compiler_params=pltpu.CompilerParams(vmem_limit_bytes=VMEM_LIMIT),
        cost_estimate=pl.CostEstimate(flops=flops, bytes_accessed=1 << 20, transcendentals=0),
        name=name,
    )

    def run(*args):
        return kernel(
            *(pltpu.with_memory_space_constraint(x, pltpu.HBM) if n in far else x for n, x in enumerate(args))
        )

    return run


def lanes(shape):
    return lax.broadcasted_iota(jnp.int32, shape, len(shape) - 1)


def rows(shape):
    return lax.broadcasted_iota(jnp.int32, shape, len(shape) - 2)


def turn(x, shift, axis):
    shift %= x.shape[axis]
    return pltpu.roll(x, shift, axis) if shift else x


def tile_fields(tracers, cotangent, land_mask, diffusion, velocity):
    levels = land_mask.shape[0]
    mask = [land_mask[level].astype(f32) for level in range(levels)]
    out = [tracers[f, level] for f in range(2) for level in range(levels)]
    out += [cotangent[f, level] for f in range(2) for level in range(levels)]
    out += [diffusion[0, level] * mask[level] for level in range(levels)]
    out += [velocity[0, level] * mask[level] for level in range(levels)]
    out += [diffusion[1, level] * mask[level] for level in range(levels)]
    out += [velocity[1, level] * mask[level] for level in range(levels)]
    out += [diffusion[2, level] * mask[level] * mask[level + 1] for level in range(levels - 1)]
    return out


def fetch(pairs, arrived):
    copies = [pltpu.make_async_copy(src, dst, arrived.at[n]) for n, (src, dst) in enumerate(pairs)]
    for copy in copies:
        copy.start()
    return copies


def pack_columns(*refs):
    inputs, (fields, to_west, to_east), scratch = refs[:7], refs[7:10], refs[12:]
    copies = fetch(zip(inputs, [*scratch[:5], *refs[10:12]]), scratch[5])
    for copy in copies[:5]:
        copy.wait()
    shape = to_west.shape[1:]
    lane = lanes(shape)
    west = [jnp.zeros(shape, f32) for _ in range(to_west.shape[0])]
    east = [jnp.zeros(shape, f32) for _ in range(to_west.shape[0])]
    for i, field in enumerate(tile_fields(*scratch[:5])):
        fields[i] = field
        part, at = divmod(i, PER_LANES)
        at *= HALO
        here = (lane >= at) & (lane < at + HALO)
        west[part] = jnp.where(here, turn(field[:, :BLOCK], at, 1), west[part])
        east[part] = jnp.where(here, turn(field[:, -BLOCK:], at + HALO, 1), east[part])
    for part in range(to_west.shape[0]):
        to_west[part] = west[part]
        to_east[part] = east[part]
    for copy in copies[5:]:
        copy.wait()


def unpack_columns(from_west, from_east, i):
    part, at = divmod(i, PER_LANES)
    at *= HALO
    lane = lanes(from_west[part].shape)
    east = turn(from_east[part], -at, 1)
    west = turn(from_west[part], -at - HALO, 1)
    return jnp.where(lane < HALO, east, jnp.where(lane >= BLOCK - HALO, west, 0.0))


def row_sources(fields, from_west, from_east):
    out = [(fields, (i, slice(None), slice(h * BLOCK, (h + 1) * BLOCK)))
           for i in range(fields.shape[0]) for h in range(fields.shape[2] // BLOCK)]
    for columns in (from_west, from_east):
        out += [(columns, (part,)) for part in range(columns.shape[0])]
    return out


def pack_rows(fields, from_west, from_east, sums, to_north, to_south, same_sums):
    sources = [ref[at] for ref, at in row_sources(fields, from_west, from_east)]
    half = to_north.shape[0]
    row = rows((8, BLOCK))
    for i in range(half):
        first = sources[i]
        second = sources[i + half] if i + half < len(sources) else jnp.zeros_like(first)
        to_north[i] = jnp.where(row < HALO, turn(first[-8:], HALO, 0), second[-8:])
        to_south[i] = jnp.where(row < HALO, first[:8], turn(second[:8], HALO, 0))


def edge_rows(from_north, from_south, i):
    half = from_north.shape[0]
    if i < half:
        north, south = from_north[i], turn(from_south[i], HALO, 0)
    else:
        north, south = turn(from_north[i - half], HALO, 0), from_south[i - half]
    return jnp.where(rows((8, BLOCK)) < HALO, north, south)


def widen(fields, from_west, from_east, from_north, from_south, wide):
    count, tile_lat, tile_lon = fields.shape
    halves = tile_lon // BLOCK
    parts = from_west.shape[0]
    corners = [edge_rows(from_north, from_south, count * halves + n) for n in range(2 * parts)]
    for i in range(count):
        wide[i, :tile_lat, :tile_lon] = fields[i]
        wide[i, :tile_lat, tile_lon:] = unpack_columns(from_west, from_east, i)
        for h in range(halves):
            wide[i, tile_lat:, h * BLOCK : (h + 1) * BLOCK] = edge_rows(from_north, from_south, i * halves + h)
        wide[i, tile_lat:, tile_lon:] = unpack_columns(corners[:parts], corners[parts:], i)


def eastward(x):
    return turn(x, -1, 1)


def westward(x):
    return turn(x, 1, 1)


def northward(x):
    return turn(x, -1, 0)


def southward(x):
    return turn(x, 1, 0)


def adjoint_step(coeffs, read, write):
    levels = coeffs.shape[1]
    above = None
    for level in range(levels):
        lam = read(level)
        step_x = eastward(lam) - lam
        step_y = northward(lam) - lam
        out = lam + coeffs[0, level] * step_x + westward(coeffs[1, level] * step_x)
        out = out + coeffs[2, level] * step_y + southward(coeffs[3, level] * step_y)
        if above is not None:
            out = out - above
        if level < levels - 1:
            above = coeffs[4, level] * (read(level + 1) - lam)
            out = out + above
        write(level, out)


def run_adjoint(
    fields, from_west, from_east, from_north, from_south, blocks, coeffs, start, lam_out, wide, state, own, sent
):
    levels = coeffs.shape[1]
    tile_lat, tile_lon = fields.shape[1:]
    halves = tile_lon // BLOCK
    widen(fields, from_west, from_east, from_north, from_south, wide)
    base = 4 * levels
    for f in range(2):
        for level in range(levels):
            start[f, level] = wide[f * levels + level]
    mask0 = None
    for level in range(levels):
        east_d, east_u = wide[base + level], wide[base + levels + level]
        north_d, north_u = wide[base + 2 * levels + level], wide[base + 3 * levels + level]
        mask = (east_d > 0.0).astype(f32)
        mask0 = mask if mask0 is None else mask0
        mask_e, mask_n = eastward(mask), northward(mask)
        east_k, east_v = east_d * mask_e, east_u * mask_e
        north_k, north_v = north_d * mask_n, north_u * mask_n
        coeffs[0, level] = jnp.maximum(east_v, 0.0) + east_k
        coeffs[1, level] = jnp.minimum(east_v, 0.0) - east_k
        coeffs[2, level] = jnp.maximum(north_v, 0.0) + north_k
        coeffs[3, level] = jnp.minimum(north_v, 0.0) - north_k
        coeffs[4, level] = wide[base + 4 * levels + level] if level < levels - 1 else jnp.zeros_like(mask)
        coeffs[5, level] = mask
    copies = []
    for f in range(2):
        surface = wide[(2 + f) * levels, :tile_lat, :tile_lon]
        for step in range(STEPS - 1):
            def read(level):
                return wide[(2 + f) * levels + level] if step == 0 else state[(step - 1) % 2, level]

            def write(level, lam):
                nonlocal surface
                if level == 0:
                    surface = surface + lam[:tile_lat, :tile_lon]
                if step == STEPS - 2:
                    lam_out[f, level] = lam
                else:
                    state[step % 2, level] = lam

            adjoint_step(coeffs, read, write)
        surface = surface * mask0[:tile_lat, :tile_lon]
        for h in range(halves):
            at = (f * halves + h) * tile_lat
            own[at : at + tile_lat] = surface[:, h * BLOCK : (h + 1) * BLOCK]
        field = pl.ds(f * halves * tile_lat, halves * tile_lat)
        copies += fetch([(own.at[field], blocks.at[k, field]) for k in range(blocks.shape[0])], sent.at[f])
    for copy in copies:
        copy.wait()


def sum_forcing(received, forcing, to_north, to_south):
    tile_lat = forcing.shape[1]
    halves = forcing.shape[2] // BLOCK - 1
    total = received[0]
    for j in range(1, received.shape[0]):
        total = total + received[j]
    lane = lanes((tile_lat, BLOCK))
    upper = total[2 * halves * tile_lat :]
    lower = jnp.where(lane[: tile_lat // 2] < BLOCK // 2, turn(upper, -2 * HALO, 1), turn(upper, 2 * HALO, 1))
    packed = jnp.concatenate([upper, lower], axis=0)
    for f in range(2):
        for h in range(halves):
            at = (f * halves + h) * tile_lat
            forcing[f, :, h * BLOCK : (h + 1) * BLOCK] = total[at : at + tile_lat]
        near = (lane < HALO) | (lane >= BLOCK - HALO)
        if f == 0:
            edge = packed
        else:
            edge = jnp.where(lane < HALO, turn(packed, -HALO, 1), turn(packed, HALO, 1))
        forcing[f, :, halves * BLOCK :] = jnp.where(near, edge, 0.0)
    row = rows((8, forcing.shape[2]))
    to_north[...] = jnp.where(row < HALO, turn(forcing[0, tile_lat - 8 :], HALO, 0), forcing[1, tile_lat - 8 :])
    to_south[...] = jnp.where(row < HALO, forcing[0, :8], turn(forcing[1, :8], HALO, 0))


def run_forward(coeffs, start, lam, forcing, from_north, from_south, final, adjoint_out, state):
    levels = coeffs.shape[1]
    tile_lat, tile_lon = final.shape[2:]
    row = rows((8, forcing.shape[2]))
    for f in range(2):

        def write(level, out):
            adjoint_out[f, level] = out[:tile_lat, :tile_lon]

        adjoint_step(coeffs, lambda level: lam[f, level], write)
        if f == 0:
            north, south = from_north[...], turn(from_south[...], HALO, 0)
        else:
            north, south = turn(from_north[...], HALO, 0), from_south[...]
        force = jnp.concatenate([forcing[f], jnp.where(row < HALO, north, south)], axis=0)
        force = force * coeffs[5, 0]
        for step in range(STEPS):
            above = None
            for level in range(levels):
                read = (lambda n: start[f, n]) if step == 0 else (lambda n: state[(step - 1) % 2, n])
                theta = read(level)
                east_flux = coeffs[0, level] * theta + coeffs[1, level] * eastward(theta)
                north_flux = coeffs[2, level] * theta + coeffs[3, level] * northward(theta)
                out = theta - (east_flux - westward(east_flux)) - (north_flux - southward(north_flux))
                if level < levels - 1:
                    vertical = coeffs[4, level] * (theta - read(level + 1))
                    out = out - vertical
                if above is not None:
                    out = out + above
                above = vertical if level < levels - 1 else None
                if level == 0:
                    out = out + force
                if step == STEPS - 1:
                    final[f, level] = out[:tile_lat, :tile_lon]
                else:
                    state[step % 2, level] = out


def split(x):
    high = x.astype(bf16)
    return high, (x - high.astype(f32)).astype(bf16)


def weight_copies(weights, held, arrived):
    for g in range(held.shape[0]):
        yield pltpu.make_async_copy(weights.at[pl.ds(g * GROUP, GROUP)], held.at[g], arrived.at[g])


def fetch_weights(weights, held, arrived):
    for copy in weight_copies(weights, held, arrived):
        copy.start()


def wait_weights(weights, held, arrived):
    for copy in weight_copies(weights, held, arrived):
        copy.wait()


def one_hot(where):
    return jnp.where(where, 1.0, 0.0).astype(bf16)


def places(slots, blocks):
    return 8 * (-(-2 * slots // (8 * blocks)) + 1)


def as_row(ids):
    return jnp.concatenate([ids[k : k + 1, :] for k in range(ids.shape[0])], axis=1)


def rank_slots(block_row, blocks):
    slots = block_row.shape[1]
    mine = rows((blocks, slots)) == block_row
    upper = one_hot(rows((slots, slots)) < lanes((slots, slots)))
    before = jnp.dot(one_hot(mine), upper, preferred_element_type=f32)
    return jnp.sum(jnp.where(mine, before, 0.0), axis=0, keepdims=True)


def find_slots(r, code, block_row, rank, capacity, column):
    slots = block_row.shape[1]
    place = rank.astype(jnp.int32) - r * capacity
    place = jnp.where((place >= 0) & (place < capacity), block_row * capacity + place, -1)
    for at in range(0, column.shape[0], BLOCK):
        here = rows((BLOCK, slots)) + at == place
        found = jnp.sum(jnp.where(here, code + 1.0, 0.0), axis=1, keepdims=True) - 1.0
        column[at : at + BLOCK] = jnp.broadcast_to(found, (BLOCK, BLOCK))


def couple(blocks, part, table, size, capacity, rounds, prepare, column, gather_first, transposed, result, scratch):
    vectors, products = scratch
    total_rows = column.shape[0]
    result[...] = jnp.zeros_like(result)

    def one_round(r, carry):
        prepare(r)
        eye = rows((BLOCK, BLOCK)) == lanes((BLOCK, BLOCK))
        place_hot = []
        for at in range(0, total_rows, BLOCK):
            found = column[at : at + BLOCK]
            first = jnp.floor((found + 0.5) * (1.0 / size))
            second = found - first * size
            gather, put = (first, second) if gather_first else (second, first)
            width = table.shape[0]
            gather = jnp.concatenate([gather] * (width // BLOCK), axis=1)
            hot = one_hot(gather == lanes((BLOCK, width)).astype(f32))
            vectors[at : at + BLOCK] = jnp.dot(hot, table, preferred_element_type=f32)
            put = jnp.sum(jnp.where(eye, put, 0.0), axis=0, keepdims=True)
            place_hot.append(one_hot(rows((result.shape[0], BLOCK)).astype(f32) == put))

        def group(g, carry):
            for u in range(GROUP):
                at = pl.multiple_of((g * GROUP + u) * capacity, 8)
                own = vectors[pl.ds(at, capacity)]
                left = jnp.concatenate([own[:, n * BLOCK : (n + 1) * BLOCK] for n in range(4)], axis=0)
                high, low = part(g, u)
                right = jnp.concatenate([high, low], axis=1 if transposed else 0)
                contract = (((1,), (0 if transposed else 1,)), ((), ()))
                product = lax.dot_general(left.astype(bf16), right, contract, preferred_element_type=f32)
                for f in range(2):
                    high_part = product[f * capacity : (f + 1) * capacity]
                    low_part = product[(f + 2) * capacity : (f + 3) * capacity, :BLOCK]
                    products[pl.ds(at, capacity), f * BLOCK : (f + 1) * BLOCK] = (
                        high_part[:, BLOCK:] + low_part
                    ) + high_part[:, :BLOCK]
            return carry

        lax.fori_loop(0, blocks // GROUP, group, 0)
        summed = jnp.dot(
            jnp.concatenate(place_hot, axis=1),
            jnp.concatenate(split(products[...]), axis=1),
            preferred_element_type=f32,
        )
        result[...] += summed[:, : 2 * BLOCK] + summed[:, 2 * BLOCK :]
        return carry

    lax.fori_loop(0, rounds, one_round, 0)


def slot_keys(ids, tile_lat, atm):
    lon_count, cap = ids.shape[3:]
    ocean, atm_ids, block_ids = (ids[n, 0, 0] for n in range(3))
    order = (ocean & 1) * tile_lat + (ocean >> 1) + rows((lon_count, cap)) * (2 * tile_lat)
    order = jnp.where(ocean >= 0, order, lon_count * 2 * tile_lat)
    return as_row((order * atm + atm_ids).astype(f32)), as_row(block_ids)


def weigh(atm_near, margins, weights, after, sums, found, keys, parted, result, *scratch):
    scratch, (held, arrived) = scratch[:2], scratch[2:]
    fetch_weights(weights, held, arrived)
    lon_count = margins.shape[3]
    atm = atm_near.shape[2]
    blocks = weights.shape[0]
    tile_lat = 2 * sums.shape[1] // 9
    code, block_row = slot_keys(margins, tile_lat, atm)
    rank = rank_slots(block_row, blocks)
    keys[0:1] = code
    keys[1:2] = block_row.astype(f32)
    keys[2:3] = rank
    capacity = places(code.shape[1], blocks)
    rounds = jnp.max(rank).astype(jnp.int32) // capacity + 1
    parts = [split(atm_near[f, 0]) for f in range(2)]
    table = jnp.concatenate([parts[f][n] for n in range(2) for f in range(2)], axis=1)

    def prepare(r):
        find_slots(rounds - 1 - r, code, block_row, rank, capacity, found)
        pl.when(r == 0)(lambda: wait_weights(weights, held, arrived))

    def part(g, u):
        high, low = split(held[g, u])
        parted[g * GROUP + u, 0] = high
        parted[g * GROUP + u, 1] = low
        return high, low

    couple(blocks, part, table, atm, capacity, rounds, prepare, found, False, False, result, scratch)
    lane = lanes((tile_lat, BLOCK))

    def block_sums(k, f, h):
        at = (2 * k + h) * tile_lat
        return result[at : at + tile_lat, f * BLOCK : (f + 1) * BLOCK]

    for k in range(lon_count):
        edge = jnp.zeros((tile_lat, BLOCK), f32)
        for f in range(2):
            for h in range(2):
                sums[k, (2 * f + h) * tile_lat : (2 * f + h + 1) * tile_lat] = block_sums(k, f, h)
            at = f * HALO
            after = turn(block_sums((k + 1) % lon_count, f, 0), at, 1)
            before = turn(block_sums((k - 1) % lon_count, f, 1), -at, 1)
            edge = jnp.where((lane >= at) & (lane < at + HALO), after, edge)
            end = BLOCK - at
            edge = jnp.where((lane >= end - HALO) & (lane < end), before, edge)
        upper, lower = edge[: tile_lat // 2], edge[tile_lat // 2 :]
        near = lane[: tile_lat // 2]
        lower = jnp.where(near < BLOCK // 2, turn(lower, 2 * HALO, 1), turn(lower, -2 * HALO, 1))
        sums[k, 4 * tile_lat :] = jnp.where((near < 2 * HALO) | (near >= BLOCK - 2 * HALO), upper, lower)


def unweigh(gathered, found, keys, parted, gradient, result, column, *scratch):
    atm = gradient.shape[2]
    blocks = parted.shape[0]
    lon_count, ocean_blocks = gathered.shape[0], gathered.shape[1] // 2
    capacity = places(keys.shape[1], blocks)
    rounds = jnp.max(keys[2:3]).astype(jnp.int32) // capacity + 1
    parts = [
        split(
            jnp.concatenate(
                [gathered[k, f * ocean_blocks : (f + 1) * ocean_blocks] for k in range(lon_count)], axis=0
            )
        )
        for f in range(2)
    ]
    table = jnp.concatenate([parts[f][n] for n in range(2) for f in range(2)], axis=1)

    def prepare(r):
        @pl.when(r == 0)
        def _():
            column[...] = found[...]

        @pl.when(r > 0)
        def _():
            find_slots(r, keys[0:1], keys[1:2].astype(jnp.int32), keys[2:3], capacity, column)

    couple(
        blocks,
        lambda g, u: (parted[g * GROUP + u, 0], parted[g * GROUP + u, 1]),
        table,
        atm,
        capacity,
        rounds,
        prepare,
        column,
        True,
        True,
        result,
        scratch,
    )
    for f in range(2):
        gradient[f, 0] = result[:, f * BLOCK : (f + 1) * BLOCK]


def on_device(tracers, cotangent, land_mask, diffusion, velocity, weights, atm_state, margins):
    levels, tile_lat, tile_lon = land_mask.shape
    lon_count, lat_count = lax.axis_size("lon"), lax.axis_size("lat")
    slots = lon_count * margins.shape[4]
    halves = tile_lon // BLOCK
    count = 9 * levels - 1
    parts = -(-count // PER_LANES)
    to_next = [(i, (i + 1) % lon_count) for i in range(lon_count)]
    to_prev = [(j, i) for i, j in to_next]
    up = [(i, i + 1) for i in range(lat_count - 1)]
    down = [(j, i) for i, j in up]
    inputs = (tracers, cotangent, land_mask, diffusion, velocity)

    def in_vmem(s):
        return pltpu.VMEM(s.shape, s.dtype)

    message = (parts, tile_lat, BLOCK)
    fields, to_west, to_east, atm_near, margins_near = call(
        pack_columns,
        [
            (count, tile_lat, tile_lon),
            message,
            message,
            atm_state.shape,
            jax.ShapeDtypeStruct(margins.shape, margins.dtype),
        ],
        [*map(in_vmem, inputs), pltpu.SemaphoreType.DMA((7,))],
        name="pack_columns",
        inputs=7,
        far=range(7),
    )(*inputs, atm_state, margins)
    from_east = lax.ppermute(to_west, "lon", to_prev)
    from_west = lax.ppermute(to_east, "lon", to_next)

    blocks_of, atm = weights.shape[0], atm_state.shape[2]
    groups = blocks_of // GROUP
    sum_rows = 2 * halves * tile_lat + tile_lat // 2
    ocean_blocks = lon_count * halves * tile_lat
    held_rows = -(-places(slots, blocks_of) * blocks_of // BLOCK) * BLOCK

    def coupling_scratch(result_rows):
        return [
            pltpu.VMEM((result_rows, 2 * BLOCK), f32),
            pltpu.VMEM((held_rows, 4 * BLOCK), f32),
            pltpu.VMEM((held_rows, 2 * BLOCK), f32),
        ]

    coupling_flops = 4 * slots * blocks_of * 2 * BLOCK * BLOCK * 2
    parted = jax.ShapeDtypeStruct((blocks_of, 2, BLOCK, BLOCK), bf16)
    sums, found, keys, parted = call(
        weigh,
        [(lon_count, sum_rows, BLOCK), (held_rows, BLOCK), (8, slots), parted],
        [
            *coupling_scratch(ocean_blocks),
            pltpu.VMEM((groups, GROUP, BLOCK, BLOCK), f32),
            pltpu.SemaphoreType.DMA((groups,)),
        ],
        coupling_flops,
        name="weigh",
        inputs=4,
        far=(2,),
    )(atm_near, margins_near, weights, to_west)

    sources = count * halves + 2 * parts
    message = (-(-sources // 2), 8, BLOCK)
    to_north, to_south, sums = call(
        pack_rows, [message, message, sums.shape], name="pack_rows", inputs=4, aliases={3: 2}
    )(fields, from_west, from_east, sums)
    received = lax.all_to_all(sums, "lon", split_axis=0, concat_axis=0, tiled=True)
    from_south = lax.ppermute(to_north, "lat", up)
    from_north = lax.ppermute(to_south, "lat", down)

    wide = (tile_lat + 8, tile_lon + BLOCK)
    own = (2 * halves * tile_lat, BLOCK)
    blocks, coeffs, start, lam = call(
        run_adjoint,
        [(lon_count, *own), (6, levels, *wide), (2, levels, *wide), (2, levels, *wide)],
        [
            pltpu.VMEM((count, *wide), f32),
            pltpu.VMEM((2, levels, *wide), f32),
            pltpu.VMEM(own, f32),
            pltpu.SemaphoreType.DMA((2, lon_count)),
        ],
        name="run_adjoint",
        inputs=5,
        far_outs=(0,),
    )(fields, from_west, from_east, from_north, from_south)
    gathered = lax.all_to_all(blocks, "lon", split_axis=0, concat_axis=0, tiled=True)

    message = (8, tile_lon + BLOCK)
    forcing, to_north, to_south = call(
        sum_forcing, [(2, tile_lat, tile_lon + BLOCK), message, message], name="sum_forcing", inputs=1
    )(received)
    force_south = lax.ppermute(to_north, "lat", up)
    force_north = lax.ppermute(to_south, "lat", down)
    final, adjoint = call(
        run_forward,
        [tracers.shape, cotangent.shape],
        [pltpu.VMEM((2, levels, *wide), f32)],
        name="run_forward",
        inputs=6,
    )(coeffs, start, lam, forcing, force_north, force_south)

    (gradient,) = call(
        unweigh,
        [atm_state.shape],
        [coupling_scratch(atm)[0], in_vmem(found), *coupling_scratch(atm)[1:]],
        coupling_flops,
        name="unweigh",
        inputs=4,
    )(gathered, found, keys, parted)
    return (final, adjoint, gradient)


def solution(mesh):
    return jax.shard_map(
        on_device,
        mesh=mesh,
        in_specs=(
            P(None, None, "lat", "lon"),
            P(None, None, "lat", "lon"),
            P(None, "lat", "lon"),
            P(None, None, "lat", "lon"),
            P(None, None, "lat", "lon"),
            P(),
            P(None, "lat", "lon", None),
            P(None, "lat", "lon", None, None),
        ),
        out_specs=(
            P(None, None, "lat", "lon"),
            P(None, None, "lat", "lon"),
            P(None, "lat", "lon", None),
        ),
        check_vma=False,
    )
```

```python
import jax
import jax.numpy as jnp
from jax import lax
from jax.experimental import pallas as pl
from jax.experimental.pallas import tpu as pltpu
from jax.sharding import PartitionSpec as P

BLOCK = 128
STEPS = 4
HALO = STEPS
PER_LANES = BLOCK // HALO
GROUP = 8
f32 = jnp.float32
bf16 = jnp.bfloat16
VMEM_LIMIT = 32 * 1024 * 1024


def call(body, outs, scratch=(), flops=0, name=None, inputs=0, far=(), far_outs=(), aliases=None):
    outs = [s if isinstance(s, jax.ShapeDtypeStruct) else jax.ShapeDtypeStruct(s, f32) for s in outs]
    near = pl.BlockSpec(memory_space=pltpu.VMEM)
    aliases = aliases or {}
    kernel = pl.pallas_call(
        body,
        out_shape=outs,
        in_specs=[
            pl.BlockSpec(memory_space=pl.ANY)
            if n in aliases
            else pl.BlockSpec(memory_space=pltpu.HBM)
            if n in far
            else near
            for n in range(inputs)
        ],
        out_specs=[
            pl.BlockSpec(memory_space=pl.ANY) if n in aliases.values() or n in far_outs else near
            for n in range(len(outs))
        ],
        input_output_aliases=aliases,
        scratch_shapes=list(scratch),
        compiler_params=pltpu.CompilerParams(vmem_limit_bytes=VMEM_LIMIT),
        cost_estimate=pl.CostEstimate(flops=flops, bytes_accessed=1 << 20, transcendentals=0),
        name=name,
    )

    def run(*args):
        return kernel(
            *(pltpu.with_memory_space_constraint(x, pltpu.HBM) if n in far else x for n, x in enumerate(args))
        )

    return run


def lanes(shape):
    return lax.broadcasted_iota(jnp.int32, shape, len(shape) - 1)


def rows(shape):
    return lax.broadcasted_iota(jnp.int32, shape, len(shape) - 2)


def turn(x, shift, axis):
    shift %= x.shape[axis]
    return pltpu.roll(x, shift, axis) if shift else x


def swap(near, far, axis, wrap):
    count = lax.axis_size(axis)
    pairs = [[], []]
    for i in range(count if wrap else count - 1):
        j = (i + 1) % count
        pairs[i % 2] += [(i, j), (j, i)]
    far = lax.ppermute(far, axis, pairs[1])
    return lax.ppermute(near, axis, pairs[0]), far


def sort_swap(axis, after, before):
    odd = lax.rem(lax.axis_index(axis), 2) == 1
    return jnp.where(odd, before, after), jnp.where(odd, after, before)


def tile_fields(tracers, cotangent, land_mask, diffusion, velocity):
    levels = land_mask.shape[0]
    mask = [land_mask[level].astype(f32) for level in range(levels)]
    out = [tracers[f, level] for f in range(2) for level in range(levels)]
    out += [cotangent[f, level] for f in range(2) for level in range(levels)]
    out += [diffusion[0, level] * mask[level] for level in range(levels)]
    out += [velocity[0, level] * mask[level] for level in range(levels)]
    out += [diffusion[1, level] * mask[level] for level in range(levels)]
    out += [velocity[1, level] * mask[level] for level in range(levels)]
    out += [diffusion[2, level] * mask[level] * mask[level + 1] for level in range(levels - 1)]
    return out


def fetch(pairs, arrived):
    copies = [pltpu.make_async_copy(src, dst, arrived.at[n]) for n, (src, dst) in enumerate(pairs)]
    for copy in copies:
        copy.start()
    return copies


def pack_columns(*refs):
    inputs, (fields, near, far), scratch = refs[:7], refs[7:10], refs[12:]
    copies = fetch(zip(inputs, [*scratch[:5], *refs[10:12]]), scratch[5])
    for copy in copies[:5]:
        copy.wait()
    shape = near.shape[1:]
    lane = lanes(shape)
    west = [jnp.zeros(shape, f32) for _ in range(near.shape[0])]
    east = [jnp.zeros(shape, f32) for _ in range(near.shape[0])]
    for i, field in enumerate(tile_fields(*scratch[:5])):
        fields[i] = field
        part, at = divmod(i, PER_LANES)
        at *= HALO
        here = (lane >= at) & (lane < at + HALO)
        west[part] = jnp.where(here, turn(field[:, :BLOCK], at, 1), west[part])
        east[part] = jnp.where(here, turn(field[:, -BLOCK:], at + HALO, 1), east[part])
    for part in range(near.shape[0]):
        near[part], far[part] = sort_swap("lon", east[part], west[part])
    for copy in copies[5:]:
        copy.wait()


def unpack_columns(from_west, from_east, i):
    part, at = divmod(i, PER_LANES)
    at *= HALO
    lane = lanes(from_west[part].shape)
    east = turn(from_east[part], -at, 1)
    west = turn(from_west[part], -at - HALO, 1)
    return jnp.where(lane < HALO, east, jnp.where(lane >= BLOCK - HALO, west, 0.0))


def row_sources(fields, from_west, from_east):
    out = [(fields, (i, slice(None), slice(h * BLOCK, (h + 1) * BLOCK)))
           for i in range(fields.shape[0]) for h in range(fields.shape[2] // BLOCK)]
    for columns in (from_west, from_east):
        out += [(columns, (part,)) for part in range(columns.shape[0])]
    return out


def pack_rows(fields, near_columns, far_columns, sums, near, far, from_west, from_east, same_sums):
    for part in range(from_west.shape[0]):
        from_east[part], from_west[part] = sort_swap("lon", near_columns[part], far_columns[part])
    sources = [ref[at] for ref, at in row_sources(fields, from_west, from_east)]
    half = near.shape[0]
    row = rows((8, BLOCK))
    for i in range(half):
        first = sources[i]
        second = sources[i + half] if i + half < len(sources) else jnp.zeros_like(first)
        to_north = jnp.where(row < HALO, turn(first[-8:], HALO, 0), second[-8:])
        to_south = jnp.where(row < HALO, first[:8], turn(second[:8], HALO, 0))
        near[i], far[i] = sort_swap("lat", to_north, to_south)


def edge_rows(near, far, i):
    half = near.shape[0]
    from_north, from_south = sort_swap("lat", near[i % half], far[i % half])
    if i < half:
        from_south = turn(from_south, HALO, 0)
    else:
        from_north = turn(from_north, HALO, 0)
    return jnp.where(rows(from_north.shape) < HALO, from_north, from_south)


def widen(fields, from_west, from_east, near, far, wide):
    count, tile_lat, tile_lon = fields.shape
    halves = tile_lon // BLOCK
    parts = from_west.shape[0]
    corners = [edge_rows(near, far, count * halves + n) for n in range(2 * parts)]
    for i in range(count):
        wide[i, :tile_lat, :tile_lon] = fields[i]
        wide[i, :tile_lat, tile_lon:] = unpack_columns(from_west, from_east, i)
        for h in range(halves):
            wide[i, tile_lat:, h * BLOCK : (h + 1) * BLOCK] = edge_rows(near, far, i * halves + h)
        wide[i, tile_lat:, tile_lon:] = unpack_columns(corners[:parts], corners[parts:], i)


def eastward(x):
    return turn(x, -1, 1)


def westward(x):
    return turn(x, 1, 1)


def northward(x):
    return turn(x, -1, 0)


def southward(x):
    return turn(x, 1, 0)


def adjoint_step(coeffs, read, write):
    levels = coeffs.shape[1]
    above = None
    for level in range(levels):
        lam = read(level)
        step_x = eastward(lam) - lam
        step_y = northward(lam) - lam
        out = lam + coeffs[0, level] * step_x + westward(coeffs[1, level] * step_x)
        out = out + coeffs[2, level] * step_y + southward(coeffs[3, level] * step_y)
        if above is not None:
            out = out - above
        if level < levels - 1:
            above = coeffs[4, level] * (read(level + 1) - lam)
            out = out + above
        write(level, out)


def run_adjoint(
    fields, from_west, from_east, near, far, blocks, coeffs, start, lam_out, wide, state, own, sent
):
    levels = coeffs.shape[1]
    tile_lat, tile_lon = fields.shape[1:]
    halves = tile_lon // BLOCK
    widen(fields, from_west, from_east, near, far, wide)
    base = 4 * levels
    for f in range(2):
        for level in range(levels):
            start[f, level] = wide[f * levels + level]
    mask0 = None
    for level in range(levels):
        east_d, east_u = wide[base + level], wide[base + levels + level]
        north_d, north_u = wide[base + 2 * levels + level], wide[base + 3 * levels + level]
        mask = (east_d > 0.0).astype(f32)
        mask0 = mask if mask0 is None else mask0
        mask_e, mask_n = eastward(mask), northward(mask)
        east_k, east_v = east_d * mask_e, east_u * mask_e
        north_k, north_v = north_d * mask_n, north_u * mask_n
        coeffs[0, level] = jnp.maximum(east_v, 0.0) + east_k
        coeffs[1, level] = jnp.minimum(east_v, 0.0) - east_k
        coeffs[2, level] = jnp.maximum(north_v, 0.0) + north_k
        coeffs[3, level] = jnp.minimum(north_v, 0.0) - north_k
        coeffs[4, level] = wide[base + 4 * levels + level] if level < levels - 1 else jnp.zeros_like(mask)
        coeffs[5, level] = mask
    copies = []
    for f in range(2):
        surface = wide[(2 + f) * levels, :tile_lat, :tile_lon]
        for step in range(STEPS - 1):
            def read(level):
                return wide[(2 + f) * levels + level] if step == 0 else state[(step - 1) % 2, level]

            def write(level, lam):
                nonlocal surface
                if level == 0:
                    surface = surface + lam[:tile_lat, :tile_lon]
                if step == STEPS - 2:
                    lam_out[f, level] = lam
                else:
                    state[step % 2, level] = lam

            adjoint_step(coeffs, read, write)
        surface = surface * mask0[:tile_lat, :tile_lon]
        for h in range(halves):
            at = (f * halves + h) * tile_lat
            own[at : at + tile_lat] = surface[:, h * BLOCK : (h + 1) * BLOCK]
        field = pl.ds(f * halves * tile_lat, halves * tile_lat)
        copies += fetch([(own.at[field], blocks.at[k, field]) for k in range(blocks.shape[0])], sent.at[f])
    for copy in copies:
        copy.wait()


def sum_forcing(received, forcing, near, far):
    tile_lat = forcing.shape[1]
    halves = forcing.shape[2] // BLOCK - 1
    total = received[0]
    for j in range(1, received.shape[0]):
        total = total + received[j]
    lane = lanes((tile_lat, BLOCK))
    upper = total[2 * halves * tile_lat :]
    lower = jnp.where(lane[: tile_lat // 2] < BLOCK // 2, turn(upper, -2 * HALO, 1), turn(upper, 2 * HALO, 1))
    packed = jnp.concatenate([upper, lower], axis=0)
    for f in range(2):
        for h in range(halves):
            at = (f * halves + h) * tile_lat
            forcing[f, :, h * BLOCK : (h + 1) * BLOCK] = total[at : at + tile_lat]
        used = (lane < HALO) | (lane >= BLOCK - HALO)
        if f == 0:
            edge = packed
        else:
            edge = jnp.where(lane < HALO, turn(packed, -HALO, 1), turn(packed, HALO, 1))
        forcing[f, :, halves * BLOCK :] = jnp.where(used, edge, 0.0)
    row = rows((8, forcing.shape[2]))
    to_north = jnp.where(row < HALO, turn(forcing[0, tile_lat - 8 :], HALO, 0), forcing[1, tile_lat - 8 :])
    to_south = jnp.where(row < HALO, forcing[0, :8], turn(forcing[1, :8], HALO, 0))
    near[0], far[0] = sort_swap("lat", to_north, to_south)


def run_forward(coeffs, start, lam, forcing, near, far, final, adjoint_out, state):
    levels = coeffs.shape[1]
    tile_lat, tile_lon = final.shape[2:]
    for f in range(2):

        def write(level, out):
            adjoint_out[f, level] = out[:tile_lat, :tile_lon]

        adjoint_step(coeffs, lambda level: lam[f, level], write)
        force = jnp.concatenate([forcing[f], edge_rows(near, far, f)], axis=0)
        force = force * coeffs[5, 0]
        for step in range(STEPS):
            above = None
            for level in range(levels):
                read = (lambda n: start[f, n]) if step == 0 else (lambda n: state[(step - 1) % 2, n])
                theta = read(level)
                east_flux = coeffs[0, level] * theta + coeffs[1, level] * eastward(theta)
                north_flux = coeffs[2, level] * theta + coeffs[3, level] * northward(theta)
                out = theta - (east_flux - westward(east_flux)) - (north_flux - southward(north_flux))
                if level < levels - 1:
                    vertical = coeffs[4, level] * (theta - read(level + 1))
                    out = out - vertical
                if above is not None:
                    out = out + above
                above = vertical if level < levels - 1 else None
                if level == 0:
                    out = out + force
                if step == STEPS - 1:
                    final[f, level] = out[:tile_lat, :tile_lon]
                else:
                    state[step % 2, level] = out


def split(x):
    high = x.astype(bf16)
    return high, (x - high.astype(f32)).astype(bf16)


def weight_copies(weights, held, arrived):
    for g in range(held.shape[0]):
        yield pltpu.make_async_copy(weights.at[pl.ds(g * GROUP, GROUP)], held.at[g], arrived.at[g])


def fetch_weights(weights, held, arrived):
    for copy in weight_copies(weights, held, arrived):
        copy.start()


def held_part(weights, held, arrived):
    def part(r, g, u):
        if u == 0:

            @pl.when(r == 0)
            def _():
                pltpu.make_async_copy(weights.at[pl.ds(g * GROUP, GROUP)], held.at[g], arrived.at[g]).wait()

        return split(held[g, u])

    return part


def one_hot(where):
    return jnp.where(where, 1.0, 0.0).astype(bf16)


def places(slots, blocks):
    return 8 * (-(-2 * slots // (8 * blocks)) + 1)


def as_row(ids):
    return jnp.concatenate([ids[k : k + 1, :] for k in range(ids.shape[0])], axis=1)


def rank_slots(block_row, blocks):
    slots = block_row.shape[1]
    mine = rows((blocks, slots)) == block_row
    upper = one_hot(rows((slots, slots)) < lanes((slots, slots)))
    before = jnp.dot(one_hot(mine), upper, preferred_element_type=f32)
    return jnp.sum(jnp.where(mine, before, 0.0), axis=0, keepdims=True)


def find_slots(r, code, block_row, rank, capacity, column):
    slots = block_row.shape[1]
    place = rank.astype(jnp.int32) - r * capacity
    place = jnp.where((place >= 0) & (place < capacity), block_row * capacity + place, -1)
    for at in range(0, column.shape[0], BLOCK):
        here = rows((BLOCK, slots)) + at == place
        found = jnp.sum(jnp.where(here, code + 1.0, 0.0), axis=1, keepdims=True) - 1.0
        column[at : at + BLOCK] = jnp.broadcast_to(found, (BLOCK, BLOCK))


def couple(blocks, part, table, size, capacity, rounds, prepare, column, gather_first, transposed, result, scratch):
    vectors, products = scratch
    total_rows = column.shape[0]
    result[...] = jnp.zeros_like(result)

    def one_round(r, carry):
        prepare(r)
        eye = rows((BLOCK, BLOCK)) == lanes((BLOCK, BLOCK))
        place_hot = []
        for at in range(0, total_rows, BLOCK):
            found = column[at : at + BLOCK]
            first = jnp.floor((found + 0.5) * (1.0 / size))
            second = found - first * size
            gather, put = (first, second) if gather_first else (second, first)
            width = table.shape[0]
            gather = jnp.concatenate([gather] * (width // BLOCK), axis=1)
            hot = one_hot(gather == lanes((BLOCK, width)).astype(f32))
            vectors[at : at + BLOCK] = jnp.dot(hot, table, preferred_element_type=f32)
            put = jnp.sum(jnp.where(eye, put, 0.0), axis=0, keepdims=True)
            place_hot.append(one_hot(rows((result.shape[0], BLOCK)).astype(f32) == put))

        def group(g, carry):
            for u in range(GROUP):
                at = pl.multiple_of((g * GROUP + u) * capacity, 8)
                own = vectors[pl.ds(at, capacity)]
                left = jnp.concatenate([own[:, n * BLOCK : (n + 1) * BLOCK] for n in range(4)], axis=0)
                high, low = part(r, g, u)
                right = jnp.concatenate([high, low], axis=1 if transposed else 0)
                contract = (((1,), (0 if transposed else 1,)), ((), ()))
                product = lax.dot_general(left.astype(bf16), right, contract, preferred_element_type=f32)
                for f in range(2):
                    high_part = product[f * capacity : (f + 1) * capacity]
                    low_part = product[(f + 2) * capacity : (f + 3) * capacity, :BLOCK]
                    products[pl.ds(at, capacity), f * BLOCK : (f + 1) * BLOCK] = (
                        high_part[:, BLOCK:] + low_part
                    ) + high_part[:, :BLOCK]
            return carry

        lax.fori_loop(0, blocks // GROUP, group, 0)
        summed = jnp.dot(
            jnp.concatenate(place_hot, axis=1),
            jnp.concatenate(split(products[...]), axis=1),
            preferred_element_type=f32,
        )
        result[...] += summed[:, : 2 * BLOCK] + summed[:, 2 * BLOCK :]
        return carry

    lax.fori_loop(0, rounds, one_round, 0)


def slot_keys(ids, tile_lat, atm):
    lon_count, cap = ids.shape[3:]
    ocean, atm_ids, block_ids = (ids[n, 0, 0] for n in range(3))
    order = (ocean & 1) * tile_lat + (ocean >> 1) + rows((lon_count, cap)) * (2 * tile_lat)
    order = jnp.where(ocean >= 0, order, lon_count * 2 * tile_lat)
    return as_row((order * atm + atm_ids).astype(f32)), as_row(block_ids)


def weigh(atm_near, margins, weights, after, sums, found, keys, result, *scratch):
    scratch, (held, arrived) = scratch[:2], scratch[2:]
    fetch_weights(weights, held, arrived)
    lon_count = margins.shape[3]
    atm = atm_near.shape[2]
    blocks = weights.shape[0]
    tile_lat = 2 * sums.shape[1] // 9
    code, block_row = slot_keys(margins, tile_lat, atm)
    rank = rank_slots(block_row, blocks)
    keys[0:1] = code
    keys[1:2] = block_row.astype(f32)
    keys[2:3] = rank
    capacity = places(code.shape[1], blocks)
    rounds = jnp.max(rank).astype(jnp.int32) // capacity + 1
    parts = [split(atm_near[f, 0]) for f in range(2)]
    table = jnp.concatenate([parts[f][n] for n in range(2) for f in range(2)], axis=1)

    def prepare(r):
        find_slots(rounds - 1 - r, code, block_row, rank, capacity, found)

    part = held_part(weights, held, arrived)
    couple(blocks, part, table, atm, capacity, rounds, prepare, found, False, False, result, scratch)
    lane = lanes((tile_lat, BLOCK))

    def block_sums(k, f, h):
        at = (2 * k + h) * tile_lat
        return result[at : at + tile_lat, f * BLOCK : (f + 1) * BLOCK]

    for k in range(lon_count):
        edge = jnp.zeros((tile_lat, BLOCK), f32)
        for f in range(2):
            for h in range(2):
                sums[k, (2 * f + h) * tile_lat : (2 * f + h + 1) * tile_lat] = block_sums(k, f, h)
            at = f * HALO
            after = turn(block_sums((k + 1) % lon_count, f, 0), at, 1)
            before = turn(block_sums((k - 1) % lon_count, f, 1), -at, 1)
            edge = jnp.where((lane >= at) & (lane < at + HALO), after, edge)
            end = BLOCK - at
            edge = jnp.where((lane >= end - HALO) & (lane < end), before, edge)
        upper, lower = edge[: tile_lat // 2], edge[tile_lat // 2 :]
        near = lane[: tile_lat // 2]
        lower = jnp.where(near < BLOCK // 2, turn(lower, 2 * HALO, 1), turn(lower, -2 * HALO, 1))
        sums[k, 4 * tile_lat :] = jnp.where((near < 2 * HALO) | (near >= BLOCK - 2 * HALO), upper, lower)


def unweigh(gathered, found, keys, weights, gradient, result, column, *scratch):
    scratch, (held, arrived) = scratch[:2], scratch[2:]
    fetch_weights(weights, held, arrived)
    atm = gradient.shape[2]
    blocks = weights.shape[0]
    lon_count, ocean_blocks = gathered.shape[0], gathered.shape[1] // 2
    capacity = places(keys.shape[1], blocks)
    rounds = jnp.max(keys[2:3]).astype(jnp.int32) // capacity + 1
    parts = [
        split(
            jnp.concatenate(
                [gathered[k, f * ocean_blocks : (f + 1) * ocean_blocks] for k in range(lon_count)], axis=0
            )
        )
        for f in range(2)
    ]
    table = jnp.concatenate([parts[f][n] for n in range(2) for f in range(2)], axis=1)

    def prepare(r):
        @pl.when(r == 0)
        def _():
            column[...] = found[...]

        @pl.when(r > 0)
        def _():
            find_slots(r, keys[0:1], keys[1:2].astype(jnp.int32), keys[2:3], capacity, column)

    couple(
        blocks,
        held_part(weights, held, arrived),
        table,
        atm,
        capacity,
        rounds,
        prepare,
        column,
        True,
        True,
        result,
        scratch,
    )
    for f in range(2):
        gradient[f, 0] = result[:, f * BLOCK : (f + 1) * BLOCK]


def on_device(tracers, cotangent, land_mask, diffusion, velocity, weights, atm_state, margins):
    levels, tile_lat, tile_lon = land_mask.shape
    lon_count = lax.axis_size("lon")
    slots = lon_count * margins.shape[4]
    halves = tile_lon // BLOCK
    count = 9 * levels - 1
    parts = -(-count // PER_LANES)
    inputs = (tracers, cotangent, land_mask, diffusion, velocity)

    def in_vmem(s):
        return pltpu.VMEM(s.shape, s.dtype)

    message = (parts, tile_lat, BLOCK)
    fields, near, far, atm_near, margins_near = call(
        pack_columns,
        [
            (count, tile_lat, tile_lon),
            message,
            message,
            atm_state.shape,
            jax.ShapeDtypeStruct(margins.shape, margins.dtype),
        ],
        [*map(in_vmem, inputs), pltpu.SemaphoreType.DMA((7,))],
        name="pack_columns",
        inputs=7,
        far=range(7),
    )(*inputs, atm_state, margins)
    near_columns, far_columns = swap(near, far, "lon", True)

    blocks_of, atm = weights.shape[0], atm_state.shape[2]
    groups = blocks_of // GROUP
    sum_rows = 2 * halves * tile_lat + tile_lat // 2
    ocean_blocks = lon_count * halves * tile_lat
    held_rows = -(-places(slots, blocks_of) * blocks_of // BLOCK) * BLOCK

    def coupling_scratch(result_rows):
        return [
            pltpu.VMEM((result_rows, 2 * BLOCK), f32),
            pltpu.VMEM((held_rows, 4 * BLOCK), f32),
            pltpu.VMEM((held_rows, 2 * BLOCK), f32),
            pltpu.VMEM((groups, GROUP, BLOCK, BLOCK), f32),
            pltpu.SemaphoreType.DMA((groups,)),
        ]

    coupling_flops = 4 * slots * blocks_of * 2 * BLOCK * BLOCK * 2
    sums, found, keys = call(
        weigh,
        [(lon_count, sum_rows, BLOCK), (held_rows, BLOCK), (8, slots)],
        coupling_scratch(ocean_blocks),
        coupling_flops,
        name="weigh",
        inputs=4,
        far=(2,),
    )(atm_near, margins_near, weights, near)

    sources = count * halves + 2 * parts
    message = (-(-sources // 2), 8, BLOCK)
    columns = (parts, tile_lat, BLOCK)
    near, far, from_west, from_east, sums = call(
        pack_rows,
        [message, message, columns, columns, sums.shape],
        name="pack_rows",
        inputs=4,
        aliases={3: 4},
    )(fields, near_columns, far_columns, sums)
    received = lax.all_to_all(sums, "lon", split_axis=0, concat_axis=0, tiled=True)
    near_rows, far_rows = swap(near, far, "lat", False)

    wide = (tile_lat + 8, tile_lon + BLOCK)
    own = (2 * halves * tile_lat, BLOCK)
    blocks, coeffs, start, lam = call(
        run_adjoint,
        [(lon_count, *own), (6, levels, *wide), (2, levels, *wide), (2, levels, *wide)],
        [
            pltpu.VMEM((count, *wide), f32),
            pltpu.VMEM((2, levels, *wide), f32),
            pltpu.VMEM(own, f32),
            pltpu.SemaphoreType.DMA((2, lon_count)),
        ],
        name="run_adjoint",
        inputs=5,
        far_outs=(0,),
    )(fields, from_west, from_east, near_rows, far_rows)
    gathered = lax.all_to_all(blocks, "lon", split_axis=0, concat_axis=0, tiled=True)

    message = (1, 8, tile_lon + BLOCK)
    forcing, near, far = call(
        sum_forcing, [(2, tile_lat, tile_lon + BLOCK), message, message], name="sum_forcing", inputs=1
    )(received)
    near_rows, far_rows = swap(near, far, "lat", False)
    final, adjoint = call(
        run_forward,
        [tracers.shape, cotangent.shape],
        [pltpu.VMEM((2, levels, *wide), f32)],
        name="run_forward",
        inputs=6,
    )(coeffs, start, lam, forcing, near_rows, far_rows)

    (gradient,) = call(
        unweigh,
        [atm_state.shape],
        [coupling_scratch(atm)[0], in_vmem(found), *coupling_scratch(atm)[1:]],
        coupling_flops,
        name="unweigh",
        inputs=4,
        far=(3,),
    )(gathered, found, keys, weights)
    return (final, adjoint, gradient)


def solution(mesh):
    return jax.shard_map(
        on_device,
        mesh=mesh,
        in_specs=(
            P(None, None, "lat", "lon"),
            P(None, None, "lat", "lon"),
            P(None, "lat", "lon"),
            P(None, None, "lat", "lon"),
            P(None, None, "lat", "lon"),
            P(),
            P(None, "lat", "lon", None),
            P(None, "lat", "lon", None, None),
        ),
        out_specs=(
            P(None, None, "lat", "lon"),
            P(None, None, "lat", "lon"),
            P(None, "lat", "lon", None),
        ),
        check_vma=False,
    )
```

```python
import jax
import jax.numpy as jnp
from jax import lax
from jax.experimental import pallas as pl
from jax.experimental.pallas import tpu as pltpu
from jax.sharding import PartitionSpec as P

BLOCK = 128
STEPS = 4
HALO = STEPS
PER_LANES = BLOCK // HALO
GROUP = 8
f32 = jnp.float32
bf16 = jnp.bfloat16
VMEM_LIMIT = 32 * 1024 * 1024


def call(body, outs, scratch=(), flops=0, name=None, inputs=0, far=(), far_outs=(), aliases=None):
    outs = [s if isinstance(s, jax.ShapeDtypeStruct) else jax.ShapeDtypeStruct(s, f32) for s in outs]
    near = pl.BlockSpec(memory_space=pltpu.VMEM)
    aliases = aliases or {}
    kernel = pl.pallas_call(
        body,
        out_shape=outs,
        in_specs=[
            pl.BlockSpec(memory_space=pl.ANY)
            if n in aliases
            else pl.BlockSpec(memory_space=pltpu.HBM)
            if n in far
            else near
            for n in range(inputs)
        ],
        out_specs=[
            pl.BlockSpec(memory_space=pl.ANY) if n in aliases.values() or n in far_outs else near
            for n in range(len(outs))
        ],
        input_output_aliases=aliases,
        scratch_shapes=list(scratch),
        compiler_params=pltpu.CompilerParams(vmem_limit_bytes=VMEM_LIMIT),
        cost_estimate=pl.CostEstimate(flops=flops, bytes_accessed=1 << 20, transcendentals=0),
        name=name,
    )

    def run(*args):
        return kernel(
            *(pltpu.with_memory_space_constraint(x, pltpu.HBM) if n in far else x for n, x in enumerate(args))
        )

    return run


def lanes(shape):
    return lax.broadcasted_iota(jnp.int32, shape, len(shape) - 1)


def rows(shape):
    return lax.broadcasted_iota(jnp.int32, shape, len(shape) - 2)


def turn(x, shift, axis):
    shift %= x.shape[axis]
    return pltpu.roll(x, shift, axis) if shift else x


def swap(near, far, axis, wrap):
    count = lax.axis_size(axis)
    pairs = [[], []]
    for i in range(count if wrap else count - 1):
        j = (i + 1) % count
        pairs[i % 2] += [(i, j), (j, i)]
    far = lax.ppermute(far, axis, pairs[1])
    return lax.ppermute(near, axis, pairs[0]), far


def sort_swap(axis, after, before):
    odd = lax.rem(lax.axis_index(axis), 2) == 1
    return jnp.where(odd, before, after), jnp.where(odd, after, before)


def tile_fields(tracers, cotangent, land_mask, diffusion, velocity):
    levels = land_mask.shape[0]
    mask = [land_mask[level].astype(f32) for level in range(levels)]
    out = [tracers[f, level] for f in range(2) for level in range(levels)]
    out += [cotangent[f, level] for f in range(2) for level in range(levels)]
    out += [diffusion[0, level] * mask[level] for level in range(levels)]
    out += [velocity[0, level] * mask[level] for level in range(levels)]
    out += [diffusion[1, level] * mask[level] for level in range(levels)]
    out += [velocity[1, level] * mask[level] for level in range(levels)]
    out += [diffusion[2, level] * mask[level] * mask[level + 1] for level in range(levels - 1)]
    return out


def fetch(pairs, arrived):
    copies = [pltpu.make_async_copy(src, dst, arrived.at[n]) for n, (src, dst) in enumerate(pairs)]
    for copy in copies:
        copy.start()
    return copies


def pack_columns(*refs):
    inputs, (fields, near, far), scratch = refs[:7], refs[7:10], refs[12:]
    copies = fetch(zip(inputs, [*scratch[:5], *refs[10:12]]), scratch[5])
    for copy in copies[:5]:
        copy.wait()
    shape = near.shape[1:]
    lane = lanes(shape)
    west = [jnp.zeros(shape, f32) for _ in range(near.shape[0])]
    east = [jnp.zeros(shape, f32) for _ in range(near.shape[0])]
    for i, field in enumerate(tile_fields(*scratch[:5])):
        fields[i] = field
        part, at = divmod(i, PER_LANES)
        at *= HALO
        here = (lane >= at) & (lane < at + HALO)
        west[part] = jnp.where(here, turn(field[:, :BLOCK], at, 1), west[part])
        east[part] = jnp.where(here, turn(field[:, -BLOCK:], at + HALO, 1), east[part])
    for part in range(near.shape[0]):
        near[part], far[part] = sort_swap("lon", east[part], west[part])
    for copy in copies[5:]:
        copy.wait()


def unpack_columns(from_west, from_east, i):
    part, at = divmod(i, PER_LANES)
    at *= HALO
    lane = lanes(from_west[part].shape)
    east = turn(from_east[part], -at, 1)
    west = turn(from_west[part], -at - HALO, 1)
    return jnp.where(lane < HALO, east, jnp.where(lane >= BLOCK - HALO, west, 0.0))


def row_sources(fields, from_west, from_east):
    out = [(fields, (i, slice(None), slice(h * BLOCK, (h + 1) * BLOCK)))
           for i in range(fields.shape[0]) for h in range(fields.shape[2] // BLOCK)]
    for columns in (from_west, from_east):
        out += [(columns, (part,)) for part in range(columns.shape[0])]
    return out


def pack_rows(fields, near_columns, far_columns, sums, near, far, from_west, from_east, same_sums):
    for part in range(from_west.shape[0]):
        from_east[part], from_west[part] = sort_swap("lon", near_columns[part], far_columns[part])
    sources = [ref[at] for ref, at in row_sources(fields, from_west, from_east)]
    half = near.shape[0]
    row = rows((8, BLOCK))
    for i in range(half):
        first = sources[i]
        second = sources[i + half] if i + half < len(sources) else jnp.zeros_like(first)
        to_north = jnp.where(row < HALO, turn(first[-8:], HALO, 0), second[-8:])
        to_south = jnp.where(row < HALO, first[:8], turn(second[:8], HALO, 0))
        near[i], far[i] = sort_swap("lat", to_north, to_south)


def edge_rows(near, far, i):
    half = near.shape[0]
    from_north, from_south = sort_swap("lat", near[i % half], far[i % half])
    if i < half:
        from_south = turn(from_south, HALO, 0)
    else:
        from_north = turn(from_north, HALO, 0)
    return jnp.where(rows(from_north.shape) < HALO, from_north, from_south)


def widen(fields, from_west, from_east, near, far, wide):
    count, tile_lat, tile_lon = fields.shape
    halves = tile_lon // BLOCK
    parts = from_west.shape[0]
    corners = [edge_rows(near, far, count * halves + n) for n in range(2 * parts)]
    for i in range(count):
        wide[i, :tile_lat, :tile_lon] = fields[i]
        wide[i, :tile_lat, tile_lon:] = unpack_columns(from_west, from_east, i)
        for h in range(halves):
            wide[i, tile_lat:, h * BLOCK : (h + 1) * BLOCK] = edge_rows(near, far, i * halves + h)
        wide[i, tile_lat:, tile_lon:] = unpack_columns(corners[:parts], corners[parts:], i)


def eastward(x):
    return turn(x, -1, 1)


def westward(x):
    return turn(x, 1, 1)


def northward(x):
    return turn(x, -1, 0)


def southward(x):
    return turn(x, 1, 0)


def adjoint_step(coeffs, read, write):
    levels = coeffs.shape[1]
    above = None
    for level in range(levels):
        lam = read(level)
        step_x = eastward(lam) - lam
        step_y = northward(lam) - lam
        out = lam + coeffs[0, level] * step_x + westward(coeffs[1, level] * step_x)
        out = out + coeffs[2, level] * step_y + southward(coeffs[3, level] * step_y)
        if above is not None:
            out = out - above
        if level < levels - 1:
            above = coeffs[4, level] * (read(level + 1) - lam)
            out = out + above
        write(level, out)


def run_adjoint(
    fields, from_west, from_east, far, near, blocks, coeffs, start, lam_out, wide, state, own, sent
):
    levels = coeffs.shape[1]
    tile_lat, tile_lon = fields.shape[1:]
    halves = tile_lon // BLOCK
    widen(fields, from_west, from_east, near, far, wide)
    base = 4 * levels
    for f in range(2):
        for level in range(levels):
            start[f, level] = wide[f * levels + level]
    mask0 = None
    for level in range(levels):
        east_d, east_u = wide[base + level], wide[base + levels + level]
        north_d, north_u = wide[base + 2 * levels + level], wide[base + 3 * levels + level]
        mask = (east_d > 0.0).astype(f32)
        mask0 = mask if mask0 is None else mask0
        mask_e, mask_n = eastward(mask), northward(mask)
        east_k, east_v = east_d * mask_e, east_u * mask_e
        north_k, north_v = north_d * mask_n, north_u * mask_n
        coeffs[0, level] = jnp.maximum(east_v, 0.0) + east_k
        coeffs[1, level] = jnp.minimum(east_v, 0.0) - east_k
        coeffs[2, level] = jnp.maximum(north_v, 0.0) + north_k
        coeffs[3, level] = jnp.minimum(north_v, 0.0) - north_k
        coeffs[4, level] = wide[base + 4 * levels + level] if level < levels - 1 else jnp.zeros_like(mask)
        coeffs[5, level] = mask
    copies = []
    for f in range(2):
        surface = wide[(2 + f) * levels, :tile_lat, :tile_lon]
        for step in range(STEPS - 1):
            def read(level):
                return wide[(2 + f) * levels + level] if step == 0 else state[(step - 1) % 2, level]

            def write(level, lam):
                nonlocal surface
                if level == 0:
                    surface = surface + lam[:tile_lat, :tile_lon]
                if step == STEPS - 2:
                    lam_out[f, level] = lam
                else:
                    state[step % 2, level] = lam

            adjoint_step(coeffs, read, write)
        surface = surface * mask0[:tile_lat, :tile_lon]
        for h in range(halves):
            at = (f * halves + h) * tile_lat
            own[at : at + tile_lat] = surface[:, h * BLOCK : (h + 1) * BLOCK]
        field = pl.ds(f * halves * tile_lat, halves * tile_lat)
        copies += fetch([(own.at[field], blocks.at[k, field]) for k in range(blocks.shape[0])], sent.at[f])
    for copy in copies:
        copy.wait()


def sum_forcing(received, forcing, near, far):
    tile_lat = forcing.shape[1]
    halves = forcing.shape[2] // BLOCK - 1
    total = received[0]
    for j in range(1, received.shape[0]):
        total = total + received[j]
    lane = lanes((tile_lat, BLOCK))
    upper = total[2 * halves * tile_lat :]
    lower = jnp.where(lane[: tile_lat // 2] < BLOCK // 2, turn(upper, -2 * HALO, 1), turn(upper, 2 * HALO, 1))
    packed = jnp.concatenate([upper, lower], axis=0)
    for f in range(2):
        for h in range(halves):
            at = (f * halves + h) * tile_lat
            forcing[f, :, h * BLOCK : (h + 1) * BLOCK] = total[at : at + tile_lat]
        used = (lane < HALO) | (lane >= BLOCK - HALO)
        if f == 0:
            edge = packed
        else:
            edge = jnp.where(lane < HALO, turn(packed, -HALO, 1), turn(packed, HALO, 1))
        forcing[f, :, halves * BLOCK :] = jnp.where(used, edge, 0.0)
    row = rows((8, forcing.shape[2]))
    to_north = jnp.where(row < HALO, turn(forcing[0, tile_lat - 8 :], HALO, 0), forcing[1, tile_lat - 8 :])
    to_south = jnp.where(row < HALO, forcing[0, :8], turn(forcing[1, :8], HALO, 0))
    near[0], far[0] = sort_swap("lat", to_north, to_south)


def run_forward(coeffs, start, lam, forcing, far, near, final, adjoint_out, state):
    levels = coeffs.shape[1]
    tile_lat, tile_lon = final.shape[2:]
    for f in range(2):

        def write(level, out):
            adjoint_out[f, level] = out[:tile_lat, :tile_lon]

        adjoint_step(coeffs, lambda level: lam[f, level], write)
        force = jnp.concatenate([forcing[f], edge_rows(near, far, f)], axis=0)
        force = force * coeffs[5, 0]
        for step in range(STEPS):
            above = None
            for level in range(levels):
                read = (lambda n: start[f, n]) if step == 0 else (lambda n: state[(step - 1) % 2, n])
                theta = read(level)
                east_flux = coeffs[0, level] * theta + coeffs[1, level] * eastward(theta)
                north_flux = coeffs[2, level] * theta + coeffs[3, level] * northward(theta)
                out = theta - (east_flux - westward(east_flux)) - (north_flux - southward(north_flux))
                if level < levels - 1:
                    vertical = coeffs[4, level] * (theta - read(level + 1))
                    out = out - vertical
                if above is not None:
                    out = out + above
                above = vertical if level < levels - 1 else None
                if level == 0:
                    out = out + force
                if step == STEPS - 1:
                    final[f, level] = out[:tile_lat, :tile_lon]
                else:
                    state[step % 2, level] = out


def split(x):
    high = x.astype(bf16)
    return high, (x - high.astype(f32)).astype(bf16)


def weight_copies(weights, held, arrived):
    for g in range(held.shape[0]):
        yield pltpu.make_async_copy(weights.at[pl.ds(g * GROUP, GROUP)], held.at[g], arrived.at[g])


def fetch_weights(weights, held, arrived):
    for copy in weight_copies(weights, held, arrived):
        copy.start()


def held_part(weights, held, arrived):
    def part(r, g, u):
        if u == 0:

            @pl.when(r == 0)
            def _():
                pltpu.make_async_copy(weights.at[pl.ds(g * GROUP, GROUP)], held.at[g], arrived.at[g]).wait()

        return split(held[g, u])

    return part


def one_hot(where):
    return jnp.where(where, 1.0, 0.0).astype(bf16)


def places(slots, blocks):
    return 8 * (-(-2 * slots // (8 * blocks)) + 1)


def as_row(ids):
    return jnp.concatenate([ids[k : k + 1, :] for k in range(ids.shape[0])], axis=1)


def rank_slots(block_row, blocks):
    slots = block_row.shape[1]
    mine = rows((blocks, slots)) == block_row
    cuts = range(0, slots, BLOCK)
    stacked = jnp.concatenate([one_hot(mine[:, at : at + BLOCK]) for at in cuts], axis=0)
    shape = (BLOCK, 2 * BLOCK)
    counts = jnp.dot(stacked, one_hot(rows(shape) < lanes(shape)), preferred_element_type=f32)
    before, out = jnp.zeros((blocks, BLOCK), f32), []
    for n, at in enumerate(cuts):
        run = counts[n * blocks : (n + 1) * blocks]
        here = jnp.where(mine[:, at : at + BLOCK], run[:, :BLOCK] + before, 0.0)
        out.append(jnp.sum(here, axis=0, keepdims=True))
        before = before + run[:, BLOCK:]
    return jnp.concatenate(out, axis=1)


def find_slots(r, code, block_row, rank, capacity, blocks, column):
    slots = block_row.shape[1]
    mine = rows((blocks, slots)) == block_row
    ranked = one_hot(rows((capacity, slots)) == rank.astype(jnp.int32) - r * capacity)
    rest, found = code + 1.0, None
    for base in (4096.0, 64.0, 1.0):
        digit = jnp.floor(rest * (1.0 / base))
        rest = rest - digit * base
        part = lax.dot_general(
            ranked,
            jnp.where(mine, digit, 0.0).astype(bf16),
            (((1,), (1,)), ((), ())),
            preferred_element_type=f32,
        )
        found = part * base if found is None else found + part * base
    found = found - 1.0
    for w in range(blocks):
        column[w * capacity : (w + 1) * capacity] = jnp.broadcast_to(found[:, w : w + 1], (capacity, BLOCK))


def couple(blocks, part, table, size, capacity, rounds, prepare, column, gather_first, transposed, result, scratch):
    vectors, products = scratch
    total_rows = column.shape[0]
    result[...] = jnp.zeros_like(result)

    def one_round(r, carry):
        prepare(r)
        eye = rows((BLOCK, BLOCK)) == lanes((BLOCK, BLOCK))
        place_hot = []
        for at in range(0, total_rows, BLOCK):
            found = column[at : at + BLOCK]
            first = jnp.floor((found + 0.5) * (1.0 / size))
            second = found - first * size
            gather, put = (first, second) if gather_first else (second, first)
            width = table.shape[0]
            gather = jnp.concatenate([gather] * (width // BLOCK), axis=1)
            hot = one_hot(gather == lanes((BLOCK, width)).astype(f32))
            vectors[at : at + BLOCK] = jnp.dot(hot, table, preferred_element_type=f32)
            put = jnp.sum(jnp.where(eye, put, 0.0), axis=0, keepdims=True)
            place_hot.append(one_hot(rows((result.shape[0], BLOCK)).astype(f32) == put))

        def group(g, carry):
            for u in range(GROUP):
                at = pl.multiple_of((g * GROUP + u) * capacity, 8)
                own = vectors[pl.ds(at, capacity)]
                left = jnp.concatenate([own[:, n * BLOCK : (n + 1) * BLOCK] for n in range(4)], axis=0)
                high, low = part(r, g, u)
                right = jnp.concatenate([high, low], axis=1 if transposed else 0)
                contract = (((1,), (0 if transposed else 1,)), ((), ()))
                product = lax.dot_general(left.astype(bf16), right, contract, preferred_element_type=f32)
                for f in range(2):
                    high_part = product[f * capacity : (f + 1) * capacity]
                    low_part = product[(f + 2) * capacity : (f + 3) * capacity, :BLOCK]
                    products[pl.ds(at, capacity), f * BLOCK : (f + 1) * BLOCK] = (
                        high_part[:, BLOCK:] + low_part
                    ) + high_part[:, :BLOCK]
            return carry

        lax.fori_loop(0, blocks // GROUP, group, 0)
        summed = jnp.dot(
            jnp.concatenate(place_hot, axis=1),
            jnp.concatenate(split(products[...]), axis=1),
            preferred_element_type=f32,
        )
        result[...] += summed[:, : 2 * BLOCK] + summed[:, 2 * BLOCK :]
        return carry

    lax.fori_loop(0, rounds, one_round, 0)


def slot_keys(ids, tile_lat, atm):
    lon_count, cap = ids.shape[3:]
    ocean, atm_ids, block_ids = (ids[n, 0, 0] for n in range(3))
    order = (ocean & 1) * tile_lat + (ocean >> 1) + rows((lon_count, cap)) * (2 * tile_lat)
    order = jnp.where(ocean >= 0, order, lon_count * 2 * tile_lat)
    return as_row((order * atm + atm_ids).astype(f32)), as_row(block_ids)


def weigh(atm_near, margins, weights, after, sums, found, keys, result, *scratch):
    scratch, (held, arrived) = scratch[:2], scratch[2:]
    fetch_weights(weights, held, arrived)
    lon_count = margins.shape[3]
    atm = atm_near.shape[2]
    blocks = weights.shape[0]
    tile_lat = 2 * sums.shape[1] // 9
    code, block_row = slot_keys(margins, tile_lat, atm)
    rank = rank_slots(block_row, blocks)
    keys[0:1] = code
    keys[1:2] = block_row.astype(f32)
    keys[2:3] = rank
    capacity = places(code.shape[1], blocks)
    rounds = jnp.max(rank).astype(jnp.int32) // capacity + 1
    parts = [split(atm_near[f, 0]) for f in range(2)]
    table = jnp.concatenate([parts[f][n] for n in range(2) for f in range(2)], axis=1)

    def prepare(r):
        find_slots(rounds - 1 - r, code, block_row, rank, capacity, blocks, found)

    part = held_part(weights, held, arrived)
    couple(blocks, part, table, atm, capacity, rounds, prepare, found, False, False, result, scratch)
    lane = lanes((tile_lat, BLOCK))

    def block_sums(k, f, h):
        at = (2 * k + h) * tile_lat
        return result[at : at + tile_lat, f * BLOCK : (f + 1) * BLOCK]

    for k in range(lon_count):
        edge = jnp.zeros((tile_lat, BLOCK), f32)
        for f in range(2):
            for h in range(2):
                sums[k, (2 * f + h) * tile_lat : (2 * f + h + 1) * tile_lat] = block_sums(k, f, h)
            at = f * HALO
            after = turn(block_sums((k + 1) % lon_count, f, 0), at, 1)
            before = turn(block_sums((k - 1) % lon_count, f, 1), -at, 1)
            edge = jnp.where((lane >= at) & (lane < at + HALO), after, edge)
            end = BLOCK - at
            edge = jnp.where((lane >= end - HALO) & (lane < end), before, edge)
        upper, lower = edge[: tile_lat // 2], edge[tile_lat // 2 :]
        near = lane[: tile_lat // 2]
        lower = jnp.where(near < BLOCK // 2, turn(lower, 2 * HALO, 1), turn(lower, -2 * HALO, 1))
        sums[k, 4 * tile_lat :] = jnp.where((near < 2 * HALO) | (near >= BLOCK - 2 * HALO), upper, lower)


def unweigh(gathered, found, keys, weights, gradient, result, column, *scratch):
    scratch, (held, arrived) = scratch[:2], scratch[2:]
    fetch_weights(weights, held, arrived)
    atm = gradient.shape[2]
    blocks = weights.shape[0]
    lon_count, ocean_blocks = gathered.shape[0], gathered.shape[1] // 2
    capacity = places(keys.shape[1], blocks)
    rounds = jnp.max(keys[2:3]).astype(jnp.int32) // capacity + 1
    parts = [
        split(
            jnp.concatenate(
                [gathered[k, f * ocean_blocks : (f + 1) * ocean_blocks] for k in range(lon_count)], axis=0
            )
        )
        for f in range(2)
    ]
    table = jnp.concatenate([parts[f][n] for n in range(2) for f in range(2)], axis=1)

    def prepare(r):
        @pl.when(r == 0)
        def _():
            column[...] = found[...]

        @pl.when(r > 0)
        def _():
            find_slots(r, keys[0:1], keys[1:2].astype(jnp.int32), keys[2:3], capacity, blocks, column)

    couple(
        blocks,
        held_part(weights, held, arrived),
        table,
        atm,
        capacity,
        rounds,
        prepare,
        column,
        True,
        True,
        result,
        scratch,
    )
    for f in range(2):
        gradient[f, 0] = result[:, f * BLOCK : (f + 1) * BLOCK]


def on_device(tracers, cotangent, land_mask, diffusion, velocity, weights, atm_state, margins):
    levels, tile_lat, tile_lon = land_mask.shape
    lon_count = lax.axis_size("lon")
    slots = lon_count * margins.shape[4]
    halves = tile_lon // BLOCK
    count = 9 * levels - 1
    parts = -(-count // PER_LANES)
    inputs = (tracers, cotangent, land_mask, diffusion, velocity)

    def in_vmem(s):
        return pltpu.VMEM(s.shape, s.dtype)

    message = (parts, tile_lat, BLOCK)
    fields, near, far, atm_near, margins_near = call(
        pack_columns,
        [
            (count, tile_lat, tile_lon),
            message,
            message,
            atm_state.shape,
            jax.ShapeDtypeStruct(margins.shape, margins.dtype),
        ],
        [*map(in_vmem, inputs), pltpu.SemaphoreType.DMA((7,))],
        name="pack_columns",
        inputs=7,
        far=range(7),
    )(*inputs, atm_state, margins)
    near_columns, far_columns = swap(near, far, "lon", True)

    blocks_of, atm = weights.shape[0], atm_state.shape[2]
    groups = blocks_of // GROUP
    sum_rows = 2 * halves * tile_lat + tile_lat // 2
    ocean_blocks = lon_count * halves * tile_lat
    held_rows = -(-places(slots, blocks_of) * blocks_of // BLOCK) * BLOCK

    def coupling_scratch(result_rows):
        return [
            pltpu.VMEM((result_rows, 2 * BLOCK), f32),
            pltpu.VMEM((held_rows, 4 * BLOCK), f32),
            pltpu.VMEM((held_rows, 2 * BLOCK), f32),
            pltpu.VMEM((groups, GROUP, BLOCK, BLOCK), f32),
            pltpu.SemaphoreType.DMA((groups,)),
        ]

    coupling_flops = 4 * slots * blocks_of * 2 * BLOCK * BLOCK * 2
    sums, found, keys = call(
        weigh,
        [(lon_count, sum_rows, BLOCK), (held_rows, BLOCK), (8, slots)],
        coupling_scratch(ocean_blocks),
        coupling_flops,
        name="weigh",
        inputs=4,
        far=(2,),
    )(atm_near, margins_near, weights, near)

    sources = count * halves + 2 * parts
    message = (-(-sources // 2), 8, BLOCK)
    columns = (parts, tile_lat, BLOCK)
    near, far, from_west, from_east, sums = call(
        pack_rows,
        [message, message, columns, columns, sums.shape],
        name="pack_rows",
        inputs=4,
        aliases={3: 4},
    )(fields, near_columns, far_columns, sums)
    received = lax.all_to_all(sums, "lon", split_axis=0, concat_axis=0, tiled=True)
    near_rows, far_rows = swap(near, far, "lat", False)

    wide = (tile_lat + 8, tile_lon + BLOCK)
    own = (2 * halves * tile_lat, BLOCK)
    blocks, coeffs, start, lam = call(
        run_adjoint,
        [(lon_count, *own), (6, levels, *wide), (2, levels, *wide), (2, levels, *wide)],
        [
            pltpu.VMEM((count, *wide), f32),
            pltpu.VMEM((2, levels, *wide), f32),
            pltpu.VMEM(own, f32),
            pltpu.SemaphoreType.DMA((2, lon_count)),
        ],
        name="run_adjoint",
        inputs=5,
        far_outs=(0,),
    )(fields, from_west, from_east, far_rows, near_rows)
    gathered = lax.all_to_all(blocks, "lon", split_axis=0, concat_axis=0, tiled=True)

    message = (1, 8, tile_lon + BLOCK)
    forcing, near, far = call(
        sum_forcing, [(2, tile_lat, tile_lon + BLOCK), message, message], name="sum_forcing", inputs=1
    )(received)
    near_rows, far_rows = swap(near, far, "lat", False)
    final, adjoint = call(
        run_forward,
        [tracers.shape, cotangent.shape],
        [pltpu.VMEM((2, levels, *wide), f32)],
        name="run_forward",
        inputs=6,
    )(coeffs, start, lam, forcing, far_rows, near_rows)

    (gradient,) = call(
        unweigh,
        [atm_state.shape],
        [coupling_scratch(atm)[0], in_vmem(found), *coupling_scratch(atm)[1:]],
        coupling_flops,
        name="unweigh",
        inputs=4,
        far=(3,),
    )(gathered, found, keys, weights)
    return (final, adjoint, gradient)


def solution(mesh):
    return jax.shard_map(
        on_device,
        mesh=mesh,
        in_specs=(
            P(None, None, "lat", "lon"),
            P(None, None, "lat", "lon"),
            P(None, "lat", "lon"),
            P(None, None, "lat", "lon"),
            P(None, None, "lat", "lon"),
            P(),
            P(None, "lat", "lon", None),
            P(None, "lat", "lon", None, None),
        ),
        out_specs=(
            P(None, None, "lat", "lon"),
            P(None, None, "lat", "lon"),
            P(None, "lat", "lon", None),
        ),
        check_vma=False,
    )
```

```python
import jax
import jax.numpy as jnp
from jax import lax
from jax.experimental import pallas as pl
from jax.experimental.pallas import tpu as pltpu
from jax.sharding import PartitionSpec as P

BLOCK = 128
STEPS = 4
HALO = STEPS
PER_LANES = BLOCK // HALO
GROUP = 16
f32 = jnp.float32
bf16 = jnp.bfloat16
VMEM_LIMIT = 32 * 1024 * 1024


def call(body, outs, scratch=(), flops=0, name=None, inputs=0, far=(), far_outs=(), aliases=None):
    outs = [s if isinstance(s, jax.ShapeDtypeStruct) else jax.ShapeDtypeStruct(s, f32) for s in outs]
    near = pl.BlockSpec(memory_space=pltpu.VMEM)
    aliases = aliases or {}
    kernel = pl.pallas_call(
        body,
        out_shape=outs,
        in_specs=[
            pl.BlockSpec(memory_space=pl.ANY)
            if n in aliases
            else pl.BlockSpec(memory_space=pltpu.HBM)
            if n in far
            else near
            for n in range(inputs)
        ],
        out_specs=[
            pl.BlockSpec(memory_space=pl.ANY) if n in aliases.values() or n in far_outs else near
            for n in range(len(outs))
        ],
        input_output_aliases=aliases,
        scratch_shapes=list(scratch),
        compiler_params=pltpu.CompilerParams(vmem_limit_bytes=VMEM_LIMIT),
        cost_estimate=pl.CostEstimate(flops=flops, bytes_accessed=1 << 20, transcendentals=0),
        name=name,
    )

    def run(*args):
        return kernel(
            *(pltpu.with_memory_space_constraint(x, pltpu.HBM) if n in far else x for n, x in enumerate(args))
        )

    return run


def lanes(shape):
    return lax.broadcasted_iota(jnp.int32, shape, len(shape) - 1)


def rows(shape):
    return lax.broadcasted_iota(jnp.int32, shape, len(shape) - 2)


def turn(x, shift, axis):
    shift %= x.shape[axis]
    return pltpu.roll(x, shift, axis) if shift else x


def swap(near, far, axis, wrap):
    count = lax.axis_size(axis)
    pairs = [[], []]
    for i in range(count if wrap else count - 1):
        j = (i + 1) % count
        pairs[i % 2] += [(i, j), (j, i)]
    far = lax.ppermute(far, axis, pairs[1])
    return lax.ppermute(near, axis, pairs[0]), far


def sort_swap(axis, after, before):
    odd = lax.rem(lax.axis_index(axis), 2) == 1
    return jnp.where(odd, before, after), jnp.where(odd, after, before)


def tile_fields(tracers, cotangent, land_mask, diffusion, velocity):
    levels = land_mask.shape[0]
    mask = [land_mask[level].astype(f32) for level in range(levels)]
    out = [tracers[f, level] for f in range(2) for level in range(levels)]
    out += [cotangent[f, level] for f in range(2) for level in range(levels)]
    out += [diffusion[0, level] * mask[level] for level in range(levels)]
    out += [velocity[0, level] * mask[level] for level in range(levels)]
    out += [diffusion[1, level] * mask[level] for level in range(levels)]
    out += [velocity[1, level] * mask[level] for level in range(levels)]
    out += [diffusion[2, level] * mask[level] * mask[level + 1] for level in range(levels - 1)]
    return out


def fetch(pairs, arrived):
    copies = [pltpu.make_async_copy(src, dst, arrived.at[n]) for n, (src, dst) in enumerate(pairs)]
    for copy in copies:
        copy.start()
    return copies


def pack_columns(*refs):
    inputs, (fields, near, far), scratch = refs[:7], refs[7:10], refs[12:]
    copies = fetch(zip(inputs, [*scratch[:5], *refs[10:12]]), scratch[5])
    for copy in copies[:5]:
        copy.wait()
    shape = near.shape[1:]
    lane = lanes(shape)
    west = [jnp.zeros(shape, f32) for _ in range(near.shape[0])]
    east = [jnp.zeros(shape, f32) for _ in range(near.shape[0])]
    for i, field in enumerate(tile_fields(*scratch[:5])):
        fields[i] = field
        part, at = divmod(i, PER_LANES)
        at *= HALO
        here = (lane >= at) & (lane < at + HALO)
        west[part] = jnp.where(here, turn(field[:, :BLOCK], at, 1), west[part])
        east[part] = jnp.where(here, turn(field[:, -BLOCK:], at + HALO, 1), east[part])
    for part in range(near.shape[0]):
        near[part], far[part] = sort_swap("lon", east[part], west[part])
    for copy in copies[5:]:
        copy.wait()


def unpack_columns(from_west, from_east, i):
    part, at = divmod(i, PER_LANES)
    at *= HALO
    lane = lanes(from_west[part].shape)
    east = turn(from_east[part], -at, 1)
    west = turn(from_west[part], -at - HALO, 1)
    return jnp.where(lane < HALO, east, jnp.where(lane >= BLOCK - HALO, west, 0.0))


def row_sources(fields, from_west, from_east):
    out = [(fields, (i, slice(None), slice(h * BLOCK, (h + 1) * BLOCK)))
           for i in range(fields.shape[0]) for h in range(fields.shape[2] // BLOCK)]
    for columns in (from_west, from_east):
        out += [(columns, (part,)) for part in range(columns.shape[0])]
    return out


def pack_rows(fields, near_columns, far_columns, sums, near, far, from_west, from_east, same_sums):
    for part in range(from_west.shape[0]):
        from_east[part], from_west[part] = sort_swap("lon", near_columns[part], far_columns[part])
    sources = [ref[at] for ref, at in row_sources(fields, from_west, from_east)]
    half = near.shape[0]
    row = rows((8, BLOCK))
    for i in range(half):
        first = sources[i]
        second = sources[i + half] if i + half < len(sources) else jnp.zeros_like(first)
        to_north = jnp.where(row < HALO, turn(first[-8:], HALO, 0), second[-8:])
        to_south = jnp.where(row < HALO, first[:8], turn(second[:8], HALO, 0))
        near[i], far[i] = sort_swap("lat", to_north, to_south)


def edge_rows(near, far, i):
    half = near.shape[0]
    from_north, from_south = sort_swap("lat", near[i % half], far[i % half])
    if i < half:
        from_south = turn(from_south, HALO, 0)
    else:
        from_north = turn(from_north, HALO, 0)
    return jnp.where(rows(from_north.shape) < HALO, from_north, from_south)


def widen(fields, from_west, from_east, near, far, start, wide):
    count, tile_lat, tile_lon = fields.shape
    halves = tile_lon // BLOCK
    parts = from_west.shape[0]
    corners = [edge_rows(near, far, count * halves + n) for n in range(2 * parts)]
    for i in range(count):
        out = start.at[i] if i < start.shape[0] else wide.at[i - start.shape[0]]
        out[:tile_lat, :tile_lon] = fields[i]
        out[:tile_lat, tile_lon:] = unpack_columns(from_west, from_east, i)
        for h in range(halves):
            out[tile_lat:, h * BLOCK : (h + 1) * BLOCK] = edge_rows(near, far, i * halves + h)
        out[tile_lat:, tile_lon:] = unpack_columns(corners[:parts], corners[parts:], i)


def eastward(x):
    return turn(x, -1, 1)


def westward(x):
    return turn(x, 1, 1)


def northward(x):
    return turn(x, -1, 0)


def southward(x):
    return turn(x, 1, 0)


def adjoint_step(coeffs, read, write, first, last):
    levels = coeffs.shape[1]
    above = coeffs[4, first - 1] * (read(first) - read(first - 1)) if first else None
    for level in range(first, last):
        lam = read(level)
        step_x = eastward(lam) - lam
        step_y = northward(lam) - lam
        out = lam + coeffs[0, level] * step_x + westward(coeffs[1, level] * step_x)
        out = out + coeffs[2, level] * step_y + southward(coeffs[3, level] * step_y)
        if above is not None:
            out = out - above
        if level < levels - 1:
            above = coeffs[4, level] * (read(level + 1) - lam)
            out = out + above
        write(level, out)


def surface_levels(step, levels):
    return min(levels, STEPS - 1 - step)


def run_adjoint(
    fields, from_west, from_east, far, near, blocks, coeffs, start, states, wide, own, sent
):
    levels = coeffs.shape[1]
    tile_lat, tile_lon = fields.shape[1:]
    halves = tile_lon // BLOCK
    widen(fields, from_west, from_east, near, far, start, wide)
    base = 0
    mask0 = None
    for level in range(levels):
        east_d, east_u = wide[base + level], wide[base + levels + level]
        north_d, north_u = wide[base + 2 * levels + level], wide[base + 3 * levels + level]
        mask = (east_d > 0.0).astype(f32)
        mask0 = mask if mask0 is None else mask0
        mask_e, mask_n = eastward(mask), northward(mask)
        east_k, east_v = east_d * mask_e, east_u * mask_e
        north_k, north_v = north_d * mask_n, north_u * mask_n
        coeffs[0, level] = jnp.maximum(east_v, 0.0) + east_k
        coeffs[1, level] = jnp.minimum(east_v, 0.0) - east_k
        coeffs[2, level] = jnp.maximum(north_v, 0.0) + north_k
        coeffs[3, level] = jnp.minimum(north_v, 0.0) - north_k
        coeffs[4, level] = wide[base + 4 * levels + level] if level < levels - 1 else jnp.zeros_like(mask)
        coeffs[5, level] = mask
    copies = []
    for f in range(2):
        surface = start[(2 + f) * levels, :tile_lat, :tile_lon]
        for step in range(STEPS - 1):

            def read(level):
                return states[f, step - 1, level] if step else start[(2 + f) * levels + level]

            def write(level, lam):
                states[f, step, level] = lam

            adjoint_step(coeffs, read, write, 0, surface_levels(step, levels))
            surface = surface + states[f, step, 0, :tile_lat, :tile_lon]
        surface = surface * mask0[:tile_lat, :tile_lon]
        for h in range(halves):
            at = (f * halves + h) * tile_lat
            own[at : at + tile_lat] = surface[:, h * BLOCK : (h + 1) * BLOCK]
        field = pl.ds(f * halves * tile_lat, halves * tile_lat)
        copies += fetch([(own.at[field], blocks.at[k, field]) for k in range(blocks.shape[0])], sent.at[f])
    for copy in copies:
        copy.wait()


def finish_adjoint(coeffs, start, states, adjoint_out, rest):
    levels = coeffs.shape[1]
    tile_lat, tile_lon = adjoint_out.shape[2:]
    for f in range(2):
        for step in range(STEPS):
            done = surface_levels(step, levels)

            def read(level):
                if not step:
                    return start[(2 + f) * levels + level]
                return (states if level < surface_levels(step - 1, levels) else rest)[f, step - 1, level]

            def write(level, lam):
                if step == STEPS - 1:
                    adjoint_out[f, level] = lam[:tile_lat, :tile_lon]
                else:
                    rest[f, step, level] = lam

            adjoint_step(coeffs, read, write, done, levels)


def sum_forcing(received, forcing, near, far):
    tile_lat = forcing.shape[1]
    halves = forcing.shape[2] // BLOCK - 1
    total = received[0]
    for j in range(1, received.shape[0]):
        total = total + received[j]
    lane = lanes((tile_lat, BLOCK))
    upper = total[2 * halves * tile_lat :]
    lower = jnp.where(lane[: tile_lat // 2] < BLOCK // 2, turn(upper, -2 * HALO, 1), turn(upper, 2 * HALO, 1))
    packed = jnp.concatenate([upper, lower], axis=0)
    for f in range(2):
        for h in range(halves):
            at = (f * halves + h) * tile_lat
            forcing[f, :, h * BLOCK : (h + 1) * BLOCK] = total[at : at + tile_lat]
        used = (lane < HALO) | (lane >= BLOCK - HALO)
        if f == 0:
            edge = packed
        else:
            edge = jnp.where(lane < HALO, turn(packed, -HALO, 1), turn(packed, HALO, 1))
        forcing[f, :, halves * BLOCK :] = jnp.where(used, edge, 0.0)
    row = rows((8, forcing.shape[2]))
    to_north = jnp.where(row < HALO, turn(forcing[0, tile_lat - 8 :], HALO, 0), forcing[1, tile_lat - 8 :])
    to_south = jnp.where(row < HALO, forcing[0, :8], turn(forcing[1, :8], HALO, 0))
    near[0], far[0] = sort_swap("lat", to_north, to_south)


def run_forward(coeffs, start, forcing, far, near, final, state):
    levels = coeffs.shape[1]
    tile_lat, tile_lon = final.shape[2:]
    for f in range(2):
        force = jnp.concatenate([forcing[f], edge_rows(near, far, f)], axis=0)
        force = force * coeffs[5, 0]
        for step in range(STEPS):
            above = None
            for level in range(levels):
                read = (lambda n: start[f * levels + n]) if step == 0 else (lambda n: state[(step - 1) % 2, n])
                theta = read(level)
                east_flux = coeffs[0, level] * theta + coeffs[1, level] * eastward(theta)
                north_flux = coeffs[2, level] * theta + coeffs[3, level] * northward(theta)
                out = theta - (east_flux - westward(east_flux)) - (north_flux - southward(north_flux))
                if level < levels - 1:
                    vertical = coeffs[4, level] * (theta - read(level + 1))
                    out = out - vertical
                if above is not None:
                    out = out + above
                above = vertical if level < levels - 1 else None
                if level == 0:
                    out = out + force
                if step == STEPS - 1:
                    final[f, level] = out[:tile_lat, :tile_lon]
                else:
                    state[step % 2, level] = out


def split(x):
    high = x.astype(bf16)
    return high, (x - high.astype(f32)).astype(bf16)


def weight_copies(weights, held, arrived):
    for g in range(held.shape[0]):
        yield pltpu.make_async_copy(weights.at[pl.ds(g * GROUP, GROUP)], held.at[g], arrived.at[g])


def fetch_weights(weights, held, arrived):
    for copy in weight_copies(weights, held, arrived):
        copy.start()


def held_part(weights, held, arrived):
    def part(r, g, u):
        if u == 0:

            @pl.when(r == 0)
            def _():
                pltpu.make_async_copy(weights.at[pl.ds(g * GROUP, GROUP)], held.at[g], arrived.at[g]).wait()

        return split(held[g, u])

    return part


def one_hot(where):
    return jnp.where(where, 1.0, 0.0).astype(bf16)


def places(slots, blocks):
    return 8 * (-(-2 * slots // (8 * blocks)) + 1)


def as_row(ids):
    return jnp.concatenate([ids[k : k + 1, :] for k in range(ids.shape[0])], axis=1)


def rank_slots(block_row, blocks):
    slots = block_row.shape[1]
    mine = rows((blocks, slots)) == block_row
    cuts = range(0, slots, BLOCK)
    stacked = jnp.concatenate([one_hot(mine[:, at : at + BLOCK]) for at in cuts], axis=0)
    shape = (BLOCK, 2 * BLOCK)
    counts = jnp.dot(stacked, one_hot(rows(shape) < lanes(shape)), preferred_element_type=f32)
    before, out = jnp.zeros((blocks, BLOCK), f32), []
    for n, at in enumerate(cuts):
        run = counts[n * blocks : (n + 1) * blocks]
        here = jnp.where(mine[:, at : at + BLOCK], run[:, :BLOCK] + before, 0.0)
        out.append(jnp.sum(here, axis=0, keepdims=True))
        before = before + run[:, BLOCK:]
    return jnp.concatenate(out, axis=1)


def find_slots(r, code, block_row, rank, capacity, blocks, column):
    slots = block_row.shape[1]
    mine = rows((blocks, slots)) == block_row
    ranked = one_hot(rows((capacity, slots)) == rank.astype(jnp.int32) - r * capacity)
    rest, found = code + 1.0, None
    for base in (4096.0, 64.0, 1.0):
        digit = jnp.floor(rest * (1.0 / base))
        rest = rest - digit * base
        part = lax.dot_general(
            ranked,
            jnp.where(mine, digit, 0.0).astype(bf16),
            (((1,), (1,)), ((), ())),
            preferred_element_type=f32,
        )
        found = part * base if found is None else found + part * base
    found = found - 1.0
    for w in range(blocks):
        column[w * capacity : (w + 1) * capacity] = jnp.broadcast_to(found[:, w : w + 1], (capacity, BLOCK))


def couple(blocks, part, table, size, capacity, rounds, prepare, column, gather_first, transposed, result, scratch):
    vectors, products = scratch
    total_rows = column.shape[0]
    result[...] = jnp.zeros_like(result)

    def one_round(r, carry):
        prepare(r)
        eye = rows((BLOCK, BLOCK)) == lanes((BLOCK, BLOCK))
        place_hot = []
        for at in range(0, total_rows, BLOCK):
            found = column[at : at + BLOCK]
            first = jnp.floor((found + 0.5) * (1.0 / size))
            second = found - first * size
            gather, put = (first, second) if gather_first else (second, first)
            width = table.shape[0]
            gather = jnp.concatenate([gather] * (width // BLOCK), axis=1)
            hot = one_hot(gather == lanes((BLOCK, width)).astype(f32))
            vectors[at : at + BLOCK] = jnp.dot(hot, table, preferred_element_type=f32)
            put = jnp.sum(jnp.where(eye, put, 0.0), axis=0, keepdims=True)
            place_hot.append(one_hot(rows((result.shape[0], BLOCK)).astype(f32) == put))

        def group(g, carry):
            for u in range(GROUP):
                at = pl.multiple_of((g * GROUP + u) * capacity, 8)
                own = vectors[pl.ds(at, capacity)]
                left = jnp.concatenate([own[:, n * BLOCK : (n + 1) * BLOCK] for n in range(4)], axis=0)
                high, low = part(r, g, u)
                right = jnp.concatenate([high, low], axis=1 if transposed else 0)
                contract = (((1,), (0 if transposed else 1,)), ((), ()))
                product = lax.dot_general(left.astype(bf16), right, contract, preferred_element_type=f32)
                for f in range(2):
                    high_part = product[f * capacity : (f + 1) * capacity]
                    low_part = product[(f + 2) * capacity : (f + 3) * capacity, :BLOCK]
                    products[pl.ds(at, capacity), f * BLOCK : (f + 1) * BLOCK] = (
                        high_part[:, BLOCK:] + low_part
                    ) + high_part[:, :BLOCK]
            return carry

        lax.fori_loop(0, blocks // GROUP, group, 0)
        summed = jnp.dot(
            jnp.concatenate(place_hot, axis=1),
            jnp.concatenate(split(products[...]), axis=1),
            preferred_element_type=f32,
        )
        result[...] += summed[:, : 2 * BLOCK] + summed[:, 2 * BLOCK :]
        return carry

    lax.fori_loop(0, rounds, one_round, 0)


def slot_keys(ids, tile_lat, atm):
    lon_count, cap = ids.shape[3:]
    ocean, atm_ids, block_ids = (ids[n, 0, 0] for n in range(3))
    order = (ocean & 1) * tile_lat + (ocean >> 1) + rows((lon_count, cap)) * (2 * tile_lat)
    order = jnp.where(ocean >= 0, order, lon_count * 2 * tile_lat)
    return as_row((order * atm + atm_ids).astype(f32)), as_row(block_ids)


def weigh(atm_near, margins, weights, after, sums, found, keys, result, *scratch):
    scratch, (held, arrived) = scratch[:2], scratch[2:]
    fetch_weights(weights, held, arrived)
    lon_count = margins.shape[3]
    atm = atm_near.shape[2]
    blocks = weights.shape[0]
    tile_lat = 2 * sums.shape[1] // 9
    code, block_row = slot_keys(margins, tile_lat, atm)
    rank = rank_slots(block_row, blocks)
    keys[0:1] = code
    keys[1:2] = block_row.astype(f32)
    keys[2:3] = rank
    capacity = places(code.shape[1], blocks)
    rounds = jnp.max(rank).astype(jnp.int32) // capacity + 1
    parts = [split(atm_near[f, 0]) for f in range(2)]
    table = jnp.concatenate([parts[f][n] for n in range(2) for f in range(2)], axis=1)

    def prepare(r):
        find_slots(rounds - 1 - r, code, block_row, rank, capacity, blocks, found)

    part = held_part(weights, held, arrived)
    couple(blocks, part, table, atm, capacity, rounds, prepare, found, False, False, result, scratch)
    lane = lanes((tile_lat, BLOCK))

    def block_sums(k, f, h):
        at = (2 * k + h) * tile_lat
        return result[at : at + tile_lat, f * BLOCK : (f + 1) * BLOCK]

    for k in range(lon_count):
        edge = jnp.zeros((tile_lat, BLOCK), f32)
        for f in range(2):
            for h in range(2):
                sums[k, (2 * f + h) * tile_lat : (2 * f + h + 1) * tile_lat] = block_sums(k, f, h)
            at = f * HALO
            after = turn(block_sums((k + 1) % lon_count, f, 0), at, 1)
            before = turn(block_sums((k - 1) % lon_count, f, 1), -at, 1)
            edge = jnp.where((lane >= at) & (lane < at + HALO), after, edge)
            end = BLOCK - at
            edge = jnp.where((lane >= end - HALO) & (lane < end), before, edge)
        upper, lower = edge[: tile_lat // 2], edge[tile_lat // 2 :]
        near = lane[: tile_lat // 2]
        lower = jnp.where(near < BLOCK // 2, turn(lower, 2 * HALO, 1), turn(lower, -2 * HALO, 1))
        sums[k, 4 * tile_lat :] = jnp.where((near < 2 * HALO) | (near >= BLOCK - 2 * HALO), upper, lower)


def unweigh(gathered, found, keys, weights, gradient, result, column, *scratch):
    scratch, (held, arrived) = scratch[:2], scratch[2:]
    fetch_weights(weights, held, arrived)
    atm = gradient.shape[2]
    blocks = weights.shape[0]
    lon_count, ocean_blocks = gathered.shape[0], gathered.shape[1] // 2
    capacity = places(keys.shape[1], blocks)
    rounds = jnp.max(keys[2:3]).astype(jnp.int32) // capacity + 1
    parts = [
        split(
            jnp.concatenate(
                [gathered[k, f * ocean_blocks : (f + 1) * ocean_blocks] for k in range(lon_count)], axis=0
            )
        )
        for f in range(2)
    ]
    table = jnp.concatenate([parts[f][n] for n in range(2) for f in range(2)], axis=1)

    def prepare(r):
        @pl.when(r == 0)
        def _():
            column[...] = found[...]

        @pl.when(r > 0)
        def _():
            find_slots(r, keys[0:1], keys[1:2].astype(jnp.int32), keys[2:3], capacity, blocks, column)

    couple(
        blocks,
        held_part(weights, held, arrived),
        table,
        atm,
        capacity,
        rounds,
        prepare,
        column,
        True,
        True,
        result,
        scratch,
    )
    for f in range(2):
        gradient[f, 0] = result[:, f * BLOCK : (f + 1) * BLOCK]


def on_device(tracers, cotangent, land_mask, diffusion, velocity, weights, atm_state, margins):
    levels, tile_lat, tile_lon = land_mask.shape
    lon_count = lax.axis_size("lon")
    slots = lon_count * margins.shape[4]
    halves = tile_lon // BLOCK
    count = 9 * levels - 1
    parts = -(-count // PER_LANES)
    inputs = (tracers, cotangent, land_mask, diffusion, velocity)

    def in_vmem(s):
        return pltpu.VMEM(s.shape, s.dtype)

    message = (parts, tile_lat, BLOCK)
    fields, near, far, atm_near, margins_near = call(
        pack_columns,
        [
            (count, tile_lat, tile_lon),
            message,
            message,
            atm_state.shape,
            jax.ShapeDtypeStruct(margins.shape, margins.dtype),
        ],
        [*map(in_vmem, inputs), pltpu.SemaphoreType.DMA((7,))],
        name="pack_columns",
        inputs=7,
        far=range(7),
    )(*inputs, atm_state, margins)
    near_columns, far_columns = swap(near, far, "lon", True)

    blocks_of, atm = weights.shape[0], atm_state.shape[2]
    groups = blocks_of // GROUP
    sum_rows = 2 * halves * tile_lat + tile_lat // 2
    ocean_blocks = lon_count * halves * tile_lat
    held_rows = -(-places(slots, blocks_of) * blocks_of // BLOCK) * BLOCK

    def coupling_scratch(result_rows):
        return [
            pltpu.VMEM((result_rows, 2 * BLOCK), f32),
            pltpu.VMEM((held_rows, 4 * BLOCK), f32),
            pltpu.VMEM((held_rows, 2 * BLOCK), f32),
            pltpu.VMEM((groups, GROUP, BLOCK, BLOCK), f32),
            pltpu.SemaphoreType.DMA((groups,)),
        ]

    coupling_flops = 4 * slots * blocks_of * 2 * BLOCK * BLOCK * 2
    sums, found, keys = call(
        weigh,
        [(lon_count, sum_rows, BLOCK), (held_rows, BLOCK), (8, slots)],
        coupling_scratch(ocean_blocks),
        coupling_flops,
        name="weigh",
        inputs=4,
        far=(2,),
    )(atm_near, margins_near, weights, near)

    sources = count * halves + 2 * parts
    message = (-(-sources // 2), 8, BLOCK)
    columns = (parts, tile_lat, BLOCK)
    near, far, from_west, from_east, sums = call(
        pack_rows,
        [message, message, columns, columns, sums.shape],
        name="pack_rows",
        inputs=4,
        aliases={3: 4},
    )(fields, near_columns, far_columns, sums)
    received = lax.all_to_all(sums, "lon", split_axis=0, concat_axis=0, tiled=True)
    near_rows, far_rows = swap(near, far, "lat", False)

    wide = (tile_lat + 8, tile_lon + BLOCK)
    own = (2 * halves * tile_lat, BLOCK)
    adjoint_states = (2, STEPS - 1, levels, *wide)
    blocks, coeffs, start, states = call(
        run_adjoint,
        [(lon_count, *own), (6, levels, *wide), (4 * levels, *wide), adjoint_states],
        [
            pltpu.VMEM((count - 4 * levels, *wide), f32),
            pltpu.VMEM(own, f32),
            pltpu.SemaphoreType.DMA((2, lon_count)),
        ],
        name="run_adjoint",
        inputs=5,
        far_outs=(0,),
    )(fields, from_west, from_east, far_rows, near_rows)
    gathered = lax.all_to_all(blocks, "lon", split_axis=0, concat_axis=0, tiled=True)

    message = (1, 8, tile_lon + BLOCK)
    forcing, near, far = call(
        sum_forcing, [(2, tile_lat, tile_lon + BLOCK), message, message], name="sum_forcing", inputs=1
    )(received)
    near_rows, far_rows = swap(near, far, "lat", False)
    (adjoint,) = call(
        finish_adjoint,
        [cotangent.shape],
        [pltpu.VMEM(adjoint_states, f32)],
        name="finish_adjoint",
        inputs=3,
    )(coeffs, start, states)
    (final,) = call(
        run_forward,
        [tracers.shape],
        [pltpu.VMEM((2, levels, *wide), f32)],
        name="run_forward",
        inputs=5,
    )(coeffs, start, forcing, far_rows, near_rows)

    (gradient,) = call(
        unweigh,
        [atm_state.shape],
        [coupling_scratch(atm)[0], in_vmem(found), *coupling_scratch(atm)[1:]],
        coupling_flops,
        name="unweigh",
        inputs=4,
        far=(3,),
    )(gathered, found, keys, weights)
    return (final, adjoint, gradient)


def solution(mesh):
    return jax.shard_map(
        on_device,
        mesh=mesh,
        in_specs=(
            P(None, None, "lat", "lon"),
            P(None, None, "lat", "lon"),
            P(None, "lat", "lon"),
            P(None, None, "lat", "lon"),
            P(None, None, "lat", "lon"),
            P(),
            P(None, "lat", "lon", None),
            P(None, "lat", "lon", None, None),
        ),
        out_specs=(
            P(None, None, "lat", "lon"),
            P(None, None, "lat", "lon"),
            P(None, "lat", "lon", None),
        ),
        check_vma=False,
    )
```

```python
import jax
import jax.numpy as jnp
from jax import lax
from jax.experimental import pallas as pl
from jax.experimental.pallas import tpu as pltpu
from jax.sharding import PartitionSpec as P

BLOCK = 128
STEPS = 4
HALO = STEPS
PER_LANES = BLOCK // HALO
GROUP = 16
f32 = jnp.float32
bf16 = jnp.bfloat16
VMEM_LIMIT = 20 * 1024 * 1024


def call(body, outs, scratch=(), flops=0, name=None, inputs=0, far=(), far_outs=(), aliases=None):
    outs = [s if isinstance(s, jax.ShapeDtypeStruct) else jax.ShapeDtypeStruct(s, f32) for s in outs]
    near = pl.BlockSpec(memory_space=pltpu.VMEM)
    aliases = aliases or {}
    kernel = pl.pallas_call(
        body,
        out_shape=outs,
        in_specs=[
            pl.BlockSpec(memory_space=pl.ANY)
            if n in aliases
            else pl.BlockSpec(memory_space=pltpu.HBM)
            if n in far
            else near
            for n in range(inputs)
        ],
        out_specs=[
            pl.BlockSpec(memory_space=pl.ANY) if n in aliases.values() or n in far_outs else near
            for n in range(len(outs))
        ],
        input_output_aliases=aliases,
        scratch_shapes=list(scratch),
        compiler_params=pltpu.CompilerParams(vmem_limit_bytes=VMEM_LIMIT),
        cost_estimate=pl.CostEstimate(flops=flops, bytes_accessed=1 << 20, transcendentals=0),
        name=name,
    )

    def run(*args):
        return kernel(
            *(pltpu.with_memory_space_constraint(x, pltpu.HBM) if n in far else x for n, x in enumerate(args))
        )

    return run


def lanes(shape):
    return lax.broadcasted_iota(jnp.int32, shape, len(shape) - 1)


def rows(shape):
    return lax.broadcasted_iota(jnp.int32, shape, len(shape) - 2)


def turn(x, shift, axis):
    shift %= x.shape[axis]
    return pltpu.roll(x, shift, axis) if shift else x


def swap(near, far, axis, wrap):
    count = lax.axis_size(axis)
    pairs = [[], []]
    for i in range(count if wrap else count - 1):
        j = (i + 1) % count
        pairs[i % 2] += [(i, j), (j, i)]
    far = lax.ppermute(far, axis, pairs[1])
    return lax.ppermute(near, axis, pairs[0]), far


def sort_swap(axis, after, before):
    odd = lax.rem(lax.axis_index(axis), 2) == 1
    return jnp.where(odd, before, after), jnp.where(odd, after, before)


def tile_fields(tracers, cotangent, land_mask, diffusion, velocity):
    levels = land_mask.shape[0]
    mask = [land_mask[level].astype(f32) for level in range(levels)]
    out = [tracers[f, level] for f in range(2) for level in range(levels)]
    out += [cotangent[f, level] for f in range(2) for level in range(levels)]
    out += [diffusion[0, level] * mask[level] for level in range(levels)]
    out += [velocity[0, level] * mask[level] for level in range(levels)]
    out += [diffusion[1, level] * mask[level] for level in range(levels)]
    out += [velocity[1, level] * mask[level] for level in range(levels)]
    out += [diffusion[2, level] * mask[level] * mask[level + 1] for level in range(levels - 1)]
    return out


def fetch(pairs, arrived):
    copies = [pltpu.make_async_copy(src, dst, arrived.at[n]) for n, (src, dst) in enumerate(pairs)]
    for copy in copies:
        copy.start()
    return copies


def pack_columns(*refs):
    inputs, (fields, near, far), scratch = refs[:7], refs[7:10], refs[12:]
    copies = fetch(zip(inputs, [*scratch[:5], *refs[10:12]]), scratch[5])
    for copy in copies[:5]:
        copy.wait()
    shape = near.shape[1:]
    lane = lanes(shape)
    west = [jnp.zeros(shape, f32) for _ in range(near.shape[0])]
    east = [jnp.zeros(shape, f32) for _ in range(near.shape[0])]
    for i, field in enumerate(tile_fields(*scratch[:5])):
        fields[i] = field
        part, at = divmod(i, PER_LANES)
        at *= HALO
        here = (lane >= at) & (lane < at + HALO)
        west[part] = jnp.where(here, turn(field[:, :BLOCK], at, 1), west[part])
        east[part] = jnp.where(here, turn(field[:, -BLOCK:], at + HALO, 1), east[part])
    for part in range(near.shape[0]):
        near[part], far[part] = sort_swap("lon", east[part], west[part])
    for copy in copies[5:]:
        copy.wait()


def unpack_columns(from_west, from_east, i):
    part, at = divmod(i, PER_LANES)
    at *= HALO
    lane = lanes(from_west[part].shape)
    east = turn(from_east[part], -at, 1)
    west = turn(from_west[part], -at - HALO, 1)
    return jnp.where(lane < HALO, east, jnp.where(lane >= BLOCK - HALO, west, 0.0))


def row_sources(fields, from_west, from_east):
    out = [(fields, (i, slice(None), slice(h * BLOCK, (h + 1) * BLOCK)))
           for i in range(fields.shape[0]) for h in range(fields.shape[2] // BLOCK)]
    for columns in (from_west, from_east):
        out += [(columns, (part,)) for part in range(columns.shape[0])]
    return out


def pack_rows(fields, near_columns, far_columns, sums, near, far, from_west, from_east, same_sums):
    for part in range(from_west.shape[0]):
        from_east[part], from_west[part] = sort_swap("lon", near_columns[part], far_columns[part])
    sources = [ref[at] for ref, at in row_sources(fields, from_west, from_east)]
    half = near.shape[0]
    row = rows((8, BLOCK))
    for i in range(half):
        first = sources[i]
        second = sources[i + half] if i + half < len(sources) else jnp.zeros_like(first)
        to_north = jnp.where(row < HALO, turn(first[-8:], HALO, 0), second[-8:])
        to_south = jnp.where(row < HALO, first[:8], turn(second[:8], HALO, 0))
        near[i], far[i] = sort_swap("lat", to_north, to_south)


def edge_rows(near, far, i):
    half = near.shape[0]
    from_north, from_south = sort_swap("lat", near[i % half], far[i % half])
    if i < half:
        from_south = turn(from_south, HALO, 0)
    else:
        from_north = turn(from_north, HALO, 0)
    return jnp.where(rows(from_north.shape) < HALO, from_north, from_south)


def widen(fields, from_west, from_east, near, far, start, wide):
    count, tile_lat, tile_lon = fields.shape
    halves = tile_lon // BLOCK
    parts = from_west.shape[0]
    corners = [edge_rows(near, far, count * halves + n) for n in range(2 * parts)]
    for i in range(count):
        out = start.at[i] if i < start.shape[0] else wide.at[i - start.shape[0]]
        out[:tile_lat, :tile_lon] = fields[i]
        out[:tile_lat, tile_lon:] = unpack_columns(from_west, from_east, i)
        for h in range(halves):
            out[tile_lat:, h * BLOCK : (h + 1) * BLOCK] = edge_rows(near, far, i * halves + h)
        out[tile_lat:, tile_lon:] = unpack_columns(corners[:parts], corners[parts:], i)


def eastward(x):
    return turn(x, -1, 1)


def westward(x):
    return turn(x, 1, 1)


def northward(x):
    return turn(x, -1, 0)


def southward(x):
    return turn(x, 1, 0)


def adjoint_step(coeffs, read, write, first, last):
    levels = coeffs.shape[1]
    above = coeffs[4, first - 1] * (read(first) - read(first - 1)) if first else None
    for level in range(first, last):
        lam = read(level)
        step_x = eastward(lam) - lam
        step_y = northward(lam) - lam
        out = lam + coeffs[0, level] * step_x + westward(coeffs[1, level] * step_x)
        out = out + coeffs[2, level] * step_y + southward(coeffs[3, level] * step_y)
        if above is not None:
            out = out - above
        if level < levels - 1:
            above = coeffs[4, level] * (read(level + 1) - lam)
            out = out + above
        write(level, out)


def surface_levels(step, levels):
    return min(levels, STEPS - 1 - step)


def run_adjoint(
    fields, from_west, from_east, far, near, blocks, coeffs, start, states, wide, own, sent
):
    levels = coeffs.shape[1]
    tile_lat, tile_lon = fields.shape[1:]
    halves = tile_lon // BLOCK
    widen(fields, from_west, from_east, near, far, start, wide)
    base = 0
    mask0 = None
    for level in range(levels):
        east_d, east_u = wide[base + level], wide[base + levels + level]
        north_d, north_u = wide[base + 2 * levels + level], wide[base + 3 * levels + level]
        mask = (east_d > 0.0).astype(f32)
        mask0 = mask if mask0 is None else mask0
        mask_e, mask_n = eastward(mask), northward(mask)
        east_k, east_v = east_d * mask_e, east_u * mask_e
        north_k, north_v = north_d * mask_n, north_u * mask_n
        coeffs[0, level] = jnp.maximum(east_v, 0.0) + east_k
        coeffs[1, level] = jnp.minimum(east_v, 0.0) - east_k
        coeffs[2, level] = jnp.maximum(north_v, 0.0) + north_k
        coeffs[3, level] = jnp.minimum(north_v, 0.0) - north_k
        coeffs[4, level] = wide[base + 4 * levels + level] if level < levels - 1 else jnp.zeros_like(mask)
        coeffs[5, level] = mask
    copies = []
    for f in range(2):
        surface = start[(2 + f) * levels, :tile_lat, :tile_lon]
        for step in range(STEPS - 1):

            def read(level):
                return states[f, step - 1, level] if step else start[(2 + f) * levels + level]

            def write(level, lam):
                states[f, step, level] = lam

            adjoint_step(coeffs, read, write, 0, surface_levels(step, levels))
            surface = surface + states[f, step, 0, :tile_lat, :tile_lon]
        surface = surface * mask0[:tile_lat, :tile_lon]
        for h in range(halves):
            at = (f * halves + h) * tile_lat
            own[at : at + tile_lat] = surface[:, h * BLOCK : (h + 1) * BLOCK]
        field = pl.ds(f * halves * tile_lat, halves * tile_lat)
        copies += fetch([(own.at[field], blocks.at[k, field]) for k in range(blocks.shape[0])], sent.at[f])
    for copy in copies:
        copy.wait()


def finish_adjoint(coeffs, start, states, adjoint_out, rest):
    levels = coeffs.shape[1]
    tile_lat, tile_lon = adjoint_out.shape[2:]
    for f in range(2):
        for step in range(STEPS):
            done = surface_levels(step, levels)

            def read(level):
                if not step:
                    return start[(2 + f) * levels + level]
                return (states if level < surface_levels(step - 1, levels) else rest)[f, step - 1, level]

            def write(level, lam):
                if step == STEPS - 1:
                    adjoint_out[f, level] = lam[:tile_lat, :tile_lon]
                else:
                    rest[f, step, level] = lam

            adjoint_step(coeffs, read, write, done, levels)


def sum_forcing(received, forcing, near, far):
    tile_lat = forcing.shape[1]
    halves = forcing.shape[2] // BLOCK - 1
    total = received[0]
    for j in range(1, received.shape[0]):
        total = total + received[j]
    lane = lanes((tile_lat, BLOCK))
    upper = total[2 * halves * tile_lat :]
    lower = jnp.where(lane[: tile_lat // 2] < BLOCK // 2, turn(upper, -2 * HALO, 1), turn(upper, 2 * HALO, 1))
    packed = jnp.concatenate([upper, lower], axis=0)
    for f in range(2):
        for h in range(halves):
            at = (f * halves + h) * tile_lat
            forcing[f, :, h * BLOCK : (h + 1) * BLOCK] = total[at : at + tile_lat]
        used = (lane < HALO) | (lane >= BLOCK - HALO)
        if f == 0:
            edge = packed
        else:
            edge = jnp.where(lane < HALO, turn(packed, -HALO, 1), turn(packed, HALO, 1))
        forcing[f, :, halves * BLOCK :] = jnp.where(used, edge, 0.0)
    row = rows((8, forcing.shape[2]))
    to_north = jnp.where(row < HALO, turn(forcing[0, tile_lat - 8 :], HALO, 0), forcing[1, tile_lat - 8 :])
    to_south = jnp.where(row < HALO, forcing[0, :8], turn(forcing[1, :8], HALO, 0))
    near[0], far[0] = sort_swap("lat", to_north, to_south)


def run_forward(coeffs, start, forcing, far, near, final, state):
    levels = coeffs.shape[1]
    tile_lat, tile_lon = final.shape[2:]
    for f in range(2):
        force = jnp.concatenate([forcing[f], edge_rows(near, far, f)], axis=0)
        force = force * coeffs[5, 0]
        for step in range(STEPS):
            above = None
            for level in range(levels):
                read = (lambda n: start[f * levels + n]) if step == 0 else (lambda n: state[(step - 1) % 2, n])
                theta = read(level)
                east_flux = coeffs[0, level] * theta + coeffs[1, level] * eastward(theta)
                north_flux = coeffs[2, level] * theta + coeffs[3, level] * northward(theta)
                out = theta - (east_flux - westward(east_flux)) - (north_flux - southward(north_flux))
                if level < levels - 1:
                    vertical = coeffs[4, level] * (theta - read(level + 1))
                    out = out - vertical
                if above is not None:
                    out = out + above
                above = vertical if level < levels - 1 else None
                if level == 0:
                    out = out + force
                if step == STEPS - 1:
                    final[f, level] = out[:tile_lat, :tile_lon]
                else:
                    state[step % 2, level] = out


def split(x):
    high = x.astype(bf16)
    return high, (x - high.astype(f32)).astype(bf16)


def weight_copies(weights, held, arrived):
    for g in range(held.shape[0]):
        yield pltpu.make_async_copy(weights.at[pl.ds(g * GROUP, GROUP)], held.at[g], arrived.at[g])


def fetch_weights(weights, held, arrived):
    for copy in weight_copies(weights, held, arrived):
        copy.start()


def held_part(weights, held, arrived):
    def part(r, g, u):
        if u == 0:

            @pl.when(r == 0)
            def _():
                pltpu.make_async_copy(weights.at[pl.ds(g * GROUP, GROUP)], held.at[g], arrived.at[g]).wait()

        return split(held[g, u])

    return part


def one_hot(where):
    return jnp.where(where, 1.0, 0.0).astype(bf16)


def places(slots, blocks):
    return 8 * (-(-2 * slots // (8 * blocks)) + 1)


def as_row(ids):
    return jnp.concatenate([ids[k : k + 1, :] for k in range(ids.shape[0])], axis=1)


def rank_slots(block_row, blocks):
    slots = block_row.shape[1]
    mine = rows((blocks, slots)) == block_row
    cuts = range(0, slots, BLOCK)
    stacked = jnp.concatenate([one_hot(mine[:, at : at + BLOCK]) for at in cuts], axis=0)
    shape = (BLOCK, 2 * BLOCK)
    counts = jnp.dot(stacked, one_hot(rows(shape) < lanes(shape)), preferred_element_type=f32)
    before, out = jnp.zeros((blocks, BLOCK), f32), []
    for n, at in enumerate(cuts):
        run = counts[n * blocks : (n + 1) * blocks]
        here = jnp.where(mine[:, at : at + BLOCK], run[:, :BLOCK] + before, 0.0)
        out.append(jnp.sum(here, axis=0, keepdims=True))
        before = before + run[:, BLOCK:]
    return jnp.concatenate(out, axis=1)


def find_slots(r, code, block_row, rank, capacity, blocks, found):
    slots = block_row.shape[1]
    mine = rows((blocks, slots)) == block_row
    ranked = one_hot(rows((capacity, slots)) == rank.astype(jnp.int32) - r * capacity)
    rest, codes = code + 1.0, None
    for base in (4096.0, 64.0, 1.0):
        digit = jnp.floor(rest * (1.0 / base))
        rest = rest - digit * base
        part = lax.dot_general(
            ranked,
            jnp.where(mine, digit, 0.0).astype(bf16),
            (((1,), (1,)), ((), ())),
            preferred_element_type=f32,
        )
        codes = part * base if codes is None else codes + part * base
    found[:, :blocks] = codes - 1.0


def couple(blocks, part, table, size, capacity, rounds, prepare, found, gather_first, transposed, result, scratch):
    column, vectors, products = scratch
    total_rows = column.shape[0]
    result[...] = jnp.zeros_like(result)

    def one_round(r, carry):
        prepare(r)
        codes = found[...]
        for w in range(blocks):
            column[w * capacity : (w + 1) * capacity] = jnp.broadcast_to(codes[:, w : w + 1], (capacity, BLOCK))
        eye = rows((BLOCK, BLOCK)) == lanes((BLOCK, BLOCK))
        place_hot = []
        for at in range(0, total_rows, BLOCK):
            code = column[at : at + BLOCK]
            first = jnp.floor((code + 0.5) * (1.0 / size))
            second = code - first * size
            gather, put = (first, second) if gather_first else (second, first)
            width = table.shape[0]
            gather = jnp.concatenate([gather] * (width // BLOCK), axis=1)
            hot = one_hot(gather == lanes((BLOCK, width)).astype(f32))
            vectors[at : at + BLOCK] = jnp.dot(hot, table, preferred_element_type=f32)
            put = jnp.sum(jnp.where(eye, put, 0.0), axis=0, keepdims=True)
            place_hot.append(one_hot(rows((result.shape[0], BLOCK)).astype(f32) == put))

        def group(g, carry):
            for u in range(GROUP):
                at = pl.multiple_of((g * GROUP + u) * capacity, 8)
                own = vectors[pl.ds(at, capacity)]
                left = jnp.concatenate([own[:, n * BLOCK : (n + 1) * BLOCK] for n in range(4)], axis=0)
                high, low = part(r, g, u)
                right = jnp.concatenate([high, low], axis=1 if transposed else 0)
                contract = (((1,), (0 if transposed else 1,)), ((), ()))
                product = lax.dot_general(left.astype(bf16), right, contract, preferred_element_type=f32)
                for f in range(2):
                    high_part = product[f * capacity : (f + 1) * capacity]
                    low_part = product[(f + 2) * capacity : (f + 3) * capacity, :BLOCK]
                    products[pl.ds(at, capacity), f * BLOCK : (f + 1) * BLOCK] = (
                        high_part[:, BLOCK:] + low_part
                    ) + high_part[:, :BLOCK]
            return carry

        lax.fori_loop(0, blocks // GROUP, group, 0)
        summed = jnp.dot(
            jnp.concatenate(place_hot, axis=1),
            jnp.concatenate(split(products[...]), axis=1),
            preferred_element_type=f32,
        )
        result[...] += summed[:, : 2 * BLOCK] + summed[:, 2 * BLOCK :]
        return carry

    lax.fori_loop(0, rounds, one_round, 0)


def slot_keys(ids, tile_lat, atm):
    lon_count, cap = ids.shape[3:]
    ocean, atm_ids, block_ids = (ids[n, 0, 0] for n in range(3))
    order = (ocean & 1) * tile_lat + (ocean >> 1) + rows((lon_count, cap)) * (2 * tile_lat)
    order = jnp.where(ocean >= 0, order, lon_count * 2 * tile_lat)
    return as_row((order * atm + atm_ids).astype(f32)), as_row(block_ids)


def weigh(atm_near, margins, weights, after, sums, found, keys, result, *scratch):
    scratch, (held, arrived) = scratch[:3], scratch[3:]
    fetch_weights(weights, held, arrived)
    lon_count = margins.shape[3]
    atm = atm_near.shape[2]
    blocks = weights.shape[0]
    tile_lat = 2 * sums.shape[1] // 9
    code, block_row = slot_keys(margins, tile_lat, atm)
    rank = rank_slots(block_row, blocks)
    keys[0:1] = code
    keys[1:2] = block_row.astype(f32)
    keys[2:3] = rank
    capacity = places(code.shape[1], blocks)
    rounds = jnp.max(rank).astype(jnp.int32) // capacity + 1
    parts = [split(atm_near[f, 0]) for f in range(2)]
    table = jnp.concatenate([parts[f][n] for n in range(2) for f in range(2)], axis=1)

    def prepare(r):
        find_slots(rounds - 1 - r, code, block_row, rank, capacity, blocks, found)

    part = held_part(weights, held, arrived)
    couple(blocks, part, table, atm, capacity, rounds, prepare, found, False, False, result, scratch)
    lane = lanes((tile_lat, BLOCK))

    def block_sums(k, f, h):
        at = (2 * k + h) * tile_lat
        return result[at : at + tile_lat, f * BLOCK : (f + 1) * BLOCK]

    for k in range(lon_count):
        edge = jnp.zeros((tile_lat, BLOCK), f32)
        for f in range(2):
            for h in range(2):
                sums[k, (2 * f + h) * tile_lat : (2 * f + h + 1) * tile_lat] = block_sums(k, f, h)
            at = f * HALO
            after = turn(block_sums((k + 1) % lon_count, f, 0), at, 1)
            before = turn(block_sums((k - 1) % lon_count, f, 1), -at, 1)
            edge = jnp.where((lane >= at) & (lane < at + HALO), after, edge)
            end = BLOCK - at
            edge = jnp.where((lane >= end - HALO) & (lane < end), before, edge)
        upper, lower = edge[: tile_lat // 2], edge[tile_lat // 2 :]
        near = lane[: tile_lat // 2]
        lower = jnp.where(near < BLOCK // 2, turn(lower, 2 * HALO, 1), turn(lower, -2 * HALO, 1))
        sums[k, 4 * tile_lat :] = jnp.where((near < 2 * HALO) | (near >= BLOCK - 2 * HALO), upper, lower)


def unweigh(gathered, found, keys, weights, gradient, result, codes, *scratch):
    scratch, (held, arrived) = scratch[:3], scratch[3:]
    fetch_weights(weights, held, arrived)
    atm = gradient.shape[2]
    blocks = weights.shape[0]
    lon_count, ocean_blocks = gathered.shape[0], gathered.shape[1] // 2
    capacity = places(keys.shape[1], blocks)
    rounds = jnp.max(keys[2:3]).astype(jnp.int32) // capacity + 1
    parts = [
        split(
            jnp.concatenate(
                [gathered[k, f * ocean_blocks : (f + 1) * ocean_blocks] for k in range(lon_count)], axis=0
            )
        )
        for f in range(2)
    ]
    table = jnp.concatenate([parts[f][n] for n in range(2) for f in range(2)], axis=1)

    def prepare(r):
        @pl.when(r == 0)
        def _():
            codes[...] = found[...]

        @pl.when(r > 0)
        def _():
            find_slots(r, keys[0:1], keys[1:2].astype(jnp.int32), keys[2:3], capacity, blocks, codes)

    couple(
        blocks,
        held_part(weights, held, arrived),
        table,
        atm,
        capacity,
        rounds,
        prepare,
        codes,
        True,
        True,
        result,
        scratch,
    )
    for f in range(2):
        gradient[f, 0] = result[:, f * BLOCK : (f + 1) * BLOCK]


def on_device(tracers, cotangent, land_mask, diffusion, velocity, weights, atm_state, margins):
    levels, tile_lat, tile_lon = land_mask.shape
    lon_count = lax.axis_size("lon")
    slots = lon_count * margins.shape[4]
    halves = tile_lon // BLOCK
    count = 9 * levels - 1
    parts = -(-count // PER_LANES)
    inputs = (tracers, cotangent, land_mask, diffusion, velocity)

    def in_vmem(s):
        return pltpu.VMEM(s.shape, s.dtype)

    message = (parts, tile_lat, BLOCK)
    fields, near, far, atm_near, margins_near = call(
        pack_columns,
        [
            (count, tile_lat, tile_lon),
            message,
            message,
            atm_state.shape,
            jax.ShapeDtypeStruct(margins.shape, margins.dtype),
        ],
        [*map(in_vmem, inputs), pltpu.SemaphoreType.DMA((7,))],
        name="pack_columns",
        inputs=7,
        far=range(7),
    )(*inputs, atm_state, margins)
    near_columns, far_columns = swap(near, far, "lon", True)

    blocks_of, atm = weights.shape[0], atm_state.shape[2]
    groups = blocks_of // GROUP
    sum_rows = 2 * halves * tile_lat + tile_lat // 2
    ocean_blocks = lon_count * halves * tile_lat
    held_rows = -(-places(slots, blocks_of) * blocks_of // BLOCK) * BLOCK

    def coupling_scratch(result_rows):
        return [
            pltpu.VMEM((result_rows, 2 * BLOCK), f32),
            pltpu.VMEM((held_rows, BLOCK), f32),
            pltpu.VMEM((held_rows, 4 * BLOCK), f32),
            pltpu.VMEM((held_rows, 2 * BLOCK), f32),
            pltpu.VMEM((groups, GROUP, BLOCK, BLOCK), f32),
            pltpu.SemaphoreType.DMA((groups,)),
        ]

    coupling_flops = 4 * slots * blocks_of * 2 * BLOCK * BLOCK * 2
    sums, found, keys = call(
        weigh,
        [(lon_count, sum_rows, BLOCK), (places(slots, blocks_of), BLOCK), (8, slots)],
        coupling_scratch(ocean_blocks),
        coupling_flops,
        name="weigh",
        inputs=4,
        far=(2,),
    )(atm_near, margins_near, weights, near)

    sources = count * halves + 2 * parts
    message = (-(-sources // 2), 8, BLOCK)
    columns = (parts, tile_lat, BLOCK)
    near, far, from_west, from_east, sums = call(
        pack_rows,
        [message, message, columns, columns, sums.shape],
        name="pack_rows",
        inputs=4,
        aliases={3: 4},
    )(fields, near_columns, far_columns, sums)
    received = lax.all_to_all(sums, "lon", split_axis=0, concat_axis=0, tiled=True)
    near_rows, far_rows = swap(near, far, "lat", False)

    wide = (tile_lat + 8, tile_lon + BLOCK)
    own = (2 * halves * tile_lat, BLOCK)
    adjoint_states = (2, STEPS - 1, levels, *wide)
    blocks, coeffs, start, states = call(
        run_adjoint,
        [(lon_count, *own), (6, levels, *wide), (4 * levels, *wide), adjoint_states],
        [
            pltpu.VMEM((count - 4 * levels, *wide), f32),
            pltpu.VMEM(own, f32),
            pltpu.SemaphoreType.DMA((2, lon_count)),
        ],
        name="run_adjoint",
        inputs=5,
        far_outs=(0,),
    )(fields, from_west, from_east, far_rows, near_rows)
    gathered = lax.all_to_all(blocks, "lon", split_axis=0, concat_axis=0, tiled=True)

    message = (1, 8, tile_lon + BLOCK)
    forcing, near, far = call(
        sum_forcing, [(2, tile_lat, tile_lon + BLOCK), message, message], name="sum_forcing", inputs=1
    )(received)
    near_rows, far_rows = swap(near, far, "lat", False)
    (adjoint,) = call(
        finish_adjoint,
        [cotangent.shape],
        [pltpu.VMEM(adjoint_states, f32)],
        name="finish_adjoint",
        inputs=3,
    )(coeffs, start, states)
    (final,) = call(
        run_forward,
        [tracers.shape],
        [pltpu.VMEM((2, levels, *wide), f32)],
        name="run_forward",
        inputs=5,
    )(coeffs, start, forcing, far_rows, near_rows)

    (gradient,) = call(
        unweigh,
        [atm_state.shape],
        [coupling_scratch(atm)[0], in_vmem(found), *coupling_scratch(atm)[1:]],
        coupling_flops,
        name="unweigh",
        inputs=4,
        far=(3,),
    )(gathered, found, keys, weights)
    return (final, adjoint, gradient)


def solution(mesh):
    return jax.shard_map(
        on_device,
        mesh=mesh,
        in_specs=(
            P(None, None, "lat", "lon"),
            P(None, None, "lat", "lon"),
            P(None, "lat", "lon"),
            P(None, None, "lat", "lon"),
            P(None, None, "lat", "lon"),
            P(),
            P(None, "lat", "lon", None),
            P(None, "lat", "lon", None, None),
        ),
        out_specs=(
            P(None, None, "lat", "lon"),
            P(None, None, "lat", "lon"),
            P(None, "lat", "lon", None),
        ),
        check_vma=False,
    )
```

```python
import jax
import jax.numpy as jnp
from jax import lax
from jax.experimental import pallas as pl
from jax.experimental.pallas import tpu as pltpu
from jax.sharding import PartitionSpec as P

BLOCK = 128
STEPS = 4
HALO = STEPS
PER_LANES = BLOCK // HALO
GROUP = 16
f32 = jnp.float32
bf16 = jnp.bfloat16
VMEM_LIMIT = 20 * 1024 * 1024


def call(body, outs, scratch=(), flops=0, name=None, inputs=0, far=(), far_outs=(), aliases=None):
    outs = [s if isinstance(s, jax.ShapeDtypeStruct) else jax.ShapeDtypeStruct(s, f32) for s in outs]
    near = pl.BlockSpec(memory_space=pltpu.VMEM)
    aliases = aliases or {}
    kernel = pl.pallas_call(
        body,
        out_shape=outs,
        in_specs=[
            pl.BlockSpec(memory_space=pl.ANY)
            if n in aliases
            else pl.BlockSpec(memory_space=pltpu.HBM)
            if n in far
            else near
            for n in range(inputs)
        ],
        out_specs=[
            pl.BlockSpec(memory_space=pl.ANY) if n in aliases.values() or n in far_outs else near
            for n in range(len(outs))
        ],
        input_output_aliases=aliases,
        scratch_shapes=list(scratch),
        compiler_params=pltpu.CompilerParams(vmem_limit_bytes=VMEM_LIMIT),
        cost_estimate=pl.CostEstimate(flops=flops, bytes_accessed=1 << 20, transcendentals=0),
        name=name,
    )

    def run(*args):
        return kernel(
            *(pltpu.with_memory_space_constraint(x, pltpu.HBM) if n in far else x for n, x in enumerate(args))
        )

    return run


def lanes(shape):
    return lax.broadcasted_iota(jnp.int32, shape, len(shape) - 1)


def rows(shape):
    return lax.broadcasted_iota(jnp.int32, shape, len(shape) - 2)


def turn(x, shift, axis):
    shift %= x.shape[axis]
    return pltpu.roll(x, shift, axis) if shift else x


def group_order(count):
    middle = count // 2
    return [middle] + [k for k in range(count) if k != middle]


def exchange(x):
    order = group_order(x.shape[0])
    return lax.all_to_all(x, "lon", split_axis=0, concat_axis=0, tiled=True, axis_index_groups=[order])


def swap(near, far, axis, wrap):
    count = lax.axis_size(axis)
    pairs = [[], []]
    for i in range(count if wrap else count - 1):
        j = (i + 1) % count
        pairs[i % 2] += [(i, j), (j, i)]
    far = lax.ppermute(far, axis, pairs[1])
    return lax.ppermute(near, axis, pairs[0]), far


def sort_swap(axis, after, before):
    odd = lax.rem(lax.axis_index(axis), 2) == 1
    return jnp.where(odd, before, after), jnp.where(odd, after, before)


def tile_fields(tracers, cotangent, land_mask, diffusion, velocity):
    levels = land_mask.shape[0]
    mask = [land_mask[level].astype(f32) for level in range(levels)]
    out = [tracers[f, level] for f in range(2) for level in range(levels)]
    out += [cotangent[f, level] for f in range(2) for level in range(levels)]
    out += [diffusion[0, level] * mask[level] for level in range(levels)]
    out += [velocity[0, level] * mask[level] for level in range(levels)]
    out += [diffusion[1, level] * mask[level] for level in range(levels)]
    out += [velocity[1, level] * mask[level] for level in range(levels)]
    out += [diffusion[2, level] * mask[level] * mask[level + 1] for level in range(levels - 1)]
    return out


def fetch(pairs, arrived):
    copies = [pltpu.make_async_copy(src, dst, arrived.at[n]) for n, (src, dst) in enumerate(pairs)]
    for copy in copies:
        copy.start()
    return copies


def pack_columns(*refs):
    inputs, (fields, near, far), scratch = refs[:7], refs[7:10], refs[12:]
    copies = fetch(zip(inputs, [*scratch[:5], *refs[10:12]]), scratch[5])
    for copy in copies[:5]:
        copy.wait()
    shape = near.shape[1:]
    lane = lanes(shape)
    west = [jnp.zeros(shape, f32) for _ in range(near.shape[0])]
    east = [jnp.zeros(shape, f32) for _ in range(near.shape[0])]
    for i, field in enumerate(tile_fields(*scratch[:5])):
        fields[i] = field
        part, at = divmod(i, PER_LANES)
        at *= HALO
        here = (lane >= at) & (lane < at + HALO)
        west[part] = jnp.where(here, turn(field[:, :BLOCK], at, 1), west[part])
        east[part] = jnp.where(here, turn(field[:, -BLOCK:], at + HALO, 1), east[part])
    for part in range(near.shape[0]):
        near[part], far[part] = sort_swap("lon", east[part], west[part])
    for copy in copies[5:]:
        copy.wait()


def unpack_columns(from_west, from_east, i):
    part, at = divmod(i, PER_LANES)
    at *= HALO
    lane = lanes(from_west[part].shape)
    east = turn(from_east[part], -at, 1)
    west = turn(from_west[part], -at - HALO, 1)
    return jnp.where(lane < HALO, east, jnp.where(lane >= BLOCK - HALO, west, 0.0))


def row_sources(fields, from_west, from_east):
    out = [(fields, (i, slice(None), slice(h * BLOCK, (h + 1) * BLOCK)))
           for i in range(fields.shape[0]) for h in range(fields.shape[2] // BLOCK)]
    for columns in (from_west, from_east):
        out += [(columns, (part,)) for part in range(columns.shape[0])]
    return out


def pack_rows(fields, near_columns, far_columns, sums, near, far, from_west, from_east, same_sums):
    for part in range(from_west.shape[0]):
        from_east[part], from_west[part] = sort_swap("lon", near_columns[part], far_columns[part])
    sources = [ref[at] for ref, at in row_sources(fields, from_west, from_east)]
    half = near.shape[0]
    row = rows((8, BLOCK))
    for i in range(half):
        first = sources[i]
        second = sources[i + half] if i + half < len(sources) else jnp.zeros_like(first)
        to_north = jnp.where(row < HALO, turn(first[-8:], HALO, 0), second[-8:])
        to_south = jnp.where(row < HALO, first[:8], turn(second[:8], HALO, 0))
        near[i], far[i] = sort_swap("lat", to_north, to_south)


def edge_rows(near, far, i):
    half = near.shape[0]
    from_north, from_south = sort_swap("lat", near[i % half], far[i % half])
    if i < half:
        from_south = turn(from_south, HALO, 0)
    else:
        from_north = turn(from_north, HALO, 0)
    return jnp.where(rows(from_north.shape) < HALO, from_north, from_south)


def widen(fields, from_west, from_east, near, far, start, wide):
    count, tile_lat, tile_lon = fields.shape
    halves = tile_lon // BLOCK
    parts = from_west.shape[0]
    corners = [edge_rows(near, far, count * halves + n) for n in range(2 * parts)]
    for i in range(count):
        out = start.at[i] if i < start.shape[0] else wide.at[i - start.shape[0]]
        out[:tile_lat, :tile_lon] = fields[i]
        out[:tile_lat, tile_lon:] = unpack_columns(from_west, from_east, i)
        for h in range(halves):
            out[tile_lat:, h * BLOCK : (h + 1) * BLOCK] = edge_rows(near, far, i * halves + h)
        out[tile_lat:, tile_lon:] = unpack_columns(corners[:parts], corners[parts:], i)


def eastward(x):
    return turn(x, -1, 1)


def westward(x):
    return turn(x, 1, 1)


def northward(x):
    return turn(x, -1, 0)


def southward(x):
    return turn(x, 1, 0)


def adjoint_step(coeffs, read, write, first, last):
    levels = coeffs.shape[1]
    above = coeffs[4, first - 1] * (read(first) - read(first - 1)) if first else None
    for level in range(first, last):
        lam = read(level)
        step_x = eastward(lam) - lam
        step_y = northward(lam) - lam
        out = lam + coeffs[0, level] * step_x + westward(coeffs[1, level] * step_x)
        out = out + coeffs[2, level] * step_y + southward(coeffs[3, level] * step_y)
        if above is not None:
            out = out - above
        if level < levels - 1:
            above = coeffs[4, level] * (read(level + 1) - lam)
            out = out + above
        write(level, out)


def surface_levels(step, levels):
    return min(levels, STEPS - 1 - step)


def run_adjoint(
    fields, from_west, from_east, far, near, blocks, coeffs, start, states, wide, own, sent
):
    levels = coeffs.shape[1]
    tile_lat, tile_lon = fields.shape[1:]
    halves = tile_lon // BLOCK
    widen(fields, from_west, from_east, near, far, start, wide)
    base = 0
    mask0 = None
    for level in range(levels):
        east_d, east_u = wide[base + level], wide[base + levels + level]
        north_d, north_u = wide[base + 2 * levels + level], wide[base + 3 * levels + level]
        mask = (east_d > 0.0).astype(f32)
        mask0 = mask if mask0 is None else mask0
        mask_e, mask_n = eastward(mask), northward(mask)
        east_k, east_v = east_d * mask_e, east_u * mask_e
        north_k, north_v = north_d * mask_n, north_u * mask_n
        coeffs[0, level] = jnp.maximum(east_v, 0.0) + east_k
        coeffs[1, level] = jnp.minimum(east_v, 0.0) - east_k
        coeffs[2, level] = jnp.maximum(north_v, 0.0) + north_k
        coeffs[3, level] = jnp.minimum(north_v, 0.0) - north_k
        coeffs[4, level] = wide[base + 4 * levels + level] if level < levels - 1 else jnp.zeros_like(mask)
        coeffs[5, level] = mask
    copies = []
    for f in range(2):
        surface = start[(2 + f) * levels, :tile_lat, :tile_lon]
        for step in range(STEPS - 1):

            def read(level):
                return states[f, step - 1, level] if step else start[(2 + f) * levels + level]

            def write(level, lam):
                states[f, step, level] = lam

            adjoint_step(coeffs, read, write, 0, surface_levels(step, levels))
            surface = surface + states[f, step, 0, :tile_lat, :tile_lon]
        surface = surface * mask0[:tile_lat, :tile_lon]
        for h in range(halves):
            at = (f * halves + h) * tile_lat
            own[at : at + tile_lat] = surface[:, h * BLOCK : (h + 1) * BLOCK]
        field = pl.ds(f * halves * tile_lat, halves * tile_lat)
        copies += fetch([(own.at[field], blocks.at[k, field]) for k in range(blocks.shape[0])], sent.at[f])
    for copy in copies:
        copy.wait()


def finish_adjoint(coeffs, start, states, adjoint_out, rest):
    levels = coeffs.shape[1]
    tile_lat, tile_lon = adjoint_out.shape[2:]
    for f in range(2):
        for step in range(STEPS):
            done = surface_levels(step, levels)

            def read(level):
                if not step:
                    return start[(2 + f) * levels + level]
                return (states if level < surface_levels(step - 1, levels) else rest)[f, step - 1, level]

            def write(level, lam):
                if step == STEPS - 1:
                    adjoint_out[f, level] = lam[:tile_lat, :tile_lon]
                else:
                    rest[f, step, level] = lam

            adjoint_step(coeffs, read, write, done, levels)


def sum_forcing(received, forcing, near, far):
    tile_lat = forcing.shape[1]
    halves = forcing.shape[2] // BLOCK - 1
    total = received[0]
    for j in range(1, received.shape[0]):
        total = total + received[j]
    lane = lanes((tile_lat, BLOCK))
    upper = total[2 * halves * tile_lat :]
    lower = jnp.where(lane[: tile_lat // 2] < BLOCK // 2, turn(upper, -2 * HALO, 1), turn(upper, 2 * HALO, 1))
    packed = jnp.concatenate([upper, lower], axis=0)
    for f in range(2):
        for h in range(halves):
            at = (f * halves + h) * tile_lat
            forcing[f, :, h * BLOCK : (h + 1) * BLOCK] = total[at : at + tile_lat]
        used = (lane < HALO) | (lane >= BLOCK - HALO)
        if f == 0:
            edge = packed
        else:
            edge = jnp.where(lane < HALO, turn(packed, -HALO, 1), turn(packed, HALO, 1))
        forcing[f, :, halves * BLOCK :] = jnp.where(used, edge, 0.0)
    row = rows((8, forcing.shape[2]))
    to_north = jnp.where(row < HALO, turn(forcing[0, tile_lat - 8 :], HALO, 0), forcing[1, tile_lat - 8 :])
    to_south = jnp.where(row < HALO, forcing[0, :8], turn(forcing[1, :8], HALO, 0))
    near[0], far[0] = sort_swap("lat", to_north, to_south)


def run_forward(coeffs, start, forcing, far, near, final, state):
    levels = coeffs.shape[1]
    tile_lat, tile_lon = final.shape[2:]
    for f in range(2):
        force = jnp.concatenate([forcing[f], edge_rows(near, far, f)], axis=0)
        force = force * coeffs[5, 0]
        for step in range(STEPS):
            above = None
            for level in range(levels):
                read = (lambda n: start[f * levels + n]) if step == 0 else (lambda n: state[(step - 1) % 2, n])
                theta = read(level)
                east_flux = coeffs[0, level] * theta + coeffs[1, level] * eastward(theta)
                north_flux = coeffs[2, level] * theta + coeffs[3, level] * northward(theta)
                out = theta - (east_flux - westward(east_flux)) - (north_flux - southward(north_flux))
                if level < levels - 1:
                    vertical = coeffs[4, level] * (theta - read(level + 1))
                    out = out - vertical
                if above is not None:
                    out = out + above
                above = vertical if level < levels - 1 else None
                if level == 0:
                    out = out + force
                if step == STEPS - 1:
                    final[f, level] = out[:tile_lat, :tile_lon]
                else:
                    state[step % 2, level] = out


def split(x):
    high = x.astype(bf16)
    return high, (x - high.astype(f32)).astype(bf16)


def weight_copies(weights, held, arrived):
    for g in range(held.shape[0]):
        yield pltpu.make_async_copy(weights.at[pl.ds(g * GROUP, GROUP)], held.at[g], arrived.at[g])


def fetch_weights(weights, held, arrived):
    for copy in weight_copies(weights, held, arrived):
        copy.start()


def held_part(weights, held, arrived):
    def part(r, g, u):
        if u == 0:

            @pl.when(r == 0)
            def _():
                pltpu.make_async_copy(weights.at[pl.ds(g * GROUP, GROUP)], held.at[g], arrived.at[g]).wait()

        return split(held[g, u])

    return part


def one_hot(where):
    return jnp.where(where, 1.0, 0.0).astype(bf16)


def places(slots, blocks):
    return 8 * (-(-2 * slots // (8 * blocks)) + 1)


def as_row(ids):
    return jnp.concatenate([ids[k : k + 1, :] for k in range(ids.shape[0])], axis=1)


def rank_slots(block_row, blocks):
    slots = block_row.shape[1]
    mine = rows((blocks, slots)) == block_row
    cuts = range(0, slots, BLOCK)
    stacked = jnp.concatenate([one_hot(mine[:, at : at + BLOCK]) for at in cuts], axis=0)
    shape = (BLOCK, 2 * BLOCK)
    counts = jnp.dot(stacked, one_hot(rows(shape) < lanes(shape)), preferred_element_type=f32)
    before, out = jnp.zeros((blocks, BLOCK), f32), []
    for n, at in enumerate(cuts):
        run = counts[n * blocks : (n + 1) * blocks]
        here = jnp.where(mine[:, at : at + BLOCK], run[:, :BLOCK] + before, 0.0)
        out.append(jnp.sum(here, axis=0, keepdims=True))
        before = before + run[:, BLOCK:]
    return jnp.concatenate(out, axis=1)


def find_slots(r, code, block_row, rank, capacity, blocks, found):
    slots = block_row.shape[1]
    mine = rows((blocks, slots)) == block_row
    ranked = one_hot(rows((capacity, slots)) == rank.astype(jnp.int32) - r * capacity)
    rest, codes = code + 1.0, None
    for base in (4096.0, 64.0, 1.0):
        digit = jnp.floor(rest * (1.0 / base))
        rest = rest - digit * base
        part = lax.dot_general(
            ranked,
            jnp.where(mine, digit, 0.0).astype(bf16),
            (((1,), (1,)), ((), ())),
            preferred_element_type=f32,
        )
        codes = part * base if codes is None else codes + part * base
    found[:, :blocks] = codes - 1.0


def couple(blocks, part, table, size, capacity, rounds, prepare, found, gather_first, transposed, result, scratch):
    column, vectors, products = scratch
    total_rows = column.shape[0]
    result[...] = jnp.zeros_like(result)

    def one_round(r, carry):
        prepare(r)
        codes = found[...]
        for w in range(blocks):
            column[w * capacity : (w + 1) * capacity] = jnp.broadcast_to(codes[:, w : w + 1], (capacity, BLOCK))
        eye = rows((BLOCK, BLOCK)) == lanes((BLOCK, BLOCK))
        place_hot = []
        for at in range(0, total_rows, BLOCK):
            code = column[at : at + BLOCK]
            first = jnp.floor((code + 0.5) * (1.0 / size))
            second = code - first * size
            gather, put = (first, second) if gather_first else (second, first)
            width = table.shape[0]
            gather = jnp.concatenate([gather] * (width // BLOCK), axis=1)
            hot = one_hot(gather == lanes((BLOCK, width)).astype(f32))
            vectors[at : at + BLOCK] = jnp.dot(hot, table, preferred_element_type=f32)
            put = jnp.sum(jnp.where(eye, put, 0.0), axis=0, keepdims=True)
            place_hot.append(one_hot(rows((result.shape[0], BLOCK)).astype(f32) == put))

        def group(g, carry):
            for u in range(GROUP):
                at = pl.multiple_of((g * GROUP + u) * capacity, 8)
                own = vectors[pl.ds(at, capacity)]
                left = jnp.concatenate([own[:, n * BLOCK : (n + 1) * BLOCK] for n in range(4)], axis=0)
                high, low = part(r, g, u)
                right = jnp.concatenate([high, low], axis=1 if transposed else 0)
                contract = (((1,), (0 if transposed else 1,)), ((), ()))
                product = lax.dot_general(left.astype(bf16), right, contract, preferred_element_type=f32)
                for f in range(2):
                    high_part = product[f * capacity : (f + 1) * capacity]
                    low_part = product[(f + 2) * capacity : (f + 3) * capacity, :BLOCK]
                    products[pl.ds(at, capacity), f * BLOCK : (f + 1) * BLOCK] = (
                        high_part[:, BLOCK:] + low_part
                    ) + high_part[:, :BLOCK]
            return carry

        lax.fori_loop(0, blocks // GROUP, group, 0)
        summed = jnp.dot(
            jnp.concatenate(place_hot, axis=1),
            jnp.concatenate(split(products[...]), axis=1),
            preferred_element_type=f32,
        )
        result[...] += summed[:, : 2 * BLOCK] + summed[:, 2 * BLOCK :]
        return carry

    lax.fori_loop(0, rounds, one_round, 0)


def slot_keys(ids, tile_lat, atm):
    lon_count, cap = ids.shape[3:]
    ocean, atm_ids, block_ids = (ids[n, 0, 0] for n in range(3))
    order = (ocean & 1) * tile_lat + (ocean >> 1) + rows((lon_count, cap)) * (2 * tile_lat)
    order = jnp.where(ocean >= 0, order, lon_count * 2 * tile_lat)
    return as_row((order * atm + atm_ids).astype(f32)), as_row(block_ids)


def weigh(atm_near, margins, weights, after, sums, found, keys, result, *scratch):
    scratch, (held, arrived) = scratch[:3], scratch[3:]
    fetch_weights(weights, held, arrived)
    lon_count = margins.shape[3]
    atm = atm_near.shape[2]
    blocks = weights.shape[0]
    tile_lat = 2 * sums.shape[1] // 9
    code, block_row = slot_keys(margins, tile_lat, atm)
    rank = rank_slots(block_row, blocks)
    keys[0:1] = code
    keys[1:2] = block_row.astype(f32)
    keys[2:3] = rank
    capacity = places(code.shape[1], blocks)
    rounds = jnp.max(rank).astype(jnp.int32) // capacity + 1
    parts = [split(atm_near[f, 0]) for f in range(2)]
    table = jnp.concatenate([parts[f][n] for n in range(2) for f in range(2)], axis=1)

    def prepare(r):
        find_slots(rounds - 1 - r, code, block_row, rank, capacity, blocks, found)

    part = held_part(weights, held, arrived)
    couple(blocks, part, table, atm, capacity, rounds, prepare, found, False, False, result, scratch)
    lane = lanes((tile_lat, BLOCK))

    def block_sums(k, f, h):
        at = (2 * k + h) * tile_lat
        return result[at : at + tile_lat, f * BLOCK : (f + 1) * BLOCK]

    for n, k in enumerate(group_order(lon_count)):
        edge = jnp.zeros((tile_lat, BLOCK), f32)
        for f in range(2):
            for h in range(2):
                sums[n, (2 * f + h) * tile_lat : (2 * f + h + 1) * tile_lat] = block_sums(k, f, h)
            at = f * HALO
            after = turn(block_sums((k + 1) % lon_count, f, 0), at, 1)
            before = turn(block_sums((k - 1) % lon_count, f, 1), -at, 1)
            edge = jnp.where((lane >= at) & (lane < at + HALO), after, edge)
            end = BLOCK - at
            edge = jnp.where((lane >= end - HALO) & (lane < end), before, edge)
        upper, lower = edge[: tile_lat // 2], edge[tile_lat // 2 :]
        near = lane[: tile_lat // 2]
        lower = jnp.where(near < BLOCK // 2, turn(lower, 2 * HALO, 1), turn(lower, -2 * HALO, 1))
        sums[n, 4 * tile_lat :] = jnp.where((near < 2 * HALO) | (near >= BLOCK - 2 * HALO), upper, lower)


def unweigh(gathered, found, keys, weights, gradient, result, codes, *scratch):
    scratch, (held, arrived) = scratch[:3], scratch[3:]
    fetch_weights(weights, held, arrived)
    atm = gradient.shape[2]
    blocks = weights.shape[0]
    lon_count, ocean_blocks = gathered.shape[0], gathered.shape[1] // 2
    order = group_order(lon_count)
    capacity = places(keys.shape[1], blocks)
    rounds = jnp.max(keys[2:3]).astype(jnp.int32) // capacity + 1
    parts = [
        split(
            jnp.concatenate(
                [gathered[order.index(k), f * ocean_blocks : (f + 1) * ocean_blocks] for k in range(lon_count)],
                axis=0,
            )
        )
        for f in range(2)
    ]
    table = jnp.concatenate([parts[f][n] for n in range(2) for f in range(2)], axis=1)

    def prepare(r):
        @pl.when(r == 0)
        def _():
            codes[...] = found[...]

        @pl.when(r > 0)
        def _():
            find_slots(r, keys[0:1], keys[1:2].astype(jnp.int32), keys[2:3], capacity, blocks, codes)

    couple(
        blocks,
        held_part(weights, held, arrived),
        table,
        atm,
        capacity,
        rounds,
        prepare,
        codes,
        True,
        True,
        result,
        scratch,
    )
    for f in range(2):
        gradient[f, 0] = result[:, f * BLOCK : (f + 1) * BLOCK]


def on_device(tracers, cotangent, land_mask, diffusion, velocity, weights, atm_state, margins):
    levels, tile_lat, tile_lon = land_mask.shape
    lon_count = lax.axis_size("lon")
    slots = lon_count * margins.shape[4]
    halves = tile_lon // BLOCK
    count = 9 * levels - 1
    parts = -(-count // PER_LANES)
    inputs = (tracers, cotangent, land_mask, diffusion, velocity)

    def in_vmem(s):
        return pltpu.VMEM(s.shape, s.dtype)

    message = (parts, tile_lat, BLOCK)
    fields, near, far, atm_near, margins_near = call(
        pack_columns,
        [
            (count, tile_lat, tile_lon),
            message,
            message,
            atm_state.shape,
            jax.ShapeDtypeStruct(margins.shape, margins.dtype),
        ],
        [*map(in_vmem, inputs), pltpu.SemaphoreType.DMA((7,))],
        name="pack_columns",
        inputs=7,
        far=range(7),
    )(*inputs, atm_state, margins)
    near_columns, far_columns = swap(near, far, "lon", True)

    blocks_of, atm = weights.shape[0], atm_state.shape[2]
    groups = blocks_of // GROUP
    sum_rows = 2 * halves * tile_lat + tile_lat // 2
    ocean_blocks = lon_count * halves * tile_lat
    held_rows = -(-places(slots, blocks_of) * blocks_of // BLOCK) * BLOCK

    def coupling_scratch(result_rows):
        return [
            pltpu.VMEM((result_rows, 2 * BLOCK), f32),
            pltpu.VMEM((held_rows, BLOCK), f32),
            pltpu.VMEM((held_rows, 4 * BLOCK), f32),
            pltpu.VMEM((held_rows, 2 * BLOCK), f32),
            pltpu.VMEM((groups, GROUP, BLOCK, BLOCK), f32),
            pltpu.SemaphoreType.DMA((groups,)),
        ]

    coupling_flops = 4 * slots * blocks_of * 2 * BLOCK * BLOCK * 2
    sums, found, keys = call(
        weigh,
        [(lon_count, sum_rows, BLOCK), (places(slots, blocks_of), BLOCK), (8, slots)],
        coupling_scratch(ocean_blocks),
        coupling_flops,
        name="weigh",
        inputs=4,
        far=(2,),
    )(atm_near, margins_near, weights, near)

    sources = count * halves + 2 * parts
    message = (-(-sources // 2), 8, BLOCK)
    columns = (parts, tile_lat, BLOCK)
    near, far, from_west, from_east, sums = call(
        pack_rows,
        [message, message, columns, columns, sums.shape],
        name="pack_rows",
        inputs=4,
        aliases={3: 4},
    )(fields, near_columns, far_columns, sums)
    received = exchange(sums)
    near_rows, far_rows = swap(near, far, "lat", False)

    wide = (tile_lat + 8, tile_lon + BLOCK)
    own = (2 * halves * tile_lat, BLOCK)
    adjoint_states = (2, STEPS - 1, levels, *wide)
    blocks, coeffs, start, states = call(
        run_adjoint,
        [(lon_count, *own), (6, levels, *wide), (4 * levels, *wide), adjoint_states],
        [
            pltpu.VMEM((count - 4 * levels, *wide), f32),
            pltpu.VMEM(own, f32),
            pltpu.SemaphoreType.DMA((2, lon_count)),
        ],
        name="run_adjoint",
        inputs=5,
        far_outs=(0,),
    )(fields, from_west, from_east, far_rows, near_rows)
    gathered = exchange(blocks)

    message = (1, 8, tile_lon + BLOCK)
    forcing, near, far = call(
        sum_forcing, [(2, tile_lat, tile_lon + BLOCK), message, message], name="sum_forcing", inputs=1
    )(received)
    near_rows, far_rows = swap(near, far, "lat", False)
    (adjoint,) = call(
        finish_adjoint,
        [cotangent.shape],
        [pltpu.VMEM(adjoint_states, f32)],
        name="finish_adjoint",
        inputs=3,
    )(coeffs, start, states)
    (final,) = call(
        run_forward,
        [tracers.shape],
        [pltpu.VMEM((2, levels, *wide), f32)],
        name="run_forward",
        inputs=5,
    )(coeffs, start, forcing, far_rows, near_rows)

    (gradient,) = call(
        unweigh,
        [atm_state.shape],
        [coupling_scratch(atm)[0], in_vmem(found), *coupling_scratch(atm)[1:]],
        coupling_flops,
        name="unweigh",
        inputs=4,
        far=(3,),
    )(gathered, found, keys, weights)
    return (final, adjoint, gradient)


def solution(mesh):
    return jax.shard_map(
        on_device,
        mesh=mesh,
        in_specs=(
            P(None, None, "lat", "lon"),
            P(None, None, "lat", "lon"),
            P(None, "lat", "lon"),
            P(None, None, "lat", "lon"),
            P(None, None, "lat", "lon"),
            P(),
            P(None, "lat", "lon", None),
            P(None, "lat", "lon", None, None),
        ),
        out_specs=(
            P(None, None, "lat", "lon"),
            P(None, None, "lat", "lon"),
            P(None, "lat", "lon", None),
        ),
        check_vma=False,
    )
```

```python
import jax
import jax.numpy as jnp
from jax import lax
from jax.experimental import pallas as pl
from jax.experimental.pallas import tpu as pltpu
from jax.sharding import PartitionSpec as P

BLOCK = 128
STEPS = 4
HALO = STEPS
PER_LANES = BLOCK // HALO
GROUP = 16
f32 = jnp.float32
bf16 = jnp.bfloat16
VMEM_LIMIT = 20 * 1024 * 1024


def call(body, outs, scratch=(), flops=0, name=None, inputs=0, far=(), far_outs=(), aliases=None):
    outs = [s if isinstance(s, jax.ShapeDtypeStruct) else jax.ShapeDtypeStruct(s, f32) for s in outs]
    near = pl.BlockSpec(memory_space=pltpu.VMEM)
    aliases = aliases or {}
    kernel = pl.pallas_call(
        body,
        out_shape=outs,
        in_specs=[
            pl.BlockSpec(memory_space=pl.ANY)
            if n in aliases
            else pl.BlockSpec(memory_space=pltpu.HBM)
            if n in far
            else near
            for n in range(inputs)
        ],
        out_specs=[
            pl.BlockSpec(memory_space=pl.ANY) if n in aliases.values() or n in far_outs else near
            for n in range(len(outs))
        ],
        input_output_aliases=aliases,
        scratch_shapes=list(scratch),
        compiler_params=pltpu.CompilerParams(vmem_limit_bytes=VMEM_LIMIT),
        cost_estimate=pl.CostEstimate(flops=flops, bytes_accessed=1 << 20, transcendentals=0),
        name=name,
    )

    def run(*args):
        return kernel(
            *(pltpu.with_memory_space_constraint(x, pltpu.HBM) if n in far else x for n, x in enumerate(args))
        )

    return run


def lanes(shape):
    return lax.broadcasted_iota(jnp.int32, shape, len(shape) - 1)


def rows(shape):
    return lax.broadcasted_iota(jnp.int32, shape, len(shape) - 2)


def turn(x, shift, axis):
    shift %= x.shape[axis]
    return pltpu.roll(x, shift, axis) if shift else x


def group_order(count):
    half = count // 2
    return [k for n in range(half) for k in (half + n, n)]


def exchange(x):
    order = group_order(x.shape[0])
    return lax.all_to_all(x, "lon", split_axis=0, concat_axis=0, tiled=True, axis_index_groups=[order])


def swap(near, far, axis, wrap):
    count = lax.axis_size(axis)
    pairs = [[], []]
    for i in range(count if wrap else count - 1):
        j = (i + 1) % count
        pairs[i % 2] += [(i, j), (j, i)]
    far = lax.ppermute(far, axis, pairs[1])
    return lax.ppermute(near, axis, pairs[0]), far


def sort_swap(axis, after, before):
    odd = lax.rem(lax.axis_index(axis), 2) == 1
    return jnp.where(odd, before, after), jnp.where(odd, after, before)


def tile_fields(tracers, cotangent, land_mask, diffusion, velocity):
    levels = land_mask.shape[0]
    mask = [land_mask[level].astype(f32) for level in range(levels)]
    out = [tracers[f, level] for f in range(2) for level in range(levels)]
    out += [cotangent[f, level] for f in range(2) for level in range(levels)]
    out += [diffusion[0, level] * mask[level] for level in range(levels)]
    out += [velocity[0, level] * mask[level] for level in range(levels)]
    out += [diffusion[1, level] * mask[level] for level in range(levels)]
    out += [velocity[1, level] * mask[level] for level in range(levels)]
    out += [diffusion[2, level] * mask[level] * mask[level + 1] for level in range(levels - 1)]
    return out


def fetch(pairs, arrived):
    copies = [pltpu.make_async_copy(src, dst, arrived.at[n]) for n, (src, dst) in enumerate(pairs)]
    for copy in copies:
        copy.start()
    return copies


def pack_columns(*refs):
    inputs, (fields, near, far), scratch = refs[:7], refs[7:10], refs[12:]
    copies = fetch(zip(inputs, [*scratch[:5], *refs[10:12]]), scratch[5])
    for copy in copies[:5]:
        copy.wait()
    shape = near.shape[1:]
    lane = lanes(shape)
    west = [jnp.zeros(shape, f32) for _ in range(near.shape[0])]
    east = [jnp.zeros(shape, f32) for _ in range(near.shape[0])]
    for i, field in enumerate(tile_fields(*scratch[:5])):
        fields[i] = field
        part, at = divmod(i, PER_LANES)
        at *= HALO
        here = (lane >= at) & (lane < at + HALO)
        west[part] = jnp.where(here, turn(field[:, :BLOCK], at, 1), west[part])
        east[part] = jnp.where(here, turn(field[:, -BLOCK:], at + HALO, 1), east[part])
    for part in range(near.shape[0]):
        near[part], far[part] = sort_swap("lon", east[part], west[part])
    for copy in copies[5:]:
        copy.wait()


def unpack_columns(from_west, from_east, i):
    part, at = divmod(i, PER_LANES)
    at *= HALO
    lane = lanes(from_west[part].shape)
    east = turn(from_east[part], -at, 1)
    west = turn(from_west[part], -at - HALO, 1)
    return jnp.where(lane < HALO, east, jnp.where(lane >= BLOCK - HALO, west, 0.0))


def row_sources(fields, from_west, from_east):
    out = [(fields, (i, slice(None), slice(h * BLOCK, (h + 1) * BLOCK)))
           for i in range(fields.shape[0]) for h in range(fields.shape[2] // BLOCK)]
    for columns in (from_west, from_east):
        out += [(columns, (part,)) for part in range(columns.shape[0])]
    return out


def pack_rows(fields, near_columns, far_columns, sums, near, far, from_west, from_east, same_sums):
    for part in range(from_west.shape[0]):
        from_east[part], from_west[part] = sort_swap("lon", near_columns[part], far_columns[part])
    sources = [ref[at] for ref, at in row_sources(fields, from_west, from_east)]
    half = near.shape[0]
    row = rows((8, BLOCK))
    for i in range(half):
        first = sources[i]
        second = sources[i + half] if i + half < len(sources) else jnp.zeros_like(first)
        to_north = jnp.where(row < HALO, turn(first[-8:], HALO, 0), second[-8:])
        to_south = jnp.where(row < HALO, first[:8], turn(second[:8], HALO, 0))
        near[i], far[i] = sort_swap("lat", to_north, to_south)


def edge_rows(near, far, i):
    half = near.shape[0]
    from_north, from_south = sort_swap("lat", near[i % half], far[i % half])
    if i < half:
        from_south = turn(from_south, HALO, 0)
    else:
        from_north = turn(from_north, HALO, 0)
    return jnp.where(rows(from_north.shape) < HALO, from_north, from_south)


def widen(fields, from_west, from_east, near, far, start, wide):
    count, tile_lat, tile_lon = fields.shape
    halves = tile_lon // BLOCK
    parts = from_west.shape[0]
    corners = [edge_rows(near, far, count * halves + n) for n in range(2 * parts)]
    for i in range(count):
        out = start.at[i] if i < start.shape[0] else wide.at[i - start.shape[0]]
        out[:tile_lat, :tile_lon] = fields[i]
        out[:tile_lat, tile_lon:] = unpack_columns(from_west, from_east, i)
        for h in range(halves):
            out[tile_lat:, h * BLOCK : (h + 1) * BLOCK] = edge_rows(near, far, i * halves + h)
        out[tile_lat:, tile_lon:] = unpack_columns(corners[:parts], corners[parts:], i)


def eastward(x):
    return turn(x, -1, 1)


def westward(x):
    return turn(x, 1, 1)


def northward(x):
    return turn(x, -1, 0)


def southward(x):
    return turn(x, 1, 0)


def adjoint_step(coeffs, read, write, first, last):
    levels = coeffs.shape[1]
    above = coeffs[4, first - 1] * (read(first) - read(first - 1)) if first else None
    for level in range(first, last):
        lam = read(level)
        step_x = eastward(lam) - lam
        step_y = northward(lam) - lam
        out = lam + coeffs[0, level] * step_x + westward(coeffs[1, level] * step_x)
        out = out + coeffs[2, level] * step_y + southward(coeffs[3, level] * step_y)
        if above is not None:
            out = out - above
        if level < levels - 1:
            above = coeffs[4, level] * (read(level + 1) - lam)
            out = out + above
        write(level, out)


def surface_levels(step, levels):
    return min(levels, STEPS - 1 - step)


def run_adjoint(
    fields, from_west, from_east, far, near, blocks, coeffs, start, states, wide, own, sent
):
    levels = coeffs.shape[1]
    tile_lat, tile_lon = fields.shape[1:]
    halves = tile_lon // BLOCK
    widen(fields, from_west, from_east, near, far, start, wide)
    base = 0
    mask0 = None
    for level in range(levels):
        east_d, east_u = wide[base + level], wide[base + levels + level]
        north_d, north_u = wide[base + 2 * levels + level], wide[base + 3 * levels + level]
        mask = (east_d > 0.0).astype(f32)
        mask0 = mask if mask0 is None else mask0
        mask_e, mask_n = eastward(mask), northward(mask)
        east_k, east_v = east_d * mask_e, east_u * mask_e
        north_k, north_v = north_d * mask_n, north_u * mask_n
        coeffs[0, level] = jnp.maximum(east_v, 0.0) + east_k
        coeffs[1, level] = jnp.minimum(east_v, 0.0) - east_k
        coeffs[2, level] = jnp.maximum(north_v, 0.0) + north_k
        coeffs[3, level] = jnp.minimum(north_v, 0.0) - north_k
        coeffs[4, level] = wide[base + 4 * levels + level] if level < levels - 1 else jnp.zeros_like(mask)
        coeffs[5, level] = mask
    copies = []
    for f in range(2):
        surface = start[(2 + f) * levels, :tile_lat, :tile_lon]
        for step in range(STEPS - 1):

            def read(level):
                return states[f, step - 1, level] if step else start[(2 + f) * levels + level]

            def write(level, lam):
                states[f, step, level] = lam

            adjoint_step(coeffs, read, write, 0, surface_levels(step, levels))
            surface = surface + states[f, step, 0, :tile_lat, :tile_lon]
        surface = surface * mask0[:tile_lat, :tile_lon]
        for h in range(halves):
            at = (f * halves + h) * tile_lat
            own[at : at + tile_lat] = surface[:, h * BLOCK : (h + 1) * BLOCK]
        field = pl.ds(f * halves * tile_lat, halves * tile_lat)
        copies += fetch([(own.at[field], blocks.at[k, field]) for k in range(blocks.shape[0])], sent.at[f])
    for copy in copies:
        copy.wait()


def finish_adjoint(coeffs, start, states, adjoint_out, rest):
    levels = coeffs.shape[1]
    tile_lat, tile_lon = adjoint_out.shape[2:]
    for f in range(2):
        for step in range(STEPS):
            done = surface_levels(step, levels)

            def read(level):
                if not step:
                    return start[(2 + f) * levels + level]
                return (states if level < surface_levels(step - 1, levels) else rest)[f, step - 1, level]

            def write(level, lam):
                if step == STEPS - 1:
                    adjoint_out[f, level] = lam[:tile_lat, :tile_lon]
                else:
                    rest[f, step, level] = lam

            adjoint_step(coeffs, read, write, done, levels)


def sum_forcing(received, forcing, near, far):
    tile_lat = forcing.shape[1]
    halves = forcing.shape[2] // BLOCK - 1
    total = received[0]
    for j in range(1, received.shape[0]):
        total = total + received[j]
    lane = lanes((tile_lat, BLOCK))
    upper = total[2 * halves * tile_lat :]
    lower = jnp.where(lane[: tile_lat // 2] < BLOCK // 2, turn(upper, -2 * HALO, 1), turn(upper, 2 * HALO, 1))
    packed = jnp.concatenate([upper, lower], axis=0)
    for f in range(2):
        for h in range(halves):
            at = (f * halves + h) * tile_lat
            forcing[f, :, h * BLOCK : (h + 1) * BLOCK] = total[at : at + tile_lat]
        used = (lane < HALO) | (lane >= BLOCK - HALO)
        if f == 0:
            edge = packed
        else:
            edge = jnp.where(lane < HALO, turn(packed, -HALO, 1), turn(packed, HALO, 1))
        forcing[f, :, halves * BLOCK :] = jnp.where(used, edge, 0.0)
    row = rows((8, forcing.shape[2]))
    to_north = jnp.where(row < HALO, turn(forcing[0, tile_lat - 8 :], HALO, 0), forcing[1, tile_lat - 8 :])
    to_south = jnp.where(row < HALO, forcing[0, :8], turn(forcing[1, :8], HALO, 0))
    near[0], far[0] = sort_swap("lat", to_north, to_south)


def run_forward(coeffs, start, forcing, far, near, final, state):
    levels = coeffs.shape[1]
    tile_lat, tile_lon = final.shape[2:]
    for f in range(2):
        force = jnp.concatenate([forcing[f], edge_rows(near, far, f)], axis=0)
        force = force * coeffs[5, 0]
        for step in range(STEPS):
            above = None
            for level in range(levels):
                read = (lambda n: start[f * levels + n]) if step == 0 else (lambda n: state[(step - 1) % 2, n])
                theta = read(level)
                east_flux = coeffs[0, level] * theta + coeffs[1, level] * eastward(theta)
                north_flux = coeffs[2, level] * theta + coeffs[3, level] * northward(theta)
                out = theta - (east_flux - westward(east_flux)) - (north_flux - southward(north_flux))
                if level < levels - 1:
                    vertical = coeffs[4, level] * (theta - read(level + 1))
                    out = out - vertical
                if above is not None:
                    out = out + above
                above = vertical if level < levels - 1 else None
                if level == 0:
                    out = out + force
                if step == STEPS - 1:
                    final[f, level] = out[:tile_lat, :tile_lon]
                else:
                    state[step % 2, level] = out


def split(x):
    high = x.astype(bf16)
    return high, (x - high.astype(f32)).astype(bf16)


def weight_copies(weights, held, arrived):
    for g in range(held.shape[0]):
        yield pltpu.make_async_copy(weights.at[pl.ds(g * GROUP, GROUP)], held.at[g], arrived.at[g])


def fetch_weights(weights, held, arrived):
    for copy in weight_copies(weights, held, arrived):
        copy.start()


def held_part(weights, held, arrived):
    def part(r, g, u):
        if u == 0:

            @pl.when(r == 0)
            def _():
                pltpu.make_async_copy(weights.at[pl.ds(g * GROUP, GROUP)], held.at[g], arrived.at[g]).wait()

        return split(held[g, u])

    return part


def one_hot(where):
    return jnp.where(where, 1.0, 0.0).astype(bf16)


def places(slots, blocks):
    return 8 * (-(-2 * slots // (8 * blocks)) + 1)


def as_row(ids):
    return jnp.concatenate([ids[k : k + 1, :] for k in range(ids.shape[0])], axis=1)


def rank_slots(block_row, blocks):
    slots = block_row.shape[1]
    mine = rows((blocks, slots)) == block_row
    cuts = range(0, slots, BLOCK)
    stacked = jnp.concatenate([one_hot(mine[:, at : at + BLOCK]) for at in cuts], axis=0)
    shape = (BLOCK, 2 * BLOCK)
    counts = jnp.dot(stacked, one_hot(rows(shape) < lanes(shape)), preferred_element_type=f32)
    before, out = jnp.zeros((blocks, BLOCK), f32), []
    for n, at in enumerate(cuts):
        run = counts[n * blocks : (n + 1) * blocks]
        here = jnp.where(mine[:, at : at + BLOCK], run[:, :BLOCK] + before, 0.0)
        out.append(jnp.sum(here, axis=0, keepdims=True))
        before = before + run[:, BLOCK:]
    return jnp.concatenate(out, axis=1)


def find_slots(r, code, block_row, rank, capacity, blocks, found):
    slots = block_row.shape[1]
    mine = rows((blocks, slots)) == block_row
    ranked = one_hot(rows((capacity, slots)) == rank.astype(jnp.int32) - r * capacity)
    rest, codes = code + 1.0, None
    for base in (4096.0, 64.0, 1.0):
        digit = jnp.floor(rest * (1.0 / base))
        rest = rest - digit * base
        part = lax.dot_general(
            ranked,
            jnp.where(mine, digit, 0.0).astype(bf16),
            (((1,), (1,)), ((), ())),
            preferred_element_type=f32,
        )
        codes = part * base if codes is None else codes + part * base
    found[:, :blocks] = codes - 1.0


def couple(blocks, part, table, size, capacity, rounds, prepare, found, gather_first, transposed, result, scratch):
    column, vectors, products = scratch
    total_rows = column.shape[0]
    result[...] = jnp.zeros_like(result)

    def one_round(r, carry):
        prepare(r)
        codes = found[...]
        for w in range(blocks):
            column[w * capacity : (w + 1) * capacity] = jnp.broadcast_to(codes[:, w : w + 1], (capacity, BLOCK))
        eye = rows((BLOCK, BLOCK)) == lanes((BLOCK, BLOCK))
        place_hot = []
        for at in range(0, total_rows, BLOCK):
            code = column[at : at + BLOCK]
            first = jnp.floor((code + 0.5) * (1.0 / size))
            second = code - first * size
            gather, put = (first, second) if gather_first else (second, first)
            width = table.shape[0]
            gather = jnp.concatenate([gather] * (width // BLOCK), axis=1)
            hot = one_hot(gather == lanes((BLOCK, width)).astype(f32))
            vectors[at : at + BLOCK] = jnp.dot(hot, table, preferred_element_type=f32)
            put = jnp.sum(jnp.where(eye, put, 0.0), axis=0, keepdims=True)
            place_hot.append(one_hot(rows((result.shape[0], BLOCK)).astype(f32) == put))

        def group(g, carry):
            for u in range(GROUP):
                at = pl.multiple_of((g * GROUP + u) * capacity, 8)
                own = vectors[pl.ds(at, capacity)]
                left = jnp.concatenate([own[:, n * BLOCK : (n + 1) * BLOCK] for n in range(4)], axis=0)
                high, low = part(r, g, u)
                right = jnp.concatenate([high, low], axis=1 if transposed else 0)
                contract = (((1,), (0 if transposed else 1,)), ((), ()))
                product = lax.dot_general(left.astype(bf16), right, contract, preferred_element_type=f32)
                for f in range(2):
                    high_part = product[f * capacity : (f + 1) * capacity]
                    low_part = product[(f + 2) * capacity : (f + 3) * capacity, :BLOCK]
                    products[pl.ds(at, capacity), f * BLOCK : (f + 1) * BLOCK] = (
                        high_part[:, BLOCK:] + low_part
                    ) + high_part[:, :BLOCK]
            return carry

        lax.fori_loop(0, blocks // GROUP, group, 0)
        summed = jnp.dot(
            jnp.concatenate(place_hot, axis=1),
            jnp.concatenate(split(products[...]), axis=1),
            preferred_element_type=f32,
        )
        result[...] += summed[:, : 2 * BLOCK] + summed[:, 2 * BLOCK :]
        return carry

    lax.fori_loop(0, rounds, one_round, 0)


def slot_keys(ids, tile_lat, atm):
    lon_count, cap = ids.shape[3:]
    ocean, atm_ids, block_ids = (ids[n, 0, 0] for n in range(3))
    order = (ocean & 1) * tile_lat + (ocean >> 1) + rows((lon_count, cap)) * (2 * tile_lat)
    order = jnp.where(ocean >= 0, order, lon_count * 2 * tile_lat)
    return as_row((order * atm + atm_ids).astype(f32)), as_row(block_ids)


def weigh(atm_near, margins, weights, after, sums, found, keys, result, *scratch):
    scratch, (held, arrived) = scratch[:3], scratch[3:]
    fetch_weights(weights, held, arrived)
    lon_count = margins.shape[3]
    atm = atm_near.shape[2]
    blocks = weights.shape[0]
    tile_lat = 2 * sums.shape[1] // 9
    code, block_row = slot_keys(margins, tile_lat, atm)
    rank = rank_slots(block_row, blocks)
    keys[0:1] = code
    keys[1:2] = block_row.astype(f32)
    keys[2:3] = rank
    capacity = places(code.shape[1], blocks)
    rounds = jnp.max(rank).astype(jnp.int32) // capacity + 1
    parts = [split(atm_near[f, 0]) for f in range(2)]
    table = jnp.concatenate([parts[f][n] for n in range(2) for f in range(2)], axis=1)

    def prepare(r):
        find_slots(rounds - 1 - r, code, block_row, rank, capacity, blocks, found)

    part = held_part(weights, held, arrived)
    couple(blocks, part, table, atm, capacity, rounds, prepare, found, False, False, result, scratch)
    lane = lanes((tile_lat, BLOCK))

    def block_sums(k, f, h):
        at = (2 * k + h) * tile_lat
        return result[at : at + tile_lat, f * BLOCK : (f + 1) * BLOCK]

    for n, k in enumerate(group_order(lon_count)):
        edge = jnp.zeros((tile_lat, BLOCK), f32)
        for f in range(2):
            for h in range(2):
                sums[n, (2 * f + h) * tile_lat : (2 * f + h + 1) * tile_lat] = block_sums(k, f, h)
            at = f * HALO
            after = turn(block_sums((k + 1) % lon_count, f, 0), at, 1)
            before = turn(block_sums((k - 1) % lon_count, f, 1), -at, 1)
            edge = jnp.where((lane >= at) & (lane < at + HALO), after, edge)
            end = BLOCK - at
            edge = jnp.where((lane >= end - HALO) & (lane < end), before, edge)
        upper, lower = edge[: tile_lat // 2], edge[tile_lat // 2 :]
        near = lane[: tile_lat // 2]
        lower = jnp.where(near < BLOCK // 2, turn(lower, 2 * HALO, 1), turn(lower, -2 * HALO, 1))
        sums[n, 4 * tile_lat :] = jnp.where((near < 2 * HALO) | (near >= BLOCK - 2 * HALO), upper, lower)


def unweigh(gathered, found, keys, weights, gradient, result, codes, *scratch):
    scratch, (held, arrived) = scratch[:3], scratch[3:]
    fetch_weights(weights, held, arrived)
    atm = gradient.shape[2]
    blocks = weights.shape[0]
    lon_count, ocean_blocks = gathered.shape[0], gathered.shape[1] // 2
    order = group_order(lon_count)
    capacity = places(keys.shape[1], blocks)
    rounds = jnp.max(keys[2:3]).astype(jnp.int32) // capacity + 1
    parts = [
        split(
            jnp.concatenate(
                [gathered[order.index(k), f * ocean_blocks : (f + 1) * ocean_blocks] for k in range(lon_count)],
                axis=0,
            )
        )
        for f in range(2)
    ]
    table = jnp.concatenate([parts[f][n] for n in range(2) for f in range(2)], axis=1)

    def prepare(r):
        @pl.when(r == 0)
        def _():
            codes[...] = found[...]

        @pl.when(r > 0)
        def _():
            find_slots(r, keys[0:1], keys[1:2].astype(jnp.int32), keys[2:3], capacity, blocks, codes)

    couple(
        blocks,
        held_part(weights, held, arrived),
        table,
        atm,
        capacity,
        rounds,
        prepare,
        codes,
        True,
        True,
        result,
        scratch,
    )
    for f in range(2):
        gradient[f, 0] = result[:, f * BLOCK : (f + 1) * BLOCK]


def on_device(tracers, cotangent, land_mask, diffusion, velocity, weights, atm_state, margins):
    levels, tile_lat, tile_lon = land_mask.shape
    lon_count = lax.axis_size("lon")
    slots = lon_count * margins.shape[4]
    halves = tile_lon // BLOCK
    count = 9 * levels - 1
    parts = -(-count // PER_LANES)
    inputs = (tracers, cotangent, land_mask, diffusion, velocity)

    def in_vmem(s):
        return pltpu.VMEM(s.shape, s.dtype)

    message = (parts, tile_lat, BLOCK)
    fields, near, far, atm_near, margins_near = call(
        pack_columns,
        [
            (count, tile_lat, tile_lon),
            message,
            message,
            atm_state.shape,
            jax.ShapeDtypeStruct(margins.shape, margins.dtype),
        ],
        [*map(in_vmem, inputs), pltpu.SemaphoreType.DMA((7,))],
        name="pack_columns",
        inputs=7,
        far=range(7),
    )(*inputs, atm_state, margins)
    near_columns, far_columns = swap(near, far, "lon", True)

    blocks_of, atm = weights.shape[0], atm_state.shape[2]
    groups = blocks_of // GROUP
    sum_rows = 2 * halves * tile_lat + tile_lat // 2
    ocean_blocks = lon_count * halves * tile_lat
    held_rows = -(-places(slots, blocks_of) * blocks_of // BLOCK) * BLOCK

    def coupling_scratch(result_rows):
        return [
            pltpu.VMEM((result_rows, 2 * BLOCK), f32),
            pltpu.VMEM((held_rows, BLOCK), f32),
            pltpu.VMEM((held_rows, 4 * BLOCK), f32),
            pltpu.VMEM((held_rows, 2 * BLOCK), f32),
            pltpu.VMEM((groups, GROUP, BLOCK, BLOCK), f32),
            pltpu.SemaphoreType.DMA((groups,)),
        ]

    coupling_flops = 4 * slots * blocks_of * 2 * BLOCK * BLOCK * 2
    sums, found, keys = call(
        weigh,
        [(lon_count, sum_rows, BLOCK), (places(slots, blocks_of), BLOCK), (8, slots)],
        coupling_scratch(ocean_blocks),
        coupling_flops,
        name="weigh",
        inputs=4,
        far=(2,),
    )(atm_near, margins_near, weights, near)

    sources = count * halves + 2 * parts
    message = (-(-sources // 2), 8, BLOCK)
    columns = (parts, tile_lat, BLOCK)
    near, far, from_west, from_east, sums = call(
        pack_rows,
        [message, message, columns, columns, sums.shape],
        name="pack_rows",
        inputs=4,
        aliases={3: 4},
    )(fields, near_columns, far_columns, sums)
    received = exchange(sums)
    near_rows, far_rows = swap(near, far, "lat", False)

    wide = (tile_lat + 8, tile_lon + BLOCK)
    own = (2 * halves * tile_lat, BLOCK)
    adjoint_states = (2, STEPS - 1, levels, *wide)
    blocks, coeffs, start, states = call(
        run_adjoint,
        [(lon_count, *own), (6, levels, *wide), (4 * levels, *wide), adjoint_states],
        [
            pltpu.VMEM((count - 4 * levels, *wide), f32),
            pltpu.VMEM(own, f32),
            pltpu.SemaphoreType.DMA((2, lon_count)),
        ],
        name="run_adjoint",
        inputs=5,
        far_outs=(0,),
    )(fields, from_west, from_east, far_rows, near_rows)
    gathered = exchange(blocks)

    message = (1, 8, tile_lon + BLOCK)
    forcing, near, far = call(
        sum_forcing, [(2, tile_lat, tile_lon + BLOCK), message, message], name="sum_forcing", inputs=1
    )(received)
    near_rows, far_rows = swap(near, far, "lat", False)
    (adjoint,) = call(
        finish_adjoint,
        [cotangent.shape],
        [pltpu.VMEM(adjoint_states, f32)],
        name="finish_adjoint",
        inputs=3,
    )(coeffs, start, states)
    (final,) = call(
        run_forward,
        [tracers.shape],
        [pltpu.VMEM((2, levels, *wide), f32)],
        name="run_forward",
        inputs=5,
    )(coeffs, start, forcing, far_rows, near_rows)

    (gradient,) = call(
        unweigh,
        [atm_state.shape],
        [coupling_scratch(atm)[0], in_vmem(found), *coupling_scratch(atm)[1:]],
        coupling_flops,
        name="unweigh",
        inputs=4,
        far=(3,),
    )(gathered, found, keys, weights)
    return (final, adjoint, gradient)


def solution(mesh):
    return jax.shard_map(
        on_device,
        mesh=mesh,
        in_specs=(
            P(None, None, "lat", "lon"),
            P(None, None, "lat", "lon"),
            P(None, "lat", "lon"),
            P(None, None, "lat", "lon"),
            P(None, None, "lat", "lon"),
            P(),
            P(None, "lat", "lon", None),
            P(None, "lat", "lon", None, None),
        ),
        out_specs=(
            P(None, None, "lat", "lon"),
            P(None, None, "lat", "lon"),
            P(None, "lat", "lon", None),
        ),
        check_vma=False,
    )
```

```python
import jax
import jax.numpy as jnp
from jax import lax
from jax.experimental import pallas as pl
from jax.experimental.pallas import tpu as pltpu
from jax.sharding import PartitionSpec as P

BLOCK = 128
STEPS = 4
HALO = STEPS
PER_LANES = BLOCK // HALO
GROUP = 16
f32 = jnp.float32
bf16 = jnp.bfloat16
VMEM_LIMIT = 20 * 1024 * 1024


def call(body, outs, scratch=(), flops=0, name=None, inputs=0, far=(), far_outs=(), aliases=None):
    outs = [s if isinstance(s, jax.ShapeDtypeStruct) else jax.ShapeDtypeStruct(s, f32) for s in outs]
    near = pl.BlockSpec(memory_space=pltpu.VMEM)
    aliases = aliases or {}
    kernel = pl.pallas_call(
        body,
        out_shape=outs,
        in_specs=[
            pl.BlockSpec(memory_space=pl.ANY)
            if n in aliases
            else pl.BlockSpec(memory_space=pltpu.HBM)
            if n in far
            else near
            for n in range(inputs)
        ],
        out_specs=[
            pl.BlockSpec(memory_space=pl.ANY) if n in aliases.values() or n in far_outs else near
            for n in range(len(outs))
        ],
        input_output_aliases=aliases,
        scratch_shapes=list(scratch),
        compiler_params=pltpu.CompilerParams(vmem_limit_bytes=VMEM_LIMIT),
        cost_estimate=pl.CostEstimate(flops=flops, bytes_accessed=1 << 20, transcendentals=0),
        name=name,
    )

    def run(*args):
        return kernel(
            *(pltpu.with_memory_space_constraint(x, pltpu.HBM) if n in far else x for n, x in enumerate(args))
        )

    return run


def lanes(shape):
    return lax.broadcasted_iota(jnp.int32, shape, len(shape) - 1)


def rows(shape):
    return lax.broadcasted_iota(jnp.int32, shape, len(shape) - 2)


def turn(x, shift, axis):
    shift %= x.shape[axis]
    return pltpu.roll(x, shift, axis) if shift else x


def group_order(count):
    half = count // 2
    return [k for n in range(half) for k in (half + n, n)]


def exchange(x):
    order = group_order(x.shape[0])
    return lax.all_to_all(x, "lon", split_axis=0, concat_axis=0, tiled=True, axis_index_groups=[order])


def swap(near, far, axis, wrap):
    count = lax.axis_size(axis)
    pairs = [[], []]
    for i in range(count if wrap else count - 1):
        j = (i + 1) % count
        pairs[i % 2] += [(i, j), (j, i)]
    far = lax.ppermute(far, axis, pairs[1])
    return lax.ppermute(near, axis, pairs[0]), far


def sort_swap(axis, after, before):
    odd = lax.rem(lax.axis_index(axis), 2) == 1
    return jnp.where(odd, before, after), jnp.where(odd, after, before)


def tile_fields(tracers, cotangent, land_mask, diffusion, velocity):
    levels = land_mask.shape[0]
    mask = [land_mask[level].astype(f32) for level in range(levels)]
    out = [tracers[f, level] for f in range(2) for level in range(levels)]
    out += [cotangent[f, level] for f in range(2) for level in range(levels)]
    out += [diffusion[0, level] * mask[level] for level in range(levels)]
    out += [velocity[0, level] * mask[level] for level in range(levels)]
    out += [diffusion[1, level] * mask[level] for level in range(levels)]
    out += [velocity[1, level] * mask[level] for level in range(levels)]
    out += [diffusion[2, level] * mask[level] * mask[level + 1] for level in range(levels - 1)]
    return out


def fetch(pairs, arrived):
    copies = [pltpu.make_async_copy(src, dst, arrived.at[n]) for n, (src, dst) in enumerate(pairs)]
    for copy in copies:
        copy.start()
    return copies


def pack_columns(*refs):
    inputs, (fields, near, far), scratch = refs[:7], refs[7:10], refs[12:]
    copies = fetch(zip(inputs, [*scratch[:5], *refs[10:12]]), scratch[5])
    for copy in copies[:5]:
        copy.wait()
    shape = near.shape[1:]
    lane = lanes(shape)
    west = [jnp.zeros(shape, f32) for _ in range(near.shape[0])]
    east = [jnp.zeros(shape, f32) for _ in range(near.shape[0])]
    for i, field in enumerate(tile_fields(*scratch[:5])):
        fields[i] = field
        part, at = divmod(i, PER_LANES)
        at *= HALO
        here = (lane >= at) & (lane < at + HALO)
        west[part] = jnp.where(here, turn(field[:, :BLOCK], at, 1), west[part])
        east[part] = jnp.where(here, turn(field[:, -BLOCK:], at + HALO, 1), east[part])
    for part in range(near.shape[0]):
        near[part], far[part] = sort_swap("lon", east[part], west[part])
    for copy in copies[5:]:
        copy.wait()


def unpack_columns(from_west, from_east, i):
    part, at = divmod(i, PER_LANES)
    at *= HALO
    lane = lanes(from_west[part].shape)
    east = turn(from_east[part], -at, 1)
    west = turn(from_west[part], -at - HALO, 1)
    return jnp.where(lane < HALO, east, jnp.where(lane >= BLOCK - HALO, west, 0.0))


def row_sources(fields, from_west, from_east):
    out = [(fields, (i, slice(None), slice(h * BLOCK, (h + 1) * BLOCK)))
           for i in range(fields.shape[0]) for h in range(fields.shape[2] // BLOCK)]
    for columns in (from_west, from_east):
        out += [(columns, (part,)) for part in range(columns.shape[0])]
    return out


def pack_rows(fields, near_columns, far_columns, sums, near, far, from_west, from_east, same_sums):
    for part in range(from_west.shape[0]):
        from_east[part], from_west[part] = sort_swap("lon", near_columns[part], far_columns[part])
    sources = [ref[at] for ref, at in row_sources(fields, from_west, from_east)]
    half = near.shape[0]
    row = rows((8, BLOCK))
    for i in range(half):
        first = sources[i]
        second = sources[i + half] if i + half < len(sources) else jnp.zeros_like(first)
        to_north = jnp.where(row < HALO, turn(first[-8:], HALO, 0), second[-8:])
        to_south = jnp.where(row < HALO, first[:8], turn(second[:8], HALO, 0))
        near[i], far[i] = sort_swap("lat", to_north, to_south)


def edge_rows(near, far, i):
    half = near.shape[0]
    from_north, from_south = sort_swap("lat", near[i % half], far[i % half])
    if i < half:
        from_south = turn(from_south, HALO, 0)
    else:
        from_north = turn(from_north, HALO, 0)
    return jnp.where(rows(from_north.shape) < HALO, from_north, from_south)


def widen(fields, from_west, from_east, near, far, start, wide):
    count, tile_lat, tile_lon = fields.shape
    halves = tile_lon // BLOCK
    parts = from_west.shape[0]
    corners = [edge_rows(near, far, count * halves + n) for n in range(2 * parts)]
    for i in range(count):
        out = start.at[i] if i < start.shape[0] else wide.at[i - start.shape[0]]
        out[:tile_lat, :tile_lon] = fields[i]
        out[:tile_lat, tile_lon:] = unpack_columns(from_west, from_east, i)
        for h in range(halves):
            out[tile_lat:, h * BLOCK : (h + 1) * BLOCK] = edge_rows(near, far, i * halves + h)
        out[tile_lat:, tile_lon:] = unpack_columns(corners[:parts], corners[parts:], i)


def eastward(x):
    return turn(x, -1, 1)


def westward(x):
    return turn(x, 1, 1)


def northward(x):
    return turn(x, -1, 0)


def southward(x):
    return turn(x, 1, 0)


def adjoint_step(coeffs, read, write, first, last):
    levels = coeffs.shape[1]
    above = coeffs[4, first - 1] * (read(first) - read(first - 1)) if first else None
    for level in range(first, last):
        lam = read(level)
        step_x = eastward(lam) - lam
        step_y = northward(lam) - lam
        out = lam + coeffs[0, level] * step_x + westward(coeffs[1, level] * step_x)
        out = out + coeffs[2, level] * step_y + southward(coeffs[3, level] * step_y)
        if above is not None:
            out = out - above
        if level < levels - 1:
            above = coeffs[4, level] * (read(level + 1) - lam)
            out = out + above
        write(level, out)


def surface_levels(step, levels):
    return min(levels, STEPS - 1 - step)


def run_adjoint(
    fields, from_west, from_east, far, near, blocks, coeffs, start, states, wide, own, sent
):
    levels = coeffs.shape[1]
    tile_lat, tile_lon = fields.shape[1:]
    halves = tile_lon // BLOCK
    widen(fields, from_west, from_east, near, far, start, wide)
    base = 0
    mask0 = None
    for level in range(levels):
        east_d, east_u = wide[base + level], wide[base + levels + level]
        north_d, north_u = wide[base + 2 * levels + level], wide[base + 3 * levels + level]
        mask = (east_d > 0.0).astype(f32)
        mask0 = mask if mask0 is None else mask0
        mask_e, mask_n = eastward(mask), northward(mask)
        east_k, east_v = east_d * mask_e, east_u * mask_e
        north_k, north_v = north_d * mask_n, north_u * mask_n
        coeffs[0, level] = jnp.maximum(east_v, 0.0) + east_k
        coeffs[1, level] = jnp.minimum(east_v, 0.0) - east_k
        coeffs[2, level] = jnp.maximum(north_v, 0.0) + north_k
        coeffs[3, level] = jnp.minimum(north_v, 0.0) - north_k
        coeffs[4, level] = wide[base + 4 * levels + level] if level < levels - 1 else jnp.zeros_like(mask)
        coeffs[5, level] = mask
    copies = []
    for f in range(2):
        surface = start[(2 + f) * levels, :tile_lat, :tile_lon]
        for step in range(STEPS - 1):

            def read(level):
                return states[f, step - 1, level] if step else start[(2 + f) * levels + level]

            def write(level, lam):
                states[f, step, level] = lam

            adjoint_step(coeffs, read, write, 0, surface_levels(step, levels))
            surface = surface + states[f, step, 0, :tile_lat, :tile_lon]
        surface = surface * mask0[:tile_lat, :tile_lon]
        for h in range(halves):
            at = (f * halves + h) * tile_lat
            own[at : at + tile_lat] = surface[:, h * BLOCK : (h + 1) * BLOCK]
        field = pl.ds(f * halves * tile_lat, halves * tile_lat)
        copies += fetch([(own.at[field], blocks.at[k, field]) for k in range(blocks.shape[0])], sent.at[f])
    for copy in copies:
        copy.wait()


def finish_adjoint(coeffs, start, states, adjoint_out, rest):
    levels = coeffs.shape[1]
    tile_lat, tile_lon = adjoint_out.shape[2:]
    for f in range(2):
        for step in range(STEPS):
            done = surface_levels(step, levels)

            def read(level):
                if not step:
                    return start[(2 + f) * levels + level]
                return (states if level < surface_levels(step - 1, levels) else rest)[f, step - 1, level]

            def write(level, lam):
                if step == STEPS - 1:
                    adjoint_out[f, level] = lam[:tile_lat, :tile_lon]
                else:
                    rest[f, step, level] = lam

            adjoint_step(coeffs, read, write, done, levels)


def sum_forcing(received, forcing, near, far):
    tile_lat = forcing.shape[1]
    halves = forcing.shape[2] // BLOCK - 1
    total = received[0]
    for j in range(1, received.shape[0]):
        total = total + received[j]
    lane = lanes((tile_lat, BLOCK))
    upper = total[2 * halves * tile_lat :]
    lower = jnp.where(lane[: tile_lat // 2] < BLOCK // 2, turn(upper, -2 * HALO, 1), turn(upper, 2 * HALO, 1))
    packed = jnp.concatenate([upper, lower], axis=0)
    for f in range(2):
        for h in range(halves):
            at = (f * halves + h) * tile_lat
            forcing[f, :, h * BLOCK : (h + 1) * BLOCK] = total[at : at + tile_lat]
        used = (lane < HALO) | (lane >= BLOCK - HALO)
        if f == 0:
            edge = packed
        else:
            edge = jnp.where(lane < HALO, turn(packed, -HALO, 1), turn(packed, HALO, 1))
        forcing[f, :, halves * BLOCK :] = jnp.where(used, edge, 0.0)
    row = rows((8, forcing.shape[2]))
    to_north = jnp.where(row < HALO, turn(forcing[0, tile_lat - 8 :], HALO, 0), forcing[1, tile_lat - 8 :])
    to_south = jnp.where(row < HALO, forcing[0, :8], turn(forcing[1, :8], HALO, 0))
    near[0], far[0] = sort_swap("lat", to_north, to_south)


def run_forward(coeffs, start, forcing, far, near, final, state):
    levels = coeffs.shape[1]
    tile_lat, tile_lon = final.shape[2:]
    for f in range(2):
        force = jnp.concatenate([forcing[f], edge_rows(near, far, f)], axis=0)
        force = force * coeffs[5, 0]
        for step in range(STEPS):
            above = None
            for level in range(levels):
                read = (lambda n: start[f * levels + n]) if step == 0 else (lambda n: state[(step - 1) % 2, n])
                theta = read(level)
                east_flux = coeffs[0, level] * theta + coeffs[1, level] * eastward(theta)
                north_flux = coeffs[2, level] * theta + coeffs[3, level] * northward(theta)
                out = theta - (east_flux - westward(east_flux)) - (north_flux - southward(north_flux))
                if level < levels - 1:
                    vertical = coeffs[4, level] * (theta - read(level + 1))
                    out = out - vertical
                if above is not None:
                    out = out + above
                above = vertical if level < levels - 1 else None
                if level == 0:
                    out = out + force
                if step == STEPS - 1:
                    final[f, level] = out[:tile_lat, :tile_lon]
                else:
                    state[step % 2, level] = out


def split(x):
    high = x.astype(bf16)
    return high, (x - high.astype(f32)).astype(bf16)


def weight_copies(weights, held, arrived):
    for g in range(held.shape[0]):
        yield pltpu.make_async_copy(weights.at[pl.ds(g * GROUP, GROUP)], held.at[g], arrived.at[g])


def fetch_weights(weights, held, arrived):
    for copy in weight_copies(weights, held, arrived):
        copy.start()


def held_part(weights, held, arrived):
    def part(r, g, u):
        if u == 0:

            @pl.when(r == 0)
            def _():
                pltpu.make_async_copy(weights.at[pl.ds(g * GROUP, GROUP)], held.at[g], arrived.at[g]).wait()

        return split(held[g, u])

    return part


def one_hot(where):
    return jnp.where(where, 1.0, 0.0).astype(bf16)


def places(slots, blocks):
    return 8 * (-(-2 * slots // (8 * blocks)) + 1)


def as_row(ids):
    return jnp.concatenate([ids[k : k + 1, :] for k in range(ids.shape[0])], axis=1)


def rank_slots(block_row, blocks):
    slots = block_row.shape[1]
    mine = rows((blocks, slots)) == block_row
    cuts = range(0, slots, BLOCK)
    stacked = jnp.concatenate([one_hot(mine[:, at : at + BLOCK]) for at in cuts], axis=0)
    shape = (BLOCK, 2 * BLOCK)
    counts = jnp.dot(stacked, one_hot(rows(shape) < lanes(shape)), preferred_element_type=f32)
    before, out = jnp.zeros((blocks, BLOCK), f32), []
    for n, at in enumerate(cuts):
        run = counts[n * blocks : (n + 1) * blocks]
        here = jnp.where(mine[:, at : at + BLOCK], run[:, :BLOCK] + before, 0.0)
        out.append(jnp.sum(here, axis=0, keepdims=True))
        before = before + run[:, BLOCK:]
    return jnp.concatenate(out, axis=1)


def find_slots(r, code, block_row, rank, capacity, blocks, found):
    slots = block_row.shape[1]
    mine = rows((blocks, slots)) == block_row
    ranked = one_hot(rows((capacity, slots)) == rank.astype(jnp.int32) - r * capacity)
    rest, codes = code + 1.0, None
    for base in (4096.0, 64.0, 1.0):
        digit = jnp.floor(rest * (1.0 / base))
        rest = rest - digit * base
        part = lax.dot_general(
            ranked,
            jnp.where(mine, digit, 0.0).astype(bf16),
            (((1,), (1,)), ((), ())),
            preferred_element_type=f32,
        )
        codes = part * base if codes is None else codes + part * base
    found[:, :blocks] = codes - 1.0


def couple(blocks, part, table, size, capacity, rounds, prepare, found, gather_first, transposed, result, scratch):
    column, vectors, products = scratch
    total_rows = column.shape[0]
    result[...] = jnp.zeros_like(result)

    def one_round(r, carry):
        prepare(r)
        codes = found[...]
        for w in range(blocks):
            column[w * capacity : (w + 1) * capacity] = jnp.broadcast_to(codes[:, w : w + 1], (capacity, BLOCK))
        eye = rows((BLOCK, BLOCK)) == lanes((BLOCK, BLOCK))
        place_hot = []
        for at in range(0, total_rows, BLOCK):
            code = column[at : at + BLOCK]
            first = jnp.floor((code + 0.5) * (1.0 / size))
            second = code - first * size
            gather, put = (first, second) if gather_first else (second, first)
            width = table.shape[0]
            gather = jnp.concatenate([gather] * (width // BLOCK), axis=1)
            hot = one_hot(gather == lanes((BLOCK, width)).astype(f32))
            vectors[at : at + BLOCK] = jnp.dot(hot, table, preferred_element_type=f32)
            put = jnp.sum(jnp.where(eye, put, 0.0), axis=0, keepdims=True)
            place_hot.append(one_hot(rows((result.shape[0], BLOCK)).astype(f32) == put))

        def group(g, carry):
            for u in range(GROUP):
                at = pl.multiple_of((g * GROUP + u) * capacity, 8)
                own = vectors[pl.ds(at, capacity)]
                left = jnp.concatenate([own[:, n * BLOCK : (n + 1) * BLOCK] for n in range(4)], axis=0)
                high, low = part(r, g, u)
                right = jnp.concatenate([high, low], axis=1 if transposed else 0)
                contract = (((1,), (0 if transposed else 1,)), ((), ()))
                product = lax.dot_general(left.astype(bf16), right, contract, preferred_element_type=f32)
                for f in range(2):
                    high_part = product[f * capacity : (f + 1) * capacity]
                    low_part = product[(f + 2) * capacity : (f + 3) * capacity, :BLOCK]
                    products[pl.ds(at, capacity), f * BLOCK : (f + 1) * BLOCK] = (
                        high_part[:, BLOCK:] + low_part
                    ) + high_part[:, :BLOCK]
            return carry

        lax.fori_loop(0, blocks // GROUP, group, 0)
        summed = jnp.dot(
            jnp.concatenate(place_hot, axis=1),
            jnp.concatenate(split(products[...]), axis=1),
            preferred_element_type=f32,
        )
        result[...] += summed[:, : 2 * BLOCK] + summed[:, 2 * BLOCK :]
        return carry

    lax.fori_loop(0, rounds, one_round, 0)


def slot_keys(ids, tile_lat, atm):
    lon_count, cap = ids.shape[3:]
    ocean, atm_ids, block_ids = (ids[n, 0, 0] for n in range(3))
    order = (ocean & 1) * tile_lat + (ocean >> 1) + rows((lon_count, cap)) * (2 * tile_lat)
    order = jnp.where(ocean >= 0, order, lon_count * 2 * tile_lat)
    return as_row((order * atm + atm_ids).astype(f32)), as_row(block_ids)


def weigh(atm_near, margins, weights, after, sums, found, keys, result, *scratch):
    scratch, (held, arrived) = scratch[:3], scratch[3:]
    fetch_weights(weights, held, arrived)
    lon_count = margins.shape[3]
    atm = atm_near.shape[2]
    blocks = weights.shape[0]
    tile_lat = 2 * sums.shape[1] // 9
    code, block_row = slot_keys(margins, tile_lat, atm)
    rank = rank_slots(block_row, blocks)
    keys[0:1] = code
    keys[1:2] = block_row.astype(f32)
    keys[2:3] = rank
    capacity = places(code.shape[1], blocks)
    rounds = jnp.max(rank).astype(jnp.int32) // capacity + 1
    parts = [split(atm_near[f, 0]) for f in range(2)]
    table = jnp.concatenate([parts[f][n] for n in range(2) for f in range(2)], axis=1)

    def prepare(r):
        find_slots(rounds - 1 - r, code, block_row, rank, capacity, blocks, found)

    part = held_part(weights, held, arrived)
    couple(blocks, part, table, atm, capacity, rounds, prepare, found, False, False, result, scratch)
    lane = lanes((tile_lat, BLOCK))

    def block_sums(k, f, h):
        at = (2 * k + h) * tile_lat
        return result[at : at + tile_lat, f * BLOCK : (f + 1) * BLOCK]

    for n, k in enumerate(group_order(lon_count)):
        edge = jnp.zeros((tile_lat, BLOCK), f32)
        for f in range(2):
            for h in range(2):
                sums[n, (2 * f + h) * tile_lat : (2 * f + h + 1) * tile_lat] = block_sums(k, f, h)
            at = f * HALO
            after = turn(block_sums((k + 1) % lon_count, f, 0), at, 1)
            before = turn(block_sums((k - 1) % lon_count, f, 1), -at, 1)
            edge = jnp.where((lane >= at) & (lane < at + HALO), after, edge)
            end = BLOCK - at
            edge = jnp.where((lane >= end - HALO) & (lane < end), before, edge)
        upper, lower = edge[: tile_lat // 2], edge[tile_lat // 2 :]
        near = lane[: tile_lat // 2]
        lower = jnp.where(near < BLOCK // 2, turn(lower, 2 * HALO, 1), turn(lower, -2 * HALO, 1))
        sums[n, 4 * tile_lat :] = jnp.where((near < 2 * HALO) | (near >= BLOCK - 2 * HALO), upper, lower)


def unweigh(gathered, found, keys, weights, gradient, result, codes, *scratch):
    scratch, (held, arrived) = scratch[:3], scratch[3:]
    fetch_weights(weights, held, arrived)
    atm = gradient.shape[2]
    blocks = weights.shape[0]
    lon_count, ocean_blocks = gathered.shape[0], gathered.shape[1] // 2
    order = group_order(lon_count)
    capacity = places(keys.shape[1], blocks)
    rounds = jnp.max(keys[2:3]).astype(jnp.int32) // capacity + 1
    parts = [
        split(
            jnp.concatenate(
                [gathered[order.index(k), f * ocean_blocks : (f + 1) * ocean_blocks] for k in range(lon_count)],
                axis=0,
            )
        )
        for f in range(2)
    ]
    table = jnp.concatenate([parts[f][n] for n in range(2) for f in range(2)], axis=1)

    def prepare(r):
        @pl.when(r == 0)
        def _():
            codes[...] = found[...]

        @pl.when(r > 0)
        def _():
            find_slots(r, keys[0:1], keys[1:2].astype(jnp.int32), keys[2:3], capacity, blocks, codes)

    couple(
        blocks,
        held_part(weights, held, arrived),
        table,
        atm,
        capacity,
        rounds,
        prepare,
        codes,
        True,
        True,
        result,
        scratch,
    )
    for f in range(2):
        gradient[f, 0] = result[:, f * BLOCK : (f + 1) * BLOCK]


def on_device(tracers, cotangent, land_mask, diffusion, velocity, weights, atm_state, margins):
    levels, tile_lat, tile_lon = land_mask.shape
    lon_count = lax.axis_size("lon")
    slots = lon_count * margins.shape[4]
    halves = tile_lon // BLOCK
    count = 9 * levels - 1
    parts = -(-count // PER_LANES)
    inputs = (tracers, cotangent, land_mask, diffusion, velocity)

    def in_vmem(s):
        return pltpu.VMEM(s.shape, s.dtype)

    message = (parts, tile_lat, BLOCK)
    fields, near, far, atm_near, margins_near = call(
        pack_columns,
        [
            (count, tile_lat, tile_lon),
            message,
            message,
            atm_state.shape,
            jax.ShapeDtypeStruct(margins.shape, margins.dtype),
        ],
        [*map(in_vmem, inputs), pltpu.SemaphoreType.DMA((7,))],
        name="pack_columns",
        inputs=7,
        far=range(7),
    )(*inputs, atm_state, margins)
    near_columns, far_columns = swap(near, far, "lon", True)

    blocks_of, atm = weights.shape[0], atm_state.shape[2]
    groups = blocks_of // GROUP
    sum_rows = 2 * halves * tile_lat + tile_lat // 2
    ocean_blocks = lon_count * halves * tile_lat
    held_rows = -(-places(slots, blocks_of) * blocks_of // BLOCK) * BLOCK

    def coupling_scratch(result_rows):
        return [
            pltpu.VMEM((result_rows, 2 * BLOCK), f32),
            pltpu.VMEM((held_rows, BLOCK), f32),
            pltpu.VMEM((held_rows, 4 * BLOCK), f32),
            pltpu.VMEM((held_rows, 2 * BLOCK), f32),
            pltpu.VMEM((groups, GROUP, BLOCK, BLOCK), f32),
            pltpu.SemaphoreType.DMA((groups,)),
        ]

    coupling_flops = 4 * slots * blocks_of * 2 * BLOCK * BLOCK * 2
    sums, found, keys = call(
        weigh,
        [(lon_count, sum_rows, BLOCK), (places(slots, blocks_of), BLOCK), (8, slots)],
        coupling_scratch(ocean_blocks),
        coupling_flops,
        name="weigh",
        inputs=4,
        far=(2,),
    )(atm_near, margins_near, weights, far)

    sources = count * halves + 2 * parts
    message = (-(-sources // 2), 8, BLOCK)
    columns = (parts, tile_lat, BLOCK)
    near, far, from_west, from_east, sums = call(
        pack_rows,
        [message, message, columns, columns, sums.shape],
        name="pack_rows",
        inputs=4,
        aliases={3: 4},
    )(fields, near_columns, far_columns, sums)
    received = exchange(sums)
    near_rows, far_rows = swap(near, far, "lat", False)

    wide = (tile_lat + 8, tile_lon + BLOCK)
    own = (2 * halves * tile_lat, BLOCK)
    adjoint_states = (2, STEPS - 1, levels, *wide)
    blocks, coeffs, start, states = call(
        run_adjoint,
        [(lon_count, *own), (6, levels, *wide), (4 * levels, *wide), adjoint_states],
        [
            pltpu.VMEM((count - 4 * levels, *wide), f32),
            pltpu.VMEM(own, f32),
            pltpu.SemaphoreType.DMA((2, lon_count)),
        ],
        name="run_adjoint",
        inputs=5,
        far_outs=(0,),
    )(fields, from_west, from_east, far_rows, near_rows)
    gathered = exchange(blocks)

    message = (1, 8, tile_lon + BLOCK)
    forcing, near, far = call(
        sum_forcing, [(2, tile_lat, tile_lon + BLOCK), message, message], name="sum_forcing", inputs=1
    )(received)
    near_rows, far_rows = swap(near, far, "lat", False)
    (adjoint,) = call(
        finish_adjoint,
        [cotangent.shape],
        [pltpu.VMEM(adjoint_states, f32)],
        name="finish_adjoint",
        inputs=3,
    )(coeffs, start, states)
    (final,) = call(
        run_forward,
        [tracers.shape],
        [pltpu.VMEM((2, levels, *wide), f32)],
        name="run_forward",
        inputs=5,
    )(coeffs, start, forcing, far_rows, near_rows)

    (gradient,) = call(
        unweigh,
        [atm_state.shape],
        [coupling_scratch(atm)[0], in_vmem(found), *coupling_scratch(atm)[1:]],
        coupling_flops,
        name="unweigh",
        inputs=4,
        far=(3,),
    )(gathered, found, keys, weights)
    return (final, adjoint, gradient)


def solution(mesh):
    return jax.shard_map(
        on_device,
        mesh=mesh,
        in_specs=(
            P(None, None, "lat", "lon"),
            P(None, None, "lat", "lon"),
            P(None, "lat", "lon"),
            P(None, None, "lat", "lon"),
            P(None, None, "lat", "lon"),
            P(),
            P(None, "lat", "lon", None),
            P(None, "lat", "lon", None, None),
        ),
        out_specs=(
            P(None, None, "lat", "lon"),
            P(None, None, "lat", "lon"),
            P(None, "lat", "lon", None),
        ),
        check_vma=False,
    )
```

```python
import jax
import jax.numpy as jnp
from jax import lax
from jax.experimental import pallas as pl
from jax.experimental.pallas import tpu as pltpu
from jax.sharding import PartitionSpec as P

BLOCK = 128
STEPS = 4
HALO = STEPS
PER_LANES = BLOCK // HALO
GROUP = 16
f32 = jnp.float32
bf16 = jnp.bfloat16
VMEM_LIMIT = 20 * 1024 * 1024


def call(body, outs, scratch=(), flops=0, name=None, inputs=0, far=(), far_outs=(), aliases=None):
    outs = [s if isinstance(s, jax.ShapeDtypeStruct) else jax.ShapeDtypeStruct(s, f32) for s in outs]
    near = pl.BlockSpec(memory_space=pltpu.VMEM)
    aliases = aliases or {}
    kernel = pl.pallas_call(
        body,
        out_shape=outs,
        in_specs=[
            pl.BlockSpec(memory_space=pl.ANY)
            if n in aliases
            else pl.BlockSpec(memory_space=pltpu.HBM)
            if n in far
            else near
            for n in range(inputs)
        ],
        out_specs=[
            pl.BlockSpec(memory_space=pl.ANY) if n in aliases.values() or n in far_outs else near
            for n in range(len(outs))
        ],
        input_output_aliases=aliases,
        scratch_shapes=list(scratch),
        compiler_params=pltpu.CompilerParams(vmem_limit_bytes=VMEM_LIMIT),
        cost_estimate=pl.CostEstimate(flops=flops, bytes_accessed=1 << 20, transcendentals=0),
        name=name,
    )

    def run(*args):
        return kernel(
            *(pltpu.with_memory_space_constraint(x, pltpu.HBM) if n in far else x for n, x in enumerate(args))
        )

    return run


def lanes(shape):
    return lax.broadcasted_iota(jnp.int32, shape, len(shape) - 1)


def rows(shape):
    return lax.broadcasted_iota(jnp.int32, shape, len(shape) - 2)


def turn(x, shift, axis):
    shift %= x.shape[axis]
    return pltpu.roll(x, shift, axis) if shift else x


def group_order(count):
    half = count // 2
    return [k for n in range(half) for k in (half + n, n)]


def exchange(x):
    order = group_order(x.shape[0])
    return lax.all_to_all(x, "lon", split_axis=0, concat_axis=0, tiled=True, axis_index_groups=[order])


def swap(near, far, axis, wrap):
    count = lax.axis_size(axis)
    pairs = [[], []]
    for i in range(count if wrap else count - 1):
        j = (i + 1) % count
        pairs[i % 2] += [(i, j), (j, i)]
    far = lax.ppermute(far, axis, pairs[1])
    return lax.ppermute(near, axis, pairs[0]), far


def sort_swap(axis, after, before):
    odd = lax.rem(lax.axis_index(axis), 2) == 1
    return jnp.where(odd, before, after), jnp.where(odd, after, before)


def tile_fields(tracers, cotangent, land_mask, diffusion, velocity):
    levels = land_mask.shape[0]
    mask = [land_mask[level].astype(f32) for level in range(levels)]
    out = [tracers[f, level] for f in range(2) for level in range(levels)]
    out += [cotangent[f, level] for f in range(2) for level in range(levels)]
    out += [diffusion[0, level] * mask[level] for level in range(levels)]
    out += [velocity[0, level] * mask[level] for level in range(levels)]
    out += [diffusion[1, level] * mask[level] for level in range(levels)]
    out += [velocity[1, level] * mask[level] for level in range(levels)]
    out += [diffusion[2, level] * mask[level] * mask[level + 1] for level in range(levels - 1)]
    return out


def fetch(pairs, arrived):
    copies = [pltpu.make_async_copy(src, dst, arrived.at[n]) for n, (src, dst) in enumerate(pairs)]
    for copy in copies:
        copy.start()
    return copies


def pack_columns(*refs):
    inputs, (fields, near, far), scratch = refs[:7], refs[7:10], refs[12:]
    copies = fetch(zip(inputs, [*scratch[:5], *refs[10:12]]), scratch[5])
    for copy in copies[:5]:
        copy.wait()
    shape = near.shape[1:]
    lane = lanes(shape)
    west = [jnp.zeros(shape, f32) for _ in range(near.shape[0])]
    east = [jnp.zeros(shape, f32) for _ in range(near.shape[0])]
    for i, field in enumerate(tile_fields(*scratch[:5])):
        fields[i] = field
        part, at = divmod(i, PER_LANES)
        at *= HALO
        here = (lane >= at) & (lane < at + HALO)
        west[part] = jnp.where(here, turn(field[:, :BLOCK], at, 1), west[part])
        east[part] = jnp.where(here, turn(field[:, -BLOCK:], at + HALO, 1), east[part])
    for part in range(near.shape[0]):
        near[part], far[part] = sort_swap("lon", east[part], west[part])
    for copy in copies[5:]:
        copy.wait()


def unpack_columns(from_west, from_east, i):
    part, at = divmod(i, PER_LANES)
    at *= HALO
    lane = lanes(from_west[part].shape)
    east = turn(from_east[part], -at, 1)
    west = turn(from_west[part], -at - HALO, 1)
    return jnp.where(lane < HALO, east, jnp.where(lane >= BLOCK - HALO, west, 0.0))


def row_sources(fields, from_west, from_east):
    out = [(fields, (i, slice(None), slice(h * BLOCK, (h + 1) * BLOCK)))
           for i in range(fields.shape[0]) for h in range(fields.shape[2] // BLOCK)]
    for columns in (from_west, from_east):
        out += [(columns, (part,)) for part in range(columns.shape[0])]
    return out


def hold(sums, near_columns, same_sums):
    pass


def pack_rows(fields, near_columns, far_columns, near, far, from_west, from_east):
    for part in range(from_west.shape[0]):
        from_east[part], from_west[part] = sort_swap("lon", near_columns[part], far_columns[part])
    sources = [ref[at] for ref, at in row_sources(fields, from_west, from_east)]
    half = near.shape[0]
    row = rows((8, BLOCK))
    for i in range(half):
        first = sources[i]
        second = sources[i + half] if i + half < len(sources) else jnp.zeros_like(first)
        to_north = jnp.where(row < HALO, turn(first[-8:], HALO, 0), second[-8:])
        to_south = jnp.where(row < HALO, first[:8], turn(second[:8], HALO, 0))
        near[i], far[i] = sort_swap("lat", to_north, to_south)


def edge_rows(near, far, i):
    half = near.shape[0]
    from_north, from_south = sort_swap("lat", near[i % half], far[i % half])
    if i < half:
        from_south = turn(from_south, HALO, 0)
    else:
        from_north = turn(from_north, HALO, 0)
    return jnp.where(rows(from_north.shape) < HALO, from_north, from_south)


def widen(fields, from_west, from_east, near, far, start, wide):
    count, tile_lat, tile_lon = fields.shape
    halves = tile_lon // BLOCK
    parts = from_west.shape[0]
    corners = [edge_rows(near, far, count * halves + n) for n in range(2 * parts)]
    for i in range(count):
        out = start.at[i] if i < start.shape[0] else wide.at[i - start.shape[0]]
        out[:tile_lat, :tile_lon] = fields[i]
        out[:tile_lat, tile_lon:] = unpack_columns(from_west, from_east, i)
        for h in range(halves):
            out[tile_lat:, h * BLOCK : (h + 1) * BLOCK] = edge_rows(near, far, i * halves + h)
        out[tile_lat:, tile_lon:] = unpack_columns(corners[:parts], corners[parts:], i)


def eastward(x):
    return turn(x, -1, 1)


def westward(x):
    return turn(x, 1, 1)


def northward(x):
    return turn(x, -1, 0)


def southward(x):
    return turn(x, 1, 0)


def adjoint_step(coeffs, read, write, first, last):
    levels = coeffs.shape[1]
    above = coeffs[4, first - 1] * (read(first) - read(first - 1)) if first else None
    for level in range(first, last):
        lam = read(level)
        step_x = eastward(lam) - lam
        step_y = northward(lam) - lam
        out = lam + coeffs[0, level] * step_x + westward(coeffs[1, level] * step_x)
        out = out + coeffs[2, level] * step_y + southward(coeffs[3, level] * step_y)
        if above is not None:
            out = out - above
        if level < levels - 1:
            above = coeffs[4, level] * (read(level + 1) - lam)
            out = out + above
        write(level, out)


def surface_levels(step, levels):
    return min(levels, STEPS - 1 - step)


def run_adjoint(
    fields, from_west, from_east, far, near, blocks, coeffs, start, states, wide, own, sent
):
    levels = coeffs.shape[1]
    tile_lat, tile_lon = fields.shape[1:]
    halves = tile_lon // BLOCK
    widen(fields, from_west, from_east, near, far, start, wide)
    base = 0
    mask0 = None
    for level in range(levels):
        east_d, east_u = wide[base + level], wide[base + levels + level]
        north_d, north_u = wide[base + 2 * levels + level], wide[base + 3 * levels + level]
        mask = (east_d > 0.0).astype(f32)
        mask0 = mask if mask0 is None else mask0
        mask_e, mask_n = eastward(mask), northward(mask)
        east_k, east_v = east_d * mask_e, east_u * mask_e
        north_k, north_v = north_d * mask_n, north_u * mask_n
        coeffs[0, level] = jnp.maximum(east_v, 0.0) + east_k
        coeffs[1, level] = jnp.minimum(east_v, 0.0) - east_k
        coeffs[2, level] = jnp.maximum(north_v, 0.0) + north_k
        coeffs[3, level] = jnp.minimum(north_v, 0.0) - north_k
        coeffs[4, level] = wide[base + 4 * levels + level] if level < levels - 1 else jnp.zeros_like(mask)
        coeffs[5, level] = mask
    copies = []
    for f in range(2):
        surface = start[(2 + f) * levels, :tile_lat, :tile_lon]
        for step in range(STEPS - 1):

            def read(level):
                return states[f, step - 1, level] if step else start[(2 + f) * levels + level]

            def write(level, lam):
                states[f, step, level] = lam

            adjoint_step(coeffs, read, write, 0, surface_levels(step, levels))
            surface = surface + states[f, step, 0, :tile_lat, :tile_lon]
        surface = surface * mask0[:tile_lat, :tile_lon]
        for h in range(halves):
            at = (f * halves + h) * tile_lat
            own[at : at + tile_lat] = surface[:, h * BLOCK : (h + 1) * BLOCK]
        field = pl.ds(f * halves * tile_lat, halves * tile_lat)
        copies += fetch([(own.at[field], blocks.at[k, field]) for k in range(blocks.shape[0])], sent.at[f])
    for copy in copies:
        copy.wait()


def finish_adjoint(coeffs, start, states, adjoint_out, rest):
    levels = coeffs.shape[1]
    tile_lat, tile_lon = adjoint_out.shape[2:]
    for f in range(2):
        for step in range(STEPS):
            done = surface_levels(step, levels)

            def read(level):
                if not step:
                    return start[(2 + f) * levels + level]
                return (states if level < surface_levels(step - 1, levels) else rest)[f, step - 1, level]

            def write(level, lam):
                if step == STEPS - 1:
                    adjoint_out[f, level] = lam[:tile_lat, :tile_lon]
                else:
                    rest[f, step, level] = lam

            adjoint_step(coeffs, read, write, done, levels)


def sum_forcing(received, forcing, near, far):
    tile_lat = forcing.shape[1]
    halves = forcing.shape[2] // BLOCK - 1
    total = received[0]
    for j in range(1, received.shape[0]):
        total = total + received[j]
    lane = lanes((tile_lat, BLOCK))
    upper = total[2 * halves * tile_lat :]
    lower = jnp.where(lane[: tile_lat // 2] < BLOCK // 2, turn(upper, -2 * HALO, 1), turn(upper, 2 * HALO, 1))
    packed = jnp.concatenate([upper, lower], axis=0)
    for f in range(2):
        for h in range(halves):
            at = (f * halves + h) * tile_lat
            forcing[f, :, h * BLOCK : (h + 1) * BLOCK] = total[at : at + tile_lat]
        used = (lane < HALO) | (lane >= BLOCK - HALO)
        if f == 0:
            edge = packed
        else:
            edge = jnp.where(lane < HALO, turn(packed, -HALO, 1), turn(packed, HALO, 1))
        forcing[f, :, halves * BLOCK :] = jnp.where(used, edge, 0.0)
    row = rows((8, forcing.shape[2]))
    to_north = jnp.where(row < HALO, turn(forcing[0, tile_lat - 8 :], HALO, 0), forcing[1, tile_lat - 8 :])
    to_south = jnp.where(row < HALO, forcing[0, :8], turn(forcing[1, :8], HALO, 0))
    near[0], far[0] = sort_swap("lat", to_north, to_south)


def run_forward(coeffs, start, forcing, far, near, final, state):
    levels = coeffs.shape[1]
    tile_lat, tile_lon = final.shape[2:]
    for f in range(2):
        force = jnp.concatenate([forcing[f], edge_rows(near, far, f)], axis=0)
        force = force * coeffs[5, 0]
        for step in range(STEPS):
            above = None
            for level in range(levels):
                read = (lambda n: start[f * levels + n]) if step == 0 else (lambda n: state[(step - 1) % 2, n])
                theta = read(level)
                east_flux = coeffs[0, level] * theta + coeffs[1, level] * eastward(theta)
                north_flux = coeffs[2, level] * theta + coeffs[3, level] * northward(theta)
                out = theta - (east_flux - westward(east_flux)) - (north_flux - southward(north_flux))
                if level < levels - 1:
                    vertical = coeffs[4, level] * (theta - read(level + 1))
                    out = out - vertical
                if above is not None:
                    out = out + above
                above = vertical if level < levels - 1 else None
                if level == 0:
                    out = out + force
                if step == STEPS - 1:
                    final[f, level] = out[:tile_lat, :tile_lon]
                else:
                    state[step % 2, level] = out


def split(x):
    high = x.astype(bf16)
    return high, (x - high.astype(f32)).astype(bf16)


def weight_copies(weights, held, arrived):
    for g in range(held.shape[0]):
        yield pltpu.make_async_copy(weights.at[pl.ds(g * GROUP, GROUP)], held.at[g], arrived.at[g])


def fetch_weights(weights, held, arrived):
    for copy in weight_copies(weights, held, arrived):
        copy.start()


def held_part(weights, held, arrived):
    def part(r, g, u):
        if u == 0:

            @pl.when(r == 0)
            def _():
                pltpu.make_async_copy(weights.at[pl.ds(g * GROUP, GROUP)], held.at[g], arrived.at[g]).wait()

        return split(held[g, u])

    return part


def one_hot(where):
    return jnp.where(where, 1.0, 0.0).astype(bf16)


def places(slots, blocks):
    return 8 * (-(-2 * slots // (8 * blocks)) + 1)


def as_row(ids):
    return jnp.concatenate([ids[k : k + 1, :] for k in range(ids.shape[0])], axis=1)


def rank_slots(block_row, blocks):
    slots = block_row.shape[1]
    mine = rows((blocks, slots)) == block_row
    cuts = range(0, slots, BLOCK)
    stacked = jnp.concatenate([one_hot(mine[:, at : at + BLOCK]) for at in cuts], axis=0)
    shape = (BLOCK, 2 * BLOCK)
    counts = jnp.dot(stacked, one_hot(rows(shape) < lanes(shape)), preferred_element_type=f32)
    before, out = jnp.zeros((blocks, BLOCK), f32), []
    for n, at in enumerate(cuts):
        run = counts[n * blocks : (n + 1) * blocks]
        here = jnp.where(mine[:, at : at + BLOCK], run[:, :BLOCK] + before, 0.0)
        out.append(jnp.sum(here, axis=0, keepdims=True))
        before = before + run[:, BLOCK:]
    return jnp.concatenate(out, axis=1)


def find_slots(r, code, block_row, rank, capacity, blocks, found):
    slots = block_row.shape[1]
    mine = rows((blocks, slots)) == block_row
    ranked = one_hot(rows((capacity, slots)) == rank.astype(jnp.int32) - r * capacity)
    rest, codes = code + 1.0, None
    for base in (4096.0, 64.0, 1.0):
        digit = jnp.floor(rest * (1.0 / base))
        rest = rest - digit * base
        part = lax.dot_general(
            ranked,
            jnp.where(mine, digit, 0.0).astype(bf16),
            (((1,), (1,)), ((), ())),
            preferred_element_type=f32,
        )
        codes = part * base if codes is None else codes + part * base
    found[:, :blocks] = codes - 1.0


def couple(blocks, part, table, size, capacity, rounds, prepare, found, gather_first, transposed, result, scratch):
    column, vectors, products = scratch
    total_rows = column.shape[0]
    result[...] = jnp.zeros_like(result)

    def one_round(r, carry):
        prepare(r)
        codes = found[...]
        for w in range(blocks):
            column[w * capacity : (w + 1) * capacity] = jnp.broadcast_to(codes[:, w : w + 1], (capacity, BLOCK))
        eye = rows((BLOCK, BLOCK)) == lanes((BLOCK, BLOCK))
        place_hot = []
        for at in range(0, total_rows, BLOCK):
            code = column[at : at + BLOCK]
            first = jnp.floor((code + 0.5) * (1.0 / size))
            second = code - first * size
            gather, put = (first, second) if gather_first else (second, first)
            width = table.shape[0]
            gather = jnp.concatenate([gather] * (width // BLOCK), axis=1)
            hot = one_hot(gather == lanes((BLOCK, width)).astype(f32))
            vectors[at : at + BLOCK] = jnp.dot(hot, table, preferred_element_type=f32)
            put = jnp.sum(jnp.where(eye, put, 0.0), axis=0, keepdims=True)
            place_hot.append(one_hot(rows((result.shape[0], BLOCK)).astype(f32) == put))

        def group(g, carry):
            for u in range(GROUP):
                at = pl.multiple_of((g * GROUP + u) * capacity, 8)
                own = vectors[pl.ds(at, capacity)]
                left = jnp.concatenate([own[:, n * BLOCK : (n + 1) * BLOCK] for n in range(4)], axis=0)
                high, low = part(r, g, u)
                right = jnp.concatenate([high, low], axis=1 if transposed else 0)
                contract = (((1,), (0 if transposed else 1,)), ((), ()))
                product = lax.dot_general(left.astype(bf16), right, contract, preferred_element_type=f32)
                for f in range(2):
                    high_part = product[f * capacity : (f + 1) * capacity]
                    low_part = product[(f + 2) * capacity : (f + 3) * capacity, :BLOCK]
                    products[pl.ds(at, capacity), f * BLOCK : (f + 1) * BLOCK] = (
                        high_part[:, BLOCK:] + low_part
                    ) + high_part[:, :BLOCK]
            return carry

        lax.fori_loop(0, blocks // GROUP, group, 0)
        summed = jnp.dot(
            jnp.concatenate(place_hot, axis=1),
            jnp.concatenate(split(products[...]), axis=1),
            preferred_element_type=f32,
        )
        result[...] += summed[:, : 2 * BLOCK] + summed[:, 2 * BLOCK :]
        return carry

    lax.fori_loop(0, rounds, one_round, 0)


def slot_keys(ids, tile_lat, atm):
    lon_count, cap = ids.shape[3:]
    ocean, atm_ids, block_ids = (ids[n, 0, 0] for n in range(3))
    order = (ocean & 1) * tile_lat + (ocean >> 1) + rows((lon_count, cap)) * (2 * tile_lat)
    order = jnp.where(ocean >= 0, order, lon_count * 2 * tile_lat)
    return as_row((order * atm + atm_ids).astype(f32)), as_row(block_ids)


def weigh(atm_near, margins, weights, after, sums, found, keys, result, *scratch):
    scratch, (held, arrived) = scratch[:3], scratch[3:]
    fetch_weights(weights, held, arrived)
    lon_count = margins.shape[3]
    atm = atm_near.shape[2]
    blocks = weights.shape[0]
    tile_lat = 2 * sums.shape[1] // 9
    code, block_row = slot_keys(margins, tile_lat, atm)
    rank = rank_slots(block_row, blocks)
    keys[0:1] = code
    keys[1:2] = block_row.astype(f32)
    keys[2:3] = rank
    capacity = places(code.shape[1], blocks)
    rounds = jnp.max(rank).astype(jnp.int32) // capacity + 1
    parts = [split(atm_near[f, 0]) for f in range(2)]
    table = jnp.concatenate([parts[f][n] for n in range(2) for f in range(2)], axis=1)

    def prepare(r):
        find_slots(rounds - 1 - r, code, block_row, rank, capacity, blocks, found)

    part = held_part(weights, held, arrived)
    couple(blocks, part, table, atm, capacity, rounds, prepare, found, False, False, result, scratch)
    lane = lanes((tile_lat, BLOCK))

    def block_sums(k, f, h):
        at = (2 * k + h) * tile_lat
        return result[at : at + tile_lat, f * BLOCK : (f + 1) * BLOCK]

    for n, k in enumerate(group_order(lon_count)):
        edge = jnp.zeros((tile_lat, BLOCK), f32)
        for f in range(2):
            for h in range(2):
                sums[n, (2 * f + h) * tile_lat : (2 * f + h + 1) * tile_lat] = block_sums(k, f, h)
            at = f * HALO
            after = turn(block_sums((k + 1) % lon_count, f, 0), at, 1)
            before = turn(block_sums((k - 1) % lon_count, f, 1), -at, 1)
            edge = jnp.where((lane >= at) & (lane < at + HALO), after, edge)
            end = BLOCK - at
            edge = jnp.where((lane >= end - HALO) & (lane < end), before, edge)
        upper, lower = edge[: tile_lat // 2], edge[tile_lat // 2 :]
        near = lane[: tile_lat // 2]
        lower = jnp.where(near < BLOCK // 2, turn(lower, 2 * HALO, 1), turn(lower, -2 * HALO, 1))
        sums[n, 4 * tile_lat :] = jnp.where((near < 2 * HALO) | (near >= BLOCK - 2 * HALO), upper, lower)


def unweigh(gathered, found, keys, weights, gradient, result, codes, *scratch):
    scratch, (held, arrived) = scratch[:3], scratch[3:]
    fetch_weights(weights, held, arrived)
    atm = gradient.shape[2]
    blocks = weights.shape[0]
    lon_count, ocean_blocks = gathered.shape[0], gathered.shape[1] // 2
    order = group_order(lon_count)
    capacity = places(keys.shape[1], blocks)
    rounds = jnp.max(keys[2:3]).astype(jnp.int32) // capacity + 1
    parts = [
        split(
            jnp.concatenate(
                [gathered[order.index(k), f * ocean_blocks : (f + 1) * ocean_blocks] for k in range(lon_count)],
                axis=0,
            )
        )
        for f in range(2)
    ]
    table = jnp.concatenate([parts[f][n] for n in range(2) for f in range(2)], axis=1)

    def prepare(r):
        @pl.when(r == 0)
        def _():
            codes[...] = found[...]

        @pl.when(r > 0)
        def _():
            find_slots(r, keys[0:1], keys[1:2].astype(jnp.int32), keys[2:3], capacity, blocks, codes)

    couple(
        blocks,
        held_part(weights, held, arrived),
        table,
        atm,
        capacity,
        rounds,
        prepare,
        codes,
        True,
        True,
        result,
        scratch,
    )
    for f in range(2):
        gradient[f, 0] = result[:, f * BLOCK : (f + 1) * BLOCK]


def on_device(tracers, cotangent, land_mask, diffusion, velocity, weights, atm_state, margins):
    levels, tile_lat, tile_lon = land_mask.shape
    lon_count = lax.axis_size("lon")
    slots = lon_count * margins.shape[4]
    halves = tile_lon // BLOCK
    count = 9 * levels - 1
    parts = -(-count // PER_LANES)
    inputs = (tracers, cotangent, land_mask, diffusion, velocity)

    def in_vmem(s):
        return pltpu.VMEM(s.shape, s.dtype)

    message = (parts, tile_lat, BLOCK)
    fields, near, far, atm_near, margins_near = call(
        pack_columns,
        [
            (count, tile_lat, tile_lon),
            message,
            message,
            atm_state.shape,
            jax.ShapeDtypeStruct(margins.shape, margins.dtype),
        ],
        [*map(in_vmem, inputs), pltpu.SemaphoreType.DMA((7,))],
        name="pack_columns",
        inputs=7,
        far=range(7),
    )(*inputs, atm_state, margins)
    near_columns, far_columns = swap(near, far, "lon", True)

    blocks_of, atm = weights.shape[0], atm_state.shape[2]
    groups = blocks_of // GROUP
    sum_rows = 2 * halves * tile_lat + tile_lat // 2
    ocean_blocks = lon_count * halves * tile_lat
    held_rows = -(-places(slots, blocks_of) * blocks_of // BLOCK) * BLOCK

    def coupling_scratch(result_rows):
        return [
            pltpu.VMEM((result_rows, 2 * BLOCK), f32),
            pltpu.VMEM((held_rows, BLOCK), f32),
            pltpu.VMEM((held_rows, 4 * BLOCK), f32),
            pltpu.VMEM((held_rows, 2 * BLOCK), f32),
            pltpu.VMEM((groups, GROUP, BLOCK, BLOCK), f32),
            pltpu.SemaphoreType.DMA((groups,)),
        ]

    coupling_flops = 4 * slots * blocks_of * 2 * BLOCK * BLOCK * 2
    sums, found, keys = call(
        weigh,
        [(lon_count, sum_rows, BLOCK), (places(slots, blocks_of), BLOCK), (8, slots)],
        coupling_scratch(ocean_blocks),
        coupling_flops,
        name="weigh",
        inputs=4,
        far=(2,),
    )(atm_near, margins_near, weights, far)

    sources = count * halves + 2 * parts
    message = (-(-sources // 2), 8, BLOCK)
    columns = (parts, tile_lat, BLOCK)
    (sums,) = call(hold, [sums.shape], name="hold", inputs=2, aliases={0: 0})(sums, near_columns)
    near, far, from_west, from_east = call(
        pack_rows, [message, message, columns, columns], name="pack_rows", inputs=3
    )(fields, near_columns, far_columns)
    received = exchange(sums)
    near_rows, far_rows = swap(near, far, "lat", False)

    wide = (tile_lat + 8, tile_lon + BLOCK)
    own = (2 * halves * tile_lat, BLOCK)
    adjoint_states = (2, STEPS - 1, levels, *wide)
    blocks, coeffs, start, states = call(
        run_adjoint,
        [(lon_count, *own), (6, levels, *wide), (4 * levels, *wide), adjoint_states],
        [
            pltpu.VMEM((count - 4 * levels, *wide), f32),
            pltpu.VMEM(own, f32),
            pltpu.SemaphoreType.DMA((2, lon_count)),
        ],
        name="run_adjoint",
        inputs=5,
        far_outs=(0,),
    )(fields, from_west, from_east, far_rows, near_rows)
    gathered = exchange(blocks)

    message = (1, 8, tile_lon + BLOCK)
    forcing, near, far = call(
        sum_forcing, [(2, tile_lat, tile_lon + BLOCK), message, message], name="sum_forcing", inputs=1
    )(received)
    near_rows, far_rows = swap(near, far, "lat", False)
    (adjoint,) = call(
        finish_adjoint,
        [cotangent.shape],
        [pltpu.VMEM(adjoint_states, f32)],
        name="finish_adjoint",
        inputs=3,
    )(coeffs, start, states)
    (final,) = call(
        run_forward,
        [tracers.shape],
        [pltpu.VMEM((2, levels, *wide), f32)],
        name="run_forward",
        inputs=5,
    )(coeffs, start, forcing, far_rows, near_rows)

    (gradient,) = call(
        unweigh,
        [atm_state.shape],
        [coupling_scratch(atm)[0], in_vmem(found), *coupling_scratch(atm)[1:]],
        coupling_flops,
        name="unweigh",
        inputs=4,
        far=(3,),
    )(gathered, found, keys, weights)
    return (final, adjoint, gradient)


def solution(mesh):
    return jax.shard_map(
        on_device,
        mesh=mesh,
        in_specs=(
            P(None, None, "lat", "lon"),
            P(None, None, "lat", "lon"),
            P(None, "lat", "lon"),
            P(None, None, "lat", "lon"),
            P(None, None, "lat", "lon"),
            P(),
            P(None, "lat", "lon", None),
            P(None, "lat", "lon", None, None),
        ),
        out_specs=(
            P(None, None, "lat", "lon"),
            P(None, None, "lat", "lon"),
            P(None, "lat", "lon", None),
        ),
        check_vma=False,
    )
```

```python
import jax
import jax.numpy as jnp
from jax import lax
from jax.experimental import pallas as pl
from jax.experimental.pallas import tpu as pltpu
from jax.sharding import PartitionSpec as P

BLOCK = 128
STEPS = 4
HALO = STEPS
PER_LANES = BLOCK // HALO
GROUP = 16
f32 = jnp.float32
bf16 = jnp.bfloat16
VMEM_LIMIT = 20 * 1024 * 1024


def call(body, outs, scratch=(), flops=0, name=None, inputs=0, far=(), far_outs=(), aliases=None):
    outs = [s if isinstance(s, jax.ShapeDtypeStruct) else jax.ShapeDtypeStruct(s, f32) for s in outs]
    near = pl.BlockSpec(memory_space=pltpu.VMEM)
    aliases = aliases or {}
    kernel = pl.pallas_call(
        body,
        out_shape=outs,
        in_specs=[
            pl.BlockSpec(memory_space=pl.ANY)
            if n in aliases
            else pl.BlockSpec(memory_space=pltpu.HBM)
            if n in far
            else near
            for n in range(inputs)
        ],
        out_specs=[
            pl.BlockSpec(memory_space=pl.ANY) if n in aliases.values() or n in far_outs else near
            for n in range(len(outs))
        ],
        input_output_aliases=aliases,
        scratch_shapes=list(scratch),
        compiler_params=pltpu.CompilerParams(vmem_limit_bytes=VMEM_LIMIT),
        cost_estimate=pl.CostEstimate(flops=flops, bytes_accessed=1 << 20, transcendentals=0),
        name=name,
    )

    def run(*args):
        return kernel(
            *(pltpu.with_memory_space_constraint(x, pltpu.HBM) if n in far else x for n, x in enumerate(args))
        )

    return run


def lanes(shape):
    return lax.broadcasted_iota(jnp.int32, shape, len(shape) - 1)


def rows(shape):
    return lax.broadcasted_iota(jnp.int32, shape, len(shape) - 2)


def turn(x, shift, axis):
    shift %= x.shape[axis]
    return pltpu.roll(x, shift, axis) if shift else x


def group_order(count):
    half = count // 2
    return [k for n in range(half) for k in (half + n, n)]


def exchange(x):
    order = group_order(x.shape[0])
    return lax.all_to_all(x, "lon", split_axis=0, concat_axis=0, tiled=True, axis_index_groups=[order])


def swap(near, far, axis, wrap):
    count = lax.axis_size(axis)
    pairs = [[], []]
    for i in range(count if wrap else count - 1):
        j = (i + 1) % count
        pairs[i % 2] += [(i, j), (j, i)]
    far = lax.ppermute(far, axis, pairs[1])
    return lax.ppermute(near, axis, pairs[0]), far


def sort_swap(axis, after, before):
    odd = lax.rem(lax.axis_index(axis), 2) == 1
    return jnp.where(odd, before, after), jnp.where(odd, after, before)


def tile_fields(tracers, cotangent, land_mask, diffusion, velocity):
    levels = land_mask.shape[0]
    mask = [land_mask[level].astype(f32) for level in range(levels)]
    out = [tracers[f, level] for f in range(2) for level in range(levels)]
    out += [cotangent[f, level] for f in range(2) for level in range(levels)]
    out += [diffusion[0, level] * mask[level] for level in range(levels)]
    out += [velocity[0, level] * mask[level] for level in range(levels)]
    out += [diffusion[1, level] * mask[level] for level in range(levels)]
    out += [velocity[1, level] * mask[level] for level in range(levels)]
    out += [diffusion[2, level] * mask[level] * mask[level + 1] for level in range(levels - 1)]
    return out


def fetch(pairs, arrived):
    copies = [pltpu.make_async_copy(src, dst, arrived.at[n]) for n, (src, dst) in enumerate(pairs)]
    for copy in copies:
        copy.start()
    return copies


def pack_columns(*refs):
    inputs, (fields, near, far), scratch = refs[:7], refs[7:10], refs[12:]
    copies = fetch(zip(inputs, [*scratch[:5], *refs[10:12]]), scratch[5])
    for copy in copies[:5]:
        copy.wait()
    shape = near.shape[1:]
    lane = lanes(shape)
    west = [jnp.zeros(shape, f32) for _ in range(near.shape[0])]
    east = [jnp.zeros(shape, f32) for _ in range(near.shape[0])]
    for i, field in enumerate(tile_fields(*scratch[:5])):
        fields[i] = field
        part, at = divmod(i, PER_LANES)
        at *= HALO
        here = (lane >= at) & (lane < at + HALO)
        west[part] = jnp.where(here, turn(field[:, :BLOCK], at, 1), west[part])
        east[part] = jnp.where(here, turn(field[:, -BLOCK:], at + HALO, 1), east[part])
    for part in range(near.shape[0]):
        near[part], far[part] = sort_swap("lon", east[part], west[part])
    for copy in copies[5:]:
        copy.wait()


def unpack_columns(from_west, from_east, i):
    part, at = divmod(i, PER_LANES)
    at *= HALO
    lane = lanes(from_west[part].shape)
    east = turn(from_east[part], -at, 1)
    west = turn(from_west[part], -at - HALO, 1)
    return jnp.where(lane < HALO, east, jnp.where(lane >= BLOCK - HALO, west, 0.0))


def row_sources(fields, from_west, from_east):
    out = [(fields, (i, slice(None), slice(h * BLOCK, (h + 1) * BLOCK)))
           for i in range(fields.shape[0]) for h in range(fields.shape[2] // BLOCK)]
    for columns in (from_west, from_east):
        out += [(columns, (part,)) for part in range(columns.shape[0])]
    return out


def pack_rows(fields, near_columns, far_columns, sums, near, far, from_west, from_east, same_sums):
    for part in range(from_west.shape[0]):
        from_east[part], from_west[part] = sort_swap("lon", near_columns[part], far_columns[part])
    sources = [ref[at] for ref, at in row_sources(fields, from_west, from_east)]
    half = near.shape[0]
    row = rows((8, BLOCK))
    for i in range(half):
        first = sources[i]
        second = sources[i + half] if i + half < len(sources) else jnp.zeros_like(first)
        to_north = jnp.where(row < HALO, turn(first[-8:], HALO, 0), second[-8:])
        to_south = jnp.where(row < HALO, first[:8], turn(second[:8], HALO, 0))
        near[i], far[i] = sort_swap("lat", to_north, to_south)


def edge_rows(near, far, i):
    half = near.shape[0]
    from_north, from_south = sort_swap("lat", near[i % half], far[i % half])
    if i < half:
        from_south = turn(from_south, HALO, 0)
    else:
        from_north = turn(from_north, HALO, 0)
    return jnp.where(rows(from_north.shape) < HALO, from_north, from_south)


def widen(fields, from_west, from_east, near, far, start, wide):
    count, tile_lat, tile_lon = fields.shape
    halves = tile_lon // BLOCK
    parts = from_west.shape[0]
    corners = [edge_rows(near, far, count * halves + n) for n in range(2 * parts)]
    for i in range(count):
        out = start.at[i] if i < start.shape[0] else wide.at[i - start.shape[0]]
        out[:tile_lat, :tile_lon] = fields[i]
        out[:tile_lat, tile_lon:] = unpack_columns(from_west, from_east, i)
        for h in range(halves):
            out[tile_lat:, h * BLOCK : (h + 1) * BLOCK] = edge_rows(near, far, i * halves + h)
        out[tile_lat:, tile_lon:] = unpack_columns(corners[:parts], corners[parts:], i)


def eastward(x):
    return turn(x, -1, 1)


def westward(x):
    return turn(x, 1, 1)


def northward(x):
    return turn(x, -1, 0)


def southward(x):
    return turn(x, 1, 0)


def adjoint_step(coeffs, read, write, first, last):
    levels = coeffs.shape[1]
    above = coeffs[4, first - 1] * (read(first) - read(first - 1)) if first else None
    for level in range(first, last):
        lam = read(level)
        step_x = eastward(lam) - lam
        step_y = northward(lam) - lam
        out = lam + coeffs[0, level] * step_x + westward(coeffs[1, level] * step_x)
        out = out + coeffs[2, level] * step_y + southward(coeffs[3, level] * step_y)
        if above is not None:
            out = out - above
        if level < levels - 1:
            above = coeffs[4, level] * (read(level + 1) - lam)
            out = out + above
        write(level, out)


def surface_levels(step, levels):
    return min(levels, STEPS - 1 - step)


def run_adjoint(
    fields, from_west, from_east, far, near, blocks, coeffs, start, states, wide, own, sent
):
    levels = coeffs.shape[1]
    tile_lat, tile_lon = fields.shape[1:]
    halves = tile_lon // BLOCK
    widen(fields, from_west, from_east, near, far, start, wide)
    base = 0
    mask0 = None
    for level in range(levels):
        east_d, east_u = wide[base + level], wide[base + levels + level]
        north_d, north_u = wide[base + 2 * levels + level], wide[base + 3 * levels + level]
        mask = (east_d > 0.0).astype(f32)
        mask0 = mask if mask0 is None else mask0
        mask_e, mask_n = eastward(mask), northward(mask)
        east_k, east_v = east_d * mask_e, east_u * mask_e
        north_k, north_v = north_d * mask_n, north_u * mask_n
        coeffs[0, level] = jnp.maximum(east_v, 0.0) + east_k
        coeffs[1, level] = jnp.minimum(east_v, 0.0) - east_k
        coeffs[2, level] = jnp.maximum(north_v, 0.0) + north_k
        coeffs[3, level] = jnp.minimum(north_v, 0.0) - north_k
        coeffs[4, level] = wide[base + 4 * levels + level] if level < levels - 1 else jnp.zeros_like(mask)
        coeffs[5, level] = mask
    copies = []
    for f in range(2):
        surface = start[(2 + f) * levels, :tile_lat, :tile_lon]
        for step in range(STEPS - 1):

            def read(level):
                return states[f, step - 1, level] if step else start[(2 + f) * levels + level]

            def write(level, lam):
                states[f, step, level] = lam

            adjoint_step(coeffs, read, write, 0, surface_levels(step, levels))
            surface = surface + states[f, step, 0, :tile_lat, :tile_lon]
        surface = surface * mask0[:tile_lat, :tile_lon]
        for h in range(halves):
            at = (f * halves + h) * tile_lat
            own[at : at + tile_lat] = surface[:, h * BLOCK : (h + 1) * BLOCK]
        field = pl.ds(f * halves * tile_lat, halves * tile_lat)
        copies += fetch([(own.at[field], blocks.at[k, field]) for k in range(blocks.shape[0])], sent.at[f])
    for copy in copies:
        copy.wait()


def finish_adjoint(coeffs, start, states, adjoint_out, rest):
    levels = coeffs.shape[1]
    tile_lat, tile_lon = adjoint_out.shape[2:]
    for f in range(2):
        for step in range(STEPS):
            done = surface_levels(step, levels)

            def read(level):
                if not step:
                    return start[(2 + f) * levels + level]
                return (states if level < surface_levels(step - 1, levels) else rest)[f, step - 1, level]

            def write(level, lam):
                if step == STEPS - 1:
                    adjoint_out[f, level] = lam[:tile_lat, :tile_lon]
                else:
                    rest[f, step, level] = lam

            adjoint_step(coeffs, read, write, done, levels)


def sum_forcing(received, forcing, near, far):
    tile_lat = forcing.shape[1]
    halves = forcing.shape[2] // BLOCK - 1
    total = received[0]
    for j in range(1, received.shape[0]):
        total = total + received[j]
    lane = lanes((tile_lat, BLOCK))
    upper = total[2 * halves * tile_lat :]
    lower = jnp.where(lane[: tile_lat // 2] < BLOCK // 2, turn(upper, -2 * HALO, 1), turn(upper, 2 * HALO, 1))
    packed = jnp.concatenate([upper, lower], axis=0)
    for f in range(2):
        for h in range(halves):
            at = (f * halves + h) * tile_lat
            forcing[f, :, h * BLOCK : (h + 1) * BLOCK] = total[at : at + tile_lat]
        used = (lane < HALO) | (lane >= BLOCK - HALO)
        if f == 0:
            edge = packed
        else:
            edge = jnp.where(lane < HALO, turn(packed, -HALO, 1), turn(packed, HALO, 1))
        forcing[f, :, halves * BLOCK :] = jnp.where(used, edge, 0.0)
    row = rows((8, forcing.shape[2]))
    to_north = jnp.where(row < HALO, turn(forcing[0, tile_lat - 8 :], HALO, 0), forcing[1, tile_lat - 8 :])
    to_south = jnp.where(row < HALO, forcing[0, :8], turn(forcing[1, :8], HALO, 0))
    near[0], far[0] = sort_swap("lat", to_north, to_south)


def run_forward(coeffs, start, forcing, far, near, final, state):
    levels = coeffs.shape[1]
    tile_lat, tile_lon = final.shape[2:]
    for f in range(2):
        force = jnp.concatenate([forcing[f], edge_rows(near, far, f)], axis=0)
        force = force * coeffs[5, 0]
        for step in range(STEPS):
            above = None
            for level in range(levels):
                read = (lambda n: start[f * levels + n]) if step == 0 else (lambda n: state[(step - 1) % 2, n])
                theta = read(level)
                east_flux = coeffs[0, level] * theta + coeffs[1, level] * eastward(theta)
                north_flux = coeffs[2, level] * theta + coeffs[3, level] * northward(theta)
                out = theta - (east_flux - westward(east_flux)) - (north_flux - southward(north_flux))
                if level < levels - 1:
                    vertical = coeffs[4, level] * (theta - read(level + 1))
                    out = out - vertical
                if above is not None:
                    out = out + above
                above = vertical if level < levels - 1 else None
                if level == 0:
                    out = out + force
                if step == STEPS - 1:
                    final[f, level] = out[:tile_lat, :tile_lon]
                else:
                    state[step % 2, level] = out


def split(x):
    high = x.astype(bf16)
    return high, (x - high.astype(f32)).astype(bf16)


def weight_copies(weights, held, arrived):
    for g in range(held.shape[0]):
        yield pltpu.make_async_copy(weights.at[pl.ds(g * GROUP, GROUP)], held.at[g], arrived.at[g])


def fetch_weights(weights, held, arrived):
    for copy in weight_copies(weights, held, arrived):
        copy.start()


def held_part(weights, held, arrived):
    def part(r, g, u):
        if u == 0:

            @pl.when(r == 0)
            def _():
                pltpu.make_async_copy(weights.at[pl.ds(g * GROUP, GROUP)], held.at[g], arrived.at[g]).wait()

        return split(held[g, u])

    return part


def one_hot(where):
    return jnp.where(where, 1.0, 0.0).astype(bf16)


def places(slots, blocks):
    return 8 * (-(-2 * slots // (8 * blocks)) + 1)


def round_chunks(slots, blocks):
    return -(-(slots + 7 * blocks) // BLOCK)


def as_row(ids):
    return jnp.concatenate([ids[k : k + 1, :] for k in range(ids.shape[0])], axis=1)


def rank_slots(block_row, blocks):
    slots = block_row.shape[1]
    mine = rows((blocks, slots)) == block_row
    cuts = range(0, slots, BLOCK)
    stacked = jnp.concatenate([one_hot(mine[:, at : at + BLOCK]) for at in cuts], axis=0)
    shape = (BLOCK, 2 * BLOCK)
    counts = jnp.dot(stacked, one_hot(rows(shape) < lanes(shape)), preferred_element_type=f32)
    before, out = jnp.zeros((blocks, BLOCK), f32), []
    for n, at in enumerate(cuts):
        run = counts[n * blocks : (n + 1) * blocks]
        here = jnp.where(mine[:, at : at + BLOCK], run[:, :BLOCK] + before, 0.0)
        out.append(jnp.sum(here, axis=0, keepdims=True))
        before = before + run[:, BLOCK:]
    return jnp.concatenate(out, axis=1), before


def find_slots(r, keys, counts, capacity, columns, lines, starts):
    slots = keys.shape[1]
    blocks = counts.shape[0]
    atm_row, ocean_row, block_row, rank = (keys[n : n + 1] for n in range(4))
    count = jnp.clip(counts - r * capacity, 0.0, capacity)
    tiles = jnp.floor((count + 7.0) * 0.125) * 8.0
    shape = (blocks, blocks)
    first = jnp.dot(one_hot(lanes(shape) < rows(shape)), tiles.astype(bf16), preferred_element_type=f32)
    starts[...] = first.astype(jnp.int32)
    mine = rows((blocks, slots)).astype(f32) == block_row
    own = jnp.where(mine, jnp.concatenate([first] * (slots // BLOCK), axis=1), 0.0)
    place = rank - r * capacity
    here = (place >= 0.0) & (place < capacity)
    place = jnp.where(here, jnp.sum(own, axis=0, keepdims=True) + place, -1.0)
    run = jnp.floor(place * (1.0 / BLOCK))
    low = one_hot(rows((BLOCK, slots)).astype(f32) == place - run * BLOCK)
    size = lines.shape[1]
    in_run = rows((size, slots)).astype(f32) == run
    ocean_high = jnp.floor(ocean_row * (1.0 / BLOCK))
    digits = [atm_row, ocean_high, ocean_row - ocean_high * BLOCK]
    digits = [jnp.where(in_run, digit, 0.0).astype(bf16) for digit in digits]
    across = (((1,), (1,)), ((), ()))
    down = [lax.dot_general(low, digit, across, preferred_element_type=f32) for digit in digits]
    along = [lax.dot_general(digit, low, across, preferred_element_type=f32) for digit in digits]
    columns[0, :, :size], columns[1, :, :size] = down[0], down[1] * BLOCK + down[2] - 1.0
    ocean = along[1] * BLOCK + along[2] - 1.0
    lines[0], lines[1] = jnp.where(ocean < 0.0, -1.0, along[0]), ocean


def couple(part, table, capacity, rounds, prepare, columns, lines, starts, transposed, result, scratch):
    vectors, products, starts_near, moved = scratch
    blocks = starts.shape[0]
    total_rows = vectors.shape[0] - capacity
    width = table.shape[0]
    result[...] = jnp.zeros_like(result)
    products[...] = jnp.zeros_like(products)

    def one_round(r, carry):
        prepare(r)
        move = pltpu.make_async_copy(starts, starts_near, moved)
        move.start()
        place_hot = []
        for n in range(total_rows // BLOCK):
            gather = jnp.broadcast_to(columns[int(transposed), :, n : n + 1], (BLOCK, BLOCK))
            gather = jnp.concatenate([gather] * (width // BLOCK), axis=1)
            hot = one_hot(gather == lanes((BLOCK, width)).astype(f32))
            vectors[n * BLOCK : (n + 1) * BLOCK] = jnp.dot(hot, table, preferred_element_type=f32)
            put = lines[1 - int(transposed), n : n + 1]
            place_hot.append(one_hot(rows((result.shape[0], BLOCK)).astype(f32) == put))
        move.wait()

        def group(g, carry):
            for u in range(GROUP):
                at = pl.ds(pl.multiple_of(starts_near[g * GROUP + u, 0], 8), capacity)
                own = vectors[at]
                left = jnp.concatenate([own[:, n * BLOCK : (n + 1) * BLOCK] for n in range(4)], axis=0)
                high, low = part(r, g, u)
                right = jnp.concatenate([high, low], axis=1 if transposed else 0)
                contract = (((1,), (0 if transposed else 1,)), ((), ()))
                product = lax.dot_general(left.astype(bf16), right, contract, preferred_element_type=f32)
                for f in range(2):
                    high_part = product[f * capacity : (f + 1) * capacity]
                    low_part = product[(f + 2) * capacity : (f + 3) * capacity, :BLOCK]
                    products[at, f * BLOCK : (f + 1) * BLOCK] = (
                        high_part[:, BLOCK:] + low_part
                    ) + high_part[:, :BLOCK]
            return carry

        lax.fori_loop(0, blocks // GROUP, group, 0)
        summed = jnp.dot(
            jnp.concatenate(place_hot, axis=1),
            jnp.concatenate(split(products[:total_rows]), axis=1),
            preferred_element_type=f32,
        )
        result[...] += summed[:, : 2 * BLOCK] + summed[:, 2 * BLOCK :]
        return carry

    lax.fori_loop(0, rounds, one_round, 0)


def slot_keys(ids, tile_lat, keys):
    lon_count, cap = ids.shape[3:]
    ocean, atm_ids, block_ids = (ids[n, 0, 0] for n in range(3))
    order = (ocean & 1) * tile_lat + (ocean >> 1) + rows((lon_count, cap)) * (2 * tile_lat)
    order = jnp.where(ocean >= 0, order, lon_count * 2 * tile_lat) + 1
    for n, part in enumerate((atm_ids, order, block_ids)):
        keys[n : n + 1] = as_row(part.astype(f32))


def weigh(
    atm_near, margins, weights, after, sums, keys, counts, columns, lines, starts, result, *scratch
):
    scratch, (held, arrived) = scratch[:4], scratch[4:]
    fetch_weights(weights, held, arrived)
    lon_count = margins.shape[3]
    blocks = weights.shape[0]
    tile_lat = 2 * sums.shape[1] // 9
    slot_keys(margins, tile_lat, keys)
    rank, count = rank_slots(keys[2:3].astype(jnp.int32), blocks)
    keys[3:4] = rank
    counts[...] = count
    capacity = places(keys.shape[1], blocks)
    rounds = jnp.max(rank).astype(jnp.int32) // capacity + 1
    parts = [split(atm_near[f, 0]) for f in range(2)]
    table = jnp.concatenate([parts[f][n] for n in range(2) for f in range(2)], axis=1)
    part = held_part(weights, held, arrived)

    def prepare(r):
        find_slots((rounds - 1 - r).astype(f32), keys, counts[...], capacity, columns, lines, starts)

    couple(part, table, capacity, rounds, prepare, columns, lines, starts, False, result, scratch)
    lane = lanes((tile_lat, BLOCK))

    def block_sums(k, f, h):
        at = (2 * k + h) * tile_lat
        return result[at : at + tile_lat, f * BLOCK : (f + 1) * BLOCK]

    for n, k in enumerate(group_order(lon_count)):
        edge = jnp.zeros((tile_lat, BLOCK), f32)
        for f in range(2):
            for h in range(2):
                sums[n, (2 * f + h) * tile_lat : (2 * f + h + 1) * tile_lat] = block_sums(k, f, h)
            at = f * HALO
            after = turn(block_sums((k + 1) % lon_count, f, 0), at, 1)
            before = turn(block_sums((k - 1) % lon_count, f, 1), -at, 1)
            edge = jnp.where((lane >= at) & (lane < at + HALO), after, edge)
            end = BLOCK - at
            edge = jnp.where((lane >= end - HALO) & (lane < end), before, edge)
        upper, lower = edge[: tile_lat // 2], edge[tile_lat // 2 :]
        near = lane[: tile_lat // 2]
        lower = jnp.where(near < BLOCK // 2, turn(lower, 2 * HALO, 1), turn(lower, -2 * HALO, 1))
        sums[n, 4 * tile_lat :] = jnp.where((near < 2 * HALO) | (near >= BLOCK - 2 * HALO), upper, lower)


def unweigh(
    gathered, keys, counts, columns_in, lines_in, starts_in, weights, gradient, result, columns, lines, starts, *scratch
):
    scratch, (held, arrived) = scratch[:4], scratch[4:]
    fetch_weights(weights, held, arrived)
    blocks = weights.shape[0]
    lon_count, ocean_blocks = gathered.shape[0], gathered.shape[1] // 2
    order = group_order(lon_count)
    capacity = places(keys.shape[1], blocks)
    rounds = jnp.max(keys[3:4]).astype(jnp.int32) // capacity + 1
    parts = [
        split(
            jnp.concatenate(
                [gathered[order.index(k), f * ocean_blocks : (f + 1) * ocean_blocks] for k in range(lon_count)],
                axis=0,
            )
        )
        for f in range(2)
    ]
    table = jnp.concatenate([parts[f][n] for n in range(2) for f in range(2)], axis=1)

    def prepare(r):
        @pl.when(r == 0)
        def _():
            columns[...] = columns_in[...]
            lines[...] = lines_in[...]
            starts[...] = starts_in[...]

        @pl.when(r > 0)
        def _():
            find_slots(r.astype(f32), keys, counts[...], capacity, columns, lines, starts)

    part = held_part(weights, held, arrived)
    couple(part, table, capacity, rounds, prepare, columns, lines, starts, True, result, scratch)
    for f in range(2):
        gradient[f, 0] = result[:, f * BLOCK : (f + 1) * BLOCK]


def on_device(tracers, cotangent, land_mask, diffusion, velocity, weights, atm_state, margins):
    levels, tile_lat, tile_lon = land_mask.shape
    lon_count = lax.axis_size("lon")
    slots = lon_count * margins.shape[4]
    halves = tile_lon // BLOCK
    count = 9 * levels - 1
    parts = -(-count // PER_LANES)
    inputs = (tracers, cotangent, land_mask, diffusion, velocity)

    def in_vmem(s):
        return pltpu.VMEM(s.shape, s.dtype)

    message = (parts, tile_lat, BLOCK)
    fields, near, far, atm_near, margins_near = call(
        pack_columns,
        [
            (count, tile_lat, tile_lon),
            message,
            message,
            atm_state.shape,
            jax.ShapeDtypeStruct(margins.shape, margins.dtype),
        ],
        [*map(in_vmem, inputs), pltpu.SemaphoreType.DMA((7,))],
        name="pack_columns",
        inputs=7,
        far=range(7),
    )(*inputs, atm_state, margins)
    near_columns, far_columns = swap(near, far, "lon", True)

    blocks_of, atm = weights.shape[0], atm_state.shape[2]
    groups = blocks_of // GROUP
    sum_rows = 2 * halves * tile_lat + tile_lat // 2
    ocean_blocks = lon_count * halves * tile_lat
    chunks = round_chunks(slots, blocks_of)
    held_rows = chunks * BLOCK + places(slots, blocks_of)

    def coupling_scratch(result_rows):
        return [
            pltpu.VMEM((result_rows, 2 * BLOCK), f32),
            pltpu.VMEM((held_rows, 4 * BLOCK), f32),
            pltpu.VMEM((held_rows, 2 * BLOCK), f32),
            pltpu.SMEM((blocks_of, BLOCK), jnp.int32),
            pltpu.SemaphoreType.DMA,
            pltpu.VMEM((groups, GROUP, BLOCK, BLOCK), f32),
            pltpu.SemaphoreType.DMA((groups,)),
        ]

    coupling_flops = 4 * slots * blocks_of * 2 * BLOCK * BLOCK * 2
    found = [
        jax.ShapeDtypeStruct((2, BLOCK, BLOCK), f32),
        jax.ShapeDtypeStruct((2, -(-chunks // 8) * 8, BLOCK), f32),
        jax.ShapeDtypeStruct((blocks_of, BLOCK), jnp.int32),
    ]
    sums, *slot_data = call(
        weigh,
        [(lon_count, sum_rows, BLOCK), (8, slots), (blocks_of, BLOCK), *found],
        coupling_scratch(ocean_blocks),
        coupling_flops,
        name="weigh",
        inputs=4,
        far=(2,),
    )(atm_near, margins_near, weights, far)

    sources = count * halves + 2 * parts
    message = (-(-sources // 2), 8, BLOCK)
    columns = (parts, tile_lat, BLOCK)
    near, far, from_west, from_east, sums = call(
        pack_rows,
        [message, message, columns, columns, sums.shape],
        name="pack_rows",
        inputs=4,
        aliases={3: 4},
    )(fields, near_columns, far_columns, sums)
    received = exchange(sums)
    near_rows, far_rows = swap(near, far, "lat", False)

    wide = (tile_lat + 8, tile_lon + BLOCK)
    own = (2 * halves * tile_lat, BLOCK)
    adjoint_states = (2, STEPS - 1, levels, *wide)
    blocks, coeffs, start, states = call(
        run_adjoint,
        [(lon_count, *own), (6, levels, *wide), (4 * levels, *wide), adjoint_states],
        [
            pltpu.VMEM((count - 4 * levels, *wide), f32),
            pltpu.VMEM(own, f32),
            pltpu.SemaphoreType.DMA((2, lon_count)),
        ],
        name="run_adjoint",
        inputs=5,
        far_outs=(0,),
    )(fields, from_west, from_east, far_rows, near_rows)
    gathered = exchange(blocks)

    message = (1, 8, tile_lon + BLOCK)
    forcing, near, far = call(
        sum_forcing, [(2, tile_lat, tile_lon + BLOCK), message, message], name="sum_forcing", inputs=1
    )(received)
    near_rows, far_rows = swap(near, far, "lat", False)
    (adjoint,) = call(
        finish_adjoint,
        [cotangent.shape],
        [pltpu.VMEM(adjoint_states, f32)],
        name="finish_adjoint",
        inputs=3,
    )(coeffs, start, states)
    (final,) = call(
        run_forward,
        [tracers.shape],
        [pltpu.VMEM((2, levels, *wide), f32)],
        name="run_forward",
        inputs=5,
    )(coeffs, start, forcing, far_rows, near_rows)

    (gradient,) = call(
        unweigh,
        [atm_state.shape],
        [coupling_scratch(atm)[0], *map(in_vmem, found), *coupling_scratch(atm)[1:]],
        coupling_flops,
        name="unweigh",
        inputs=7,
        far=(6,),
    )(gathered, *slot_data, weights)
    return (final, adjoint, gradient)


def solution(mesh):
    return jax.shard_map(
        on_device,
        mesh=mesh,
        in_specs=(
            P(None, None, "lat", "lon"),
            P(None, None, "lat", "lon"),
            P(None, "lat", "lon"),
            P(None, None, "lat", "lon"),
            P(None, None, "lat", "lon"),
            P(),
            P(None, "lat", "lon", None),
            P(None, "lat", "lon", None, None),
        ),
        out_specs=(
            P(None, None, "lat", "lon"),
            P(None, None, "lat", "lon"),
            P(None, "lat", "lon", None),
        ),
        check_vma=False,
    )
```

```python
import jax
import jax.numpy as jnp
from jax import lax
from jax.experimental import pallas as pl
from jax.experimental.pallas import tpu as pltpu
from jax.sharding import PartitionSpec as P

BLOCK = 128
STEPS = 4
HALO = STEPS
PER_LANES = BLOCK // HALO
GROUP = 16
f32 = jnp.float32
bf16 = jnp.bfloat16
VMEM_LIMIT = 20 * 1024 * 1024


def call(body, outs, scratch=(), flops=0, name=None, inputs=0, far=(), far_outs=(), aliases=None):
    outs = [s if isinstance(s, jax.ShapeDtypeStruct) else jax.ShapeDtypeStruct(s, f32) for s in outs]
    near = pl.BlockSpec(memory_space=pltpu.VMEM)
    aliases = aliases or {}
    kernel = pl.pallas_call(
        body,
        out_shape=outs,
        in_specs=[
            pl.BlockSpec(memory_space=pl.ANY)
            if n in aliases
            else pl.BlockSpec(memory_space=pltpu.HBM)
            if n in far
            else near
            for n in range(inputs)
        ],
        out_specs=[
            pl.BlockSpec(memory_space=pl.ANY) if n in aliases.values() or n in far_outs else near
            for n in range(len(outs))
        ],
        input_output_aliases=aliases,
        scratch_shapes=list(scratch),
        compiler_params=pltpu.CompilerParams(vmem_limit_bytes=VMEM_LIMIT),
        cost_estimate=pl.CostEstimate(flops=flops, bytes_accessed=1 << 20, transcendentals=0),
        name=name,
    )

    def run(*args):
        return kernel(
            *(pltpu.with_memory_space_constraint(x, pltpu.HBM) if n in far else x for n, x in enumerate(args))
        )

    return run


def lanes(shape):
    return lax.broadcasted_iota(jnp.int32, shape, len(shape) - 1)


def rows(shape):
    return lax.broadcasted_iota(jnp.int32, shape, len(shape) - 2)


def turn(x, shift, axis):
    shift %= x.shape[axis]
    return pltpu.roll(x, shift, axis) if shift else x


def group_order(count):
    half = count // 2
    return [k for n in range(half) for k in (half + n, n)]


def exchange(x):
    order = group_order(x.shape[0])
    return lax.all_to_all(x, "lon", split_axis=0, concat_axis=0, tiled=True, axis_index_groups=[order])


def swap(near, far, axis, wrap):
    count = lax.axis_size(axis)
    pairs = [[], []]
    for i in range(count if wrap else count - 1):
        j = (i + 1) % count
        pairs[i % 2] += [(i, j), (j, i)]
    far = lax.ppermute(far, axis, pairs[1])
    return lax.ppermute(near, axis, pairs[0]), far


def sort_swap(axis, after, before):
    odd = lax.rem(lax.axis_index(axis), 2) == 1
    return jnp.where(odd, before, after), jnp.where(odd, after, before)


def tile_fields(tracers, cotangent, land_mask, diffusion, velocity):
    levels = land_mask.shape[0]
    mask = [land_mask[level].astype(f32) for level in range(levels)]
    out = [tracers[f, level] for f in range(2) for level in range(levels)]
    out += [cotangent[f, level] for f in range(2) for level in range(levels)]
    out += [diffusion[0, level] * mask[level] for level in range(levels)]
    out += [velocity[0, level] * mask[level] for level in range(levels)]
    out += [diffusion[1, level] * mask[level] for level in range(levels)]
    out += [velocity[1, level] * mask[level] for level in range(levels)]
    out += [diffusion[2, level] * mask[level] * mask[level + 1] for level in range(levels - 1)]
    return out


def fetch(pairs, arrived):
    copies = [pltpu.make_async_copy(src, dst, arrived.at[n]) for n, (src, dst) in enumerate(pairs)]
    for copy in copies:
        copy.start()
    return copies


def pack_columns(*refs):
    inputs, (fields, near, far), scratch = refs[:7], refs[7:10], refs[12:]
    copies = fetch(zip(inputs, [*scratch[:5], *refs[10:12]]), scratch[5])
    for copy in copies[:5]:
        copy.wait()
    shape = near.shape[1:]
    lane = lanes(shape)
    west = [jnp.zeros(shape, f32) for _ in range(near.shape[0])]
    east = [jnp.zeros(shape, f32) for _ in range(near.shape[0])]
    for i, field in enumerate(tile_fields(*scratch[:5])):
        fields[i] = field
        part, at = divmod(i, PER_LANES)
        at *= HALO
        here = (lane >= at) & (lane < at + HALO)
        west[part] = jnp.where(here, turn(field[:, :BLOCK], at, 1), west[part])
        east[part] = jnp.where(here, turn(field[:, -BLOCK:], at + HALO, 1), east[part])
    for part in range(near.shape[0]):
        near[part], far[part] = sort_swap("lon", east[part], west[part])
    for copy in copies[5:]:
        copy.wait()


def unpack_columns(from_west, from_east, i):
    part, at = divmod(i, PER_LANES)
    at *= HALO
    lane = lanes(from_west[part].shape)
    east = turn(from_east[part], -at, 1)
    west = turn(from_west[part], -at - HALO, 1)
    return jnp.where(lane < HALO, east, jnp.where(lane >= BLOCK - HALO, west, 0.0))


def row_sources(fields, from_west, from_east):
    out = [(fields, (i, slice(None), slice(h * BLOCK, (h + 1) * BLOCK)))
           for i in range(fields.shape[0]) for h in range(fields.shape[2] // BLOCK)]
    for columns in (from_west, from_east):
        out += [(columns, (part,)) for part in range(columns.shape[0])]
    return out


def pack_rows(fields, near_columns, far_columns, sums, near, far, from_west, from_east, same_sums):
    for part in range(from_west.shape[0]):
        from_east[part], from_west[part] = sort_swap("lon", near_columns[part], far_columns[part])
    sources = [ref[at] for ref, at in row_sources(fields, from_west, from_east)]
    half = near.shape[0]
    row = rows((8, BLOCK))
    for i in range(half):
        first = sources[i]
        second = sources[i + half] if i + half < len(sources) else jnp.zeros_like(first)
        to_north = jnp.where(row < HALO, turn(first[-8:], HALO, 0), second[-8:])
        to_south = jnp.where(row < HALO, first[:8], turn(second[:8], HALO, 0))
        near[i], far[i] = sort_swap("lat", to_north, to_south)


def edge_rows(near, far, i):
    half = near.shape[0]
    from_north, from_south = sort_swap("lat", near[i % half], far[i % half])
    if i < half:
        from_south = turn(from_south, HALO, 0)
    else:
        from_north = turn(from_north, HALO, 0)
    return jnp.where(rows(from_north.shape) < HALO, from_north, from_south)


def widen(fields, from_west, from_east, near, far, start, wide):
    count, tile_lat, tile_lon = fields.shape
    halves = tile_lon // BLOCK
    parts = from_west.shape[0]
    corners = [edge_rows(near, far, count * halves + n) for n in range(2 * parts)]
    for i in range(count):
        out = start.at[i] if i < start.shape[0] else wide.at[i - start.shape[0]]
        out[:tile_lat, :tile_lon] = fields[i]
        out[:tile_lat, tile_lon:] = unpack_columns(from_west, from_east, i)
        for h in range(halves):
            out[tile_lat:, h * BLOCK : (h + 1) * BLOCK] = edge_rows(near, far, i * halves + h)
        out[tile_lat:, tile_lon:] = unpack_columns(corners[:parts], corners[parts:], i)


def eastward(x):
    return turn(x, -1, 1)


def westward(x):
    return turn(x, 1, 1)


def northward(x):
    return turn(x, -1, 0)


def southward(x):
    return turn(x, 1, 0)


def adjoint_step(coeffs, read, write, first, last):
    levels = coeffs.shape[1]
    above = coeffs[4, first - 1] * (read(first) - read(first - 1)) if first else None
    for level in range(first, last):
        lam = read(level)
        step_x = eastward(lam) - lam
        step_y = northward(lam) - lam
        out = lam + coeffs[0, level] * step_x + westward(coeffs[1, level] * step_x)
        out = out + coeffs[2, level] * step_y + southward(coeffs[3, level] * step_y)
        if above is not None:
            out = out - above
        if level < levels - 1:
            above = coeffs[4, level] * (read(level + 1) - lam)
            out = out + above
        write(level, out)


def surface_levels(step, levels):
    return min(levels, STEPS - 1 - step)


def run_adjoint(
    fields, from_west, from_east, far, near, blocks, coeffs, start, states, wide, own, sent
):
    levels = coeffs.shape[1]
    tile_lat, tile_lon = fields.shape[1:]
    halves = tile_lon // BLOCK
    widen(fields, from_west, from_east, near, far, start, wide)
    base = 0
    mask0 = None
    for level in range(levels):
        east_d, east_u = wide[base + level], wide[base + levels + level]
        north_d, north_u = wide[base + 2 * levels + level], wide[base + 3 * levels + level]
        mask = (east_d > 0.0).astype(f32)
        mask0 = mask if mask0 is None else mask0
        mask_e, mask_n = eastward(mask), northward(mask)
        east_k, east_v = east_d * mask_e, east_u * mask_e
        north_k, north_v = north_d * mask_n, north_u * mask_n
        coeffs[0, level] = jnp.maximum(east_v, 0.0) + east_k
        coeffs[1, level] = jnp.minimum(east_v, 0.0) - east_k
        coeffs[2, level] = jnp.maximum(north_v, 0.0) + north_k
        coeffs[3, level] = jnp.minimum(north_v, 0.0) - north_k
        coeffs[4, level] = wide[base + 4 * levels + level] if level < levels - 1 else jnp.zeros_like(mask)
        coeffs[5, level] = mask
    copies = []
    for f in range(2):
        surface = start[(2 + f) * levels, :tile_lat, :tile_lon]
        for step in range(STEPS - 1):

            def read(level):
                return states[f, step - 1, level] if step else start[(2 + f) * levels + level]

            def write(level, lam):
                states[f, step, level] = lam

            adjoint_step(coeffs, read, write, 0, surface_levels(step, levels))
            surface = surface + states[f, step, 0, :tile_lat, :tile_lon]
        surface = surface * mask0[:tile_lat, :tile_lon]
        for h in range(halves):
            at = (f * halves + h) * tile_lat
            own[at : at + tile_lat] = surface[:, h * BLOCK : (h + 1) * BLOCK]
        field = pl.ds(f * halves * tile_lat, halves * tile_lat)
        copies += fetch([(own.at[field], blocks.at[k, field]) for k in range(blocks.shape[0])], sent.at[f])
    for copy in copies:
        copy.wait()


def finish_adjoint(coeffs, start, states, adjoint_out, rest):
    levels = coeffs.shape[1]
    tile_lat, tile_lon = adjoint_out.shape[2:]
    for f in range(2):
        for step in range(STEPS):
            done = surface_levels(step, levels)

            def read(level):
                if not step:
                    return start[(2 + f) * levels + level]
                return (states if level < surface_levels(step - 1, levels) else rest)[f, step - 1, level]

            def write(level, lam):
                if step == STEPS - 1:
                    adjoint_out[f, level] = lam[:tile_lat, :tile_lon]
                else:
                    rest[f, step, level] = lam

            adjoint_step(coeffs, read, write, done, levels)


def sum_forcing(received, forcing, near, far):
    tile_lat = forcing.shape[1]
    halves = forcing.shape[2] // BLOCK - 1
    total = received[0]
    for j in range(1, received.shape[0]):
        total = total + received[j]
    lane = lanes((tile_lat, BLOCK))
    upper = total[2 * halves * tile_lat :]
    lower = jnp.where(lane[: tile_lat // 2] < BLOCK // 2, turn(upper, -2 * HALO, 1), turn(upper, 2 * HALO, 1))
    packed = jnp.concatenate([upper, lower], axis=0)
    for f in range(2):
        for h in range(halves):
            at = (f * halves + h) * tile_lat
            forcing[f, :, h * BLOCK : (h + 1) * BLOCK] = total[at : at + tile_lat]
        used = (lane < HALO) | (lane >= BLOCK - HALO)
        if f == 0:
            edge = packed
        else:
            edge = jnp.where(lane < HALO, turn(packed, -HALO, 1), turn(packed, HALO, 1))
        forcing[f, :, halves * BLOCK :] = jnp.where(used, edge, 0.0)
    row = rows((8, forcing.shape[2]))
    to_north = jnp.where(row < HALO, turn(forcing[0, tile_lat - 8 :], HALO, 0), forcing[1, tile_lat - 8 :])
    to_south = jnp.where(row < HALO, forcing[0, :8], turn(forcing[1, :8], HALO, 0))
    near[0], far[0] = sort_swap("lat", to_north, to_south)


def run_forward(coeffs, start, forcing, far, near, weights, final, weights_near, state, arrived):
    fetch_weights(weights, weights_near, arrived)
    levels = coeffs.shape[1]
    tile_lat, tile_lon = final.shape[2:]
    for f in range(2):
        force = jnp.concatenate([forcing[f], edge_rows(near, far, f)], axis=0)
        force = force * coeffs[5, 0]
        for step in range(STEPS):
            above = None
            for level in range(levels):
                read = (lambda n: start[f * levels + n]) if step == 0 else (lambda n: state[(step - 1) % 2, n])
                theta = read(level)
                east_flux = coeffs[0, level] * theta + coeffs[1, level] * eastward(theta)
                north_flux = coeffs[2, level] * theta + coeffs[3, level] * northward(theta)
                out = theta - (east_flux - westward(east_flux)) - (north_flux - southward(north_flux))
                if level < levels - 1:
                    vertical = coeffs[4, level] * (theta - read(level + 1))
                    out = out - vertical
                if above is not None:
                    out = out + above
                above = vertical if level < levels - 1 else None
                if level == 0:
                    out = out + force
                if step == STEPS - 1:
                    final[f, level] = out[:tile_lat, :tile_lon]
                else:
                    state[step % 2, level] = out
    for copy in weight_copies(weights, weights_near, arrived):
        copy.wait()


def split(x):
    high = x.astype(bf16)
    return high, (x - high.astype(f32)).astype(bf16)


def weight_copies(weights, held, arrived):
    for g in range(held.shape[0]):
        yield pltpu.make_async_copy(weights.at[pl.ds(g * GROUP, GROUP)], held.at[g], arrived.at[g])


def fetch_weights(weights, held, arrived):
    for copy in weight_copies(weights, held, arrived):
        copy.start()


def held_part(weights, held, arrived):
    def part(r, g, u):
        if u == 0:

            @pl.when(r == 0)
            def _():
                pltpu.make_async_copy(weights.at[pl.ds(g * GROUP, GROUP)], held.at[g], arrived.at[g]).wait()

        return split(held[g, u])

    return part


def one_hot(where):
    return jnp.where(where, 1.0, 0.0).astype(bf16)


def places(slots, blocks):
    return 8 * (-(-2 * slots // (8 * blocks)) + 1)


def round_chunks(slots, blocks):
    return -(-(slots + 7 * blocks) // BLOCK)


def as_row(ids):
    return jnp.concatenate([ids[k : k + 1, :] for k in range(ids.shape[0])], axis=1)


def rank_slots(block_row, blocks):
    slots = block_row.shape[1]
    mine = rows((blocks, slots)) == block_row
    cuts = range(0, slots, BLOCK)
    stacked = jnp.concatenate([one_hot(mine[:, at : at + BLOCK]) for at in cuts], axis=0)
    shape = (BLOCK, 2 * BLOCK)
    counts = jnp.dot(stacked, one_hot(rows(shape) < lanes(shape)), preferred_element_type=f32)
    before, out = jnp.zeros((blocks, BLOCK), f32), []
    for n, at in enumerate(cuts):
        run = counts[n * blocks : (n + 1) * blocks]
        here = jnp.where(mine[:, at : at + BLOCK], run[:, :BLOCK] + before, 0.0)
        out.append(jnp.sum(here, axis=0, keepdims=True))
        before = before + run[:, BLOCK:]
    return jnp.concatenate(out, axis=1), before


def find_slots(r, keys, counts, capacity, columns, lines, starts):
    slots = keys.shape[1]
    blocks = counts.shape[0]
    atm_row, ocean_row, block_row, rank = (keys[n : n + 1] for n in range(4))
    count = jnp.clip(counts - r * capacity, 0.0, capacity)
    tiles = jnp.floor((count + 7.0) * 0.125) * 8.0
    shape = (blocks, blocks)
    first = jnp.dot(one_hot(lanes(shape) < rows(shape)), tiles.astype(bf16), preferred_element_type=f32)
    starts[...] = first.astype(jnp.int32)
    mine = rows((blocks, slots)).astype(f32) == block_row
    own = jnp.where(mine, jnp.concatenate([first] * (slots // BLOCK), axis=1), 0.0)
    place = rank - r * capacity
    here = (place >= 0.0) & (place < capacity)
    place = jnp.where(here, jnp.sum(own, axis=0, keepdims=True) + place, -1.0)
    run = jnp.floor(place * (1.0 / BLOCK))
    low = one_hot(rows((BLOCK, slots)).astype(f32) == place - run * BLOCK)
    size = lines.shape[1]
    in_run = rows((size, slots)).astype(f32) == run
    ocean_high = jnp.floor(ocean_row * (1.0 / BLOCK))
    digits = [atm_row, ocean_high, ocean_row - ocean_high * BLOCK]
    digits = [jnp.where(in_run, digit, 0.0).astype(bf16) for digit in digits]
    across = (((1,), (1,)), ((), ()))
    down = [lax.dot_general(low, digit, across, preferred_element_type=f32) for digit in digits]
    along = [lax.dot_general(digit, low, across, preferred_element_type=f32) for digit in digits]
    columns[0, :, :size], columns[1, :, :size] = down[0], down[1] * BLOCK + down[2] - 1.0
    ocean = along[1] * BLOCK + along[2] - 1.0
    lines[0], lines[1] = jnp.where(ocean < 0.0, -1.0, along[0]), ocean


def couple(part, table, capacity, rounds, prepare, columns, lines, starts, transposed, result, scratch):
    vectors, products, starts_near, moved = scratch
    blocks = starts.shape[0]
    total_rows = vectors.shape[0] - capacity
    width = table.shape[0]
    result[...] = jnp.zeros_like(result)
    products[...] = jnp.zeros_like(products)

    def one_round(r, carry):
        prepare(r)
        move = pltpu.make_async_copy(starts, starts_near, moved)
        move.start()
        place_hot = []
        for n in range(total_rows // BLOCK):
            gather = jnp.broadcast_to(columns[int(transposed), :, n : n + 1], (BLOCK, BLOCK))
            gather = jnp.concatenate([gather] * (width // BLOCK), axis=1)
            hot = one_hot(gather == lanes((BLOCK, width)).astype(f32))
            vectors[n * BLOCK : (n + 1) * BLOCK] = jnp.dot(hot, table, preferred_element_type=f32)
            put = lines[1 - int(transposed), n : n + 1]
            place_hot.append(one_hot(rows((result.shape[0], BLOCK)).astype(f32) == put))
        move.wait()

        def group(g, carry):
            for u in range(GROUP):
                at = pl.ds(pl.multiple_of(starts_near[g * GROUP + u, 0], 8), capacity)
                own = vectors[at]
                left = jnp.concatenate([own[:, n * BLOCK : (n + 1) * BLOCK] for n in range(4)], axis=0)
                high, low = part(r, g, u)
                right = jnp.concatenate([high, low], axis=1 if transposed else 0)
                contract = (((1,), (0 if transposed else 1,)), ((), ()))
                product = lax.dot_general(left.astype(bf16), right, contract, preferred_element_type=f32)
                for f in range(2):
                    high_part = product[f * capacity : (f + 1) * capacity]
                    low_part = product[(f + 2) * capacity : (f + 3) * capacity, :BLOCK]
                    products[at, f * BLOCK : (f + 1) * BLOCK] = (
                        high_part[:, BLOCK:] + low_part
                    ) + high_part[:, :BLOCK]
            return carry

        lax.fori_loop(0, blocks // GROUP, group, 0)
        summed = jnp.dot(
            jnp.concatenate(place_hot, axis=1),
            jnp.concatenate(split(products[:total_rows]), axis=1),
            preferred_element_type=f32,
        )
        result[...] += summed[:, : 2 * BLOCK] + summed[:, 2 * BLOCK :]
        return carry

    lax.fori_loop(0, rounds, one_round, 0)


def slot_keys(ids, tile_lat, keys):
    lon_count, cap = ids.shape[3:]
    ocean, atm_ids, block_ids = (ids[n, 0, 0] for n in range(3))
    order = (ocean & 1) * tile_lat + (ocean >> 1) + rows((lon_count, cap)) * (2 * tile_lat)
    order = jnp.where(ocean >= 0, order, lon_count * 2 * tile_lat) + 1
    for n, part in enumerate((atm_ids, order, block_ids)):
        keys[n : n + 1] = as_row(part.astype(f32))


def weigh(
    atm_near, margins, weights, after, sums, keys, counts, columns, lines, starts, result, *scratch
):
    scratch, (held, arrived) = scratch[:4], scratch[4:]
    fetch_weights(weights, held, arrived)
    lon_count = margins.shape[3]
    blocks = weights.shape[0]
    tile_lat = 2 * sums.shape[1] // 9
    slot_keys(margins, tile_lat, keys)
    rank, count = rank_slots(keys[2:3].astype(jnp.int32), blocks)
    keys[3:4] = rank
    counts[...] = count
    capacity = places(keys.shape[1], blocks)
    rounds = jnp.max(rank).astype(jnp.int32) // capacity + 1
    parts = [split(atm_near[f, 0]) for f in range(2)]
    table = jnp.concatenate([parts[f][n] for n in range(2) for f in range(2)], axis=1)
    part = held_part(weights, held, arrived)

    def prepare(r):
        find_slots((rounds - 1 - r).astype(f32), keys, counts[...], capacity, columns, lines, starts)

    couple(part, table, capacity, rounds, prepare, columns, lines, starts, False, result, scratch)
    lane = lanes((tile_lat, BLOCK))

    def block_sums(k, f, h):
        at = (2 * k + h) * tile_lat
        return result[at : at + tile_lat, f * BLOCK : (f + 1) * BLOCK]

    for n, k in enumerate(group_order(lon_count)):
        edge = jnp.zeros((tile_lat, BLOCK), f32)
        for f in range(2):
            for h in range(2):
                sums[n, (2 * f + h) * tile_lat : (2 * f + h + 1) * tile_lat] = block_sums(k, f, h)
            at = f * HALO
            after = turn(block_sums((k + 1) % lon_count, f, 0), at, 1)
            before = turn(block_sums((k - 1) % lon_count, f, 1), -at, 1)
            edge = jnp.where((lane >= at) & (lane < at + HALO), after, edge)
            end = BLOCK - at
            edge = jnp.where((lane >= end - HALO) & (lane < end), before, edge)
        upper, lower = edge[: tile_lat // 2], edge[tile_lat // 2 :]
        near = lane[: tile_lat // 2]
        lower = jnp.where(near < BLOCK // 2, turn(lower, 2 * HALO, 1), turn(lower, -2 * HALO, 1))
        sums[n, 4 * tile_lat :] = jnp.where((near < 2 * HALO) | (near >= BLOCK - 2 * HALO), upper, lower)


def unweigh(
    gathered, keys, counts, columns_in, lines_in, starts_in, weights, gradient, result, columns, lines, starts, *scratch
):
    blocks = starts.shape[0]
    lon_count, ocean_blocks = gathered.shape[0], gathered.shape[1] // 2
    order = group_order(lon_count)
    capacity = places(keys.shape[1], blocks)
    rounds = jnp.max(keys[3:4]).astype(jnp.int32) // capacity + 1
    parts = [
        split(
            jnp.concatenate(
                [gathered[order.index(k), f * ocean_blocks : (f + 1) * ocean_blocks] for k in range(lon_count)],
                axis=0,
            )
        )
        for f in range(2)
    ]
    table = jnp.concatenate([parts[f][n] for n in range(2) for f in range(2)], axis=1)

    def prepare(r):
        @pl.when(r == 0)
        def _():
            columns[...] = columns_in[...]
            lines[...] = lines_in[...]
            starts[...] = starts_in[...]

        @pl.when(r > 0)
        def _():
            find_slots(r.astype(f32), keys, counts[...], capacity, columns, lines, starts)

    couple(lambda r, g, u: split(weights[g, u]), table, capacity, rounds, prepare, columns, lines, starts, True, result, scratch)
    for f in range(2):
        gradient[f, 0] = result[:, f * BLOCK : (f + 1) * BLOCK]


def on_device(tracers, cotangent, land_mask, diffusion, velocity, weights, atm_state, margins):
    levels, tile_lat, tile_lon = land_mask.shape
    lon_count = lax.axis_size("lon")
    slots = lon_count * margins.shape[4]
    halves = tile_lon // BLOCK
    count = 9 * levels - 1
    parts = -(-count // PER_LANES)
    inputs = (tracers, cotangent, land_mask, diffusion, velocity)

    def in_vmem(s):
        return pltpu.VMEM(s.shape, s.dtype)

    message = (parts, tile_lat, BLOCK)
    fields, near, far, atm_near, margins_near = call(
        pack_columns,
        [
            (count, tile_lat, tile_lon),
            message,
            message,
            atm_state.shape,
            jax.ShapeDtypeStruct(margins.shape, margins.dtype),
        ],
        [*map(in_vmem, inputs), pltpu.SemaphoreType.DMA((7,))],
        name="pack_columns",
        inputs=7,
        far=range(7),
    )(*inputs, atm_state, margins)
    near_columns, far_columns = swap(near, far, "lon", True)

    blocks_of, atm = weights.shape[0], atm_state.shape[2]
    groups = blocks_of // GROUP
    sum_rows = 2 * halves * tile_lat + tile_lat // 2
    ocean_blocks = lon_count * halves * tile_lat
    chunks = round_chunks(slots, blocks_of)
    held_rows = chunks * BLOCK + places(slots, blocks_of)

    def coupling_scratch(result_rows):
        return [
            pltpu.VMEM((result_rows, 2 * BLOCK), f32),
            pltpu.VMEM((held_rows, 4 * BLOCK), f32),
            pltpu.VMEM((held_rows, 2 * BLOCK), f32),
            pltpu.SMEM((blocks_of, BLOCK), jnp.int32),
            pltpu.SemaphoreType.DMA,
        ]

    coupling_flops = 4 * slots * blocks_of * 2 * BLOCK * BLOCK * 2
    found = [
        jax.ShapeDtypeStruct((2, BLOCK, BLOCK), f32),
        jax.ShapeDtypeStruct((2, -(-chunks // 8) * 8, BLOCK), f32),
        jax.ShapeDtypeStruct((blocks_of, BLOCK), jnp.int32),
    ]
    sums, *slot_data = call(
        weigh,
        [(lon_count, sum_rows, BLOCK), (8, slots), (blocks_of, BLOCK), *found],
        [
            *coupling_scratch(ocean_blocks),
            pltpu.VMEM((groups, GROUP, BLOCK, BLOCK), f32),
            pltpu.SemaphoreType.DMA((groups,)),
        ],
        coupling_flops,
        name="weigh",
        inputs=4,
        far=(2,),
    )(atm_near, margins_near, weights, far)

    sources = count * halves + 2 * parts
    message = (-(-sources // 2), 8, BLOCK)
    columns = (parts, tile_lat, BLOCK)
    near, far, from_west, from_east, sums = call(
        pack_rows,
        [message, message, columns, columns, sums.shape],
        name="pack_rows",
        inputs=4,
        aliases={3: 4},
    )(fields, near_columns, far_columns, sums)
    received = exchange(sums)
    near_rows, far_rows = swap(near, far, "lat", False)

    wide = (tile_lat + 8, tile_lon + BLOCK)
    own = (2 * halves * tile_lat, BLOCK)
    adjoint_states = (2, STEPS - 1, levels, *wide)
    blocks, coeffs, start, states = call(
        run_adjoint,
        [(lon_count, *own), (6, levels, *wide), (4 * levels, *wide), adjoint_states],
        [
            pltpu.VMEM((count - 4 * levels, *wide), f32),
            pltpu.VMEM(own, f32),
            pltpu.SemaphoreType.DMA((2, lon_count)),
        ],
        name="run_adjoint",
        inputs=5,
        far_outs=(0,),
    )(fields, from_west, from_east, far_rows, near_rows)
    gathered = exchange(blocks)

    message = (1, 8, tile_lon + BLOCK)
    forcing, near, far = call(
        sum_forcing, [(2, tile_lat, tile_lon + BLOCK), message, message], name="sum_forcing", inputs=1
    )(received)
    near_rows, far_rows = swap(near, far, "lat", False)
    (adjoint,) = call(
        finish_adjoint,
        [cotangent.shape],
        [pltpu.VMEM(adjoint_states, f32)],
        name="finish_adjoint",
        inputs=3,
    )(coeffs, start, states)
    final, weights_near = call(
        run_forward,
        [tracers.shape, (groups, GROUP, BLOCK, BLOCK)],
        [pltpu.VMEM((2, levels, *wide), f32), pltpu.SemaphoreType.DMA((groups,))],
        name="run_forward",
        inputs=6,
        far=(5,),
    )(coeffs, start, forcing, far_rows, near_rows, weights)

    (gradient,) = call(
        unweigh,
        [atm_state.shape],
        [coupling_scratch(atm)[0], *map(in_vmem, found), *coupling_scratch(atm)[1:]],
        coupling_flops,
        name="unweigh",
        inputs=7,
    )(gathered, *slot_data, weights_near)
    return (final, adjoint, gradient)


def solution(mesh):
    return jax.shard_map(
        on_device,
        mesh=mesh,
        in_specs=(
            P(None, None, "lat", "lon"),
            P(None, None, "lat", "lon"),
            P(None, "lat", "lon"),
            P(None, None, "lat", "lon"),
            P(None, None, "lat", "lon"),
            P(),
            P(None, "lat", "lon", None),
            P(None, "lat", "lon", None, None),
        ),
        out_specs=(
            P(None, None, "lat", "lon"),
            P(None, None, "lat", "lon"),
            P(None, "lat", "lon", None),
        ),
        check_vma=False,
    )
```

```python
import jax
import jax.numpy as jnp
from jax import lax
from jax.experimental import pallas as pl
from jax.experimental.pallas import tpu as pltpu
from jax.sharding import PartitionSpec as P

BLOCK = 128
STEPS = 4
HALO = STEPS
PER_LANES = BLOCK // HALO
GROUP = 16
f32 = jnp.float32
bf16 = jnp.bfloat16
VMEM_LIMIT = 20 * 1024 * 1024


def call(body, outs, scratch=(), flops=0, name=None, inputs=0, far=(), far_outs=(), aliases=None):
    outs = [s if isinstance(s, jax.ShapeDtypeStruct) else jax.ShapeDtypeStruct(s, f32) for s in outs]
    near = pl.BlockSpec(memory_space=pltpu.VMEM)
    aliases = aliases or {}
    kernel = pl.pallas_call(
        body,
        out_shape=outs,
        in_specs=[
            pl.BlockSpec(memory_space=pl.ANY)
            if n in aliases
            else pl.BlockSpec(memory_space=pltpu.HBM)
            if n in far
            else near
            for n in range(inputs)
        ],
        out_specs=[
            pl.BlockSpec(memory_space=pl.ANY) if n in aliases.values() or n in far_outs else near
            for n in range(len(outs))
        ],
        input_output_aliases=aliases,
        scratch_shapes=list(scratch),
        compiler_params=pltpu.CompilerParams(vmem_limit_bytes=VMEM_LIMIT),
        cost_estimate=pl.CostEstimate(flops=flops, bytes_accessed=1 << 20, transcendentals=0),
        name=name,
    )

    def run(*args):
        return kernel(
            *(pltpu.with_memory_space_constraint(x, pltpu.HBM) if n in far else x for n, x in enumerate(args))
        )

    return run


def lanes(shape):
    return lax.broadcasted_iota(jnp.int32, shape, len(shape) - 1)


def rows(shape):
    return lax.broadcasted_iota(jnp.int32, shape, len(shape) - 2)


def turn(x, shift, axis):
    shift %= x.shape[axis]
    return pltpu.roll(x, shift, axis) if shift else x


def group_order(count):
    half = count // 2
    return [k for n in range(half) for k in (half + n, n)]


def exchange(x):
    order = group_order(x.shape[0])
    return lax.all_to_all(x, "lon", split_axis=0, concat_axis=0, tiled=True, axis_index_groups=[order])


def swap(near, far, axis, wrap):
    count = lax.axis_size(axis)
    pairs = [[], []]
    for i in range(count if wrap else count - 1):
        j = (i + 1) % count
        pairs[i % 2] += [(i, j), (j, i)]
    far = lax.ppermute(far, axis, pairs[1])
    return lax.ppermute(near, axis, pairs[0]), far


def sort_swap(axis, after, before):
    odd = lax.rem(lax.axis_index(axis), 2) == 1
    return jnp.where(odd, before, after), jnp.where(odd, after, before)


def tile_fields(tracers, cotangent, land_mask, diffusion, velocity):
    levels = land_mask.shape[0]
    mask = [land_mask[level].astype(f32) for level in range(levels)]
    out = [tracers[f, level] for f in range(2) for level in range(levels)]
    out += [cotangent[f, level] for f in range(2) for level in range(levels)]
    out += [diffusion[0, level] * mask[level] for level in range(levels)]
    out += [velocity[0, level] * mask[level] for level in range(levels)]
    out += [diffusion[1, level] * mask[level] for level in range(levels)]
    out += [velocity[1, level] * mask[level] for level in range(levels)]
    out += [diffusion[2, level] * mask[level] * mask[level + 1] for level in range(levels - 1)]
    return out


def fetch(pairs, arrived):
    copies = [pltpu.make_async_copy(src, dst, arrived.at[n]) for n, (src, dst) in enumerate(pairs)]
    for copy in copies:
        copy.start()
    return copies


def pack_columns(*refs):
    inputs, (fields, near, far), scratch = refs[:7], refs[7:10], refs[12:]
    copies = fetch(zip(inputs, [*scratch[:5], *refs[10:12]]), scratch[5])
    for copy in copies[:5]:
        copy.wait()
    shape = near.shape[1:]
    lane = lanes(shape)
    west = [jnp.zeros(shape, f32) for _ in range(near.shape[0])]
    east = [jnp.zeros(shape, f32) for _ in range(near.shape[0])]
    for i, field in enumerate(tile_fields(*scratch[:5])):
        fields[i] = field
        part, at = divmod(i, PER_LANES)
        at *= HALO
        here = (lane >= at) & (lane < at + HALO)
        west[part] = jnp.where(here, turn(field[:, :BLOCK], at, 1), west[part])
        east[part] = jnp.where(here, turn(field[:, -BLOCK:], at + HALO, 1), east[part])
    for part in range(near.shape[0]):
        near[part], far[part] = sort_swap("lon", east[part], west[part])
    for copy in copies[5:]:
        copy.wait()


def unpack_columns(from_west, from_east, i):
    part, at = divmod(i, PER_LANES)
    at *= HALO
    lane = lanes(from_west[part].shape)
    east = turn(from_east[part], -at, 1)
    west = turn(from_west[part], -at - HALO, 1)
    return jnp.where(lane < HALO, east, jnp.where(lane >= BLOCK - HALO, west, 0.0))


def row_sources(fields, from_west, from_east):
    out = [(fields, (i, slice(None), slice(h * BLOCK, (h + 1) * BLOCK)))
           for i in range(fields.shape[0]) for h in range(fields.shape[2] // BLOCK)]
    for columns in (from_west, from_east):
        out += [(columns, (part,)) for part in range(columns.shape[0])]
    return out


def pack_rows(fields, near_columns, far_columns, sums, near, far, from_west, from_east, same_sums):
    for part in range(from_west.shape[0]):
        from_east[part], from_west[part] = sort_swap("lon", near_columns[part], far_columns[part])
    sources = [ref[at] for ref, at in row_sources(fields, from_west, from_east)]
    half = near.shape[0]
    row = rows((8, BLOCK))
    for i in range(half):
        first = sources[i]
        second = sources[i + half] if i + half < len(sources) else jnp.zeros_like(first)
        to_north = jnp.where(row < HALO, turn(first[-8:], HALO, 0), second[-8:])
        to_south = jnp.where(row < HALO, first[:8], turn(second[:8], HALO, 0))
        near[i], far[i] = sort_swap("lat", to_north, to_south)


def edge_rows(near, far, i):
    half = near.shape[0]
    from_north, from_south = sort_swap("lat", near[i % half], far[i % half])
    if i < half:
        from_south = turn(from_south, HALO, 0)
    else:
        from_north = turn(from_north, HALO, 0)
    return jnp.where(rows(from_north.shape) < HALO, from_north, from_south)


def widen(fields, from_west, from_east, near, far, start, wide):
    count, tile_lat, tile_lon = fields.shape
    halves = tile_lon // BLOCK
    parts = from_west.shape[0]
    corners = [edge_rows(near, far, count * halves + n) for n in range(2 * parts)]
    for i in range(count):
        out = start.at[i] if i < start.shape[0] else wide.at[i - start.shape[0]]
        out[:tile_lat, :tile_lon] = fields[i]
        out[:tile_lat, tile_lon:] = unpack_columns(from_west, from_east, i)
        for h in range(halves):
            out[tile_lat:, h * BLOCK : (h + 1) * BLOCK] = edge_rows(near, far, i * halves + h)
        out[tile_lat:, tile_lon:] = unpack_columns(corners[:parts], corners[parts:], i)


def eastward(x):
    return turn(x, -1, 1)


def westward(x):
    return turn(x, 1, 1)


def northward(x):
    return turn(x, -1, 0)


def southward(x):
    return turn(x, 1, 0)


def adjoint_step(coeffs, read, write, first, last):
    levels = coeffs.shape[1]
    above = coeffs[4, first - 1] * (read(first) - read(first - 1)) if first else None
    for level in range(first, last):
        lam = read(level)
        step_x = eastward(lam) - lam
        step_y = northward(lam) - lam
        out = lam + coeffs[0, level] * step_x + westward(coeffs[1, level] * step_x)
        out = out + coeffs[2, level] * step_y + southward(coeffs[3, level] * step_y)
        if above is not None:
            out = out - above
        if level < levels - 1:
            above = coeffs[4, level] * (read(level + 1) - lam)
            out = out + above
        write(level, out)


def surface_levels(step, levels):
    return min(levels, STEPS - 1 - step)


def run_adjoint(
    fields, from_west, from_east, far, near, blocks, coeffs, start, states, wide, own, sent
):
    levels = coeffs.shape[1]
    tile_lat, tile_lon = fields.shape[1:]
    halves = tile_lon // BLOCK
    widen(fields, from_west, from_east, near, far, start, wide)
    base = 0
    mask0 = None
    for level in range(levels):
        east_d, east_u = wide[base + level], wide[base + levels + level]
        north_d, north_u = wide[base + 2 * levels + level], wide[base + 3 * levels + level]
        mask = (east_d > 0.0).astype(f32)
        mask0 = mask if mask0 is None else mask0
        mask_e, mask_n = eastward(mask), northward(mask)
        east_k, east_v = east_d * mask_e, east_u * mask_e
        north_k, north_v = north_d * mask_n, north_u * mask_n
        coeffs[0, level] = jnp.maximum(east_v, 0.0) + east_k
        coeffs[1, level] = jnp.minimum(east_v, 0.0) - east_k
        coeffs[2, level] = jnp.maximum(north_v, 0.0) + north_k
        coeffs[3, level] = jnp.minimum(north_v, 0.0) - north_k
        coeffs[4, level] = wide[base + 4 * levels + level] if level < levels - 1 else jnp.zeros_like(mask)
        coeffs[5, level] = mask
    copies = []
    for f in range(2):
        surface = start[(2 + f) * levels, :tile_lat, :tile_lon]
        for step in range(STEPS - 1):

            def read(level):
                return states[f, step - 1, level] if step else start[(2 + f) * levels + level]

            def write(level, lam):
                states[f, step, level] = lam

            adjoint_step(coeffs, read, write, 0, surface_levels(step, levels))
            surface = surface + states[f, step, 0, :tile_lat, :tile_lon]
        surface = surface * mask0[:tile_lat, :tile_lon]
        for h in range(halves):
            at = (f * halves + h) * tile_lat
            own[at : at + tile_lat] = surface[:, h * BLOCK : (h + 1) * BLOCK]
        field = pl.ds(f * halves * tile_lat, halves * tile_lat)
        copies += fetch([(own.at[field], blocks.at[k, field]) for k in range(blocks.shape[0])], sent.at[f])
    for copy in copies:
        copy.wait()


def finish_adjoint(coeffs, start, states, adjoint_out, rest):
    levels = coeffs.shape[1]
    tile_lat, tile_lon = adjoint_out.shape[2:]
    for f in range(2):
        for step in range(STEPS):
            done = surface_levels(step, levels)

            def read(level):
                if not step:
                    return start[(2 + f) * levels + level]
                return (states if level < surface_levels(step - 1, levels) else rest)[f, step - 1, level]

            def write(level, lam):
                if step == STEPS - 1:
                    adjoint_out[f, level] = lam[:tile_lat, :tile_lon]
                else:
                    rest[f, step, level] = lam

            adjoint_step(coeffs, read, write, done, levels)


def sum_forcing(received, forcing, near, far):
    tile_lat = forcing.shape[1]
    halves = forcing.shape[2] // BLOCK - 1
    total = received[0]
    for j in range(1, received.shape[0]):
        total = total + received[j]
    lane = lanes((tile_lat, BLOCK))
    upper = total[2 * halves * tile_lat :]
    lower = jnp.where(lane[: tile_lat // 2] < BLOCK // 2, turn(upper, -2 * HALO, 1), turn(upper, 2 * HALO, 1))
    packed = jnp.concatenate([upper, lower], axis=0)
    for f in range(2):
        for h in range(halves):
            at = (f * halves + h) * tile_lat
            forcing[f, :, h * BLOCK : (h + 1) * BLOCK] = total[at : at + tile_lat]
        used = (lane < HALO) | (lane >= BLOCK - HALO)
        if f == 0:
            edge = packed
        else:
            edge = jnp.where(lane < HALO, turn(packed, -HALO, 1), turn(packed, HALO, 1))
        forcing[f, :, halves * BLOCK :] = jnp.where(used, edge, 0.0)
    row = rows((8, forcing.shape[2]))
    to_north = jnp.where(row < HALO, turn(forcing[0, tile_lat - 8 :], HALO, 0), forcing[1, tile_lat - 8 :])
    to_south = jnp.where(row < HALO, forcing[0, :8], turn(forcing[1, :8], HALO, 0))
    near[0], far[0] = sort_swap("lat", to_north, to_south)


def run_forward(coeffs, start, forcing, far, near, final, state):
    levels = coeffs.shape[1]
    tile_lat, tile_lon = final.shape[2:]
    for f in range(2):
        force = jnp.concatenate([forcing[f], edge_rows(near, far, f)], axis=0)
        force = force * coeffs[5, 0]
        for step in range(STEPS):
            above = None
            for level in range(levels):
                read = (lambda n: start[f * levels + n]) if step == 0 else (lambda n: state[(step - 1) % 2, n])
                theta = read(level)
                east_flux = coeffs[0, level] * theta + coeffs[1, level] * eastward(theta)
                north_flux = coeffs[2, level] * theta + coeffs[3, level] * northward(theta)
                out = theta - (east_flux - westward(east_flux)) - (north_flux - southward(north_flux))
                if level < levels - 1:
                    vertical = coeffs[4, level] * (theta - read(level + 1))
                    out = out - vertical
                if above is not None:
                    out = out + above
                above = vertical if level < levels - 1 else None
                if level == 0:
                    out = out + force
                if step == STEPS - 1:
                    final[f, level] = out[:tile_lat, :tile_lon]
                else:
                    state[step % 2, level] = out


def split(x):
    high = x.astype(bf16)
    return high, (x - high.astype(f32)).astype(bf16)


def weight_copies(weights, held, arrived):
    for g in range(held.shape[0]):
        yield pltpu.make_async_copy(weights.at[pl.ds(g * GROUP, GROUP)], held.at[g], arrived.at[g])


def fetch_weights(weights, held, arrived):
    for copy in weight_copies(weights, held, arrived):
        copy.start()


def held_part(weights, held, arrived):
    def part(r, g, u):
        if u == 0:

            @pl.when(r == 0)
            def _():
                pltpu.make_async_copy(weights.at[pl.ds(g * GROUP, GROUP)], held.at[g], arrived.at[g]).wait()

        return split(held[g, u])

    return part


def one_hot(where):
    return jnp.where(where, 1.0, 0.0).astype(bf16)


def places(slots, blocks):
    return 8 * (-(-2 * slots // (8 * blocks)) + 1)


def round_chunks(slots, blocks):
    return -(-(slots + 7 * blocks) // BLOCK)


def as_row(ids):
    return jnp.concatenate([ids[k : k + 1, :] for k in range(ids.shape[0])], axis=1)


def rank_slots(block_row, blocks):
    slots = block_row.shape[1]
    mine = rows((blocks, slots)) == block_row
    cuts = range(0, slots, BLOCK)
    stacked = jnp.concatenate([one_hot(mine[:, at : at + BLOCK]) for at in cuts], axis=0)
    shape = (BLOCK, 2 * BLOCK)
    counts = jnp.dot(stacked, one_hot(rows(shape) < lanes(shape)), preferred_element_type=f32)
    before, out = jnp.zeros((blocks, BLOCK), f32), []
    for n, at in enumerate(cuts):
        run = counts[n * blocks : (n + 1) * blocks]
        here = jnp.where(mine[:, at : at + BLOCK], run[:, :BLOCK] + before, 0.0)
        out.append(jnp.sum(here, axis=0, keepdims=True))
        before = before + run[:, BLOCK:]
    return jnp.concatenate(out, axis=1), before


def find_slots(r, keys, counts, capacity, columns, lines, starts):
    slots = keys.shape[1]
    blocks = counts.shape[0]
    atm_row, ocean_row, block_row, rank = (keys[n : n + 1] for n in range(4))
    count = jnp.clip(counts - r * capacity, 0.0, capacity)
    tiles = jnp.floor((count + 7.0) * 0.125) * 8.0
    shape = (blocks, blocks)
    first = jnp.dot(one_hot(lanes(shape) < rows(shape)), tiles.astype(bf16), preferred_element_type=f32)
    starts[...] = first.astype(jnp.int32)
    mine = rows((blocks, slots)).astype(f32) == block_row
    own = jnp.where(mine, jnp.concatenate([first] * (slots // BLOCK), axis=1), 0.0)
    place = rank - r * capacity
    here = (place >= 0.0) & (place < capacity)
    place = jnp.where(here, jnp.sum(own, axis=0, keepdims=True) + place, -1.0)
    run = jnp.floor(place * (1.0 / BLOCK))
    low = one_hot(rows((BLOCK, slots)).astype(f32) == place - run * BLOCK)
    size = lines.shape[1]
    in_run = rows((size, slots)).astype(f32) == run
    ocean_high = jnp.floor(ocean_row * (1.0 / BLOCK))
    digits = [atm_row, ocean_high, ocean_row - ocean_high * BLOCK]
    digits = [jnp.where(in_run, digit, 0.0).astype(bf16) for digit in digits]
    across = (((1,), (1,)), ((), ()))
    down = [lax.dot_general(low, digit, across, preferred_element_type=f32) for digit in digits]
    along = [lax.dot_general(digit, low, across, preferred_element_type=f32) for digit in digits]
    columns[0, :, :size], columns[1, :, :size] = down[0], down[1] * BLOCK + down[2] - 1.0
    ocean = along[1] * BLOCK + along[2] - 1.0
    lines[0], lines[1] = jnp.where(ocean < 0.0, -1.0, along[0]), ocean


def couple(part, table, capacity, rounds, prepare, columns, lines, starts, transposed, result, scratch):
    vectors, products, starts_near, moved = scratch
    blocks = starts.shape[0]
    total_rows = vectors.shape[0] - capacity
    width = table.shape[0]
    result[...] = jnp.zeros_like(result)
    products[...] = jnp.zeros_like(products)

    def one_round(r, carry):
        prepare(r)
        move = pltpu.make_async_copy(starts, starts_near, moved)
        move.start()
        place_hot = []
        for n in range(total_rows // BLOCK):
            gather = jnp.broadcast_to(columns[int(transposed), :, n : n + 1], (BLOCK, BLOCK))
            gather = jnp.concatenate([gather] * (width // BLOCK), axis=1)
            hot = one_hot(gather == lanes((BLOCK, width)).astype(f32))
            vectors[n * BLOCK : (n + 1) * BLOCK] = jnp.dot(hot, table, preferred_element_type=f32)
            put = lines[1 - int(transposed), n : n + 1]
            place_hot.append(one_hot(rows((result.shape[0], BLOCK)).astype(f32) == put))
        move.wait()

        def group(g, carry):
            for u in range(0, GROUP, 2):
                pair = [
                    pl.ds(pl.multiple_of(starts_near[g * GROUP + u + n, 0], 8), capacity) for n in range(2)
                ]
                left, right = [], []
                for n, at in enumerate(pair):
                    own = vectors[at]
                    own = jnp.concatenate([own[:, m * BLOCK : (m + 1) * BLOCK] for m in range(4)], axis=0)
                    own, none = own.astype(bf16), jnp.zeros((4 * capacity, BLOCK), bf16)
                    left.append(jnp.concatenate([none, own] if n else [own, none], axis=1))
                    right.append(jnp.concatenate(part(r, g, u + n), axis=1 if transposed else 0))
                contract = (((1,), (0 if transposed else 1,)), ((), ()))
                product = lax.dot_general(
                    jnp.concatenate(left, axis=0),
                    jnp.concatenate(right, axis=0 if transposed else 1),
                    contract,
                    preferred_element_type=f32,
                )
                for n, at in enumerate(pair):
                    own = product[4 * n * capacity : 4 * (n + 1) * capacity]
                    for f in range(2):
                        high_part = own[f * capacity : (f + 1) * capacity]
                        low_part = own[(f + 2) * capacity : (f + 3) * capacity, :BLOCK]
                        products[at, f * BLOCK : (f + 1) * BLOCK] = (
                            high_part[:, BLOCK:] + low_part
                        ) + high_part[:, :BLOCK]
            return carry

        lax.fori_loop(0, blocks // GROUP, group, 0)
        summed = jnp.dot(
            jnp.concatenate(place_hot, axis=1),
            jnp.concatenate(split(products[:total_rows]), axis=1),
            preferred_element_type=f32,
        )
        result[...] += summed[:, : 2 * BLOCK] + summed[:, 2 * BLOCK :]
        return carry

    lax.fori_loop(0, rounds, one_round, 0)


def slot_keys(ids, tile_lat, keys):
    lon_count, cap = ids.shape[3:]
    ocean, atm_ids, block_ids = (ids[n, 0, 0] for n in range(3))
    order = (ocean & 1) * tile_lat + (ocean >> 1) + rows((lon_count, cap)) * (2 * tile_lat)
    order = jnp.where(ocean >= 0, order, lon_count * 2 * tile_lat) + 1
    for n, part in enumerate((atm_ids, order, block_ids)):
        keys[n : n + 1] = as_row(part.astype(f32))


def weigh(
    atm_near, margins, weights, after, sums, keys, counts, columns, lines, starts, result, *scratch
):
    scratch, (held, arrived) = scratch[:4], scratch[4:]
    fetch_weights(weights, held, arrived)
    lon_count = margins.shape[3]
    blocks = weights.shape[0]
    tile_lat = 2 * sums.shape[1] // 9
    slot_keys(margins, tile_lat, keys)
    rank, count = rank_slots(keys[2:3].astype(jnp.int32), blocks)
    keys[3:4] = rank
    counts[...] = count
    capacity = places(keys.shape[1], blocks)
    rounds = jnp.max(rank).astype(jnp.int32) // capacity + 1
    parts = [split(atm_near[f, 0]) for f in range(2)]
    table = jnp.concatenate([parts[f][n] for n in range(2) for f in range(2)], axis=1)
    part = held_part(weights, held, arrived)

    def prepare(r):
        find_slots((rounds - 1 - r).astype(f32), keys, counts[...], capacity, columns, lines, starts)

    couple(part, table, capacity, rounds, prepare, columns, lines, starts, False, result, scratch)
    lane = lanes((tile_lat, BLOCK))

    def block_sums(k, f, h):
        at = (2 * k + h) * tile_lat
        return result[at : at + tile_lat, f * BLOCK : (f + 1) * BLOCK]

    for n, k in enumerate(group_order(lon_count)):
        edge = jnp.zeros((tile_lat, BLOCK), f32)
        for f in range(2):
            for h in range(2):
                sums[n, (2 * f + h) * tile_lat : (2 * f + h + 1) * tile_lat] = block_sums(k, f, h)
            at = f * HALO
            after = turn(block_sums((k + 1) % lon_count, f, 0), at, 1)
            before = turn(block_sums((k - 1) % lon_count, f, 1), -at, 1)
            edge = jnp.where((lane >= at) & (lane < at + HALO), after, edge)
            end = BLOCK - at
            edge = jnp.where((lane >= end - HALO) & (lane < end), before, edge)
        upper, lower = edge[: tile_lat // 2], edge[tile_lat // 2 :]
        near = lane[: tile_lat // 2]
        lower = jnp.where(near < BLOCK // 2, turn(lower, 2 * HALO, 1), turn(lower, -2 * HALO, 1))
        sums[n, 4 * tile_lat :] = jnp.where((near < 2 * HALO) | (near >= BLOCK - 2 * HALO), upper, lower)


def unweigh(
    gathered, keys, counts, columns_in, lines_in, starts_in, weights, gradient, result, columns, lines, starts, *scratch
):
    scratch, (held, arrived) = scratch[:4], scratch[4:]
    fetch_weights(weights, held, arrived)
    blocks = weights.shape[0]
    lon_count, ocean_blocks = gathered.shape[0], gathered.shape[1] // 2
    order = group_order(lon_count)
    capacity = places(keys.shape[1], blocks)
    rounds = jnp.max(keys[3:4]).astype(jnp.int32) // capacity + 1
    parts = [
        split(
            jnp.concatenate(
                [gathered[order.index(k), f * ocean_blocks : (f + 1) * ocean_blocks] for k in range(lon_count)],
                axis=0,
            )
        )
        for f in range(2)
    ]
    table = jnp.concatenate([parts[f][n] for n in range(2) for f in range(2)], axis=1)

    def prepare(r):
        @pl.when(r == 0)
        def _():
            columns[...] = columns_in[...]
            lines[...] = lines_in[...]
            starts[...] = starts_in[...]

        @pl.when(r > 0)
        def _():
            find_slots(r.astype(f32), keys, counts[...], capacity, columns, lines, starts)

    part = held_part(weights, held, arrived)
    couple(part, table, capacity, rounds, prepare, columns, lines, starts, True, result, scratch)
    for f in range(2):
        gradient[f, 0] = result[:, f * BLOCK : (f + 1) * BLOCK]


def on_device(tracers, cotangent, land_mask, diffusion, velocity, weights, atm_state, margins):
    levels, tile_lat, tile_lon = land_mask.shape
    lon_count = lax.axis_size("lon")
    slots = lon_count * margins.shape[4]
    halves = tile_lon // BLOCK
    count = 9 * levels - 1
    parts = -(-count // PER_LANES)
    inputs = (tracers, cotangent, land_mask, diffusion, velocity)

    def in_vmem(s):
        return pltpu.VMEM(s.shape, s.dtype)

    message = (parts, tile_lat, BLOCK)
    fields, near, far, atm_near, margins_near = call(
        pack_columns,
        [
            (count, tile_lat, tile_lon),
            message,
            message,
            atm_state.shape,
            jax.ShapeDtypeStruct(margins.shape, margins.dtype),
        ],
        [*map(in_vmem, inputs), pltpu.SemaphoreType.DMA((7,))],
        name="pack_columns",
        inputs=7,
        far=range(7),
    )(*inputs, atm_state, margins)
    near_columns, far_columns = swap(near, far, "lon", True)

    blocks_of, atm = weights.shape[0], atm_state.shape[2]
    groups = blocks_of // GROUP
    sum_rows = 2 * halves * tile_lat + tile_lat // 2
    ocean_blocks = lon_count * halves * tile_lat
    chunks = round_chunks(slots, blocks_of)
    held_rows = chunks * BLOCK + places(slots, blocks_of)

    def coupling_scratch(result_rows):
        return [
            pltpu.VMEM((result_rows, 2 * BLOCK), f32),
            pltpu.VMEM((held_rows, 4 * BLOCK), f32),
            pltpu.VMEM((held_rows, 2 * BLOCK), f32),
            pltpu.SMEM((blocks_of, BLOCK), jnp.int32),
            pltpu.SemaphoreType.DMA,
            pltpu.VMEM((groups, GROUP, BLOCK, BLOCK), f32),
            pltpu.SemaphoreType.DMA((groups,)),
        ]

    coupling_flops = 4 * slots * blocks_of * 2 * BLOCK * BLOCK * 2
    found = [
        jax.ShapeDtypeStruct((2, BLOCK, BLOCK), f32),
        jax.ShapeDtypeStruct((2, -(-chunks // 8) * 8, BLOCK), f32),
        jax.ShapeDtypeStruct((blocks_of, BLOCK), jnp.int32),
    ]
    sums, *slot_data = call(
        weigh,
        [(lon_count, sum_rows, BLOCK), (8, slots), (blocks_of, BLOCK), *found],
        coupling_scratch(ocean_blocks),
        coupling_flops,
        name="weigh",
        inputs=4,
        far=(2,),
    )(atm_near, margins_near, weights, far)

    sources = count * halves + 2 * parts
    message = (-(-sources // 2), 8, BLOCK)
    columns = (parts, tile_lat, BLOCK)
    near, far, from_west, from_east, sums = call(
        pack_rows,
        [message, message, columns, columns, sums.shape],
        name="pack_rows",
        inputs=4,
        aliases={3: 4},
    )(fields, near_columns, far_columns, sums)
    received = exchange(sums)
    near_rows, far_rows = swap(near, far, "lat", False)

    wide = (tile_lat + 8, tile_lon + BLOCK)
    own = (2 * halves * tile_lat, BLOCK)
    adjoint_states = (2, STEPS - 1, levels, *wide)
    blocks, coeffs, start, states = call(
        run_adjoint,
        [(lon_count, *own), (6, levels, *wide), (4 * levels, *wide), adjoint_states],
        [
            pltpu.VMEM((count - 4 * levels, *wide), f32),
            pltpu.VMEM(own, f32),
            pltpu.SemaphoreType.DMA((2, lon_count)),
        ],
        name="run_adjoint",
        inputs=5,
        far_outs=(0,),
    )(fields, from_west, from_east, far_rows, near_rows)
    gathered = exchange(blocks)

    message = (1, 8, tile_lon + BLOCK)
    forcing, near, far = call(
        sum_forcing, [(2, tile_lat, tile_lon + BLOCK), message, message], name="sum_forcing", inputs=1
    )(received)
    near_rows, far_rows = swap(near, far, "lat", False)
    (adjoint,) = call(
        finish_adjoint,
        [cotangent.shape],
        [pltpu.VMEM(adjoint_states, f32)],
        name="finish_adjoint",
        inputs=3,
    )(coeffs, start, states)
    (final,) = call(
        run_forward,
        [tracers.shape],
        [pltpu.VMEM((2, levels, *wide), f32)],
        name="run_forward",
        inputs=5,
    )(coeffs, start, forcing, far_rows, near_rows)

    (gradient,) = call(
        unweigh,
        [atm_state.shape],
        [coupling_scratch(atm)[0], *map(in_vmem, found), *coupling_scratch(atm)[1:]],
        coupling_flops,
        name="unweigh",
        inputs=7,
        far=(6,),
    )(gathered, *slot_data, weights)
    return (final, adjoint, gradient)


def solution(mesh):
    return jax.shard_map(
        on_device,
        mesh=mesh,
        in_specs=(
            P(None, None, "lat", "lon"),
            P(None, None, "lat", "lon"),
            P(None, "lat", "lon"),
            P(None, None, "lat", "lon"),
            P(None, None, "lat", "lon"),
            P(),
            P(None, "lat", "lon", None),
            P(None, "lat", "lon", None, None),
        ),
        out_specs=(
            P(None, None, "lat", "lon"),
            P(None, None, "lat", "lon"),
            P(None, "lat", "lon", None),
        ),
        check_vma=False,
    )
```

```python
import jax
import jax.numpy as jnp
from jax import lax
from jax.experimental import pallas as pl
from jax.experimental.pallas import tpu as pltpu
from jax.sharding import PartitionSpec as P

BLOCK = 128
STEPS = 4
HALO = STEPS
PER_LANES = BLOCK // HALO
GROUP = 16
FETCH = 4
f32 = jnp.float32
bf16 = jnp.bfloat16
VMEM_LIMIT = 20 * 1024 * 1024


def call(body, outs, scratch=(), flops=0, name=None, inputs=0, far=(), far_outs=(), aliases=None):
    outs = [s if isinstance(s, jax.ShapeDtypeStruct) else jax.ShapeDtypeStruct(s, f32) for s in outs]
    near = pl.BlockSpec(memory_space=pltpu.VMEM)
    aliases = aliases or {}
    kernel = pl.pallas_call(
        body,
        out_shape=outs,
        in_specs=[
            pl.BlockSpec(memory_space=pl.ANY)
            if n in aliases
            else pl.BlockSpec(memory_space=pltpu.HBM)
            if n in far
            else near
            for n in range(inputs)
        ],
        out_specs=[
            pl.BlockSpec(memory_space=pl.ANY) if n in aliases.values() or n in far_outs else near
            for n in range(len(outs))
        ],
        input_output_aliases=aliases,
        scratch_shapes=list(scratch),
        compiler_params=pltpu.CompilerParams(vmem_limit_bytes=VMEM_LIMIT),
        cost_estimate=pl.CostEstimate(flops=flops, bytes_accessed=1 << 20, transcendentals=0),
        name=name,
    )

    def run(*args):
        return kernel(
            *(pltpu.with_memory_space_constraint(x, pltpu.HBM) if n in far else x for n, x in enumerate(args))
        )

    return run


def lanes(shape):
    return lax.broadcasted_iota(jnp.int32, shape, len(shape) - 1)


def rows(shape):
    return lax.broadcasted_iota(jnp.int32, shape, len(shape) - 2)


def turn(x, shift, axis):
    shift %= x.shape[axis]
    return pltpu.roll(x, shift, axis) if shift else x


def group_order(count):
    half = count // 2
    return [k for n in range(half) for k in (half + n, n)]


def exchange(x):
    order = group_order(x.shape[0])
    return lax.all_to_all(x, "lon", split_axis=0, concat_axis=0, tiled=True, axis_index_groups=[order])


def swap(near, far, axis, wrap):
    count = lax.axis_size(axis)
    pairs = [[], []]
    for i in range(count if wrap else count - 1):
        j = (i + 1) % count
        pairs[i % 2] += [(i, j), (j, i)]
    far = lax.ppermute(far, axis, pairs[1])
    return lax.ppermute(near, axis, pairs[0]), far


def sort_swap(axis, after, before):
    odd = lax.rem(lax.axis_index(axis), 2) == 1
    return jnp.where(odd, before, after), jnp.where(odd, after, before)


def tile_fields(tracers, cotangent, land_mask, diffusion, velocity):
    levels = land_mask.shape[0]
    mask = [land_mask[level].astype(f32) for level in range(levels)]
    out = [tracers[f, level] for f in range(2) for level in range(levels)]
    out += [cotangent[f, level] for f in range(2) for level in range(levels)]
    out += [diffusion[0, level] * mask[level] for level in range(levels)]
    out += [velocity[0, level] * mask[level] for level in range(levels)]
    out += [diffusion[1, level] * mask[level] for level in range(levels)]
    out += [velocity[1, level] * mask[level] for level in range(levels)]
    out += [diffusion[2, level] * mask[level] * mask[level + 1] for level in range(levels - 1)]
    return out


def fetch(pairs, arrived):
    copies = [pltpu.make_async_copy(src, dst, arrived.at[n]) for n, (src, dst) in enumerate(pairs)]
    for copy in copies:
        copy.start()
    return copies


def pack_columns(*refs):
    inputs, (fields, near, far), scratch = refs[:7], refs[7:10], refs[12:]
    copies = fetch(zip(inputs, [*scratch[:5], *refs[10:12]]), scratch[5])
    for copy in copies[:5]:
        copy.wait()
    shape = near.shape[1:]
    lane = lanes(shape)
    west = [jnp.zeros(shape, f32) for _ in range(near.shape[0])]
    east = [jnp.zeros(shape, f32) for _ in range(near.shape[0])]
    for i, field in enumerate(tile_fields(*scratch[:5])):
        fields[i] = field
        part, at = divmod(i, PER_LANES)
        at *= HALO
        here = (lane >= at) & (lane < at + HALO)
        west[part] = jnp.where(here, turn(field[:, :BLOCK], at, 1), west[part])
        east[part] = jnp.where(here, turn(field[:, -BLOCK:], at + HALO, 1), east[part])
    for part in range(near.shape[0]):
        near[part], far[part] = sort_swap("lon", east[part], west[part])
    for copy in copies[5:]:
        copy.wait()


def unpack_columns(from_west, from_east, i):
    part, at = divmod(i, PER_LANES)
    at *= HALO
    lane = lanes(from_west[part].shape)
    east = turn(from_east[part], -at, 1)
    west = turn(from_west[part], -at - HALO, 1)
    return jnp.where(lane < HALO, east, jnp.where(lane >= BLOCK - HALO, west, 0.0))


def row_sources(fields, from_west, from_east):
    out = [(fields, (i, slice(None), slice(h * BLOCK, (h + 1) * BLOCK)))
           for i in range(fields.shape[0]) for h in range(fields.shape[2] // BLOCK)]
    for columns in (from_west, from_east):
        out += [(columns, (part,)) for part in range(columns.shape[0])]
    return out


def pack_rows(fields, near_columns, far_columns, sums, near, far, from_west, from_east, same_sums):
    for part in range(from_west.shape[0]):
        from_east[part], from_west[part] = sort_swap("lon", near_columns[part], far_columns[part])
    sources = [ref[at] for ref, at in row_sources(fields, from_west, from_east)]
    half = near.shape[0]
    row = rows((8, BLOCK))
    for i in range(half):
        first = sources[i]
        second = sources[i + half] if i + half < len(sources) else jnp.zeros_like(first)
        to_north = jnp.where(row < HALO, turn(first[-8:], HALO, 0), second[-8:])
        to_south = jnp.where(row < HALO, first[:8], turn(second[:8], HALO, 0))
        near[i], far[i] = sort_swap("lat", to_north, to_south)


def edge_rows(near, far, i):
    half = near.shape[0]
    from_north, from_south = sort_swap("lat", near[i % half], far[i % half])
    if i < half:
        from_south = turn(from_south, HALO, 0)
    else:
        from_north = turn(from_north, HALO, 0)
    return jnp.where(rows(from_north.shape) < HALO, from_north, from_south)


def widen(fields, from_west, from_east, near, far, start, wide):
    count, tile_lat, tile_lon = fields.shape
    halves = tile_lon // BLOCK
    parts = from_west.shape[0]
    corners = [edge_rows(near, far, count * halves + n) for n in range(2 * parts)]
    for i in range(count):
        out = start.at[i] if i < start.shape[0] else wide.at[i - start.shape[0]]
        out[:tile_lat, :tile_lon] = fields[i]
        out[:tile_lat, tile_lon:] = unpack_columns(from_west, from_east, i)
        for h in range(halves):
            out[tile_lat:, h * BLOCK : (h + 1) * BLOCK] = edge_rows(near, far, i * halves + h)
        out[tile_lat:, tile_lon:] = unpack_columns(corners[:parts], corners[parts:], i)


def eastward(x):
    return turn(x, -1, 1)


def westward(x):
    return turn(x, 1, 1)


def northward(x):
    return turn(x, -1, 0)


def southward(x):
    return turn(x, 1, 0)


def adjoint_step(coeffs, read, write, first, last):
    levels = coeffs.shape[1]
    above = coeffs[4, first - 1] * (read(first) - read(first - 1)) if first else None
    for level in range(first, last):
        lam = read(level)
        step_x = eastward(lam) - lam
        step_y = northward(lam) - lam
        out = lam + coeffs[0, level] * step_x + westward(coeffs[1, level] * step_x)
        out = out + coeffs[2, level] * step_y + southward(coeffs[3, level] * step_y)
        if above is not None:
            out = out - above
        if level < levels - 1:
            above = coeffs[4, level] * (read(level + 1) - lam)
            out = out + above
        write(level, out)


def surface_levels(step, levels):
    return min(levels, STEPS - 1 - step)


def run_adjoint(
    fields, from_west, from_east, far, near, blocks, coeffs, start, states, wide, own, sent
):
    levels = coeffs.shape[1]
    tile_lat, tile_lon = fields.shape[1:]
    halves = tile_lon // BLOCK
    widen(fields, from_west, from_east, near, far, start, wide)
    base = 0
    mask0 = None
    for level in range(levels):
        east_d, east_u = wide[base + level], wide[base + levels + level]
        north_d, north_u = wide[base + 2 * levels + level], wide[base + 3 * levels + level]
        mask = (east_d > 0.0).astype(f32)
        mask0 = mask if mask0 is None else mask0
        mask_e, mask_n = eastward(mask), northward(mask)
        east_k, east_v = east_d * mask_e, east_u * mask_e
        north_k, north_v = north_d * mask_n, north_u * mask_n
        coeffs[0, level] = jnp.maximum(east_v, 0.0) + east_k
        coeffs[1, level] = jnp.minimum(east_v, 0.0) - east_k
        coeffs[2, level] = jnp.maximum(north_v, 0.0) + north_k
        coeffs[3, level] = jnp.minimum(north_v, 0.0) - north_k
        coeffs[4, level] = wide[base + 4 * levels + level] if level < levels - 1 else jnp.zeros_like(mask)
        coeffs[5, level] = mask
    copies = []
    for f in range(2):
        surface = start[(2 + f) * levels, :tile_lat, :tile_lon]
        for step in range(STEPS - 1):

            def read(level):
                return states[f, step - 1, level] if step else start[(2 + f) * levels + level]

            def write(level, lam):
                states[f, step, level] = lam

            adjoint_step(coeffs, read, write, 0, surface_levels(step, levels))
            surface = surface + states[f, step, 0, :tile_lat, :tile_lon]
        surface = surface * mask0[:tile_lat, :tile_lon]
        for h in range(halves):
            at = (f * halves + h) * tile_lat
            own[at : at + tile_lat] = surface[:, h * BLOCK : (h + 1) * BLOCK]
        field = pl.ds(f * halves * tile_lat, halves * tile_lat)
        copies += fetch([(own.at[field], blocks.at[k, field]) for k in range(blocks.shape[0])], sent.at[f])
    for copy in copies:
        copy.wait()


def finish_adjoint(coeffs, start, states, adjoint_out, rest):
    levels = coeffs.shape[1]
    tile_lat, tile_lon = adjoint_out.shape[2:]
    for f in range(2):
        for step in range(STEPS):
            done = surface_levels(step, levels)

            def read(level):
                if not step:
                    return start[(2 + f) * levels + level]
                return (states if level < surface_levels(step - 1, levels) else rest)[f, step - 1, level]

            def write(level, lam):
                if step == STEPS - 1:
                    adjoint_out[f, level] = lam[:tile_lat, :tile_lon]
                else:
                    rest[f, step, level] = lam

            adjoint_step(coeffs, read, write, done, levels)


def sum_forcing(received, forcing, near, far):
    tile_lat = forcing.shape[1]
    halves = forcing.shape[2] // BLOCK - 1
    total = received[0]
    for j in range(1, received.shape[0]):
        total = total + received[j]
    lane = lanes((tile_lat, BLOCK))
    upper = total[2 * halves * tile_lat :]
    lower = jnp.where(lane[: tile_lat // 2] < BLOCK // 2, turn(upper, -2 * HALO, 1), turn(upper, 2 * HALO, 1))
    packed = jnp.concatenate([upper, lower], axis=0)
    for f in range(2):
        for h in range(halves):
            at = (f * halves + h) * tile_lat
            forcing[f, :, h * BLOCK : (h + 1) * BLOCK] = total[at : at + tile_lat]
        used = (lane < HALO) | (lane >= BLOCK - HALO)
        if f == 0:
            edge = packed
        else:
            edge = jnp.where(lane < HALO, turn(packed, -HALO, 1), turn(packed, HALO, 1))
        forcing[f, :, halves * BLOCK :] = jnp.where(used, edge, 0.0)
    row = rows((8, forcing.shape[2]))
    to_north = jnp.where(row < HALO, turn(forcing[0, tile_lat - 8 :], HALO, 0), forcing[1, tile_lat - 8 :])
    to_south = jnp.where(row < HALO, forcing[0, :8], turn(forcing[1, :8], HALO, 0))
    near[0], far[0] = sort_swap("lat", to_north, to_south)


def run_forward(coeffs, start, forcing, far, near, final, state):
    levels = coeffs.shape[1]
    tile_lat, tile_lon = final.shape[2:]
    for f in range(2):
        force = jnp.concatenate([forcing[f], edge_rows(near, far, f)], axis=0)
        force = force * coeffs[5, 0]
        for step in range(STEPS):
            above = None
            for level in range(levels):
                read = (lambda n: start[f * levels + n]) if step == 0 else (lambda n: state[(step - 1) % 2, n])
                theta = read(level)
                east_flux = coeffs[0, level] * theta + coeffs[1, level] * eastward(theta)
                north_flux = coeffs[2, level] * theta + coeffs[3, level] * northward(theta)
                out = theta - (east_flux - westward(east_flux)) - (north_flux - southward(north_flux))
                if level < levels - 1:
                    vertical = coeffs[4, level] * (theta - read(level + 1))
                    out = out - vertical
                if above is not None:
                    out = out + above
                above = vertical if level < levels - 1 else None
                if level == 0:
                    out = out + force
                if step == STEPS - 1:
                    final[f, level] = out[:tile_lat, :tile_lon]
                else:
                    state[step % 2, level] = out


def split(x):
    high = x.astype(bf16)
    return high, (x - high.astype(f32)).astype(bf16)


def weight_copy(weights, held, arrived, n):
    own = pl.ds(n * FETCH, FETCH)
    return pltpu.make_async_copy(weights.at[own], held.at[own], arrived.at[n])


def fetch_weights(weights, held, arrived):
    for n in range(held.shape[0] // FETCH):
        weight_copy(weights, held, arrived, n).start()


def held_part(weights, held, arrived):
    def part(r, g, u):
        if u == 0:

            @pl.when(r == 0)
            def _():
                for n in range(GROUP // FETCH):
                    weight_copy(weights, held, arrived, g * (GROUP // FETCH) + n).wait()

        return split(held[g * GROUP + u])

    return part


def one_hot(where):
    return jnp.where(where, 1.0, 0.0).astype(bf16)


def places(slots, blocks):
    return 8 * (-(-2 * slots // (8 * blocks)) + 1)


def round_chunks(slots, blocks):
    return -(-(slots + 7 * blocks) // BLOCK)


def as_row(ids):
    return jnp.concatenate([ids[k : k + 1, :] for k in range(ids.shape[0])], axis=1)


def rank_slots(block_row, blocks):
    slots = block_row.shape[1]
    mine = rows((blocks, slots)) == block_row
    cuts = range(0, slots, BLOCK)
    stacked = jnp.concatenate([one_hot(mine[:, at : at + BLOCK]) for at in cuts], axis=0)
    shape = (BLOCK, 2 * BLOCK)
    counts = jnp.dot(stacked, one_hot(rows(shape) < lanes(shape)), preferred_element_type=f32)
    before, out = jnp.zeros((blocks, BLOCK), f32), []
    for n, at in enumerate(cuts):
        run = counts[n * blocks : (n + 1) * blocks]
        here = jnp.where(mine[:, at : at + BLOCK], run[:, :BLOCK] + before, 0.0)
        out.append(jnp.sum(here, axis=0, keepdims=True))
        before = before + run[:, BLOCK:]
    return jnp.concatenate(out, axis=1), before


def find_slots(r, keys, counts, capacity, columns, lines, starts):
    slots = keys.shape[1]
    blocks = counts.shape[0]
    atm_row, ocean_row, block_row, rank = (keys[n : n + 1] for n in range(4))
    count = jnp.clip(counts - r * capacity, 0.0, capacity)
    tiles = jnp.floor((count + 7.0) * 0.125) * 8.0
    shape = (blocks, blocks)
    first = jnp.dot(one_hot(lanes(shape) < rows(shape)), tiles.astype(bf16), preferred_element_type=f32)
    starts[...] = first.astype(jnp.int32)
    mine = rows((blocks, slots)).astype(f32) == block_row
    own = jnp.where(mine, jnp.concatenate([first] * (slots // BLOCK), axis=1), 0.0)
    place = rank - r * capacity
    here = (place >= 0.0) & (place < capacity)
    place = jnp.where(here, jnp.sum(own, axis=0, keepdims=True) + place, -1.0)
    run = jnp.floor(place * (1.0 / BLOCK))
    low = one_hot(rows((BLOCK, slots)).astype(f32) == place - run * BLOCK)
    size = lines.shape[1]
    in_run = rows((size, slots)).astype(f32) == run
    ocean_high = jnp.floor(ocean_row * (1.0 / BLOCK))
    digits = [atm_row, ocean_high, ocean_row - ocean_high * BLOCK]
    digits = [jnp.where(in_run, digit, 0.0).astype(bf16) for digit in digits]
    across = (((1,), (1,)), ((), ()))
    down = [lax.dot_general(low, digit, across, preferred_element_type=f32) for digit in digits]
    along = [lax.dot_general(digit, low, across, preferred_element_type=f32) for digit in digits]
    columns[0, :, :size], columns[1, :, :size] = down[0], down[1] * BLOCK + down[2] - 1.0
    ocean = along[1] * BLOCK + along[2] - 1.0
    lines[0], lines[1] = jnp.where(ocean < 0.0, -1.0, along[0]), ocean


def couple(part, table, capacity, rounds, prepare, columns, lines, starts, transposed, result, scratch):
    vectors, products, starts_near = scratch
    blocks = starts.shape[0]
    total_rows = vectors.shape[0] - capacity
    width = table.shape[0]
    result[...] = jnp.zeros_like(result)
    products[...] = jnp.zeros_like(products)

    def one_round(r, carry):
        prepare(r)
        first_rows = starts[...]
        for w in range(blocks):
            starts_near[w] = first_rows[w, 0]
        place_hot = []
        for n in range(total_rows // BLOCK):
            gather = jnp.broadcast_to(columns[int(transposed), :, n : n + 1], (BLOCK, BLOCK))
            gather = jnp.concatenate([gather] * (width // BLOCK), axis=1)
            hot = one_hot(gather == lanes((BLOCK, width)).astype(f32))
            vectors[n * BLOCK : (n + 1) * BLOCK] = jnp.dot(hot, table, preferred_element_type=f32)
            put = lines[1 - int(transposed), n : n + 1]
            place_hot.append(one_hot(rows((result.shape[0], BLOCK)).astype(f32) == put))

        def group(g, carry):
            for u in range(GROUP):
                at = pl.ds(pl.multiple_of(starts_near[g * GROUP + u], 8), capacity)
                own = vectors[at]
                left = jnp.concatenate([own[:, n * BLOCK : (n + 1) * BLOCK] for n in range(4)], axis=0)
                high, low = part(r, g, u)
                right = jnp.concatenate([high, low], axis=1 if transposed else 0)
                contract = (((1,), (0 if transposed else 1,)), ((), ()))
                product = lax.dot_general(left.astype(bf16), right, contract, preferred_element_type=f32)
                for f in range(2):
                    high_part = product[f * capacity : (f + 1) * capacity]
                    low_part = product[(f + 2) * capacity : (f + 3) * capacity, :BLOCK]
                    products[at, f * BLOCK : (f + 1) * BLOCK] = (
                        high_part[:, BLOCK:] + low_part
                    ) + high_part[:, :BLOCK]
            return carry

        lax.fori_loop(0, blocks // GROUP, group, 0)
        summed = jnp.dot(
            jnp.concatenate(place_hot, axis=1),
            jnp.concatenate(split(products[:total_rows]), axis=1),
            preferred_element_type=f32,
        )
        result[...] += summed[:, : 2 * BLOCK] + summed[:, 2 * BLOCK :]
        return carry

    lax.fori_loop(0, rounds, one_round, 0)


def slot_keys(ids, tile_lat, keys):
    lon_count, cap = ids.shape[3:]
    ocean, atm_ids, block_ids = (ids[n, 0, 0] for n in range(3))
    order = (ocean & 1) * tile_lat + (ocean >> 1) + rows((lon_count, cap)) * (2 * tile_lat)
    order = jnp.where(ocean >= 0, order, lon_count * 2 * tile_lat) + 1
    for n, part in enumerate((atm_ids, order, block_ids)):
        keys[n : n + 1] = as_row(part.astype(f32))


def weigh(
    atm_near, margins, weights, after, sums, keys, counts, columns, lines, starts, result, *scratch
):
    scratch, (held, arrived) = scratch[:3], scratch[3:]
    fetch_weights(weights, held, arrived)
    lon_count = margins.shape[3]
    blocks = weights.shape[0]
    tile_lat = 2 * sums.shape[1] // 9
    slot_keys(margins, tile_lat, keys)
    rank, count = rank_slots(keys[2:3].astype(jnp.int32), blocks)
    keys[3:4] = rank
    counts[...] = count
    capacity = places(keys.shape[1], blocks)
    rounds = jnp.max(rank).astype(jnp.int32) // capacity + 1
    parts = [split(atm_near[f, 0]) for f in range(2)]
    table = jnp.concatenate([parts[f][n] for n in range(2) for f in range(2)], axis=1)
    part = held_part(weights, held, arrived)

    def prepare(r):
        find_slots((rounds - 1 - r).astype(f32), keys, counts[...], capacity, columns, lines, starts)

    couple(part, table, capacity, rounds, prepare, columns, lines, starts, False, result, scratch)
    lane = lanes((tile_lat, BLOCK))

    def block_sums(k, f, h):
        at = (2 * k + h) * tile_lat
        return result[at : at + tile_lat, f * BLOCK : (f + 1) * BLOCK]

    for n, k in enumerate(group_order(lon_count)):
        edge = jnp.zeros((tile_lat, BLOCK), f32)
        for f in range(2):
            for h in range(2):
                sums[n, (2 * f + h) * tile_lat : (2 * f + h + 1) * tile_lat] = block_sums(k, f, h)
            at = f * HALO
            after = turn(block_sums((k + 1) % lon_count, f, 0), at, 1)
            before = turn(block_sums((k - 1) % lon_count, f, 1), -at, 1)
            edge = jnp.where((lane >= at) & (lane < at + HALO), after, edge)
            end = BLOCK - at
            edge = jnp.where((lane >= end - HALO) & (lane < end), before, edge)
        upper, lower = edge[: tile_lat // 2], edge[tile_lat // 2 :]
        near = lane[: tile_lat // 2]
        lower = jnp.where(near < BLOCK // 2, turn(lower, 2 * HALO, 1), turn(lower, -2 * HALO, 1))
        sums[n, 4 * tile_lat :] = jnp.where((near < 2 * HALO) | (near >= BLOCK - 2 * HALO), upper, lower)


def unweigh(
    gathered, keys, counts, columns_in, lines_in, starts_in, weights, gradient, result, columns, lines, starts, *scratch
):
    scratch, (held, arrived) = scratch[:3], scratch[3:]
    fetch_weights(weights, held, arrived)
    blocks = weights.shape[0]
    lon_count, ocean_blocks = gathered.shape[0], gathered.shape[1] // 2
    order = group_order(lon_count)
    capacity = places(keys.shape[1], blocks)
    rounds = jnp.max(keys[3:4]).astype(jnp.int32) // capacity + 1
    parts = [
        split(
            jnp.concatenate(
                [gathered[order.index(k), f * ocean_blocks : (f + 1) * ocean_blocks] for k in range(lon_count)],
                axis=0,
            )
        )
        for f in range(2)
    ]
    table = jnp.concatenate([parts[f][n] for n in range(2) for f in range(2)], axis=1)

    def prepare(r):
        @pl.when(r == 0)
        def _():
            columns[...] = columns_in[...]
            lines[...] = lines_in[...]
            starts[...] = starts_in[...]

        @pl.when(r > 0)
        def _():
            find_slots(r.astype(f32), keys, counts[...], capacity, columns, lines, starts)

    part = held_part(weights, held, arrived)
    couple(part, table, capacity, rounds, prepare, columns, lines, starts, True, result, scratch)
    for f in range(2):
        gradient[f, 0] = result[:, f * BLOCK : (f + 1) * BLOCK]


def on_device(tracers, cotangent, land_mask, diffusion, velocity, weights, atm_state, margins):
    levels, tile_lat, tile_lon = land_mask.shape
    lon_count = lax.axis_size("lon")
    slots = lon_count * margins.shape[4]
    halves = tile_lon // BLOCK
    count = 9 * levels - 1
    parts = -(-count // PER_LANES)
    inputs = (tracers, cotangent, land_mask, diffusion, velocity)

    def in_vmem(s):
        return pltpu.VMEM(s.shape, s.dtype)

    message = (parts, tile_lat, BLOCK)
    fields, near, far, atm_near, margins_near = call(
        pack_columns,
        [
            (count, tile_lat, tile_lon),
            message,
            message,
            atm_state.shape,
            jax.ShapeDtypeStruct(margins.shape, margins.dtype),
        ],
        [*map(in_vmem, inputs), pltpu.SemaphoreType.DMA((7,))],
        name="pack_columns",
        inputs=7,
        far=range(7),
    )(*inputs, atm_state, margins)
    near_columns, far_columns = swap(near, far, "lon", True)

    blocks_of, atm = weights.shape[0], atm_state.shape[2]
    sum_rows = 2 * halves * tile_lat + tile_lat // 2
    ocean_blocks = lon_count * halves * tile_lat
    chunks = round_chunks(slots, blocks_of)
    held_rows = chunks * BLOCK + places(slots, blocks_of)

    def coupling_scratch(result_rows):
        return [
            pltpu.VMEM((result_rows, 2 * BLOCK), f32),
            pltpu.VMEM((held_rows, 4 * BLOCK), f32),
            pltpu.VMEM((held_rows, 2 * BLOCK), f32),
            pltpu.SMEM((blocks_of,), jnp.int32),
            pltpu.VMEM(weights.shape, f32),
            pltpu.SemaphoreType.DMA((blocks_of // FETCH,)),
        ]

    coupling_flops = 4 * slots * blocks_of * 2 * BLOCK * BLOCK * 2
    found = [
        jax.ShapeDtypeStruct((2, BLOCK, BLOCK), f32),
        jax.ShapeDtypeStruct((2, -(-chunks // 8) * 8, BLOCK), f32),
        jax.ShapeDtypeStruct((blocks_of, BLOCK), jnp.int32),
    ]
    sums, *slot_data = call(
        weigh,
        [(lon_count, sum_rows, BLOCK), (8, slots), (blocks_of, BLOCK), *found],
        coupling_scratch(ocean_blocks),
        coupling_flops,
        name="weigh",
        inputs=4,
        far=(2,),
    )(atm_near, margins_near, weights, far)

    sources = count * halves + 2 * parts
    message = (-(-sources // 2), 8, BLOCK)
    columns = (parts, tile_lat, BLOCK)
    near, far, from_west, from_east, sums = call(
        pack_rows,
        [message, message, columns, columns, sums.shape],
        name="pack_rows",
        inputs=4,
        aliases={3: 4},
    )(fields, near_columns, far_columns, sums)
    received = exchange(sums)
    near_rows, far_rows = swap(near, far, "lat", False)

    wide = (tile_lat + 8, tile_lon + BLOCK)
    own = (2 * halves * tile_lat, BLOCK)
    adjoint_states = (2, STEPS - 1, levels, *wide)
    blocks, coeffs, start, states = call(
        run_adjoint,
        [(lon_count, *own), (6, levels, *wide), (4 * levels, *wide), adjoint_states],
        [
            pltpu.VMEM((count - 4 * levels, *wide), f32),
            pltpu.VMEM(own, f32),
            pltpu.SemaphoreType.DMA((2, lon_count)),
        ],
        name="run_adjoint",
        inputs=5,
        far_outs=(0,),
    )(fields, from_west, from_east, far_rows, near_rows)
    gathered = exchange(blocks)

    message = (1, 8, tile_lon + BLOCK)
    forcing, near, far = call(
        sum_forcing, [(2, tile_lat, tile_lon + BLOCK), message, message], name="sum_forcing", inputs=1
    )(received)
    near_rows, far_rows = swap(near, far, "lat", False)
    (adjoint,) = call(
        finish_adjoint,
        [cotangent.shape],
        [pltpu.VMEM(adjoint_states, f32)],
        name="finish_adjoint",
        inputs=3,
    )(coeffs, start, states)
    (final,) = call(
        run_forward,
        [tracers.shape],
        [pltpu.VMEM((2, levels, *wide), f32)],
        name="run_forward",
        inputs=5,
    )(coeffs, start, forcing, far_rows, near_rows)

    (gradient,) = call(
        unweigh,
        [atm_state.shape],
        [coupling_scratch(atm)[0], *map(in_vmem, found), *coupling_scratch(atm)[1:]],
        coupling_flops,
        name="unweigh",
        inputs=7,
        far=(6,),
    )(gathered, *slot_data, weights)
    return (final, adjoint, gradient)


def solution(mesh):
    return jax.shard_map(
        on_device,
        mesh=mesh,
        in_specs=(
            P(None, None, "lat", "lon"),
            P(None, None, "lat", "lon"),
            P(None, "lat", "lon"),
            P(None, None, "lat", "lon"),
            P(None, None, "lat", "lon"),
            P(),
            P(None, "lat", "lon", None),
            P(None, "lat", "lon", None, None),
        ),
        out_specs=(
            P(None, None, "lat", "lon"),
            P(None, None, "lat", "lon"),
            P(None, "lat", "lon", None),
        ),
        check_vma=False,
    )
```

```python
import jax
import jax.numpy as jnp
from jax import lax
from jax.experimental import pallas as pl
from jax.experimental.pallas import tpu as pltpu
from jax.sharding import PartitionSpec as P

BLOCK = 128
STEPS = 4
HALO = STEPS
PER_LANES = BLOCK // HALO
GROUP = 16
FETCH = 4
f32 = jnp.float32
bf16 = jnp.bfloat16
VMEM_LIMIT = 20 * 1024 * 1024


def call(body, outs, scratch=(), flops=0, name=None, inputs=0, far=(), far_outs=(), aliases=None):
    outs = [s if isinstance(s, jax.ShapeDtypeStruct) else jax.ShapeDtypeStruct(s, f32) for s in outs]
    near = pl.BlockSpec(memory_space=pltpu.VMEM)
    aliases = aliases or {}
    kernel = pl.pallas_call(
        body,
        out_shape=outs,
        in_specs=[
            pl.BlockSpec(memory_space=pl.ANY)
            if n in aliases
            else pl.BlockSpec(memory_space=pltpu.HBM)
            if n in far
            else near
            for n in range(inputs)
        ],
        out_specs=[
            pl.BlockSpec(memory_space=pl.ANY) if n in aliases.values() or n in far_outs else near
            for n in range(len(outs))
        ],
        input_output_aliases=aliases,
        scratch_shapes=list(scratch),
        compiler_params=pltpu.CompilerParams(vmem_limit_bytes=VMEM_LIMIT),
        cost_estimate=pl.CostEstimate(flops=flops, bytes_accessed=1 << 20, transcendentals=0),
        name=name,
    )

    def run(*args):
        return kernel(
            *(pltpu.with_memory_space_constraint(x, pltpu.HBM) if n in far else x for n, x in enumerate(args))
        )

    return run


def lanes(shape):
    return lax.broadcasted_iota(jnp.int32, shape, len(shape) - 1)


def rows(shape):
    return lax.broadcasted_iota(jnp.int32, shape, len(shape) - 2)


def turn(x, shift, axis):
    shift %= x.shape[axis]
    return pltpu.roll(x, shift, axis) if shift else x


def group_order(count):
    half = count // 2
    return [k for n in range(half) for k in (half + n, n)]


def exchange(x):
    order = group_order(x.shape[0])
    return lax.all_to_all(x, "lon", split_axis=0, concat_axis=0, tiled=True, axis_index_groups=[order])


def swap(near, far, axis, wrap):
    count = lax.axis_size(axis)
    pairs = [[], []]
    for i in range(count if wrap else count - 1):
        j = (i + 1) % count
        pairs[i % 2] += [(i, j), (j, i)]
    far = lax.ppermute(far, axis, pairs[1])
    return lax.ppermute(near, axis, pairs[0]), far


def sort_swap(axis, after, before):
    odd = lax.rem(lax.axis_index(axis), 2) == 1
    return jnp.where(odd, before, after), jnp.where(odd, after, before)


def tile_fields(tracers, cotangent, land_mask, diffusion, velocity):
    levels = land_mask.shape[0]
    mask = [land_mask[level].astype(f32) for level in range(levels)]
    out = [tracers[f, level] for f in range(2) for level in range(levels)]
    out += [cotangent[f, level] for f in range(2) for level in range(levels)]
    out += [diffusion[0, level] * mask[level] for level in range(levels)]
    out += [velocity[0, level] * mask[level] for level in range(levels)]
    out += [diffusion[1, level] * mask[level] for level in range(levels)]
    out += [velocity[1, level] * mask[level] for level in range(levels)]
    out += [diffusion[2, level] * mask[level] * mask[level + 1] for level in range(levels - 1)]
    return out


def fetch(pairs, arrived):
    copies = [pltpu.make_async_copy(src, dst, arrived.at[n]) for n, (src, dst) in enumerate(pairs)]
    for copy in copies:
        copy.start()
    return copies


def pack_columns(*refs):
    inputs, (fields, near, far), scratch = refs[:7], refs[7:10], refs[12:]
    copies = fetch(zip(inputs, [*scratch[:5], *refs[10:12]]), scratch[5])
    for copy in copies[:5]:
        copy.wait()
    shape = near.shape[1:]
    lane = lanes(shape)
    west = [jnp.zeros(shape, f32) for _ in range(near.shape[0])]
    east = [jnp.zeros(shape, f32) for _ in range(near.shape[0])]
    for i, field in enumerate(tile_fields(*scratch[:5])):
        fields[i] = field
        part, at = divmod(i, PER_LANES)
        at *= HALO
        here = (lane >= at) & (lane < at + HALO)
        west[part] = jnp.where(here, turn(field[:, :BLOCK], at, 1), west[part])
        east[part] = jnp.where(here, turn(field[:, -BLOCK:], at + HALO, 1), east[part])
    for part in range(near.shape[0]):
        near[part], far[part] = sort_swap("lon", east[part], west[part])
    for copy in copies[5:]:
        copy.wait()


def unpack_columns(from_west, from_east, i):
    part, at = divmod(i, PER_LANES)
    at *= HALO
    lane = lanes(from_west[part].shape)
    east = turn(from_east[part], -at, 1)
    west = turn(from_west[part], -at - HALO, 1)
    return jnp.where(lane < HALO, east, jnp.where(lane >= BLOCK - HALO, west, 0.0))


def row_sources(fields, from_west, from_east):
    out = [(fields, (i, slice(None), slice(h * BLOCK, (h + 1) * BLOCK)))
           for i in range(fields.shape[0]) for h in range(fields.shape[2] // BLOCK)]
    for columns in (from_west, from_east):
        out += [(columns, (part,)) for part in range(columns.shape[0])]
    return out


def pack_rows(fields, near_columns, far_columns, sums, near, far, from_west, from_east, same_sums):
    for part in range(from_west.shape[0]):
        from_east[part], from_west[part] = sort_swap("lon", near_columns[part], far_columns[part])
    sources = [ref[at] for ref, at in row_sources(fields, from_west, from_east)]
    half = near.shape[0]
    row = rows((8, BLOCK))
    for i in range(half):
        first = sources[i]
        second = sources[i + half] if i + half < len(sources) else jnp.zeros_like(first)
        to_north = jnp.where(row < HALO, turn(first[-8:], HALO, 0), second[-8:])
        to_south = jnp.where(row < HALO, first[:8], turn(second[:8], HALO, 0))
        near[i], far[i] = sort_swap("lat", to_north, to_south)


def edge_rows(near, far, i):
    half = near.shape[0]
    from_north, from_south = sort_swap("lat", near[i % half], far[i % half])
    if i < half:
        from_south = turn(from_south, HALO, 0)
    else:
        from_north = turn(from_north, HALO, 0)
    return jnp.where(rows(from_north.shape) < HALO, from_north, from_south)


def widen(fields, from_west, from_east, near, far, start, wide):
    count, tile_lat, tile_lon = fields.shape
    halves = tile_lon // BLOCK
    parts = from_west.shape[0]
    corners = [edge_rows(near, far, count * halves + n) for n in range(2 * parts)]
    for i in range(count):
        out = start.at[i] if i < start.shape[0] else wide.at[i - start.shape[0]]
        out[:tile_lat, :tile_lon] = fields[i]
        out[:tile_lat, tile_lon:] = unpack_columns(from_west, from_east, i)
        for h in range(halves):
            out[tile_lat:, h * BLOCK : (h + 1) * BLOCK] = edge_rows(near, far, i * halves + h)
        out[tile_lat:, tile_lon:] = unpack_columns(corners[:parts], corners[parts:], i)


def eastward(x):
    return turn(x, -1, 1)


def westward(x):
    return turn(x, 1, 1)


def northward(x):
    return turn(x, -1, 0)


def southward(x):
    return turn(x, 1, 0)


def adjoint_step(coeffs, read, write, first, last):
    levels = coeffs.shape[1]
    above = coeffs[4, first - 1] * (read(first) - read(first - 1)) if first else None
    for level in range(first, last):
        lam = read(level)
        step_x = eastward(lam) - lam
        step_y = northward(lam) - lam
        out = lam + coeffs[0, level] * step_x + westward(coeffs[1, level] * step_x)
        out = out + coeffs[2, level] * step_y + southward(coeffs[3, level] * step_y)
        if above is not None:
            out = out - above
        if level < levels - 1:
            above = coeffs[4, level] * (read(level + 1) - lam)
            out = out + above
        write(level, out)


def surface_levels(step, levels):
    return min(levels, STEPS - 1 - step)


def run_adjoint(
    fields, from_west, from_east, far, near, blocks, coeffs, start, states, wide, own, sent
):
    levels = coeffs.shape[1]
    tile_lat, tile_lon = fields.shape[1:]
    halves = tile_lon // BLOCK
    widen(fields, from_west, from_east, near, far, start, wide)
    base = 0
    mask0 = None
    for level in range(levels):
        east_d, east_u = wide[base + level], wide[base + levels + level]
        north_d, north_u = wide[base + 2 * levels + level], wide[base + 3 * levels + level]
        mask = (east_d > 0.0).astype(f32)
        mask0 = mask if mask0 is None else mask0
        mask_e, mask_n = eastward(mask), northward(mask)
        east_k, east_v = east_d * mask_e, east_u * mask_e
        north_k, north_v = north_d * mask_n, north_u * mask_n
        coeffs[0, level] = jnp.maximum(east_v, 0.0) + east_k
        coeffs[1, level] = jnp.minimum(east_v, 0.0) - east_k
        coeffs[2, level] = jnp.maximum(north_v, 0.0) + north_k
        coeffs[3, level] = jnp.minimum(north_v, 0.0) - north_k
        coeffs[4, level] = wide[base + 4 * levels + level] if level < levels - 1 else jnp.zeros_like(mask)
        coeffs[5, level] = mask
    copies = []
    for f in range(2):
        surface = start[(2 + f) * levels, :tile_lat, :tile_lon]
        for step in range(STEPS - 1):

            def read(level):
                return states[f, step - 1, level] if step else start[(2 + f) * levels + level]

            def write(level, lam):
                states[f, step, level] = lam

            adjoint_step(coeffs, read, write, 0, surface_levels(step, levels))
            surface = surface + states[f, step, 0, :tile_lat, :tile_lon]
        surface = surface * mask0[:tile_lat, :tile_lon]
        for h in range(halves):
            at = (f * halves + h) * tile_lat
            own[at : at + tile_lat] = surface[:, h * BLOCK : (h + 1) * BLOCK]
        field = pl.ds(f * halves * tile_lat, halves * tile_lat)
        copies += fetch([(own.at[field], blocks.at[k, field]) for k in range(blocks.shape[0])], sent.at[f])
    for copy in copies:
        copy.wait()


def finish_adjoint(coeffs, start, states, adjoint_out, rest):
    levels = coeffs.shape[1]
    tile_lat, tile_lon = adjoint_out.shape[2:]
    for f in range(2):
        for step in range(STEPS):
            done = surface_levels(step, levels)

            def read(level):
                if not step:
                    return start[(2 + f) * levels + level]
                return (states if level < surface_levels(step - 1, levels) else rest)[f, step - 1, level]

            def write(level, lam):
                if step == STEPS - 1:
                    adjoint_out[f, level] = lam[:tile_lat, :tile_lon]
                else:
                    rest[f, step, level] = lam

            adjoint_step(coeffs, read, write, done, levels)


def sum_forcing(received, forcing, near, far):
    tile_lat = forcing.shape[1]
    halves = forcing.shape[2] // BLOCK - 1
    total = received[0]
    for j in range(1, received.shape[0]):
        total = total + received[j]
    lane = lanes((tile_lat, BLOCK))
    upper = total[2 * halves * tile_lat :]
    lower = jnp.where(lane[: tile_lat // 2] < BLOCK // 2, turn(upper, -2 * HALO, 1), turn(upper, 2 * HALO, 1))
    packed = jnp.concatenate([upper, lower], axis=0)
    for f in range(2):
        for h in range(halves):
            at = (f * halves + h) * tile_lat
            forcing[f, :, h * BLOCK : (h + 1) * BLOCK] = total[at : at + tile_lat]
        used = (lane < HALO) | (lane >= BLOCK - HALO)
        if f == 0:
            edge = packed
        else:
            edge = jnp.where(lane < HALO, turn(packed, -HALO, 1), turn(packed, HALO, 1))
        forcing[f, :, halves * BLOCK :] = jnp.where(used, edge, 0.0)
    row = rows((8, forcing.shape[2]))
    to_north = jnp.where(row < HALO, turn(forcing[0, tile_lat - 8 :], HALO, 0), forcing[1, tile_lat - 8 :])
    to_south = jnp.where(row < HALO, forcing[0, :8], turn(forcing[1, :8], HALO, 0))
    near[0], far[0] = sort_swap("lat", to_north, to_south)


def run_forward(coeffs, start, forcing, far, near, final, state):
    levels = coeffs.shape[1]
    tile_lat, tile_lon = final.shape[2:]
    for f in range(2):
        force = jnp.concatenate([forcing[f], edge_rows(near, far, f)], axis=0)
        force = force * coeffs[5, 0]
        for step in range(STEPS):
            above = None
            for level in range(levels):
                read = (lambda n: start[f * levels + n]) if step == 0 else (lambda n: state[(step - 1) % 2, n])
                theta = read(level)
                east_flux = coeffs[0, level] * theta + coeffs[1, level] * eastward(theta)
                north_flux = coeffs[2, level] * theta + coeffs[3, level] * northward(theta)
                out = theta - (east_flux - westward(east_flux)) - (north_flux - southward(north_flux))
                if level < levels - 1:
                    vertical = coeffs[4, level] * (theta - read(level + 1))
                    out = out - vertical
                if above is not None:
                    out = out + above
                above = vertical if level < levels - 1 else None
                if level == 0:
                    out = out + force
                if step == STEPS - 1:
                    final[f, level] = out[:tile_lat, :tile_lon]
                else:
                    state[step % 2, level] = out


def split(x):
    high = x.astype(bf16)
    return high, (x - high.astype(f32)).astype(bf16)


def weight_copy(weights, held, arrived, n):
    own = pl.ds(n * FETCH, FETCH)
    return pltpu.make_async_copy(weights.at[own], held.at[own], arrived.at[n])


def fetch_weights(weights, held, arrived):
    for n in range(held.shape[0] // FETCH):
        weight_copy(weights, held, arrived, n).start()


def held_part(weights, held, arrived):
    def part(r, g, u):
        if u == 0:

            @pl.when(r == 0)
            def _():
                for n in range(GROUP // FETCH):
                    weight_copy(weights, held, arrived, g * (GROUP // FETCH) + n).wait()

        return split(held[g * GROUP + u])

    return part


def one_hot(where):
    return jnp.where(where, 1.0, 0.0).astype(bf16)


def places(slots, blocks):
    return 8 * (-(-2 * slots // (8 * blocks)) + 1)


def round_chunks(slots, blocks):
    return -(-(slots + 7 * blocks) // BLOCK)


def as_row(ids):
    return jnp.concatenate([ids[k : k + 1, :] for k in range(ids.shape[0])], axis=1)


def rank_slots(block_row, blocks):
    slots = block_row.shape[1]
    mine = rows((blocks, slots)) == block_row
    cuts = range(0, slots, BLOCK)
    stacked = jnp.concatenate([one_hot(mine[:, at : at + BLOCK]) for at in cuts], axis=0)
    shape = (BLOCK, 2 * BLOCK)
    counts = jnp.dot(stacked, one_hot(rows(shape) < lanes(shape)), preferred_element_type=f32)
    before, out = jnp.zeros((blocks, BLOCK), f32), []
    for n, at in enumerate(cuts):
        run = counts[n * blocks : (n + 1) * blocks]
        here = jnp.where(mine[:, at : at + BLOCK], run[:, :BLOCK] + before, 0.0)
        out.append(jnp.sum(here, axis=0, keepdims=True))
        before = before + run[:, BLOCK:]
    return jnp.concatenate(out, axis=1), before


def find_slots(r, keys, counts, capacity, columns, lines, starts):
    slots = keys.shape[1]
    blocks = counts.shape[0]
    atm_row, ocean_row, block_row, rank = (keys[n : n + 1] for n in range(4))
    count = jnp.clip(counts - r * capacity, 0.0, capacity)
    tiles = jnp.floor((count + 7.0) * 0.125) * 8.0
    shape = (blocks, blocks)
    first = jnp.dot(one_hot(lanes(shape) < rows(shape)), tiles.astype(bf16), preferred_element_type=f32)
    starts[...] = first.astype(jnp.int32)
    mine = rows((blocks, slots)).astype(f32) == block_row
    own = jnp.where(mine, jnp.concatenate([first] * (slots // BLOCK), axis=1), 0.0)
    place = rank - r * capacity
    here = (place >= 0.0) & (place < capacity)
    place = jnp.where(here, jnp.sum(own, axis=0, keepdims=True) + place, -1.0)
    run = jnp.floor(place * (1.0 / BLOCK))
    low = one_hot(rows((BLOCK, slots)).astype(f32) == place - run * BLOCK)
    size = lines.shape[1]
    in_run = rows((size, slots)).astype(f32) == run
    ocean_high = jnp.floor(ocean_row * (1.0 / BLOCK))
    digits = [atm_row, ocean_high, ocean_row - ocean_high * BLOCK]
    digits = [jnp.where(in_run, digit, 0.0).astype(bf16) for digit in digits]
    across = (((1,), (1,)), ((), ()))
    down = [lax.dot_general(low, digit, across, preferred_element_type=f32) for digit in digits]
    along = [lax.dot_general(digit, low, across, preferred_element_type=f32) for digit in digits]
    columns[0, :, :size], columns[1, :, :size] = down[0], down[1] * BLOCK + down[2] - 1.0
    ocean = along[1] * BLOCK + along[2] - 1.0
    lines[0], lines[1] = jnp.where(ocean < 0.0, -1.0, along[0]), ocean


def couple(part, table, capacity, rounds, prepare, columns, lines, starts, transposed, result, scratch):
    vectors, products, starts_near = scratch
    blocks = starts.shape[0]
    total_rows = vectors.shape[0] - capacity
    width = table.shape[0]
    result[...] = jnp.zeros_like(result)
    products[...] = jnp.zeros_like(products)

    def one_round(r, carry):
        prepare(r)
        first_rows = starts[...]
        for w in range(blocks):
            starts_near[w] = first_rows[w, 0]
        place_hot = []
        for n in range(total_rows // BLOCK):
            gather = jnp.broadcast_to(columns[int(transposed), :, n : n + 1], (BLOCK, BLOCK))
            gather = jnp.concatenate([gather] * (width // BLOCK), axis=1)
            hot = one_hot(gather == lanes((BLOCK, width)).astype(f32))
            vectors[n * BLOCK : (n + 1) * BLOCK] = jnp.dot(hot, table, preferred_element_type=f32)
            put = lines[1 - int(transposed), n : n + 1]
            place_hot.append(one_hot(rows((result.shape[0], BLOCK)).astype(f32) == put))

        def group(g, carry):
            for u in range(GROUP):
                at = pl.ds(pl.multiple_of(starts_near[g * GROUP + u], 8), capacity)
                own = vectors[at]
                left = jnp.concatenate([own[:, : 2 * BLOCK], own[:, 2 * BLOCK :]], axis=0)
                both = jnp.concatenate(part(r, g, u), axis=1 if transposed else 0)
                right = jnp.concatenate([both, both], axis=0 if transposed else 1)
                contract = (((1,), (0 if transposed else 1,)), ((), ()))
                product = lax.dot_general(left.astype(bf16), right, contract, preferred_element_type=f32)
                for f in range(2):
                    field = product[f * capacity : (f + 1) * capacity]
                    products[at, f * BLOCK : (f + 1) * BLOCK] = field[:, :BLOCK] + field[:, BLOCK:]
            return carry

        lax.fori_loop(0, blocks // GROUP, group, 0)
        summed = jnp.dot(
            jnp.concatenate(place_hot, axis=1),
            jnp.concatenate(split(products[:total_rows]), axis=1),
            preferred_element_type=f32,
        )
        result[...] += summed[:, : 2 * BLOCK] + summed[:, 2 * BLOCK :]
        return carry

    lax.fori_loop(0, rounds, one_round, 0)


def slot_keys(ids, tile_lat, keys):
    lon_count, cap = ids.shape[3:]
    ocean, atm_ids, block_ids = (ids[n, 0, 0] for n in range(3))
    order = (ocean & 1) * tile_lat + (ocean >> 1) + rows((lon_count, cap)) * (2 * tile_lat)
    order = jnp.where(ocean >= 0, order, lon_count * 2 * tile_lat) + 1
    for n, part in enumerate((atm_ids, order, block_ids)):
        keys[n : n + 1] = as_row(part.astype(f32))


def weigh(
    atm_near, margins, weights, after, sums, keys, counts, columns, lines, starts, result, *scratch
):
    scratch, (held, arrived) = scratch[:3], scratch[3:]
    fetch_weights(weights, held, arrived)
    lon_count = margins.shape[3]
    blocks = weights.shape[0]
    tile_lat = 2 * sums.shape[1] // 9
    slot_keys(margins, tile_lat, keys)
    rank, count = rank_slots(keys[2:3].astype(jnp.int32), blocks)
    keys[3:4] = rank
    counts[...] = count
    capacity = places(keys.shape[1], blocks)
    rounds = jnp.max(rank).astype(jnp.int32) // capacity + 1
    parts = [split(atm_near[f, 0]) for f in range(2)]
    table = jnp.concatenate([parts[f][n] for f in range(2) for n in range(2)], axis=1)
    part = held_part(weights, held, arrived)

    def prepare(r):
        find_slots((rounds - 1 - r).astype(f32), keys, counts[...], capacity, columns, lines, starts)

    couple(part, table, capacity, rounds, prepare, columns, lines, starts, False, result, scratch)
    lane = lanes((tile_lat, BLOCK))

    def block_sums(k, f, h):
        at = (2 * k + h) * tile_lat
        return result[at : at + tile_lat, f * BLOCK : (f + 1) * BLOCK]

    for n, k in enumerate(group_order(lon_count)):
        edge = jnp.zeros((tile_lat, BLOCK), f32)
        for f in range(2):
            for h in range(2):
                sums[n, (2 * f + h) * tile_lat : (2 * f + h + 1) * tile_lat] = block_sums(k, f, h)
            at = f * HALO
            after = turn(block_sums((k + 1) % lon_count, f, 0), at, 1)
            before = turn(block_sums((k - 1) % lon_count, f, 1), -at, 1)
            edge = jnp.where((lane >= at) & (lane < at + HALO), after, edge)
            end = BLOCK - at
            edge = jnp.where((lane >= end - HALO) & (lane < end), before, edge)
        upper, lower = edge[: tile_lat // 2], edge[tile_lat // 2 :]
        near = lane[: tile_lat // 2]
        lower = jnp.where(near < BLOCK // 2, turn(lower, 2 * HALO, 1), turn(lower, -2 * HALO, 1))
        sums[n, 4 * tile_lat :] = jnp.where((near < 2 * HALO) | (near >= BLOCK - 2 * HALO), upper, lower)


def unweigh(
    gathered, keys, counts, columns_in, lines_in, starts_in, weights, gradient, result, columns, lines, starts, *scratch
):
    scratch, (held, arrived) = scratch[:3], scratch[3:]
    fetch_weights(weights, held, arrived)
    blocks = weights.shape[0]
    lon_count, ocean_blocks = gathered.shape[0], gathered.shape[1] // 2
    order = group_order(lon_count)
    capacity = places(keys.shape[1], blocks)
    rounds = jnp.max(keys[3:4]).astype(jnp.int32) // capacity + 1
    parts = [
        split(
            jnp.concatenate(
                [gathered[order.index(k), f * ocean_blocks : (f + 1) * ocean_blocks] for k in range(lon_count)],
                axis=0,
            )
        )
        for f in range(2)
    ]
    table = jnp.concatenate([parts[f][n] for f in range(2) for n in range(2)], axis=1)

    def prepare(r):
        @pl.when(r == 0)
        def _():
            columns[...] = columns_in[...]
            lines[...] = lines_in[...]
            starts[...] = starts_in[...]

        @pl.when(r > 0)
        def _():
            find_slots(r.astype(f32), keys, counts[...], capacity, columns, lines, starts)

    part = held_part(weights, held, arrived)
    couple(part, table, capacity, rounds, prepare, columns, lines, starts, True, result, scratch)
    for f in range(2):
        gradient[f, 0] = result[:, f * BLOCK : (f + 1) * BLOCK]


def on_device(tracers, cotangent, land_mask, diffusion, velocity, weights, atm_state, margins):
    levels, tile_lat, tile_lon = land_mask.shape
    lon_count = lax.axis_size("lon")
    slots = lon_count * margins.shape[4]
    halves = tile_lon // BLOCK
    count = 9 * levels - 1
    parts = -(-count // PER_LANES)
    inputs = (tracers, cotangent, land_mask, diffusion, velocity)

    def in_vmem(s):
        return pltpu.VMEM(s.shape, s.dtype)

    message = (parts, tile_lat, BLOCK)
    fields, near, far, atm_near, margins_near = call(
        pack_columns,
        [
            (count, tile_lat, tile_lon),
            message,
            message,
            atm_state.shape,
            jax.ShapeDtypeStruct(margins.shape, margins.dtype),
        ],
        [*map(in_vmem, inputs), pltpu.SemaphoreType.DMA((7,))],
        name="pack_columns",
        inputs=7,
        far=range(7),
    )(*inputs, atm_state, margins)
    near_columns, far_columns = swap(near, far, "lon", True)

    blocks_of, atm = weights.shape[0], atm_state.shape[2]
    sum_rows = 2 * halves * tile_lat + tile_lat // 2
    ocean_blocks = lon_count * halves * tile_lat
    chunks = round_chunks(slots, blocks_of)
    held_rows = chunks * BLOCK + places(slots, blocks_of)

    def coupling_scratch(result_rows):
        return [
            pltpu.VMEM((result_rows, 2 * BLOCK), f32),
            pltpu.VMEM((held_rows, 4 * BLOCK), f32),
            pltpu.VMEM((held_rows, 2 * BLOCK), f32),
            pltpu.SMEM((blocks_of,), jnp.int32),
            pltpu.VMEM(weights.shape, f32),
            pltpu.SemaphoreType.DMA((blocks_of // FETCH,)),
        ]

    coupling_flops = 4 * slots * blocks_of * 2 * BLOCK * BLOCK * 2
    found = [
        jax.ShapeDtypeStruct((2, BLOCK, BLOCK), f32),
        jax.ShapeDtypeStruct((2, -(-chunks // 8) * 8, BLOCK), f32),
        jax.ShapeDtypeStruct((blocks_of, BLOCK), jnp.int32),
    ]
    sums, *slot_data = call(
        weigh,
        [(lon_count, sum_rows, BLOCK), (8, slots), (blocks_of, BLOCK), *found],
        coupling_scratch(ocean_blocks),
        coupling_flops,
        name="weigh",
        inputs=4,
        far=(2,),
    )(atm_near, margins_near, weights, far)

    sources = count * halves + 2 * parts
    message = (-(-sources // 2), 8, BLOCK)
    columns = (parts, tile_lat, BLOCK)
    near, far, from_west, from_east, sums = call(
        pack_rows,
        [message, message, columns, columns, sums.shape],
        name="pack_rows",
        inputs=4,
        aliases={3: 4},
    )(fields, near_columns, far_columns, sums)
    received = exchange(sums)
    near_rows, far_rows = swap(near, far, "lat", False)

    wide = (tile_lat + 8, tile_lon + BLOCK)
    own = (2 * halves * tile_lat, BLOCK)
    adjoint_states = (2, STEPS - 1, levels, *wide)
    blocks, coeffs, start, states = call(
        run_adjoint,
        [(lon_count, *own), (6, levels, *wide), (4 * levels, *wide), adjoint_states],
        [
            pltpu.VMEM((count - 4 * levels, *wide), f32),
            pltpu.VMEM(own, f32),
            pltpu.SemaphoreType.DMA((2, lon_count)),
        ],
        name="run_adjoint",
        inputs=5,
        far_outs=(0,),
    )(fields, from_west, from_east, far_rows, near_rows)
    gathered = exchange(blocks)

    message = (1, 8, tile_lon + BLOCK)
    forcing, near, far = call(
        sum_forcing, [(2, tile_lat, tile_lon + BLOCK), message, message], name="sum_forcing", inputs=1
    )(received)
    near_rows, far_rows = swap(near, far, "lat", False)
    (adjoint,) = call(
        finish_adjoint,
        [cotangent.shape],
        [pltpu.VMEM(adjoint_states, f32)],
        name="finish_adjoint",
        inputs=3,
    )(coeffs, start, states)
    (final,) = call(
        run_forward,
        [tracers.shape],
        [pltpu.VMEM((2, levels, *wide), f32)],
        name="run_forward",
        inputs=5,
    )(coeffs, start, forcing, far_rows, near_rows)

    (gradient,) = call(
        unweigh,
        [atm_state.shape],
        [coupling_scratch(atm)[0], *map(in_vmem, found), *coupling_scratch(atm)[1:]],
        coupling_flops,
        name="unweigh",
        inputs=7,
        far=(6,),
    )(gathered, *slot_data, weights)
    return (final, adjoint, gradient)


def solution(mesh):
    return jax.shard_map(
        on_device,
        mesh=mesh,
        in_specs=(
            P(None, None, "lat", "lon"),
            P(None, None, "lat", "lon"),
            P(None, "lat", "lon"),
            P(None, None, "lat", "lon"),
            P(None, None, "lat", "lon"),
            P(),
            P(None, "lat", "lon", None),
            P(None, "lat", "lon", None, None),
        ),
        out_specs=(
            P(None, None, "lat", "lon"),
            P(None, None, "lat", "lon"),
            P(None, "lat", "lon", None),
        ),
        check_vma=False,
    )
```

```python
import jax
import jax.numpy as jnp
from jax import lax
from jax.experimental import pallas as pl
from jax.experimental.pallas import tpu as pltpu
from jax.sharding import PartitionSpec as P

BLOCK = 128
STEPS = 4
HALO = STEPS
PER_LANES = BLOCK // HALO
GROUP = 16
FETCH = 4
f32 = jnp.float32
bf16 = jnp.bfloat16
VMEM_LIMIT = 20 * 1024 * 1024


def call(body, outs, scratch=(), flops=0, name=None, inputs=0, far=(), far_outs=(), aliases=None):
    outs = [s if isinstance(s, jax.ShapeDtypeStruct) else jax.ShapeDtypeStruct(s, f32) for s in outs]
    near = pl.BlockSpec(memory_space=pltpu.VMEM)
    aliases = aliases or {}
    kernel = pl.pallas_call(
        body,
        out_shape=outs,
        in_specs=[
            pl.BlockSpec(memory_space=pl.ANY)
            if n in aliases
            else pl.BlockSpec(memory_space=pltpu.HBM)
            if n in far
            else near
            for n in range(inputs)
        ],
        out_specs=[
            pl.BlockSpec(memory_space=pl.ANY) if n in aliases.values() or n in far_outs else near
            for n in range(len(outs))
        ],
        input_output_aliases=aliases,
        scratch_shapes=list(scratch),
        compiler_params=pltpu.CompilerParams(vmem_limit_bytes=VMEM_LIMIT),
        cost_estimate=pl.CostEstimate(flops=flops, bytes_accessed=1 << 20, transcendentals=0),
        name=name,
    )

    def run(*args):
        return kernel(
            *(pltpu.with_memory_space_constraint(x, pltpu.HBM) if n in far else x for n, x in enumerate(args))
        )

    return run


def lanes(shape):
    return lax.broadcasted_iota(jnp.int32, shape, len(shape) - 1)


def rows(shape):
    return lax.broadcasted_iota(jnp.int32, shape, len(shape) - 2)


def turn(x, shift, axis):
    shift %= x.shape[axis]
    return pltpu.roll(x, shift, axis) if shift else x


def group_order(count):
    half, quarter = count // 2, count // 4
    return [k for n in range(half) for k in ((n + quarter) % half, half + (n + quarter) % half)]


def exchange(x):
    order = group_order(x.shape[0])
    return lax.all_to_all(x, "lon", split_axis=0, concat_axis=0, tiled=True, axis_index_groups=[order])


def swap(near, far, axis, wrap):
    count = lax.axis_size(axis)
    pairs = [[], []]
    for i in range(count if wrap else count - 1):
        j = (i + 1) % count
        pairs[i % 2] += [(i, j), (j, i)]
    far = lax.ppermute(far, axis, pairs[1])
    return lax.ppermute(near, axis, pairs[0]), far


def sort_swap(axis, after, before):
    odd = lax.rem(lax.axis_index(axis), 2) == 1
    return jnp.where(odd, before, after), jnp.where(odd, after, before)


def tile_fields(tracers, cotangent, land_mask, diffusion, velocity):
    levels = land_mask.shape[0]
    mask = [land_mask[level].astype(f32) for level in range(levels)]
    out = [tracers[f, level] for f in range(2) for level in range(levels)]
    out += [cotangent[f, level] for f in range(2) for level in range(levels)]
    out += [diffusion[0, level] * mask[level] for level in range(levels)]
    out += [velocity[0, level] * mask[level] for level in range(levels)]
    out += [diffusion[1, level] * mask[level] for level in range(levels)]
    out += [velocity[1, level] * mask[level] for level in range(levels)]
    out += [diffusion[2, level] * mask[level] * mask[level + 1] for level in range(levels - 1)]
    return out


def fetch(pairs, arrived):
    copies = [pltpu.make_async_copy(src, dst, arrived.at[n]) for n, (src, dst) in enumerate(pairs)]
    for copy in copies:
        copy.start()
    return copies


def pack_columns(*refs):
    inputs, (fields, near, far), scratch = refs[:7], refs[7:10], refs[12:]
    copies = fetch(zip(inputs, [*scratch[:5], *refs[10:12]]), scratch[5])
    for copy in copies[:5]:
        copy.wait()
    shape = near.shape[1:]
    lane = lanes(shape)
    west = [jnp.zeros(shape, f32) for _ in range(near.shape[0])]
    east = [jnp.zeros(shape, f32) for _ in range(near.shape[0])]
    for i, field in enumerate(tile_fields(*scratch[:5])):
        fields[i] = field
        part, at = divmod(i, PER_LANES)
        at *= HALO
        here = (lane >= at) & (lane < at + HALO)
        west[part] = jnp.where(here, turn(field[:, :BLOCK], at, 1), west[part])
        east[part] = jnp.where(here, turn(field[:, -BLOCK:], at + HALO, 1), east[part])
    for part in range(near.shape[0]):
        near[part], far[part] = sort_swap("lon", east[part], west[part])
    for copy in copies[5:]:
        copy.wait()


def unpack_columns(from_west, from_east, i):
    part, at = divmod(i, PER_LANES)
    at *= HALO
    lane = lanes(from_west[part].shape)
    east = turn(from_east[part], -at, 1)
    west = turn(from_west[part], -at - HALO, 1)
    return jnp.where(lane < HALO, east, jnp.where(lane >= BLOCK - HALO, west, 0.0))


def row_sources(fields, from_west, from_east):
    out = [(fields, (i, slice(None), slice(h * BLOCK, (h + 1) * BLOCK)))
           for i in range(fields.shape[0]) for h in range(fields.shape[2] // BLOCK)]
    for columns in (from_west, from_east):
        out += [(columns, (part,)) for part in range(columns.shape[0])]
    return out


def pack_rows(fields, near_columns, far_columns, sums, near, far, from_west, from_east, same_sums):
    for part in range(from_west.shape[0]):
        from_east[part], from_west[part] = sort_swap("lon", near_columns[part], far_columns[part])
    sources = [ref[at] for ref, at in row_sources(fields, from_west, from_east)]
    half = near.shape[0]
    row = rows((8, BLOCK))
    for i in range(half):
        first = sources[i]
        second = sources[i + half] if i + half < len(sources) else jnp.zeros_like(first)
        to_north = jnp.where(row < HALO, turn(first[-8:], HALO, 0), second[-8:])
        to_south = jnp.where(row < HALO, first[:8], turn(second[:8], HALO, 0))
        near[i], far[i] = sort_swap("lat", to_north, to_south)


def edge_rows(near, far, i):
    half = near.shape[0]
    from_north, from_south = sort_swap("lat", near[i % half], far[i % half])
    if i < half:
        from_south = turn(from_south, HALO, 0)
    else:
        from_north = turn(from_north, HALO, 0)
    return jnp.where(rows(from_north.shape) < HALO, from_north, from_south)


def widen(fields, from_west, from_east, near, far, start, wide):
    count, tile_lat, tile_lon = fields.shape
    halves = tile_lon // BLOCK
    parts = from_west.shape[0]
    corners = [edge_rows(near, far, count * halves + n) for n in range(2 * parts)]
    for i in range(count):
        out = start.at[i] if i < start.shape[0] else wide.at[i - start.shape[0]]
        out[:tile_lat, :tile_lon] = fields[i]
        out[:tile_lat, tile_lon:] = unpack_columns(from_west, from_east, i)
        for h in range(halves):
            out[tile_lat:, h * BLOCK : (h + 1) * BLOCK] = edge_rows(near, far, i * halves + h)
        out[tile_lat:, tile_lon:] = unpack_columns(corners[:parts], corners[parts:], i)


def eastward(x):
    return turn(x, -1, 1)


def westward(x):
    return turn(x, 1, 1)


def northward(x):
    return turn(x, -1, 0)


def southward(x):
    return turn(x, 1, 0)


def adjoint_step(coeffs, read, write, first, last):
    levels = coeffs.shape[1]
    above = coeffs[4, first - 1] * (read(first) - read(first - 1)) if first else None
    for level in range(first, last):
        lam = read(level)
        step_x = eastward(lam) - lam
        step_y = northward(lam) - lam
        out = lam + coeffs[0, level] * step_x + westward(coeffs[1, level] * step_x)
        out = out + coeffs[2, level] * step_y + southward(coeffs[3, level] * step_y)
        if above is not None:
            out = out - above
        if level < levels - 1:
            above = coeffs[4, level] * (read(level + 1) - lam)
            out = out + above
        write(level, out)


def surface_levels(step, levels):
    return min(levels, STEPS - 1 - step)


def run_adjoint(
    fields, from_west, from_east, far, near, blocks, coeffs, start, states, wide, own, sent
):
    levels = coeffs.shape[1]
    tile_lat, tile_lon = fields.shape[1:]
    halves = tile_lon // BLOCK
    widen(fields, from_west, from_east, near, far, start, wide)
    base = 0
    mask0 = None
    for level in range(levels):
        east_d, east_u = wide[base + level], wide[base + levels + level]
        north_d, north_u = wide[base + 2 * levels + level], wide[base + 3 * levels + level]
        mask = (east_d > 0.0).astype(f32)
        mask0 = mask if mask0 is None else mask0
        mask_e, mask_n = eastward(mask), northward(mask)
        east_k, east_v = east_d * mask_e, east_u * mask_e
        north_k, north_v = north_d * mask_n, north_u * mask_n
        coeffs[0, level] = jnp.maximum(east_v, 0.0) + east_k
        coeffs[1, level] = jnp.minimum(east_v, 0.0) - east_k
        coeffs[2, level] = jnp.maximum(north_v, 0.0) + north_k
        coeffs[3, level] = jnp.minimum(north_v, 0.0) - north_k
        coeffs[4, level] = wide[base + 4 * levels + level] if level < levels - 1 else jnp.zeros_like(mask)
        coeffs[5, level] = mask
    copies = []
    for f in range(2):
        surface = start[(2 + f) * levels, :tile_lat, :tile_lon]
        for step in range(STEPS - 1):

            def read(level):
                return states[f, step - 1, level] if step else start[(2 + f) * levels + level]

            def write(level, lam):
                states[f, step, level] = lam

            adjoint_step(coeffs, read, write, 0, surface_levels(step, levels))
            surface = surface + states[f, step, 0, :tile_lat, :tile_lon]
        surface = surface * mask0[:tile_lat, :tile_lon]
        for h in range(halves):
            at = (f * halves + h) * tile_lat
            own[at : at + tile_lat] = surface[:, h * BLOCK : (h + 1) * BLOCK]
        field = pl.ds(f * halves * tile_lat, halves * tile_lat)
        copies += fetch([(own.at[field], blocks.at[k, field]) for k in range(blocks.shape[0])], sent.at[f])
    for copy in copies:
        copy.wait()


def finish_adjoint(coeffs, start, states, adjoint_out, rest):
    levels = coeffs.shape[1]
    tile_lat, tile_lon = adjoint_out.shape[2:]
    for f in range(2):
        for step in range(STEPS):
            done = surface_levels(step, levels)

            def read(level):
                if not step:
                    return start[(2 + f) * levels + level]
                return (states if level < surface_levels(step - 1, levels) else rest)[f, step - 1, level]

            def write(level, lam):
                if step == STEPS - 1:
                    adjoint_out[f, level] = lam[:tile_lat, :tile_lon]
                else:
                    rest[f, step, level] = lam

            adjoint_step(coeffs, read, write, done, levels)


def sum_forcing(received, forcing, near, far):
    tile_lat = forcing.shape[1]
    halves = forcing.shape[2] // BLOCK - 1
    total = received[0]
    for j in range(1, received.shape[0]):
        total = total + received[j]
    lane = lanes((tile_lat, BLOCK))
    upper = total[2 * halves * tile_lat :]
    lower = jnp.where(lane[: tile_lat // 2] < BLOCK // 2, turn(upper, -2 * HALO, 1), turn(upper, 2 * HALO, 1))
    packed = jnp.concatenate([upper, lower], axis=0)
    for f in range(2):
        for h in range(halves):
            at = (f * halves + h) * tile_lat
            forcing[f, :, h * BLOCK : (h + 1) * BLOCK] = total[at : at + tile_lat]
        used = (lane < HALO) | (lane >= BLOCK - HALO)
        if f == 0:
            edge = packed
        else:
            edge = jnp.where(lane < HALO, turn(packed, -HALO, 1), turn(packed, HALO, 1))
        forcing[f, :, halves * BLOCK :] = jnp.where(used, edge, 0.0)
    row = rows((8, forcing.shape[2]))
    to_north = jnp.where(row < HALO, turn(forcing[0, tile_lat - 8 :], HALO, 0), forcing[1, tile_lat - 8 :])
    to_south = jnp.where(row < HALO, forcing[0, :8], turn(forcing[1, :8], HALO, 0))
    near[0], far[0] = sort_swap("lat", to_north, to_south)


def run_forward(coeffs, start, forcing, near, far, final, state):
    levels = coeffs.shape[1]
    tile_lat, tile_lon = final.shape[2:]
    for f in range(2):
        force = jnp.concatenate([forcing[f], edge_rows(near, far, f)], axis=0)
        force = force * coeffs[5, 0]
        for step in range(STEPS):
            above = None
            for level in range(levels):
                read = (lambda n: start[f * levels + n]) if step == 0 else (lambda n: state[(step - 1) % 2, n])
                theta = read(level)
                east_flux = coeffs[0, level] * theta + coeffs[1, level] * eastward(theta)
                north_flux = coeffs[2, level] * theta + coeffs[3, level] * northward(theta)
                out = theta - (east_flux - westward(east_flux)) - (north_flux - southward(north_flux))
                if level < levels - 1:
                    vertical = coeffs[4, level] * (theta - read(level + 1))
                    out = out - vertical
                if above is not None:
                    out = out + above
                above = vertical if level < levels - 1 else None
                if level == 0:
                    out = out + force
                if step == STEPS - 1:
                    final[f, level] = out[:tile_lat, :tile_lon]
                else:
                    state[step % 2, level] = out


def split(x):
    high = x.astype(bf16)
    return high, (x - high.astype(f32)).astype(bf16)


def weight_copy(weights, held, arrived, n):
    own = pl.ds(n * FETCH, FETCH)
    return pltpu.make_async_copy(weights.at[own], held.at[own], arrived.at[n])


def fetch_weights(weights, held, arrived):
    for n in range(held.shape[0] // FETCH):
        weight_copy(weights, held, arrived, n).start()


def held_part(weights, held, arrived):
    def part(r, g, u):
        if u == 0:

            @pl.when(r == 0)
            def _():
                for n in range(GROUP // FETCH):
                    weight_copy(weights, held, arrived, g * (GROUP // FETCH) + n).wait()

        return split(held[g * GROUP + u])

    return part


def one_hot(where):
    return jnp.where(where, 1.0, 0.0).astype(bf16)


def places(slots, blocks):
    return 8 * (-(-2 * slots // (8 * blocks)) + 1)


def round_chunks(slots, blocks):
    return -(-(slots + 7 * blocks) // BLOCK)


def as_row(ids):
    return jnp.concatenate([ids[k : k + 1, :] for k in range(ids.shape[0])], axis=1)


def rank_slots(block_row, blocks):
    slots = block_row.shape[1]
    mine = rows((blocks, slots)) == block_row
    cuts = range(0, slots, BLOCK)
    stacked = jnp.concatenate([one_hot(mine[:, at : at + BLOCK]) for at in cuts], axis=0)
    shape = (BLOCK, 2 * BLOCK)
    counts = jnp.dot(stacked, one_hot(rows(shape) < lanes(shape)), preferred_element_type=f32)
    before, out = jnp.zeros((blocks, BLOCK), f32), []
    for n, at in enumerate(cuts):
        run = counts[n * blocks : (n + 1) * blocks]
        here = jnp.where(mine[:, at : at + BLOCK], run[:, :BLOCK] + before, 0.0)
        out.append(jnp.sum(here, axis=0, keepdims=True))
        before = before + run[:, BLOCK:]
    return jnp.concatenate(out, axis=1), before


def find_slots(r, keys, counts, capacity, columns, lines, starts):
    slots = keys.shape[1]
    blocks = counts.shape[0]
    atm_row, ocean_row, block_row, rank = (keys[n : n + 1] for n in range(4))
    count = jnp.clip(counts - r * capacity, 0.0, capacity)
    tiles = jnp.floor((count + 7.0) * 0.125) * 8.0
    shape = (blocks, blocks)
    first = jnp.dot(one_hot(lanes(shape) < rows(shape)), tiles.astype(bf16), preferred_element_type=f32)
    starts[...] = first.astype(jnp.int32)
    mine = rows((blocks, slots)).astype(f32) == block_row
    own = jnp.where(mine, jnp.concatenate([first] * (slots // BLOCK), axis=1), 0.0)
    place = rank - r * capacity
    here = (place >= 0.0) & (place < capacity)
    place = jnp.where(here, jnp.sum(own, axis=0, keepdims=True) + place, -1.0)
    run = jnp.floor(place * (1.0 / BLOCK))
    low = one_hot(rows((BLOCK, slots)).astype(f32) == place - run * BLOCK)
    size = lines.shape[1]
    in_run = rows((size, slots)).astype(f32) == run
    ocean_high = jnp.floor(ocean_row * (1.0 / BLOCK))
    digits = [atm_row, ocean_high, ocean_row - ocean_high * BLOCK]
    digits = [jnp.where(in_run, digit, 0.0).astype(bf16) for digit in digits]
    across = (((1,), (1,)), ((), ()))
    down = [lax.dot_general(low, digit, across, preferred_element_type=f32) for digit in digits]
    along = [lax.dot_general(digit, low, across, preferred_element_type=f32) for digit in digits]
    columns[0, :, :size], columns[1, :, :size] = down[0], down[1] * BLOCK + down[2] - 1.0
    ocean = along[1] * BLOCK + along[2] - 1.0
    lines[0], lines[1] = jnp.where(ocean < 0.0, -1.0, along[0]), ocean


def couple(part, table, capacity, rounds, prepare, columns, lines, starts, transposed, result, scratch):
    vectors, products, starts_near = scratch
    blocks = starts.shape[0]
    total_rows = vectors.shape[0] - capacity
    width = table.shape[0]
    result[...] = jnp.zeros_like(result)
    products[...] = jnp.zeros_like(products)

    def one_round(r, carry):
        prepare(r)
        first_rows = starts[...]
        for w in range(blocks):
            starts_near[w] = first_rows[w, 0]
        place_hot = []
        for n in range(total_rows // BLOCK):
            gather = jnp.broadcast_to(columns[int(transposed), :, n : n + 1], (BLOCK, BLOCK))
            gather = jnp.concatenate([gather] * (width // BLOCK), axis=1)
            hot = one_hot(gather == lanes((BLOCK, width)).astype(f32))
            vectors[n * BLOCK : (n + 1) * BLOCK] = jnp.dot(hot, table, preferred_element_type=f32)
            put = lines[1 - int(transposed), n : n + 1]
            place_hot.append(one_hot(rows((result.shape[0], BLOCK)).astype(f32) == put))

        def group(g, carry):
            for u in range(GROUP):
                at = pl.ds(pl.multiple_of(starts_near[g * GROUP + u], 8), capacity)
                own = vectors[at]
                left = jnp.concatenate([own[:, n * BLOCK : (n + 1) * BLOCK] for n in range(4)], axis=0)
                high, low = part(r, g, u)
                right = jnp.concatenate([high, low], axis=1 if transposed else 0)
                contract = (((1,), (0 if transposed else 1,)), ((), ()))
                product = lax.dot_general(left.astype(bf16), right, contract, preferred_element_type=f32)
                for f in range(2):
                    high_part = product[f * capacity : (f + 1) * capacity]
                    low_part = product[(f + 2) * capacity : (f + 3) * capacity, :BLOCK]
                    products[at, f * BLOCK : (f + 1) * BLOCK] = (
                        high_part[:, BLOCK:] + low_part
                    ) + high_part[:, :BLOCK]
            return carry

        lax.fori_loop(0, blocks // GROUP, group, 0)
        summed = jnp.dot(
            jnp.concatenate(place_hot, axis=1),
            jnp.concatenate(split(products[:total_rows]), axis=1),
            preferred_element_type=f32,
        )
        result[...] += summed[:, : 2 * BLOCK] + summed[:, 2 * BLOCK :]
        return carry

    lax.fori_loop(0, rounds, one_round, 0)


def slot_keys(ids, tile_lat, keys):
    lon_count, cap = ids.shape[3:]
    ocean, atm_ids, block_ids = (ids[n, 0, 0] for n in range(3))
    order = (ocean & 1) * tile_lat + (ocean >> 1) + rows((lon_count, cap)) * (2 * tile_lat)
    order = jnp.where(ocean >= 0, order, lon_count * 2 * tile_lat) + 1
    for n, part in enumerate((atm_ids, order, block_ids)):
        keys[n : n + 1] = as_row(part.astype(f32))


def weigh(
    atm_near, margins, weights, after, sums, keys, counts, columns, lines, starts, result, *scratch
):
    scratch, (held, arrived) = scratch[:3], scratch[3:]
    fetch_weights(weights, held, arrived)
    lon_count = margins.shape[3]
    blocks = weights.shape[0]
    tile_lat = 2 * sums.shape[1] // 9
    slot_keys(margins, tile_lat, keys)
    rank, count = rank_slots(keys[2:3].astype(jnp.int32), blocks)
    keys[3:4] = rank
    counts[...] = count
    capacity = places(keys.shape[1], blocks)
    rounds = jnp.max(rank).astype(jnp.int32) // capacity + 1
    parts = [split(atm_near[f, 0]) for f in range(2)]
    table = jnp.concatenate([parts[f][n] for n in range(2) for f in range(2)], axis=1)
    part = held_part(weights, held, arrived)

    def prepare(r):
        find_slots((rounds - 1 - r).astype(f32), keys, counts[...], capacity, columns, lines, starts)

    couple(part, table, capacity, rounds, prepare, columns, lines, starts, False, result, scratch)
    lane = lanes((tile_lat, BLOCK))

    def block_sums(k, f, h):
        at = (2 * k + h) * tile_lat
        return result[at : at + tile_lat, f * BLOCK : (f + 1) * BLOCK]

    for n, k in enumerate(group_order(lon_count)):
        edge = jnp.zeros((tile_lat, BLOCK), f32)
        for f in range(2):
            for h in range(2):
                sums[n, (2 * f + h) * tile_lat : (2 * f + h + 1) * tile_lat] = block_sums(k, f, h)
            at = f * HALO
            after = turn(block_sums((k + 1) % lon_count, f, 0), at, 1)
            before = turn(block_sums((k - 1) % lon_count, f, 1), -at, 1)
            edge = jnp.where((lane >= at) & (lane < at + HALO), after, edge)
            end = BLOCK - at
            edge = jnp.where((lane >= end - HALO) & (lane < end), before, edge)
        upper, lower = edge[: tile_lat // 2], edge[tile_lat // 2 :]
        near = lane[: tile_lat // 2]
        lower = jnp.where(near < BLOCK // 2, turn(lower, 2 * HALO, 1), turn(lower, -2 * HALO, 1))
        sums[n, 4 * tile_lat :] = jnp.where((near < 2 * HALO) | (near >= BLOCK - 2 * HALO), upper, lower)


def unweigh(
    gathered, keys, counts, columns_in, lines_in, starts_in, weights, gradient, result, columns, lines, starts, *scratch
):
    scratch, (held, arrived) = scratch[:3], scratch[3:]
    fetch_weights(weights, held, arrived)
    blocks = weights.shape[0]
    lon_count, ocean_blocks = gathered.shape[0], gathered.shape[1] // 2
    order = group_order(lon_count)
    capacity = places(keys.shape[1], blocks)
    rounds = jnp.max(keys[3:4]).astype(jnp.int32) // capacity + 1
    parts = [
        split(
            jnp.concatenate(
                [gathered[order.index(k), f * ocean_blocks : (f + 1) * ocean_blocks] for k in range(lon_count)],
                axis=0,
            )
        )
        for f in range(2)
    ]
    table = jnp.concatenate([parts[f][n] for n in range(2) for f in range(2)], axis=1)

    def prepare(r):
        @pl.when(r == 0)
        def _():
            columns[...] = columns_in[...]
            lines[...] = lines_in[...]
            starts[...] = starts_in[...]

        @pl.when(r > 0)
        def _():
            find_slots(r.astype(f32), keys, counts[...], capacity, columns, lines, starts)

    part = held_part(weights, held, arrived)
    couple(part, table, capacity, rounds, prepare, columns, lines, starts, True, result, scratch)
    for f in range(2):
        gradient[f, 0] = result[:, f * BLOCK : (f + 1) * BLOCK]


def on_device(tracers, cotangent, land_mask, diffusion, velocity, weights, atm_state, margins):
    levels, tile_lat, tile_lon = land_mask.shape
    lon_count = lax.axis_size("lon")
    slots = lon_count * margins.shape[4]
    halves = tile_lon // BLOCK
    count = 9 * levels - 1
    parts = -(-count // PER_LANES)
    inputs = (tracers, cotangent, land_mask, diffusion, velocity)

    def in_vmem(s):
        return pltpu.VMEM(s.shape, s.dtype)

    message = (parts, tile_lat, BLOCK)
    fields, near, far, atm_near, margins_near = call(
        pack_columns,
        [
            (count, tile_lat, tile_lon),
            message,
            message,
            atm_state.shape,
            jax.ShapeDtypeStruct(margins.shape, margins.dtype),
        ],
        [*map(in_vmem, inputs), pltpu.SemaphoreType.DMA((7,))],
        name="pack_columns",
        inputs=7,
        far=range(7),
    )(*inputs, atm_state, margins)
    near_columns, far_columns = swap(near, far, "lon", True)

    blocks_of, atm = weights.shape[0], atm_state.shape[2]
    sum_rows = 2 * halves * tile_lat + tile_lat // 2
    ocean_blocks = lon_count * halves * tile_lat
    chunks = round_chunks(slots, blocks_of)
    held_rows = chunks * BLOCK + places(slots, blocks_of)

    def coupling_scratch(result_rows):
        return [
            pltpu.VMEM((result_rows, 2 * BLOCK), f32),
            pltpu.VMEM((held_rows, 4 * BLOCK), f32),
            pltpu.VMEM((held_rows, 2 * BLOCK), f32),
            pltpu.SMEM((blocks_of,), jnp.int32),
            pltpu.VMEM(weights.shape, f32),
            pltpu.SemaphoreType.DMA((blocks_of // FETCH,)),
        ]

    coupling_flops = 4 * slots * blocks_of * 2 * BLOCK * BLOCK * 2
    found = [
        jax.ShapeDtypeStruct((2, BLOCK, BLOCK), f32),
        jax.ShapeDtypeStruct((2, -(-chunks // 8) * 8, BLOCK), f32),
        jax.ShapeDtypeStruct((blocks_of, BLOCK), jnp.int32),
    ]
    sums, *slot_data = call(
        weigh,
        [(lon_count, sum_rows, BLOCK), (8, slots), (blocks_of, BLOCK), *found],
        coupling_scratch(ocean_blocks),
        coupling_flops,
        name="weigh",
        inputs=4,
        far=(2,),
    )(atm_near, margins_near, weights, far)

    sources = count * halves + 2 * parts
    message = (-(-sources // 2), 8, BLOCK)
    columns = (parts, tile_lat, BLOCK)
    near, far, from_west, from_east, sums = call(
        pack_rows,
        [message, message, columns, columns, sums.shape],
        name="pack_rows",
        inputs=4,
        aliases={3: 4},
    )(fields, near_columns, far_columns, sums)
    received = exchange(sums)
    near_rows, far_rows = swap(near, far, "lat", False)

    wide = (tile_lat + 8, tile_lon + BLOCK)
    own = (2 * halves * tile_lat, BLOCK)
    adjoint_states = (2, STEPS - 1, levels, *wide)
    blocks, coeffs, start, states = call(
        run_adjoint,
        [(lon_count, *own), (6, levels, *wide), (4 * levels, *wide), adjoint_states],
        [
            pltpu.VMEM((count - 4 * levels, *wide), f32),
            pltpu.VMEM(own, f32),
            pltpu.SemaphoreType.DMA((2, lon_count)),
        ],
        name="run_adjoint",
        inputs=5,
        far_outs=(0,),
    )(fields, from_west, from_east, far_rows, near_rows)
    gathered = exchange(blocks)

    message = (1, 8, tile_lon + BLOCK)
    forcing, near, far = call(
        sum_forcing, [(2, tile_lat, tile_lon + BLOCK), message, message], name="sum_forcing", inputs=1
    )(received)
    near_rows, far_rows = swap(near, far, "lat", False)
    (adjoint,) = call(
        finish_adjoint,
        [cotangent.shape],
        [pltpu.VMEM(adjoint_states, f32)],
        name="finish_adjoint",
        inputs=3,
    )(coeffs, start, states)
    (final,) = call(
        run_forward,
        [tracers.shape],
        [pltpu.VMEM((2, levels, *wide), f32)],
        name="run_forward",
        inputs=5,
    )(coeffs, start, forcing, near_rows, far_rows)

    (gradient,) = call(
        unweigh,
        [atm_state.shape],
        [coupling_scratch(atm)[0], *map(in_vmem, found), *coupling_scratch(atm)[1:]],
        coupling_flops,
        name="unweigh",
        inputs=7,
        far=(6,),
    )(gathered, *slot_data, weights)
    return (final, adjoint, gradient)


def solution(mesh):
    return jax.shard_map(
        on_device,
        mesh=mesh,
        in_specs=(
            P(None, None, "lat", "lon"),
            P(None, None, "lat", "lon"),
            P(None, "lat", "lon"),
            P(None, None, "lat", "lon"),
            P(None, None, "lat", "lon"),
            P(),
            P(None, "lat", "lon", None),
            P(None, "lat", "lon", None, None),
        ),
        out_specs=(
            P(None, None, "lat", "lon"),
            P(None, None, "lat", "lon"),
            P(None, "lat", "lon", None),
        ),
        check_vma=False,
    )
```

```python
import jax
import jax.numpy as jnp
from jax import lax
from jax.experimental import pallas as pl
from jax.experimental.pallas import tpu as pltpu
from jax.sharding import PartitionSpec as P

BLOCK = 128
STEPS = 4
HALO = STEPS
PER_LANES = BLOCK // HALO
GROUP = 16
FETCH = 4
f32 = jnp.float32
bf16 = jnp.bfloat16
VMEM_LIMIT = 20 * 1024 * 1024


def call(body, outs, scratch=(), flops=0, name=None, inputs=0, far=(), far_outs=(), aliases=None):
    outs = [s if isinstance(s, jax.ShapeDtypeStruct) else jax.ShapeDtypeStruct(s, f32) for s in outs]
    near = pl.BlockSpec(memory_space=pltpu.VMEM)
    aliases = aliases or {}
    kernel = pl.pallas_call(
        body,
        out_shape=outs,
        in_specs=[
            pl.BlockSpec(memory_space=pl.ANY)
            if n in aliases
            else pl.BlockSpec(memory_space=pltpu.HBM)
            if n in far
            else near
            for n in range(inputs)
        ],
        out_specs=[
            pl.BlockSpec(memory_space=pl.ANY) if n in aliases.values() or n in far_outs else near
            for n in range(len(outs))
        ],
        input_output_aliases=aliases,
        scratch_shapes=list(scratch),
        compiler_params=pltpu.CompilerParams(vmem_limit_bytes=VMEM_LIMIT),
        cost_estimate=pl.CostEstimate(flops=flops, bytes_accessed=1 << 20, transcendentals=0),
        name=name,
    )

    def run(*args):
        return kernel(
            *(pltpu.with_memory_space_constraint(x, pltpu.HBM) if n in far else x for n, x in enumerate(args))
        )

    return run


def lanes(shape):
    return lax.broadcasted_iota(jnp.int32, shape, len(shape) - 1)


def rows(shape):
    return lax.broadcasted_iota(jnp.int32, shape, len(shape) - 2)


def turn(x, shift, axis):
    shift %= x.shape[axis]
    return pltpu.roll(x, shift, axis) if shift else x


def group_order(count):
    half, quarter = count // 2, count // 4
    return [k for n in range(half) for k in ((n + quarter) % half, half + (n + quarter) % half)]


def exchange(x):
    order = group_order(x.shape[0])
    return lax.all_to_all(x, "lon", split_axis=0, concat_axis=0, tiled=True, axis_index_groups=[order])


def swap(near, far, axis, wrap):
    count = lax.axis_size(axis)
    pairs = [[], []]
    for i in range(count if wrap else count - 1):
        j = (i + 1) % count
        pairs[i % 2] += [(i, j), (j, i)]
    far = lax.ppermute(far, axis, pairs[1])
    return lax.ppermute(near, axis, pairs[0]), far


def sort_swap(axis, after, before):
    odd = lax.rem(lax.axis_index(axis), 2) == 1
    return jnp.where(odd, before, after), jnp.where(odd, after, before)


def tile_fields(tracers, cotangent, land_mask, diffusion, velocity):
    levels = land_mask.shape[0]
    mask = [land_mask[level].astype(f32) for level in range(levels)]
    out = [tracers[f, level] for f in range(2) for level in range(levels)]
    out += [cotangent[f, level] for f in range(2) for level in range(levels)]
    out += [diffusion[0, level] * mask[level] for level in range(levels)]
    out += [velocity[0, level] * mask[level] for level in range(levels)]
    out += [diffusion[1, level] * mask[level] for level in range(levels)]
    out += [velocity[1, level] * mask[level] for level in range(levels)]
    out += [diffusion[2, level] * mask[level] * mask[level + 1] for level in range(levels - 1)]
    return out


def fetch(pairs, arrived):
    copies = [pltpu.make_async_copy(src, dst, arrived.at[n]) for n, (src, dst) in enumerate(pairs)]
    for copy in copies:
        copy.start()
    return copies


def pack_columns(*refs):
    inputs, (fields, near, far), scratch = refs[:7], refs[7:10], refs[12:]
    copies = fetch(zip(inputs, [*scratch[:5], *refs[10:12]]), scratch[5])
    for copy in copies[:5]:
        copy.wait()
    shape = near.shape[1:]
    lane = lanes(shape)
    west = [jnp.zeros(shape, f32) for _ in range(near.shape[0])]
    east = [jnp.zeros(shape, f32) for _ in range(near.shape[0])]
    for i, field in enumerate(tile_fields(*scratch[:5])):
        fields[i] = field
        part, at = divmod(i, PER_LANES)
        at *= HALO
        here = (lane >= at) & (lane < at + HALO)
        west[part] = jnp.where(here, turn(field[:, :BLOCK], at, 1), west[part])
        east[part] = jnp.where(here, turn(field[:, -BLOCK:], at + HALO, 1), east[part])
    for part in range(near.shape[0]):
        near[part], far[part] = sort_swap("lon", east[part], west[part])
    for copy in copies[5:]:
        copy.wait()


def unpack_columns(from_west, from_east, i):
    part, at = divmod(i, PER_LANES)
    at *= HALO
    lane = lanes(from_west[part].shape)
    east = turn(from_east[part], -at, 1)
    west = turn(from_west[part], -at - HALO, 1)
    return jnp.where(lane < HALO, east, jnp.where(lane >= BLOCK - HALO, west, 0.0))


def row_sources(fields, from_west, from_east):
    out = [(fields, (i, slice(None), slice(h * BLOCK, (h + 1) * BLOCK)))
           for i in range(fields.shape[0]) for h in range(fields.shape[2] // BLOCK)]
    for columns in (from_west, from_east):
        out += [(columns, (part,)) for part in range(columns.shape[0])]
    return out


def pack_rows(fields, near_columns, far_columns, sums, near, far, from_west, from_east, same_sums):
    for part in range(from_west.shape[0]):
        from_east[part], from_west[part] = sort_swap("lon", near_columns[part], far_columns[part])
    sources = [ref[at] for ref, at in row_sources(fields, from_west, from_east)]
    half = near.shape[0]
    row = rows((8, BLOCK))
    for i in range(half):
        first = sources[i]
        second = sources[i + half] if i + half < len(sources) else jnp.zeros_like(first)
        to_north = jnp.where(row < HALO, turn(first[-8:], HALO, 0), second[-8:])
        to_south = jnp.where(row < HALO, first[:8], turn(second[:8], HALO, 0))
        near[i], far[i] = sort_swap("lat", to_north, to_south)


def edge_rows(near, far, i):
    half = near.shape[0]
    from_north, from_south = sort_swap("lat", near[i % half], far[i % half])
    if i < half:
        from_south = turn(from_south, HALO, 0)
    else:
        from_north = turn(from_north, HALO, 0)
    return jnp.where(rows(from_north.shape) < HALO, from_north, from_south)


def eastward(x):
    return turn(x, -1, 1)


def westward(x):
    return turn(x, 1, 1)


def northward(x):
    return turn(x, -1, 0)


def southward(x):
    return turn(x, 1, 0)


def prepare_stencil(fields, from_west, from_east, start, coeffs):
    levels = coeffs.shape[1]

    def wide(i):
        return jnp.concatenate([fields[i], unpack_columns(from_west, from_east, i)], axis=1)

    for i in range(4 * levels):
        start[i] = wide(i)
    for level in range(levels):
        east_k, east_v, north_k, north_v = (wide((4 + n) * levels + level) for n in range(4))
        mask = (east_k > 0.0).astype(f32)
        coeffs[0, level], coeffs[1, level] = upwind(east_k, east_v, eastward(mask))
        coeffs[2, level], coeffs[3, level] = north_k, north_v
        if level < levels - 1:
            coeffs[4, level] = wide(8 * levels + level)
        coeffs[5, level] = mask


def upwind(diffusion, velocity, mask):
    diffusion, velocity = diffusion * mask, velocity * mask
    return jnp.maximum(velocity, 0.0) + diffusion, jnp.minimum(velocity, 0.0) - diffusion


def whole_rows(inner, outer):
    return lambda *at: jnp.concatenate([inner[at], outer[at]], axis=0)


def coefficients(inner, outer, north):
    whole = whole_rows(inner, outer)
    return lambda n, level: north[n - 2, level] if n in (2, 3) else whole(n, level)


def adjoint_step(coeffs, levels, read, write, first, last):
    above = coeffs(4, first - 1) * (read(first) - read(first - 1)) if first else None
    for level in range(first, last):
        lam = read(level)
        step_x = eastward(lam) - lam
        step_y = northward(lam) - lam
        out = lam + coeffs(0, level) * step_x + westward(coeffs(1, level) * step_x)
        out = out + coeffs(2, level) * step_y + southward(coeffs(3, level) * step_y)
        if above is not None:
            out = out - above
        if level < levels - 1:
            above = coeffs(4, level) * (read(level + 1) - lam)
            out = out + above
        write(level, out)


def surface_levels(step, levels):
    return min(levels, STEPS - 1 - step)


def run_adjoint(
    start_in, coeffs_in, from_west, from_east, far, near, blocks, start_out, coeffs_out, north, states, own, sent
):
    levels, tile_lat = coeffs_in.shape[1:3]
    tile_lon = coeffs_in.shape[3] - BLOCK
    halves = tile_lon // BLOCK
    parts = from_west.shape[0]
    count = 9 * levels - 1
    corners = [edge_rows(near, far, count * halves + n) for n in range(2 * parts)]

    def outer(i):
        out = [edge_rows(near, far, i * halves + h) for h in range(halves)]
        return jnp.concatenate([*out, unpack_columns(corners[:parts], corners[parts:], i)], axis=1)

    for i in range(4 * levels):
        start_out[i] = outer(i)
    for level in range(levels):
        east_k, east_v, north_k, north_v = (outer((4 + n) * levels + level) for n in range(4))
        mask = (east_k > 0.0).astype(f32)
        coeffs_out[0, level], coeffs_out[1, level] = upwind(east_k, east_v, eastward(mask))
        if level < levels - 1:
            coeffs_out[4, level] = outer(8 * levels + level)
        coeffs_out[5, level] = mask
        whole_k = jnp.concatenate([coeffs_in[2, level], north_k], axis=0)
        whole_v = jnp.concatenate([coeffs_in[3, level], north_v], axis=0)
        whole_mask = jnp.concatenate([coeffs_in[5, level], mask], axis=0)
        north[0, level], north[1, level] = upwind(whole_k, whole_v, northward(whole_mask))
    start, coeffs = whole_rows(start_in, start_out), coefficients(coeffs_in, coeffs_out, north)
    mask0 = coeffs_in[5, 0, :, :tile_lon]
    copies = []
    for f in range(2):
        surface = start_in[(2 + f) * levels, :, :tile_lon]
        for step in range(STEPS - 1):

            def read(level):
                return states[f, step - 1, level] if step else start((2 + f) * levels + level)

            def write(level, lam):
                states[f, step, level] = lam

            adjoint_step(coeffs, levels, read, write, 0, surface_levels(step, levels))
            surface = surface + states[f, step, 0, :tile_lat, :tile_lon]
        surface = surface * mask0
        for h in range(halves):
            at = (f * halves + h) * tile_lat
            own[at : at + tile_lat] = surface[:, h * BLOCK : (h + 1) * BLOCK]
        field = pl.ds(f * halves * tile_lat, halves * tile_lat)
        copies += fetch([(own.at[field], blocks.at[k, field]) for k in range(blocks.shape[0])], sent.at[f])
    for copy in copies:
        copy.wait()


def finish_adjoint(start_in, coeffs_in, start_out, coeffs_out, north, states, adjoint_out, rest):
    levels = coeffs_in.shape[1]
    start, coeffs = whole_rows(start_in, start_out), coefficients(coeffs_in, coeffs_out, north)
    tile_lat, tile_lon = adjoint_out.shape[2:]
    for f in range(2):
        for step in range(STEPS):
            done = surface_levels(step, levels)

            def read(level):
                if not step:
                    return start((2 + f) * levels + level)
                return (states if level < surface_levels(step - 1, levels) else rest)[f, step - 1, level]

            def write(level, lam):
                if step == STEPS - 1:
                    adjoint_out[f, level] = lam[:tile_lat, :tile_lon]
                else:
                    rest[f, step, level] = lam

            adjoint_step(coeffs, levels, read, write, done, levels)


def sum_forcing(received, forcing, near, far):
    tile_lat = forcing.shape[1]
    halves = forcing.shape[2] // BLOCK - 1
    total = received[0]
    for j in range(1, received.shape[0]):
        total = total + received[j]
    lane = lanes((tile_lat, BLOCK))
    upper = total[2 * halves * tile_lat :]
    lower = jnp.where(lane[: tile_lat // 2] < BLOCK // 2, turn(upper, -2 * HALO, 1), turn(upper, 2 * HALO, 1))
    packed = jnp.concatenate([upper, lower], axis=0)
    for f in range(2):
        for h in range(halves):
            at = (f * halves + h) * tile_lat
            forcing[f, :, h * BLOCK : (h + 1) * BLOCK] = total[at : at + tile_lat]
        used = (lane < HALO) | (lane >= BLOCK - HALO)
        if f == 0:
            edge = packed
        else:
            edge = jnp.where(lane < HALO, turn(packed, -HALO, 1), turn(packed, HALO, 1))
        forcing[f, :, halves * BLOCK :] = jnp.where(used, edge, 0.0)
    row = rows((8, forcing.shape[2]))
    to_north = jnp.where(row < HALO, turn(forcing[0, tile_lat - 8 :], HALO, 0), forcing[1, tile_lat - 8 :])
    to_south = jnp.where(row < HALO, forcing[0, :8], turn(forcing[1, :8], HALO, 0))
    near[0], far[0] = sort_swap("lat", to_north, to_south)


def run_forward(start_in, coeffs_in, start_out, coeffs_out, north, forcing, near, far, final, state):
    levels = coeffs_in.shape[1]
    start, coeffs = whole_rows(start_in, start_out), coefficients(coeffs_in, coeffs_out, north)
    tile_lat, tile_lon = final.shape[2:]
    for f in range(2):
        force = jnp.concatenate([forcing[f], edge_rows(near, far, f)], axis=0)
        force = force * coeffs(5, 0)
        for step in range(STEPS):
            above = None
            for level in range(levels):
                read = (lambda n: start(f * levels + n)) if step == 0 else (lambda n: state[(step - 1) % 2, n])
                theta = read(level)
                east_flux = coeffs(0, level) * theta + coeffs(1, level) * eastward(theta)
                north_flux = coeffs(2, level) * theta + coeffs(3, level) * northward(theta)
                out = theta - (east_flux - westward(east_flux)) - (north_flux - southward(north_flux))
                if level < levels - 1:
                    vertical = coeffs(4, level) * (theta - read(level + 1))
                    out = out - vertical
                if above is not None:
                    out = out + above
                above = vertical if level < levels - 1 else None
                if level == 0:
                    out = out + force
                if step == STEPS - 1:
                    final[f, level] = out[:tile_lat, :tile_lon]
                else:
                    state[step % 2, level] = out


def split(x):
    high = x.astype(bf16)
    return high, (x - high.astype(f32)).astype(bf16)


def weight_copy(weights, held, arrived, n):
    own = pl.ds(n * FETCH, FETCH)
    return pltpu.make_async_copy(weights.at[own], held.at[own], arrived.at[n])


def fetch_weights(weights, held, arrived):
    for n in range(held.shape[0] // FETCH):
        weight_copy(weights, held, arrived, n).start()


def held_part(weights, held, arrived):
    def part(r, g, u):
        if u == 0:

            @pl.when(r == 0)
            def _():
                for n in range(GROUP // FETCH):
                    weight_copy(weights, held, arrived, g * (GROUP // FETCH) + n).wait()

        return split(held[g * GROUP + u])

    return part


def one_hot(where):
    return jnp.where(where, 1.0, 0.0).astype(bf16)


def places(slots, blocks):
    return 8 * (-(-2 * slots // (8 * blocks)) + 1)


def round_chunks(slots, blocks):
    return -(-(slots + 7 * blocks) // BLOCK)


def as_row(ids):
    return jnp.concatenate([ids[k : k + 1, :] for k in range(ids.shape[0])], axis=1)


def rank_slots(block_row, blocks):
    slots = block_row.shape[1]
    mine = rows((blocks, slots)) == block_row
    cuts = range(0, slots, BLOCK)
    stacked = jnp.concatenate([one_hot(mine[:, at : at + BLOCK]) for at in cuts], axis=0)
    shape = (BLOCK, 2 * BLOCK)
    counts = jnp.dot(stacked, one_hot(rows(shape) < lanes(shape)), preferred_element_type=f32)
    before, out = jnp.zeros((blocks, BLOCK), f32), []
    for n, at in enumerate(cuts):
        run = counts[n * blocks : (n + 1) * blocks]
        here = jnp.where(mine[:, at : at + BLOCK], run[:, :BLOCK] + before, 0.0)
        out.append(jnp.sum(here, axis=0, keepdims=True))
        before = before + run[:, BLOCK:]
    return jnp.concatenate(out, axis=1), before


def find_slots(r, keys, counts, capacity, columns, lines, starts):
    slots = keys.shape[1]
    blocks = counts.shape[0]
    atm_row, ocean_row, block_row, rank = (keys[n : n + 1] for n in range(4))
    count = jnp.clip(counts - r * capacity, 0.0, capacity)
    tiles = jnp.floor((count + 7.0) * 0.125) * 8.0
    shape = (blocks, blocks)
    first = jnp.dot(one_hot(lanes(shape) < rows(shape)), tiles.astype(bf16), preferred_element_type=f32)
    starts[...] = first.astype(jnp.int32)
    mine = rows((blocks, slots)).astype(f32) == block_row
    own = jnp.where(mine, jnp.concatenate([first] * (slots // BLOCK), axis=1), 0.0)
    place = rank - r * capacity
    here = (place >= 0.0) & (place < capacity)
    place = jnp.where(here, jnp.sum(own, axis=0, keepdims=True) + place, -1.0)
    run = jnp.floor(place * (1.0 / BLOCK))
    low = one_hot(rows((BLOCK, slots)).astype(f32) == place - run * BLOCK)
    size = lines.shape[1]
    in_run = rows((size, slots)).astype(f32) == run
    ocean_high = jnp.floor(ocean_row * (1.0 / BLOCK))
    digits = [atm_row, ocean_high, ocean_row - ocean_high * BLOCK]
    digits = [jnp.where(in_run, digit, 0.0).astype(bf16) for digit in digits]
    across = (((1,), (1,)), ((), ()))
    down = [lax.dot_general(low, digit, across, preferred_element_type=f32) for digit in digits]
    along = [lax.dot_general(digit, low, across, preferred_element_type=f32) for digit in digits]
    columns[0, :, :size], columns[1, :, :size] = down[0], down[1] * BLOCK + down[2] - 1.0
    ocean = along[1] * BLOCK + along[2] - 1.0
    lines[0], lines[1] = jnp.where(ocean < 0.0, -1.0, along[0]), ocean


def couple(part, table, capacity, rounds, prepare, columns, lines, starts, transposed, result, scratch):
    vectors, products, starts_near = scratch
    blocks = starts.shape[0]
    total_rows = vectors.shape[0] - capacity
    width = table.shape[0]
    result[...] = jnp.zeros_like(result)
    products[...] = jnp.zeros_like(products)

    def one_round(r, carry):
        prepare(r)
        first_rows = starts[...]
        for w in range(blocks):
            starts_near[w] = first_rows[w, 0]
        place_hot = []
        for n in range(total_rows // BLOCK):
            gather = jnp.broadcast_to(columns[int(transposed), :, n : n + 1], (BLOCK, BLOCK))
            gather = jnp.concatenate([gather] * (width // BLOCK), axis=1)
            hot = one_hot(gather == lanes((BLOCK, width)).astype(f32))
            vectors[n * BLOCK : (n + 1) * BLOCK] = jnp.dot(hot, table, preferred_element_type=f32)
            put = lines[1 - int(transposed), n : n + 1]
            place_hot.append(one_hot(rows((result.shape[0], BLOCK)).astype(f32) == put))

        def group(g, carry):
            for u in range(GROUP):
                at = pl.ds(pl.multiple_of(starts_near[g * GROUP + u], 8), capacity)
                own = vectors[at]
                left = jnp.concatenate([own[:, n * BLOCK : (n + 1) * BLOCK] for n in range(4)], axis=0)
                high, low = part(r, g, u)
                right = jnp.concatenate([high, low], axis=1 if transposed else 0)
                contract = (((1,), (0 if transposed else 1,)), ((), ()))
                product = lax.dot_general(left.astype(bf16), right, contract, preferred_element_type=f32)
                for f in range(2):
                    high_part = product[f * capacity : (f + 1) * capacity]
                    low_part = product[(f + 2) * capacity : (f + 3) * capacity, :BLOCK]
                    products[at, f * BLOCK : (f + 1) * BLOCK] = (
                        high_part[:, BLOCK:] + low_part
                    ) + high_part[:, :BLOCK]
            return carry

        lax.fori_loop(0, blocks // GROUP, group, 0)
        summed = jnp.dot(
            jnp.concatenate(place_hot, axis=1),
            jnp.concatenate(split(products[:total_rows]), axis=1),
            preferred_element_type=f32,
        )
        result[...] += summed[:, : 2 * BLOCK] + summed[:, 2 * BLOCK :]
        return carry

    lax.fori_loop(0, rounds, one_round, 0)


def slot_keys(ids, tile_lat, keys):
    lon_count, cap = ids.shape[3:]
    ocean, atm_ids, block_ids = (ids[n, 0, 0] for n in range(3))
    order = (ocean & 1) * tile_lat + (ocean >> 1) + rows((lon_count, cap)) * (2 * tile_lat)
    order = jnp.where(ocean >= 0, order, lon_count * 2 * tile_lat) + 1
    for n, part in enumerate((atm_ids, order, block_ids)):
        keys[n : n + 1] = as_row(part.astype(f32))


def weigh(
    atm_near, margins, weights, after, sums, keys, counts, columns, lines, starts, result, *scratch
):
    scratch, (held, arrived) = scratch[:3], scratch[3:]
    fetch_weights(weights, held, arrived)
    lon_count = margins.shape[3]
    blocks = weights.shape[0]
    tile_lat = 2 * sums.shape[1] // 9
    slot_keys(margins, tile_lat, keys)
    rank, count = rank_slots(keys[2:3].astype(jnp.int32), blocks)
    keys[3:4] = rank
    counts[...] = count
    capacity = places(keys.shape[1], blocks)
    rounds = jnp.max(rank).astype(jnp.int32) // capacity + 1
    parts = [split(atm_near[f, 0]) for f in range(2)]
    table = jnp.concatenate([parts[f][n] for n in range(2) for f in range(2)], axis=1)
    part = held_part(weights, held, arrived)

    def prepare(r):
        find_slots((rounds - 1 - r).astype(f32), keys, counts[...], capacity, columns, lines, starts)

    couple(part, table, capacity, rounds, prepare, columns, lines, starts, False, result, scratch)
    lane = lanes((tile_lat, BLOCK))

    def block_sums(k, f, h):
        at = (2 * k + h) * tile_lat
        return result[at : at + tile_lat, f * BLOCK : (f + 1) * BLOCK]

    for n, k in enumerate(group_order(lon_count)):
        edge = jnp.zeros((tile_lat, BLOCK), f32)
        for f in range(2):
            for h in range(2):
                sums[n, (2 * f + h) * tile_lat : (2 * f + h + 1) * tile_lat] = block_sums(k, f, h)
            at = f * HALO
            after = turn(block_sums((k + 1) % lon_count, f, 0), at, 1)
            before = turn(block_sums((k - 1) % lon_count, f, 1), -at, 1)
            edge = jnp.where((lane >= at) & (lane < at + HALO), after, edge)
            end = BLOCK - at
            edge = jnp.where((lane >= end - HALO) & (lane < end), before, edge)
        upper, lower = edge[: tile_lat // 2], edge[tile_lat // 2 :]
        near = lane[: tile_lat // 2]
        lower = jnp.where(near < BLOCK // 2, turn(lower, 2 * HALO, 1), turn(lower, -2 * HALO, 1))
        sums[n, 4 * tile_lat :] = jnp.where((near < 2 * HALO) | (near >= BLOCK - 2 * HALO), upper, lower)


def unweigh(
    gathered, keys, counts, columns_in, lines_in, starts_in, weights, gradient, result, columns, lines, starts, *scratch
):
    scratch, (held, arrived) = scratch[:3], scratch[3:]
    fetch_weights(weights, held, arrived)
    blocks = weights.shape[0]
    lon_count, ocean_blocks = gathered.shape[0], gathered.shape[1] // 2
    order = group_order(lon_count)
    capacity = places(keys.shape[1], blocks)
    rounds = jnp.max(keys[3:4]).astype(jnp.int32) // capacity + 1
    parts = [
        split(
            jnp.concatenate(
                [gathered[order.index(k), f * ocean_blocks : (f + 1) * ocean_blocks] for k in range(lon_count)],
                axis=0,
            )
        )
        for f in range(2)
    ]
    table = jnp.concatenate([parts[f][n] for n in range(2) for f in range(2)], axis=1)

    def prepare(r):
        @pl.when(r == 0)
        def _():
            columns[...] = columns_in[...]
            lines[...] = lines_in[...]
            starts[...] = starts_in[...]

        @pl.when(r > 0)
        def _():
            find_slots(r.astype(f32), keys, counts[...], capacity, columns, lines, starts)

    part = held_part(weights, held, arrived)
    couple(part, table, capacity, rounds, prepare, columns, lines, starts, True, result, scratch)
    for f in range(2):
        gradient[f, 0] = result[:, f * BLOCK : (f + 1) * BLOCK]


def on_device(tracers, cotangent, land_mask, diffusion, velocity, weights, atm_state, margins):
    levels, tile_lat, tile_lon = land_mask.shape
    lon_count = lax.axis_size("lon")
    slots = lon_count * margins.shape[4]
    halves = tile_lon // BLOCK
    count = 9 * levels - 1
    parts = -(-count // PER_LANES)
    inputs = (tracers, cotangent, land_mask, diffusion, velocity)

    def in_vmem(s):
        return pltpu.VMEM(s.shape, s.dtype)

    message = (parts, tile_lat, BLOCK)
    fields, near, far, atm_near, margins_near = call(
        pack_columns,
        [
            (count, tile_lat, tile_lon),
            message,
            message,
            atm_state.shape,
            jax.ShapeDtypeStruct(margins.shape, margins.dtype),
        ],
        [*map(in_vmem, inputs), pltpu.SemaphoreType.DMA((7,))],
        name="pack_columns",
        inputs=7,
        far=range(7),
    )(*inputs, atm_state, margins)
    near_columns, far_columns = swap(near, far, "lon", True)

    blocks_of, atm = weights.shape[0], atm_state.shape[2]
    sum_rows = 2 * halves * tile_lat + tile_lat // 2
    ocean_blocks = lon_count * halves * tile_lat
    chunks = round_chunks(slots, blocks_of)
    held_rows = chunks * BLOCK + places(slots, blocks_of)

    def coupling_scratch(result_rows):
        return [
            pltpu.VMEM((result_rows, 2 * BLOCK), f32),
            pltpu.VMEM((held_rows, 4 * BLOCK), f32),
            pltpu.VMEM((held_rows, 2 * BLOCK), f32),
            pltpu.SMEM((blocks_of,), jnp.int32),
            pltpu.VMEM(weights.shape, f32),
            pltpu.SemaphoreType.DMA((blocks_of // FETCH,)),
        ]

    coupling_flops = 4 * slots * blocks_of * 2 * BLOCK * BLOCK * 2
    found = [
        jax.ShapeDtypeStruct((2, BLOCK, BLOCK), f32),
        jax.ShapeDtypeStruct((2, -(-chunks // 8) * 8, BLOCK), f32),
        jax.ShapeDtypeStruct((blocks_of, BLOCK), jnp.int32),
    ]
    sums, *slot_data = call(
        weigh,
        [(lon_count, sum_rows, BLOCK), (8, slots), (blocks_of, BLOCK), *found],
        coupling_scratch(ocean_blocks),
        coupling_flops,
        name="weigh",
        inputs=4,
        far=(2,),
    )(atm_near, margins_near, weights, far)

    sources = count * halves + 2 * parts
    message = (-(-sources // 2), 8, BLOCK)
    columns = (parts, tile_lat, BLOCK)
    near, far, from_west, from_east, sums = call(
        pack_rows,
        [message, message, columns, columns, sums.shape],
        name="pack_rows",
        inputs=4,
        aliases={3: 4},
    )(fields, near_columns, far_columns, sums)
    received = exchange(sums)
    near_rows, far_rows = swap(near, far, "lat", False)

    wide = (tile_lat + 8, tile_lon + BLOCK)
    inner, outer = (tile_lat, tile_lon + BLOCK), (8, tile_lon + BLOCK)
    inner_data = call(
        prepare_stencil,
        [(4 * levels, *inner), (6, levels, *inner)],
        name="prepare_stencil",
        inputs=3,
    )(fields, from_west, from_east)
    own = (2 * halves * tile_lat, BLOCK)
    adjoint_states = (2, STEPS - 1, levels, *wide)
    blocks, *outer_data, states = call(
        run_adjoint,
        [
            (lon_count, *own),
            (4 * levels, *outer),
            (6, levels, *outer),
            (2, levels, *wide),
            adjoint_states,
        ],
        [pltpu.VMEM(own, f32), pltpu.SemaphoreType.DMA((2, lon_count))],
        name="run_adjoint",
        inputs=6,
        far_outs=(0,),
    )(*inner_data, from_west, from_east, far_rows, near_rows)
    gathered = exchange(blocks)

    message = (1, 8, tile_lon + BLOCK)
    forcing, near, far = call(
        sum_forcing, [(2, tile_lat, tile_lon + BLOCK), message, message], name="sum_forcing", inputs=1
    )(received)
    near_rows, far_rows = swap(near, far, "lat", False)
    (adjoint,) = call(
        finish_adjoint,
        [cotangent.shape],
        [pltpu.VMEM(adjoint_states, f32)],
        name="finish_adjoint",
        inputs=6,
    )(*inner_data, *outer_data, states)
    (final,) = call(
        run_forward,
        [tracers.shape],
        [pltpu.VMEM((2, levels, *wide), f32)],
        name="run_forward",
        inputs=8,
    )(*inner_data, *outer_data, forcing, near_rows, far_rows)

    (gradient,) = call(
        unweigh,
        [atm_state.shape],
        [coupling_scratch(atm)[0], *map(in_vmem, found), *coupling_scratch(atm)[1:]],
        coupling_flops,
        name="unweigh",
        inputs=7,
        far=(6,),
    )(gathered, *slot_data, weights)
    return (final, adjoint, gradient)


def solution(mesh):
    return jax.shard_map(
        on_device,
        mesh=mesh,
        in_specs=(
            P(None, None, "lat", "lon"),
            P(None, None, "lat", "lon"),
            P(None, "lat", "lon"),
            P(None, None, "lat", "lon"),
            P(None, None, "lat", "lon"),
            P(),
            P(None, "lat", "lon", None),
            P(None, "lat", "lon", None, None),
        ),
        out_specs=(
            P(None, None, "lat", "lon"),
            P(None, None, "lat", "lon"),
            P(None, "lat", "lon", None),
        ),
        check_vma=False,
    )
```

```python
import jax
import jax.numpy as jnp
from jax import lax
from jax.experimental import pallas as pl
from jax.experimental.pallas import tpu as pltpu
from jax.sharding import PartitionSpec as P

BLOCK = 128
STEPS = 4
HALO = STEPS
PER_LANES = BLOCK // HALO
GROUP = 16
FETCH = 4
f32 = jnp.float32
bf16 = jnp.bfloat16
VMEM_LIMIT = 20 * 1024 * 1024


def call(body, outs, scratch=(), flops=0, name=None, inputs=0, far=(), far_outs=(), aliases=None):
    outs = [s if isinstance(s, jax.ShapeDtypeStruct) else jax.ShapeDtypeStruct(s, f32) for s in outs]
    near = pl.BlockSpec(memory_space=pltpu.VMEM)
    aliases = aliases or {}
    kernel = pl.pallas_call(
        body,
        out_shape=outs,
        in_specs=[
            pl.BlockSpec(memory_space=pl.ANY)
            if n in aliases
            else pl.BlockSpec(memory_space=pltpu.HBM)
            if n in far
            else near
            for n in range(inputs)
        ],
        out_specs=[
            pl.BlockSpec(memory_space=pl.ANY) if n in aliases.values() or n in far_outs else near
            for n in range(len(outs))
        ],
        input_output_aliases=aliases,
        scratch_shapes=list(scratch),
        compiler_params=pltpu.CompilerParams(vmem_limit_bytes=VMEM_LIMIT),
        cost_estimate=pl.CostEstimate(flops=flops, bytes_accessed=1 << 20, transcendentals=0),
        name=name,
    )

    def run(*args):
        return kernel(
            *(pltpu.with_memory_space_constraint(x, pltpu.HBM) if n in far else x for n, x in enumerate(args))
        )

    return run


def lanes(shape):
    return lax.broadcasted_iota(jnp.int32, shape, len(shape) - 1)


def rows(shape):
    return lax.broadcasted_iota(jnp.int32, shape, len(shape) - 2)


def turn(x, shift, axis):
    shift %= x.shape[axis]
    return pltpu.roll(x, shift, axis) if shift else x


def group_order(count):
    half, quarter = count // 2, count // 4
    return [k for n in range(half) for k in ((n + quarter) % half, half + (n + quarter) % half)]


def exchange(x):
    order = group_order(x.shape[0])
    return lax.all_to_all(x, "lon", split_axis=0, concat_axis=0, tiled=True, axis_index_groups=[order])


def swap(near, far, axis, wrap):
    count = lax.axis_size(axis)
    pairs = [[], []]
    for i in range(count if wrap else count - 1):
        j = (i + 1) % count
        pairs[i % 2] += [(i, j), (j, i)]
    far = lax.ppermute(far, axis, pairs[1])
    return lax.ppermute(near, axis, pairs[0]), far


def sort_swap(axis, after, before):
    odd = lax.rem(lax.axis_index(axis), 2) == 1
    return jnp.where(odd, before, after), jnp.where(odd, after, before)


def tile_fields(tracers, cotangent, land_mask, diffusion, velocity):
    levels = land_mask.shape[0]
    mask = [land_mask[level].astype(f32) for level in range(levels)]
    out = [tracers[f, level] for f in range(2) for level in range(levels)]
    out += [cotangent[f, level] for f in range(2) for level in range(levels)]
    out += [diffusion[0, level] * mask[level] for level in range(levels)]
    out += [velocity[0, level] * mask[level] for level in range(levels)]
    out += [diffusion[1, level] * mask[level] for level in range(levels)]
    out += [velocity[1, level] * mask[level] for level in range(levels)]
    out += [diffusion[2, level] * mask[level] * mask[level + 1] for level in range(levels - 1)]
    return out


def fetch(pairs, arrived):
    copies = [pltpu.make_async_copy(src, dst, arrived.at[n]) for n, (src, dst) in enumerate(pairs)]
    for copy in copies:
        copy.start()
    return copies


def pack_columns(*refs):
    inputs, (fields, near, far), scratch = refs[:7], refs[7:10], refs[12:]
    copies = fetch(zip(inputs, [*scratch[:5], *refs[10:12]]), scratch[5])
    for copy in copies[:5]:
        copy.wait()
    shape = near.shape[1:]
    lane = lanes(shape)
    west = [jnp.zeros(shape, f32) for _ in range(near.shape[0])]
    east = [jnp.zeros(shape, f32) for _ in range(near.shape[0])]
    for i, field in enumerate(tile_fields(*scratch[:5])):
        fields[i] = field
        part, at = divmod(i, PER_LANES)
        at *= HALO
        here = (lane >= at) & (lane < at + HALO)
        west[part] = jnp.where(here, turn(field[:, :BLOCK], at, 1), west[part])
        east[part] = jnp.where(here, turn(field[:, -BLOCK:], at + HALO, 1), east[part])
    for part in range(near.shape[0]):
        near[part], far[part] = sort_swap("lon", east[part], west[part])
    for copy in copies[5:]:
        copy.wait()


def unpack_columns(from_west, from_east, i):
    part, at = divmod(i, PER_LANES)
    at *= HALO
    lane = lanes(from_west[part].shape)
    east = turn(from_east[part], -at, 1)
    west = turn(from_west[part], -at - HALO, 1)
    return jnp.where(lane < HALO, east, jnp.where(lane >= BLOCK - HALO, west, 0.0))


def row_blocks(fields, first, last):
    return [
        fields[i, :, h * BLOCK : (h + 1) * BLOCK]
        for i in range(first, last)
        for h in range(fields.shape[2] // BLOCK)
    ]


def put_rows(sources, near, far):
    half = near.shape[0]
    row = rows((8, BLOCK))
    for i in range(half):
        first = sources[i]
        second = sources[i + half] if i + half < len(sources) else jnp.zeros_like(first)
        to_north = jnp.where(row < HALO, turn(first[-8:], HALO, 0), second[-8:])
        to_south = jnp.where(row < HALO, first[:8], turn(second[:8], HALO, 0))
        near[i], far[i] = sort_swap("lat", to_north, to_south)


def pack_rows(fields, near_columns, far_columns, sums, near, far, from_west, from_east, same_sums):
    for part in range(from_west.shape[0]):
        from_east[part], from_west[part] = sort_swap("lon", near_columns[part], far_columns[part])
    skipped = tracer_fields(fields.shape[0])
    columns = [ref[part] for ref in (from_west, from_east) for part in range(ref.shape[0])]
    put_rows(row_blocks(fields, skipped, fields.shape[0]) + columns, near, far)


def tracer_fields(count):
    return 2 * (count + 1) // 9


def edge_rows(near, far, i):
    half = near.shape[0]
    from_north, from_south = sort_swap("lat", near[i % half], far[i % half])
    if i < half:
        from_south = turn(from_south, HALO, 0)
    else:
        from_north = turn(from_north, HALO, 0)
    return jnp.where(rows(from_north.shape) < HALO, from_north, from_south)


def eastward(x):
    return turn(x, -1, 1)


def westward(x):
    return turn(x, 1, 1)


def northward(x):
    return turn(x, -1, 0)


def southward(x):
    return turn(x, 1, 0)


def prepare_stencil(fields, from_west, from_east, start, coeffs):
    levels = coeffs.shape[1]

    def wide(i):
        return jnp.concatenate([fields[i], unpack_columns(from_west, from_east, i)], axis=1)

    for i in range(4 * levels):
        start[i] = wide(i)
    for level in range(levels):
        east_k, east_v, north_k, north_v = (wide((4 + n) * levels + level) for n in range(4))
        mask = (east_k > 0.0).astype(f32)
        coeffs[0, level], coeffs[1, level] = upwind(east_k, east_v, eastward(mask))
        coeffs[2, level], coeffs[3, level] = north_k, north_v
        if level < levels - 1:
            coeffs[4, level] = wide(8 * levels + level)
        coeffs[5, level] = mask


def upwind(diffusion, velocity, mask):
    diffusion, velocity = diffusion * mask, velocity * mask
    return jnp.maximum(velocity, 0.0) + diffusion, jnp.minimum(velocity, 0.0) - diffusion


def whole_rows(inner, outer):
    return lambda *at: jnp.concatenate([inner[at], outer[at]], axis=0)


def cotangent_rows(inner, outer):
    skipped = outer.shape[0]
    return lambda i: jnp.concatenate([inner[i], outer[i - skipped]], axis=0)


def coefficients(inner, outer, north):
    whole = whole_rows(inner, outer)
    return lambda n, level: north[n - 2, level] if n in (2, 3) else whole(n, level)


def adjoint_step(coeffs, levels, read, write, first, last):
    above = coeffs(4, first - 1) * (read(first) - read(first - 1)) if first else None
    for level in range(first, last):
        lam = read(level)
        step_x = eastward(lam) - lam
        step_y = northward(lam) - lam
        out = lam + coeffs(0, level) * step_x + westward(coeffs(1, level) * step_x)
        out = out + coeffs(2, level) * step_y + southward(coeffs(3, level) * step_y)
        if above is not None:
            out = out - above
        if level < levels - 1:
            above = coeffs(4, level) * (read(level + 1) - lam)
            out = out + above
        write(level, out)


def surface_levels(step, levels):
    return min(levels, STEPS - 1 - step)


def run_adjoint(
    start_in,
    coeffs_in,
    from_west,
    from_east,
    far,
    near,
    blocks,
    start_out,
    coeffs_out,
    north,
    corners_out,
    states,
    own,
    sent,
):
    levels, tile_lat = coeffs_in.shape[1:3]
    tile_lon = coeffs_in.shape[3] - BLOCK
    halves = tile_lon // BLOCK
    parts = from_west.shape[0]
    count = 9 * levels - 1
    skipped = tracer_fields(count)
    corners = [edge_rows(near, far, (count - skipped) * halves + n) for n in range(2 * parts)]

    def outer(i):
        out = [edge_rows(near, far, (i - skipped) * halves + h) for h in range(halves)]
        return jnp.concatenate([*out, unpack_columns(corners[:parts], corners[parts:], i)], axis=1)

    for n, corner in enumerate(corners):
        corners_out[n] = corner
    for i in range(2 * levels):
        start_out[i] = outer(skipped + i)
    for level in range(levels):
        east_k, east_v, north_k, north_v = (outer((4 + n) * levels + level) for n in range(4))
        mask = (east_k > 0.0).astype(f32)
        coeffs_out[0, level], coeffs_out[1, level] = upwind(east_k, east_v, eastward(mask))
        if level < levels - 1:
            coeffs_out[4, level] = outer(8 * levels + level)
        coeffs_out[5, level] = mask
        whole_k = jnp.concatenate([coeffs_in[2, level], north_k], axis=0)
        whole_v = jnp.concatenate([coeffs_in[3, level], north_v], axis=0)
        whole_mask = jnp.concatenate([coeffs_in[5, level], mask], axis=0)
        north[0, level], north[1, level] = upwind(whole_k, whole_v, northward(whole_mask))
    start, coeffs = cotangent_rows(start_in, start_out), coefficients(coeffs_in, coeffs_out, north)
    mask0 = coeffs_in[5, 0, :, :tile_lon]
    copies = []
    for f in range(2):
        surface = start_in[(2 + f) * levels, :, :tile_lon]
        for step in range(STEPS - 1):

            def read(level):
                return states[f, step - 1, level] if step else start((2 + f) * levels + level)

            def write(level, lam):
                states[f, step, level] = lam

            adjoint_step(coeffs, levels, read, write, 0, surface_levels(step, levels))
            surface = surface + states[f, step, 0, :tile_lat, :tile_lon]
        surface = surface * mask0
        for h in range(halves):
            at = (f * halves + h) * tile_lat
            own[at : at + tile_lat] = surface[:, h * BLOCK : (h + 1) * BLOCK]
        field = pl.ds(f * halves * tile_lat, halves * tile_lat)
        copies += fetch([(own.at[field], blocks.at[k, field]) for k in range(blocks.shape[0])], sent.at[f])
    for copy in copies:
        copy.wait()


def finish_adjoint(start_in, coeffs_in, start_out, coeffs_out, north, corners, states, adjoint_out, rest):
    levels = coeffs_in.shape[1]
    start, coeffs = cotangent_rows(start_in, start_out), coefficients(coeffs_in, coeffs_out, north)
    tile_lat, tile_lon = adjoint_out.shape[2:]
    for f in range(2):
        for step in range(STEPS):
            done = surface_levels(step, levels)

            def read(level):
                if not step:
                    return start((2 + f) * levels + level)
                return (states if level < surface_levels(step - 1, levels) else rest)[f, step - 1, level]

            def write(level, lam):
                if step == STEPS - 1:
                    adjoint_out[f, level] = lam[:tile_lat, :tile_lon]
                else:
                    rest[f, step, level] = lam

            adjoint_step(coeffs, levels, read, write, done, levels)


def sum_forcing(received, fields, forcing, near, far):
    tile_lat = forcing.shape[1]
    halves = forcing.shape[2] // BLOCK - 1
    total = received[0]
    for j in range(1, received.shape[0]):
        total = total + received[j]
    lane = lanes((tile_lat, BLOCK))
    upper = total[2 * halves * tile_lat :]
    lower = jnp.where(lane[: tile_lat // 2] < BLOCK // 2, turn(upper, -2 * HALO, 1), turn(upper, 2 * HALO, 1))
    packed = jnp.concatenate([upper, lower], axis=0)
    for f in range(2):
        for h in range(halves):
            at = (f * halves + h) * tile_lat
            forcing[f, :, h * BLOCK : (h + 1) * BLOCK] = total[at : at + tile_lat]
        used = (lane < HALO) | (lane >= BLOCK - HALO)
        if f == 0:
            edge = packed
        else:
            edge = jnp.where(lane < HALO, turn(packed, -HALO, 1), turn(packed, HALO, 1))
        forcing[f, :, halves * BLOCK :] = jnp.where(used, edge, 0.0)
    half = tracer_fields(fields.shape[0]) // 2
    put_rows(
        row_blocks(forcing, 0, 1) + row_blocks(fields, 0, half)
        + row_blocks(forcing, 1, 2) + row_blocks(fields, half, 2 * half),
        near,
        far,
    )


def run_forward(
    start_in, coeffs_in, start_out, coeffs_out, north, corners, forcing, near, far, final, state, tracers_out
):
    levels = coeffs_in.shape[1]
    start, coeffs = whole_rows(start_in, tracers_out), coefficients(coeffs_in, coeffs_out, north)
    sides = forcing.shape[2] // BLOCK
    parts = corners.shape[0] // 2
    columns = [corners[n] for n in range(2 * parts)]
    tile_lat, tile_lon = final.shape[2:]
    for f in range(2):
        at = f * near.shape[0]
        outer = jnp.concatenate([edge_rows(near, far, at + n) for n in range(sides)], axis=1)
        force = jnp.concatenate([forcing[f], outer], axis=0)
        for level in range(levels):
            i, at = f * levels + level, f * near.shape[0] + sides + level * (sides - 1)
            out = [edge_rows(near, far, at + h) for h in range(sides - 1)]
            out.append(unpack_columns(columns[:parts], columns[parts:], i))
            tracers_out[i] = jnp.concatenate(out, axis=1)
        force = force * coeffs(5, 0)
        for step in range(STEPS):
            above = None
            for level in range(levels):
                read = (lambda n: start(f * levels + n)) if step == 0 else (lambda n: state[(step - 1) % 2, n])
                theta = read(level)
                east_flux = coeffs(0, level) * theta + coeffs(1, level) * eastward(theta)
                north_flux = coeffs(2, level) * theta + coeffs(3, level) * northward(theta)
                out = theta - (east_flux - westward(east_flux)) - (north_flux - southward(north_flux))
                if level < levels - 1:
                    vertical = coeffs(4, level) * (theta - read(level + 1))
                    out = out - vertical
                if above is not None:
                    out = out + above
                above = vertical if level < levels - 1 else None
                if level == 0:
                    out = out + force
                if step == STEPS - 1:
                    final[f, level] = out[:tile_lat, :tile_lon]
                else:
                    state[step % 2, level] = out


def split(x):
    high = x.astype(bf16)
    return high, (x - high.astype(f32)).astype(bf16)


def weight_copy(weights, held, arrived, n):
    own = pl.ds(n * FETCH, FETCH)
    return pltpu.make_async_copy(weights.at[own], held.at[own], arrived.at[n])


def fetch_weights(weights, held, arrived):
    for n in range(held.shape[0] // FETCH):
        weight_copy(weights, held, arrived, n).start()


def held_part(weights, held, arrived):
    def part(r, g, u):
        if u == 0:

            @pl.when(r == 0)
            def _():
                for n in range(GROUP // FETCH):
                    weight_copy(weights, held, arrived, g * (GROUP // FETCH) + n).wait()

        return split(held[g * GROUP + u])

    return part


def one_hot(where):
    return jnp.where(where, 1.0, 0.0).astype(bf16)


def places(slots, blocks):
    return 8 * (-(-2 * slots // (8 * blocks)) + 1)


def round_chunks(slots, blocks):
    return -(-(slots + 7 * blocks) // BLOCK)


def as_row(ids):
    return jnp.concatenate([ids[k : k + 1, :] for k in range(ids.shape[0])], axis=1)


def rank_slots(block_row, blocks):
    slots = block_row.shape[1]
    mine = rows((blocks, slots)) == block_row
    cuts = range(0, slots, BLOCK)
    stacked = jnp.concatenate([one_hot(mine[:, at : at + BLOCK]) for at in cuts], axis=0)
    shape = (BLOCK, 2 * BLOCK)
    counts = jnp.dot(stacked, one_hot(rows(shape) < lanes(shape)), preferred_element_type=f32)
    before, out = jnp.zeros((blocks, BLOCK), f32), []
    for n, at in enumerate(cuts):
        run = counts[n * blocks : (n + 1) * blocks]
        here = jnp.where(mine[:, at : at + BLOCK], run[:, :BLOCK] + before, 0.0)
        out.append(jnp.sum(here, axis=0, keepdims=True))
        before = before + run[:, BLOCK:]
    return jnp.concatenate(out, axis=1), before


def find_slots(r, keys, counts, capacity, columns, lines, starts):
    slots = keys.shape[1]
    blocks = counts.shape[0]
    atm_row, ocean_row, block_row, rank = (keys[n : n + 1] for n in range(4))
    count = jnp.clip(counts - r * capacity, 0.0, capacity)
    tiles = jnp.floor((count + 7.0) * 0.125) * 8.0
    shape = (blocks, blocks)
    first = jnp.dot(one_hot(lanes(shape) < rows(shape)), tiles.astype(bf16), preferred_element_type=f32)
    starts[...] = first.astype(jnp.int32)
    mine = rows((blocks, slots)).astype(f32) == block_row
    own = jnp.where(mine, jnp.concatenate([first] * (slots // BLOCK), axis=1), 0.0)
    place = rank - r * capacity
    here = (place >= 0.0) & (place < capacity)
    place = jnp.where(here, jnp.sum(own, axis=0, keepdims=True) + place, -1.0)
    run = jnp.floor(place * (1.0 / BLOCK))
    low = one_hot(rows((BLOCK, slots)).astype(f32) == place - run * BLOCK)
    size = lines.shape[1]
    in_run = rows((size, slots)).astype(f32) == run
    ocean_high = jnp.floor(ocean_row * (1.0 / BLOCK))
    digits = [atm_row, ocean_high, ocean_row - ocean_high * BLOCK]
    digits = [jnp.where(in_run, digit, 0.0).astype(bf16) for digit in digits]
    across = (((1,), (1,)), ((), ()))
    down = [lax.dot_general(low, digit, across, preferred_element_type=f32) for digit in digits]
    along = [lax.dot_general(digit, low, across, preferred_element_type=f32) for digit in digits]
    columns[0, :, :size], columns[1, :, :size] = down[0], down[1] * BLOCK + down[2] - 1.0
    ocean = along[1] * BLOCK + along[2] - 1.0
    lines[0], lines[1] = jnp.where(ocean < 0.0, -1.0, along[0]), ocean


def couple(part, table, capacity, rounds, prepare, columns, lines, starts, transposed, result, scratch):
    vectors, products, starts_near = scratch
    blocks = starts.shape[0]
    total_rows = vectors.shape[0] - capacity
    width = table.shape[0]
    result[...] = jnp.zeros_like(result)
    products[...] = jnp.zeros_like(products)

    def one_round(r, carry):
        prepare(r)
        first_rows = starts[...]
        for w in range(blocks):
            starts_near[w] = first_rows[w, 0]
        place_hot = []
        for n in range(total_rows // BLOCK):
            gather = jnp.broadcast_to(columns[int(transposed), :, n : n + 1], (BLOCK, BLOCK))
            gather = jnp.concatenate([gather] * (width // BLOCK), axis=1)
            hot = one_hot(gather == lanes((BLOCK, width)).astype(f32))
            vectors[n * BLOCK : (n + 1) * BLOCK] = jnp.dot(hot, table, preferred_element_type=f32)
            put = lines[1 - int(transposed), n : n + 1]
            place_hot.append(one_hot(rows((result.shape[0], BLOCK)).astype(f32) == put))

        def group(g, carry):
            for u in range(GROUP):
                at = pl.ds(pl.multiple_of(starts_near[g * GROUP + u], 8), capacity)
                own = vectors[at]
                left = jnp.concatenate([own[:, n * BLOCK : (n + 1) * BLOCK] for n in range(4)], axis=0)
                high, low = part(r, g, u)
                right = jnp.concatenate([high, low], axis=1 if transposed else 0)
                contract = (((1,), (0 if transposed else 1,)), ((), ()))
                product = lax.dot_general(left.astype(bf16), right, contract, preferred_element_type=f32)
                for f in range(2):
                    high_part = product[f * capacity : (f + 1) * capacity]
                    low_part = product[(f + 2) * capacity : (f + 3) * capacity, :BLOCK]
                    products[at, f * BLOCK : (f + 1) * BLOCK] = (
                        high_part[:, BLOCK:] + low_part
                    ) + high_part[:, :BLOCK]
            return carry

        lax.fori_loop(0, blocks // GROUP, group, 0)
        summed = jnp.dot(
            jnp.concatenate(place_hot, axis=1),
            jnp.concatenate(split(products[:total_rows]), axis=1),
            preferred_element_type=f32,
        )
        result[...] += summed[:, : 2 * BLOCK] + summed[:, 2 * BLOCK :]
        return carry

    lax.fori_loop(0, rounds, one_round, 0)


def slot_keys(ids, tile_lat, keys):
    lon_count, cap = ids.shape[3:]
    ocean, atm_ids, block_ids = (ids[n, 0, 0] for n in range(3))
    order = (ocean & 1) * tile_lat + (ocean >> 1) + rows((lon_count, cap)) * (2 * tile_lat)
    order = jnp.where(ocean >= 0, order, lon_count * 2 * tile_lat) + 1
    for n, part in enumerate((atm_ids, order, block_ids)):
        keys[n : n + 1] = as_row(part.astype(f32))


def weigh(
    atm_near, margins, weights, after, sums, keys, counts, columns, lines, starts, result, *scratch
):
    scratch, (held, arrived) = scratch[:3], scratch[3:]
    fetch_weights(weights, held, arrived)
    lon_count = margins.shape[3]
    blocks = weights.shape[0]
    tile_lat = 2 * sums.shape[1] // 9
    slot_keys(margins, tile_lat, keys)
    rank, count = rank_slots(keys[2:3].astype(jnp.int32), blocks)
    keys[3:4] = rank
    counts[...] = count
    capacity = places(keys.shape[1], blocks)
    rounds = jnp.max(rank).astype(jnp.int32) // capacity + 1
    parts = [split(atm_near[f, 0]) for f in range(2)]
    table = jnp.concatenate([parts[f][n] for n in range(2) for f in range(2)], axis=1)
    part = held_part(weights, held, arrived)

    def prepare(r):
        find_slots((rounds - 1 - r).astype(f32), keys, counts[...], capacity, columns, lines, starts)

    couple(part, table, capacity, rounds, prepare, columns, lines, starts, False, result, scratch)
    lane = lanes((tile_lat, BLOCK))

    def block_sums(k, f, h):
        at = (2 * k + h) * tile_lat
        return result[at : at + tile_lat, f * BLOCK : (f + 1) * BLOCK]

    for n, k in enumerate(group_order(lon_count)):
        edge = jnp.zeros((tile_lat, BLOCK), f32)
        for f in range(2):
            for h in range(2):
                sums[n, (2 * f + h) * tile_lat : (2 * f + h + 1) * tile_lat] = block_sums(k, f, h)
            at = f * HALO
            after = turn(block_sums((k + 1) % lon_count, f, 0), at, 1)
            before = turn(block_sums((k - 1) % lon_count, f, 1), -at, 1)
            edge = jnp.where((lane >= at) & (lane < at + HALO), after, edge)
            end = BLOCK - at
            edge = jnp.where((lane >= end - HALO) & (lane < end), before, edge)
        upper, lower = edge[: tile_lat // 2], edge[tile_lat // 2 :]
        near = lane[: tile_lat // 2]
        lower = jnp.where(near < BLOCK // 2, turn(lower, 2 * HALO, 1), turn(lower, -2 * HALO, 1))
        sums[n, 4 * tile_lat :] = jnp.where((near < 2 * HALO) | (near >= BLOCK - 2 * HALO), upper, lower)


def unweigh(
    gathered, keys, counts, columns_in, lines_in, starts_in, weights, gradient, result, columns, lines, starts, *scratch
):
    scratch, (held, arrived) = scratch[:3], scratch[3:]
    fetch_weights(weights, held, arrived)
    blocks = weights.shape[0]
    lon_count, ocean_blocks = gathered.shape[0], gathered.shape[1] // 2
    order = group_order(lon_count)
    capacity = places(keys.shape[1], blocks)
    rounds = jnp.max(keys[3:4]).astype(jnp.int32) // capacity + 1
    parts = [
        split(
            jnp.concatenate(
                [gathered[order.index(k), f * ocean_blocks : (f + 1) * ocean_blocks] for k in range(lon_count)],
                axis=0,
            )
        )
        for f in range(2)
    ]
    table = jnp.concatenate([parts[f][n] for n in range(2) for f in range(2)], axis=1)

    def prepare(r):
        @pl.when(r == 0)
        def _():
            columns[...] = columns_in[...]
            lines[...] = lines_in[...]
            starts[...] = starts_in[...]

        @pl.when(r > 0)
        def _():
            find_slots(r.astype(f32), keys, counts[...], capacity, columns, lines, starts)

    part = held_part(weights, held, arrived)
    couple(part, table, capacity, rounds, prepare, columns, lines, starts, True, result, scratch)
    for f in range(2):
        gradient[f, 0] = result[:, f * BLOCK : (f + 1) * BLOCK]


def on_device(tracers, cotangent, land_mask, diffusion, velocity, weights, atm_state, margins):
    levels, tile_lat, tile_lon = land_mask.shape
    lon_count = lax.axis_size("lon")
    slots = lon_count * margins.shape[4]
    halves = tile_lon // BLOCK
    count = 9 * levels - 1
    parts = -(-count // PER_LANES)
    inputs = (tracers, cotangent, land_mask, diffusion, velocity)

    def in_vmem(s):
        return pltpu.VMEM(s.shape, s.dtype)

    message = (parts, tile_lat, BLOCK)
    fields, near, far, atm_near, margins_near = call(
        pack_columns,
        [
            (count, tile_lat, tile_lon),
            message,
            message,
            atm_state.shape,
            jax.ShapeDtypeStruct(margins.shape, margins.dtype),
        ],
        [*map(in_vmem, inputs), pltpu.SemaphoreType.DMA((7,))],
        name="pack_columns",
        inputs=7,
        far=range(7),
    )(*inputs, atm_state, margins)
    near_columns, far_columns = swap(near, far, "lon", True)

    blocks_of, atm = weights.shape[0], atm_state.shape[2]
    sum_rows = 2 * halves * tile_lat + tile_lat // 2
    ocean_blocks = lon_count * halves * tile_lat
    chunks = round_chunks(slots, blocks_of)
    held_rows = chunks * BLOCK + places(slots, blocks_of)

    def coupling_scratch(result_rows):
        return [
            pltpu.VMEM((result_rows, 2 * BLOCK), f32),
            pltpu.VMEM((held_rows, 4 * BLOCK), f32),
            pltpu.VMEM((held_rows, 2 * BLOCK), f32),
            pltpu.SMEM((blocks_of,), jnp.int32),
            pltpu.VMEM(weights.shape, f32),
            pltpu.SemaphoreType.DMA((blocks_of // FETCH,)),
        ]

    coupling_flops = 4 * slots * blocks_of * 2 * BLOCK * BLOCK * 2
    found = [
        jax.ShapeDtypeStruct((2, BLOCK, BLOCK), f32),
        jax.ShapeDtypeStruct((2, -(-chunks // 8) * 8, BLOCK), f32),
        jax.ShapeDtypeStruct((blocks_of, BLOCK), jnp.int32),
    ]
    sums, *slot_data = call(
        weigh,
        [(lon_count, sum_rows, BLOCK), (8, slots), (blocks_of, BLOCK), *found],
        coupling_scratch(ocean_blocks),
        coupling_flops,
        name="weigh",
        inputs=4,
        far=(2,),
    )(atm_near, margins_near, weights, far)

    sources = (count - 2 * levels) * halves + 2 * parts
    message = (-(-sources // 2), 8, BLOCK)
    columns = (parts, tile_lat, BLOCK)
    near, far, from_west, from_east, sums = call(
        pack_rows,
        [message, message, columns, columns, sums.shape],
        name="pack_rows",
        inputs=4,
        aliases={3: 4},
    )(fields, near_columns, far_columns, sums)
    received = exchange(sums)
    near_rows, far_rows = swap(near, far, "lat", False)

    wide = (tile_lat + 8, tile_lon + BLOCK)
    inner, outer = (tile_lat, tile_lon + BLOCK), (8, tile_lon + BLOCK)
    inner_data = call(
        prepare_stencil,
        [(4 * levels, *inner), (6, levels, *inner)],
        name="prepare_stencil",
        inputs=3,
    )(fields, from_west, from_east)
    own = (2 * halves * tile_lat, BLOCK)
    adjoint_states = (2, STEPS - 1, levels, *wide)
    blocks, *outer_data, states = call(
        run_adjoint,
        [
            (lon_count, *own),
            (2 * levels, *outer),
            (6, levels, *outer),
            (2, levels, *wide),
            (2 * parts, 8, BLOCK),
            adjoint_states,
        ],
        [pltpu.VMEM(own, f32), pltpu.SemaphoreType.DMA((2, lon_count))],
        name="run_adjoint",
        inputs=6,
        far_outs=(0,),
    )(*inner_data, from_west, from_east, far_rows, near_rows)
    gathered = exchange(blocks)

    message = (halves + 1 + levels * halves, 8, BLOCK)
    forcing, near, far = call(
        sum_forcing, [(2, tile_lat, tile_lon + BLOCK), message, message], name="sum_forcing", inputs=2
    )(received, fields)
    near_rows, far_rows = swap(near, far, "lat", False)
    (adjoint,) = call(
        finish_adjoint,
        [cotangent.shape],
        [pltpu.VMEM(adjoint_states, f32)],
        name="finish_adjoint",
        inputs=7,
    )(*inner_data, *outer_data, states)
    (final,) = call(
        run_forward,
        [tracers.shape],
        [pltpu.VMEM((2, levels, *wide), f32), pltpu.VMEM((2 * levels, *outer), f32)],
        name="run_forward",
        inputs=9,
    )(*inner_data, *outer_data, forcing, near_rows, far_rows)

    (gradient,) = call(
        unweigh,
        [atm_state.shape],
        [coupling_scratch(atm)[0], *map(in_vmem, found), *coupling_scratch(atm)[1:]],
        coupling_flops,
        name="unweigh",
        inputs=7,
        far=(6,),
    )(gathered, *slot_data, weights)
    return (final, adjoint, gradient)


def solution(mesh):
    return jax.shard_map(
        on_device,
        mesh=mesh,
        in_specs=(
            P(None, None, "lat", "lon"),
            P(None, None, "lat", "lon"),
            P(None, "lat", "lon"),
            P(None, None, "lat", "lon"),
            P(None, None, "lat", "lon"),
            P(),
            P(None, "lat", "lon", None),
            P(None, "lat", "lon", None, None),
        ),
        out_specs=(
            P(None, None, "lat", "lon"),
            P(None, None, "lat", "lon"),
            P(None, "lat", "lon", None),
        ),
        check_vma=False,
    )
```

```python
import jax
import jax.numpy as jnp
from jax import lax
from jax.experimental import pallas as pl
from jax.experimental.pallas import tpu as pltpu
from jax.sharding import PartitionSpec as P

BLOCK = 128
STEPS = 4
HALO = STEPS
PER_LANES = BLOCK // HALO
GROUP = 32
FETCH = 4
f32 = jnp.float32
bf16 = jnp.bfloat16
VMEM_LIMIT = 20 * 1024 * 1024


def call(body, outs, scratch=(), flops=0, name=None, inputs=0, far=(), far_outs=(), aliases=None):
    outs = [s if isinstance(s, jax.ShapeDtypeStruct) else jax.ShapeDtypeStruct(s, f32) for s in outs]
    near = pl.BlockSpec(memory_space=pltpu.VMEM)
    aliases = aliases or {}
    kernel = pl.pallas_call(
        body,
        out_shape=outs,
        in_specs=[
            pl.BlockSpec(memory_space=pl.ANY)
            if n in aliases
            else pl.BlockSpec(memory_space=pltpu.HBM)
            if n in far
            else near
            for n in range(inputs)
        ],
        out_specs=[
            pl.BlockSpec(memory_space=pl.ANY) if n in aliases.values() or n in far_outs else near
            for n in range(len(outs))
        ],
        input_output_aliases=aliases,
        scratch_shapes=list(scratch),
        compiler_params=pltpu.CompilerParams(vmem_limit_bytes=VMEM_LIMIT),
        cost_estimate=pl.CostEstimate(flops=flops, bytes_accessed=1 << 20, transcendentals=0),
        name=name,
    )

    def run(*args):
        return kernel(
            *(pltpu.with_memory_space_constraint(x, pltpu.HBM) if n in far else x for n, x in enumerate(args))
        )

    return run


def lanes(shape):
    return lax.broadcasted_iota(jnp.int32, shape, len(shape) - 1)


def rows(shape):
    return lax.broadcasted_iota(jnp.int32, shape, len(shape) - 2)


def turn(x, shift, axis):
    shift %= x.shape[axis]
    return pltpu.roll(x, shift, axis) if shift else x


def group_order(count):
    half = count // 2
    return [k for n in range(half) for k in (half + n, n)]


def exchange(x):
    order = group_order(x.shape[0])
    return lax.all_to_all(x, "lon", split_axis=0, concat_axis=0, tiled=True, axis_index_groups=[order])


def swap(near, far, axis, wrap):
    count = lax.axis_size(axis)
    pairs = [[], []]
    for i in range(count if wrap else count - 1):
        j = (i + 1) % count
        pairs[i % 2] += [(i, j), (j, i)]
    far = lax.ppermute(far, axis, pairs[1])
    return lax.ppermute(near, axis, pairs[0]), far


def sort_swap(axis, after, before):
    odd = lax.rem(lax.axis_index(axis), 2) == 1
    return jnp.where(odd, before, after), jnp.where(odd, after, before)


def tile_fields(tracers, cotangent, land_mask, diffusion, velocity):
    levels = land_mask.shape[0]
    mask = [land_mask[level].astype(f32) for level in range(levels)]
    out = [tracers[f, level] for f in range(2) for level in range(levels)]
    out += [cotangent[f, level] for f in range(2) for level in range(levels)]
    out += [diffusion[0, level] * mask[level] for level in range(levels)]
    out += [velocity[0, level] * mask[level] for level in range(levels)]
    out += [diffusion[1, level] * mask[level] for level in range(levels)]
    out += [velocity[1, level] * mask[level] for level in range(levels)]
    out += [diffusion[2, level] * mask[level] * mask[level + 1] for level in range(levels - 1)]
    return out


def fetch(pairs, arrived):
    copies = [pltpu.make_async_copy(src, dst, arrived.at[n]) for n, (src, dst) in enumerate(pairs)]
    for copy in copies:
        copy.start()
    return copies


def pack_columns(*refs):
    inputs, (fields, near, far), scratch = refs[:7], refs[7:10], refs[12:]
    copies = fetch(zip(inputs, [*scratch[:5], *refs[10:12]]), scratch[5])
    for copy in copies[:5]:
        copy.wait()
    shape = near.shape[1:]
    lane = lanes(shape)
    west = [jnp.zeros(shape, f32) for _ in range(near.shape[0])]
    east = [jnp.zeros(shape, f32) for _ in range(near.shape[0])]
    for i, field in enumerate(tile_fields(*scratch[:5])):
        fields[i] = field
        part, at = divmod(i, PER_LANES)
        at *= HALO
        here = (lane >= at) & (lane < at + HALO)
        west[part] = jnp.where(here, turn(field[:, :BLOCK], at, 1), west[part])
        east[part] = jnp.where(here, turn(field[:, -BLOCK:], at + HALO, 1), east[part])
    for part in range(near.shape[0]):
        near[part], far[part] = sort_swap("lon", east[part], west[part])
    for copy in copies[5:]:
        copy.wait()


def unpack_columns(from_west, from_east, i):
    part, at = divmod(i, PER_LANES)
    at *= HALO
    lane = lanes(from_west[part].shape)
    east = turn(from_east[part], -at, 1)
    west = turn(from_west[part], -at - HALO, 1)
    return jnp.where(lane < HALO, east, jnp.where(lane >= BLOCK - HALO, west, 0.0))


def row_sources(fields, from_west, from_east):
    out = [(fields, (i, slice(None), slice(h * BLOCK, (h + 1) * BLOCK)))
           for i in range(fields.shape[0]) for h in range(fields.shape[2] // BLOCK)]
    for columns in (from_west, from_east):
        out += [(columns, (part,)) for part in range(columns.shape[0])]
    return out


def pack_rows(fields, near_columns, far_columns, sums, near, far, from_west, from_east, same_sums):
    for part in range(from_west.shape[0]):
        from_east[part], from_west[part] = sort_swap("lon", near_columns[part], far_columns[part])
    sources = [ref[at] for ref, at in row_sources(fields, from_west, from_east)]
    half = near.shape[0]
    row = rows((8, BLOCK))
    for i in range(half):
        first = sources[i]
        second = sources[i + half] if i + half < len(sources) else jnp.zeros_like(first)
        to_north = jnp.where(row < HALO, turn(first[-8:], HALO, 0), second[-8:])
        to_south = jnp.where(row < HALO, first[:8], turn(second[:8], HALO, 0))
        near[i], far[i] = sort_swap("lat", to_north, to_south)


def edge_rows(near, far, i):
    half = near.shape[0]
    from_north, from_south = sort_swap("lat", near[i % half], far[i % half])
    if i < half:
        from_south = turn(from_south, HALO, 0)
    else:
        from_north = turn(from_north, HALO, 0)
    return jnp.where(rows(from_north.shape) < HALO, from_north, from_south)


def widen(fields, from_west, from_east, near, far, start, wide):
    count, tile_lat, tile_lon = fields.shape
    halves = tile_lon // BLOCK
    parts = from_west.shape[0]
    corners = [edge_rows(near, far, count * halves + n) for n in range(2 * parts)]
    for i in range(count):
        out = start.at[i] if i < start.shape[0] else wide.at[i - start.shape[0]]
        out[:tile_lat, :tile_lon] = fields[i]
        out[:tile_lat, tile_lon:] = unpack_columns(from_west, from_east, i)
        for h in range(halves):
            out[tile_lat:, h * BLOCK : (h + 1) * BLOCK] = edge_rows(near, far, i * halves + h)
        out[tile_lat:, tile_lon:] = unpack_columns(corners[:parts], corners[parts:], i)


def eastward(x):
    return turn(x, -1, 1)


def westward(x):
    return turn(x, 1, 1)


def northward(x):
    return turn(x, -1, 0)


def southward(x):
    return turn(x, 1, 0)


def adjoint_step(coeffs, read, write, first, last):
    levels = coeffs.shape[1]
    above = coeffs[4, first - 1] * (read(first) - read(first - 1)) if first else None
    for level in range(first, last):
        lam = read(level)
        step_x = eastward(lam) - lam
        step_y = northward(lam) - lam
        out = lam + coeffs[0, level] * step_x + westward(coeffs[1, level] * step_x)
        out = out + coeffs[2, level] * step_y + southward(coeffs[3, level] * step_y)
        if above is not None:
            out = out - above
        if level < levels - 1:
            above = coeffs[4, level] * (read(level + 1) - lam)
            out = out + above
        write(level, out)


def surface_levels(step, levels):
    return min(levels, STEPS - 1 - step)


def run_adjoint(
    fields, from_west, from_east, far, near, blocks, coeffs, start, states, wide, own, sent
):
    levels = coeffs.shape[1]
    tile_lat, tile_lon = fields.shape[1:]
    halves = tile_lon // BLOCK
    widen(fields, from_west, from_east, near, far, start, wide)
    base = 0
    mask0 = None
    for level in range(levels):
        east_d, east_u = wide[base + level], wide[base + levels + level]
        north_d, north_u = wide[base + 2 * levels + level], wide[base + 3 * levels + level]
        mask = (east_d > 0.0).astype(f32)
        mask0 = mask if mask0 is None else mask0
        mask_e, mask_n = eastward(mask), northward(mask)
        east_k, east_v = east_d * mask_e, east_u * mask_e
        north_k, north_v = north_d * mask_n, north_u * mask_n
        coeffs[0, level] = jnp.maximum(east_v, 0.0) + east_k
        coeffs[1, level] = jnp.minimum(east_v, 0.0) - east_k
        coeffs[2, level] = jnp.maximum(north_v, 0.0) + north_k
        coeffs[3, level] = jnp.minimum(north_v, 0.0) - north_k
        coeffs[4, level] = wide[base + 4 * levels + level] if level < levels - 1 else jnp.zeros_like(mask)
        coeffs[5, level] = mask
    copies = []
    for f in range(2):
        surface = start[(2 + f) * levels, :tile_lat, :tile_lon]
        for step in range(STEPS - 1):

            def read(level):
                return states[f, step - 1, level] if step else start[(2 + f) * levels + level]

            def write(level, lam):
                states[f, step, level] = lam

            adjoint_step(coeffs, read, write, 0, surface_levels(step, levels))
            surface = surface + states[f, step, 0, :tile_lat, :tile_lon]
        surface = surface * mask0[:tile_lat, :tile_lon]
        for h in range(halves):
            at = (f * halves + h) * tile_lat
            own[at : at + tile_lat] = surface[:, h * BLOCK : (h + 1) * BLOCK]
        field = pl.ds(f * halves * tile_lat, halves * tile_lat)
        copies += fetch([(own.at[field], blocks.at[k, field]) for k in range(blocks.shape[0])], sent.at[f])
    for copy in copies:
        copy.wait()


def finish_adjoint(coeffs, start, states, adjoint_out, rest):
    levels = coeffs.shape[1]
    tile_lat, tile_lon = adjoint_out.shape[2:]
    for f in range(2):
        for step in range(STEPS):
            done = surface_levels(step, levels)

            def read(level):
                if not step:
                    return start[(2 + f) * levels + level]
                return (states if level < surface_levels(step - 1, levels) else rest)[f, step - 1, level]

            def write(level, lam):
                if step == STEPS - 1:
                    adjoint_out[f, level] = lam[:tile_lat, :tile_lon]
                else:
                    rest[f, step, level] = lam

            adjoint_step(coeffs, read, write, done, levels)


def sum_forcing(received, forcing, near, far):
    tile_lat = forcing.shape[1]
    halves = forcing.shape[2] // BLOCK - 1
    total = received[0]
    for j in range(1, received.shape[0]):
        total = total + received[j]
    lane = lanes((tile_lat, BLOCK))
    upper = total[2 * halves * tile_lat :]
    lower = jnp.where(lane[: tile_lat // 2] < BLOCK // 2, turn(upper, -2 * HALO, 1), turn(upper, 2 * HALO, 1))
    packed = jnp.concatenate([upper, lower], axis=0)
    for f in range(2):
        for h in range(halves):
            at = (f * halves + h) * tile_lat
            forcing[f, :, h * BLOCK : (h + 1) * BLOCK] = total[at : at + tile_lat]
        used = (lane < HALO) | (lane >= BLOCK - HALO)
        if f == 0:
            edge = packed
        else:
            edge = jnp.where(lane < HALO, turn(packed, -HALO, 1), turn(packed, HALO, 1))
        forcing[f, :, halves * BLOCK :] = jnp.where(used, edge, 0.0)
    row = rows((8, forcing.shape[2]))
    to_north = jnp.where(row < HALO, turn(forcing[0, tile_lat - 8 :], HALO, 0), forcing[1, tile_lat - 8 :])
    to_south = jnp.where(row < HALO, forcing[0, :8], turn(forcing[1, :8], HALO, 0))
    near[0], far[0] = sort_swap("lat", to_north, to_south)


def run_forward(coeffs, start, forcing, near, far, final, state):
    levels = coeffs.shape[1]
    tile_lat, tile_lon = final.shape[2:]
    for f in range(2):
        force = jnp.concatenate([forcing[f], edge_rows(near, far, f)], axis=0)
        force = force * coeffs[5, 0]
        for step in range(STEPS):
            above = None
            for level in range(levels):
                read = (lambda n: start[f * levels + n]) if step == 0 else (lambda n: state[(step - 1) % 2, n])
                theta = read(level)
                east_flux = coeffs[0, level] * theta + coeffs[1, level] * eastward(theta)
                north_flux = coeffs[2, level] * theta + coeffs[3, level] * northward(theta)
                out = theta - (east_flux - westward(east_flux)) - (north_flux - southward(north_flux))
                if level < levels - 1:
                    vertical = coeffs[4, level] * (theta - read(level + 1))
                    out = out - vertical
                if above is not None:
                    out = out + above
                above = vertical if level < levels - 1 else None
                if level == 0:
                    out = out + force
                if step == STEPS - 1:
                    final[f, level] = out[:tile_lat, :tile_lon]
                else:
                    state[step % 2, level] = out


def split(x):
    high = x.astype(bf16)
    return high, (x - high.astype(f32)).astype(bf16)


def weight_copy(weights, held, arrived, n):
    own = pl.ds(n * FETCH, FETCH)
    return pltpu.make_async_copy(weights.at[own], held.at[own], arrived.at[n])


def fetch_weights(weights, held, arrived):
    for n in range(held.shape[0] // FETCH):
        weight_copy(weights, held, arrived, n).start()


def held_part(weights, held, arrived):
    def part(r, g, u):
        if u == 0:

            @pl.when(r == 0)
            def _():
                for n in range(GROUP // FETCH):
                    weight_copy(weights, held, arrived, g * (GROUP // FETCH) + n).wait()

        return split(held[g * GROUP + u])

    return part


def one_hot(where):
    return jnp.where(where, 1.0, 0.0).astype(bf16)


def places(slots, blocks):
    return 8 * (-(-2 * slots // (8 * blocks)) + 1)


def round_chunks(slots, blocks):
    return -(-(slots + 7 * blocks) // BLOCK)


def as_row(ids):
    return jnp.concatenate([ids[k : k + 1, :] for k in range(ids.shape[0])], axis=1)


def rank_slots(block_row, blocks):
    slots = block_row.shape[1]
    mine = rows((blocks, slots)) == block_row
    cuts = range(0, slots, BLOCK)
    stacked = jnp.concatenate([one_hot(mine[:, at : at + BLOCK]) for at in cuts], axis=0)
    shape = (BLOCK, 2 * BLOCK)
    counts = jnp.dot(stacked, one_hot(rows(shape) < lanes(shape)), preferred_element_type=f32)
    before, out = jnp.zeros((blocks, BLOCK), f32), []
    for n, at in enumerate(cuts):
        run = counts[n * blocks : (n + 1) * blocks]
        here = jnp.where(mine[:, at : at + BLOCK], run[:, :BLOCK] + before, 0.0)
        out.append(jnp.sum(here, axis=0, keepdims=True))
        before = before + run[:, BLOCK:]
    return jnp.concatenate(out, axis=1), before


def find_slots(r, keys, counts, capacity, columns, lines, starts):
    slots = keys.shape[1]
    blocks = counts.shape[0]
    atm_row, ocean_row, block_row, rank = (keys[n : n + 1] for n in range(4))
    count = jnp.clip(counts - r * capacity, 0.0, capacity)
    tiles = jnp.floor((count + 7.0) * 0.125) * 8.0
    shape = (blocks, blocks)
    first = jnp.dot(one_hot(lanes(shape) < rows(shape)), tiles.astype(bf16), preferred_element_type=f32)
    starts[...] = first.astype(jnp.int32)
    mine = rows((blocks, slots)).astype(f32) == block_row
    own = jnp.where(mine, jnp.concatenate([first] * (slots // BLOCK), axis=1), 0.0)
    place = rank - r * capacity
    here = (place >= 0.0) & (place < capacity)
    place = jnp.where(here, jnp.sum(own, axis=0, keepdims=True) + place, -1.0)
    run = jnp.floor(place * (1.0 / BLOCK))
    low = one_hot(rows((BLOCK, slots)).astype(f32) == place - run * BLOCK)
    size = lines.shape[1]
    in_run = rows((size, slots)).astype(f32) == run
    ocean_high = jnp.floor(ocean_row * (1.0 / BLOCK))
    digits = [atm_row, ocean_high, ocean_row - ocean_high * BLOCK]
    digits = [jnp.where(in_run, digit, 0.0).astype(bf16) for digit in digits]
    across = (((1,), (1,)), ((), ()))
    down = [lax.dot_general(low, digit, across, preferred_element_type=f32) for digit in digits]
    along = [lax.dot_general(digit, low, across, preferred_element_type=f32) for digit in digits]
    columns[0, :, :size], columns[1, :, :size] = down[0], down[1] * BLOCK + down[2] - 1.0
    ocean = along[1] * BLOCK + along[2] - 1.0
    lines[0], lines[1] = jnp.where(ocean < 0.0, -1.0, along[0]), ocean


def couple(part, table, capacity, rounds, prepare, columns, lines, starts, transposed, result, scratch):
    vectors, products, starts_near = scratch
    blocks = starts.shape[0]
    total_rows = vectors.shape[0] - capacity
    width = table.shape[0]
    result[...] = jnp.zeros_like(result)
    products[...] = jnp.zeros_like(products)

    def one_round(r, carry):
        prepare(r)
        first_rows = starts[...]
        for w in range(blocks):
            starts_near[w] = first_rows[w, 0]
        place_hot = []
        for n in range(total_rows // BLOCK):
            gather = jnp.broadcast_to(columns[int(transposed), :, n : n + 1], (BLOCK, BLOCK))
            gather = jnp.concatenate([gather] * (width // BLOCK), axis=1)
            hot = one_hot(gather == lanes((BLOCK, width)).astype(f32))
            vectors[n * BLOCK : (n + 1) * BLOCK] = jnp.dot(hot, table, preferred_element_type=f32)
            put = lines[1 - int(transposed), n : n + 1]
            place_hot.append(one_hot(rows((result.shape[0], BLOCK)).astype(f32) == put))

        def group(g, carry):
            for u in range(GROUP):
                at = pl.ds(pl.multiple_of(starts_near[g * GROUP + u], 8), capacity)
                own = vectors[at]
                left = jnp.concatenate([own[:, n * BLOCK : (n + 1) * BLOCK] for n in range(4)], axis=0)
                high, low = part(r, g, u)
                right = jnp.concatenate([high, low], axis=1 if transposed else 0)
                contract = (((1,), (0 if transposed else 1,)), ((), ()))
                product = lax.dot_general(left.astype(bf16), right, contract, preferred_element_type=f32)
                for f in range(2):
                    high_part = product[f * capacity : (f + 1) * capacity]
                    low_part = product[(f + 2) * capacity : (f + 3) * capacity, :BLOCK]
                    products[at, f * BLOCK : (f + 1) * BLOCK] = (
                        high_part[:, BLOCK:] + low_part
                    ) + high_part[:, :BLOCK]
            return carry

        lax.fori_loop(0, blocks // GROUP, group, 0)
        summed = jnp.dot(
            jnp.concatenate(place_hot, axis=1),
            jnp.concatenate(split(products[:total_rows]), axis=1),
            preferred_element_type=f32,
        )
        result[...] += summed[:, : 2 * BLOCK] + summed[:, 2 * BLOCK :]
        return carry

    lax.fori_loop(0, rounds, one_round, 0)


def slot_keys(ids, tile_lat, keys):
    lon_count, cap = ids.shape[3:]
    ocean, atm_ids, block_ids = (ids[n, 0, 0] for n in range(3))
    order = (ocean & 1) * tile_lat + (ocean >> 1) + rows((lon_count, cap)) * (2 * tile_lat)
    order = jnp.where(ocean >= 0, order, lon_count * 2 * tile_lat) + 1
    for n, part in enumerate((atm_ids, order, block_ids)):
        keys[n : n + 1] = as_row(part.astype(f32))


def weigh(
    atm_near, margins, weights, after, sums, keys, counts, columns, lines, starts, result, *scratch
):
    scratch, (held, arrived) = scratch[:3], scratch[3:]
    fetch_weights(weights, held, arrived)
    lon_count = margins.shape[3]
    blocks = weights.shape[0]
    tile_lat = 2 * sums.shape[1] // 9
    slot_keys(margins, tile_lat, keys)
    rank, count = rank_slots(keys[2:3].astype(jnp.int32), blocks)
    keys[3:4] = rank
    counts[...] = count
    capacity = places(keys.shape[1], blocks)
    rounds = jnp.max(rank).astype(jnp.int32) // capacity + 1
    parts = [split(atm_near[f, 0]) for f in range(2)]
    table = jnp.concatenate([parts[f][n] for n in range(2) for f in range(2)], axis=1)
    part = held_part(weights, held, arrived)

    def prepare(r):
        find_slots((rounds - 1 - r).astype(f32), keys, counts[...], capacity, columns, lines, starts)

    couple(part, table, capacity, rounds, prepare, columns, lines, starts, False, result, scratch)
    lane = lanes((tile_lat, BLOCK))

    def block_sums(k, f, h):
        at = (2 * k + h) * tile_lat
        return result[at : at + tile_lat, f * BLOCK : (f + 1) * BLOCK]

    for n, k in enumerate(group_order(lon_count)):
        edge = jnp.zeros((tile_lat, BLOCK), f32)
        for f in range(2):
            for h in range(2):
                sums[n, (2 * f + h) * tile_lat : (2 * f + h + 1) * tile_lat] = block_sums(k, f, h)
            at = f * HALO
            after = turn(block_sums((k + 1) % lon_count, f, 0), at, 1)
            before = turn(block_sums((k - 1) % lon_count, f, 1), -at, 1)
            edge = jnp.where((lane >= at) & (lane < at + HALO), after, edge)
            end = BLOCK - at
            edge = jnp.where((lane >= end - HALO) & (lane < end), before, edge)
        upper, lower = edge[: tile_lat // 2], edge[tile_lat // 2 :]
        near = lane[: tile_lat // 2]
        lower = jnp.where(near < BLOCK // 2, turn(lower, 2 * HALO, 1), turn(lower, -2 * HALO, 1))
        sums[n, 4 * tile_lat :] = jnp.where((near < 2 * HALO) | (near >= BLOCK - 2 * HALO), upper, lower)


def unweigh(
    gathered, keys, counts, columns_in, lines_in, starts_in, weights, gradient, result, columns, lines, starts, *scratch
):
    scratch, (held, arrived) = scratch[:3], scratch[3:]
    fetch_weights(weights, held, arrived)
    blocks = weights.shape[0]
    lon_count, ocean_blocks = gathered.shape[0], gathered.shape[1] // 2
    order = group_order(lon_count)
    capacity = places(keys.shape[1], blocks)
    rounds = jnp.max(keys[3:4]).astype(jnp.int32) // capacity + 1
    parts = [
        split(
            jnp.concatenate(
                [gathered[order.index(k), f * ocean_blocks : (f + 1) * ocean_blocks] for k in range(lon_count)],
                axis=0,
            )
        )
        for f in range(2)
    ]
    table = jnp.concatenate([parts[f][n] for n in range(2) for f in range(2)], axis=1)

    def prepare(r):
        @pl.when(r == 0)
        def _():
            columns[...] = columns_in[...]
            lines[...] = lines_in[...]
            starts[...] = starts_in[...]

        @pl.when(r > 0)
        def _():
            find_slots(r.astype(f32), keys, counts[...], capacity, columns, lines, starts)

    part = held_part(weights, held, arrived)
    couple(part, table, capacity, rounds, prepare, columns, lines, starts, True, result, scratch)
    for f in range(2):
        gradient[f, 0] = result[:, f * BLOCK : (f + 1) * BLOCK]


def on_device(tracers, cotangent, land_mask, diffusion, velocity, weights, atm_state, margins):
    levels, tile_lat, tile_lon = land_mask.shape
    lon_count = lax.axis_size("lon")
    slots = lon_count * margins.shape[4]
    halves = tile_lon // BLOCK
    count = 9 * levels - 1
    parts = -(-count // PER_LANES)
    inputs = (tracers, cotangent, land_mask, diffusion, velocity)

    def in_vmem(s):
        return pltpu.VMEM(s.shape, s.dtype)

    message = (parts, tile_lat, BLOCK)
    fields, near, far, atm_near, margins_near = call(
        pack_columns,
        [
            (count, tile_lat, tile_lon),
            message,
            message,
            atm_state.shape,
            jax.ShapeDtypeStruct(margins.shape, margins.dtype),
        ],
        [*map(in_vmem, inputs), pltpu.SemaphoreType.DMA((7,))],
        name="pack_columns",
        inputs=7,
        far=range(7),
    )(*inputs, atm_state, margins)
    near_columns, far_columns = swap(near, far, "lon", True)

    blocks_of, atm = weights.shape[0], atm_state.shape[2]
    sum_rows = 2 * halves * tile_lat + tile_lat // 2
    ocean_blocks = lon_count * halves * tile_lat
    chunks = round_chunks(slots, blocks_of)
    held_rows = chunks * BLOCK + places(slots, blocks_of)

    def coupling_scratch(result_rows):
        return [
            pltpu.VMEM((result_rows, 2 * BLOCK), f32),
            pltpu.VMEM((held_rows, 4 * BLOCK), f32),
            pltpu.VMEM((held_rows, 2 * BLOCK), f32),
            pltpu.SMEM((blocks_of,), jnp.int32),
            pltpu.VMEM(weights.shape, f32),
            pltpu.SemaphoreType.DMA((blocks_of // FETCH,)),
        ]

    coupling_flops = 4 * slots * blocks_of * 2 * BLOCK * BLOCK * 2
    found = [
        jax.ShapeDtypeStruct((2, BLOCK, BLOCK), f32),
        jax.ShapeDtypeStruct((2, -(-chunks // 8) * 8, BLOCK), f32),
        jax.ShapeDtypeStruct((blocks_of, BLOCK), jnp.int32),
    ]
    sums, *slot_data = call(
        weigh,
        [(lon_count, sum_rows, BLOCK), (8, slots), (blocks_of, BLOCK), *found],
        coupling_scratch(ocean_blocks),
        coupling_flops,
        name="weigh",
        inputs=4,
        far=(2,),
    )(atm_near, margins_near, weights, far)

    sources = count * halves + 2 * parts
    message = (-(-sources // 2), 8, BLOCK)
    columns = (parts, tile_lat, BLOCK)
    near, far, from_west, from_east, sums = call(
        pack_rows,
        [message, message, columns, columns, sums.shape],
        name="pack_rows",
        inputs=4,
        aliases={3: 4},
    )(fields, near_columns, far_columns, sums)
    received = exchange(sums)
    near_rows, far_rows = swap(near, far, "lat", False)

    wide = (tile_lat + 8, tile_lon + BLOCK)
    own = (2 * halves * tile_lat, BLOCK)
    adjoint_states = (2, STEPS - 1, levels, *wide)
    blocks, coeffs, start, states = call(
        run_adjoint,
        [(lon_count, *own), (6, levels, *wide), (4 * levels, *wide), adjoint_states],
        [
            pltpu.VMEM((count - 4 * levels, *wide), f32),
            pltpu.VMEM(own, f32),
            pltpu.SemaphoreType.DMA((2, lon_count)),
        ],
        name="run_adjoint",
        inputs=5,
        far_outs=(0,),
    )(fields, from_west, from_east, far_rows, near_rows)
    gathered = exchange(blocks)

    message = (1, 8, tile_lon + BLOCK)
    forcing, near, far = call(
        sum_forcing, [(2, tile_lat, tile_lon + BLOCK), message, message], name="sum_forcing", inputs=1
    )(received)
    near_rows, far_rows = swap(near, far, "lat", False)
    (adjoint,) = call(
        finish_adjoint,
        [cotangent.shape],
        [pltpu.VMEM(adjoint_states, f32)],
        name="finish_adjoint",
        inputs=3,
    )(coeffs, start, states)
    (final,) = call(
        run_forward,
        [tracers.shape],
        [pltpu.VMEM((2, levels, *wide), f32)],
        name="run_forward",
        inputs=5,
    )(coeffs, start, forcing, near_rows, far_rows)

    (gradient,) = call(
        unweigh,
        [atm_state.shape],
        [coupling_scratch(atm)[0], *map(in_vmem, found), *coupling_scratch(atm)[1:]],
        coupling_flops,
        name="unweigh",
        inputs=7,
        far=(6,),
    )(gathered, *slot_data, weights)
    return (final, adjoint, gradient)


def solution(mesh):
    return jax.shard_map(
        on_device,
        mesh=mesh,
        in_specs=(
            P(None, None, "lat", "lon"),
            P(None, None, "lat", "lon"),
            P(None, "lat", "lon"),
            P(None, None, "lat", "lon"),
            P(None, None, "lat", "lon"),
            P(),
            P(None, "lat", "lon", None),
            P(None, "lat", "lon", None, None),
        ),
        out_specs=(
            P(None, None, "lat", "lon"),
            P(None, None, "lat", "lon"),
            P(None, "lat", "lon", None),
        ),
        check_vma=False,
    )
```

```python
import jax
import jax.numpy as jnp
from jax import lax
from jax.experimental import pallas as pl
from jax.experimental.pallas import tpu as pltpu
from jax.sharding import PartitionSpec as P

BLOCK = 128
STEPS = 4
HALO = STEPS
PER_LANES = BLOCK // HALO
GROUP = 16
FETCH = 4
f32 = jnp.float32
bf16 = jnp.bfloat16
VMEM_LIMIT = 20 * 1024 * 1024


def call(body, outs, scratch=(), flops=0, name=None, inputs=0, far=(), far_outs=(), aliases=None):
    outs = [s if isinstance(s, jax.ShapeDtypeStruct) else jax.ShapeDtypeStruct(s, f32) for s in outs]
    near = pl.BlockSpec(memory_space=pltpu.VMEM)
    aliases = aliases or {}
    kernel = pl.pallas_call(
        body,
        out_shape=outs,
        in_specs=[
            pl.BlockSpec(memory_space=pl.ANY)
            if n in aliases
            else pl.BlockSpec(memory_space=pltpu.HBM)
            if n in far
            else near
            for n in range(inputs)
        ],
        out_specs=[
            pl.BlockSpec(memory_space=pl.ANY) if n in aliases.values() or n in far_outs else near
            for n in range(len(outs))
        ],
        input_output_aliases=aliases,
        scratch_shapes=list(scratch),
        compiler_params=pltpu.CompilerParams(vmem_limit_bytes=VMEM_LIMIT),
        cost_estimate=pl.CostEstimate(flops=flops, bytes_accessed=1 << 20, transcendentals=0),
        name=name,
    )

    def run(*args):
        return kernel(
            *(pltpu.with_memory_space_constraint(x, pltpu.HBM) if n in far else x for n, x in enumerate(args))
        )

    return run


def lanes(shape):
    return lax.broadcasted_iota(jnp.int32, shape, len(shape) - 1)


def rows(shape):
    return lax.broadcasted_iota(jnp.int32, shape, len(shape) - 2)


def turn(x, shift, axis):
    shift %= x.shape[axis]
    return pltpu.roll(x, shift, axis) if shift else x


def group_order(count):
    half = count // 2
    return [k for n in range(half) for k in (half + n, n)]


def exchange(x):
    order = group_order(x.shape[0])
    return lax.all_to_all(x, "lon", split_axis=0, concat_axis=0, tiled=True, axis_index_groups=[order])


def swap(near, far, axis, wrap):
    count = lax.axis_size(axis)
    pairs = [[], []]
    for i in range(count if wrap else count - 1):
        j = (i + 1) % count
        pairs[i % 2] += [(i, j), (j, i)]
    far = lax.ppermute(far, axis, pairs[1])
    return lax.ppermute(near, axis, pairs[0]), far


def sort_swap(axis, after, before):
    odd = lax.rem(lax.axis_index(axis), 2) == 1
    return jnp.where(odd, before, after), jnp.where(odd, after, before)


def tile_fields(tracers, cotangent, land_mask, diffusion, velocity):
    levels = land_mask.shape[0]
    mask = [land_mask[level].astype(f32) for level in range(levels)]
    out = [tracers[f, level] for f in range(2) for level in range(levels)]
    out += [cotangent[f, level] for f in range(2) for level in range(levels)]
    out += [diffusion[0, level] * mask[level] for level in range(levels)]
    out += [velocity[0, level] * mask[level] for level in range(levels)]
    out += [diffusion[1, level] * mask[level] for level in range(levels)]
    out += [velocity[1, level] * mask[level] for level in range(levels)]
    out += [diffusion[2, level] * mask[level] * mask[level + 1] for level in range(levels - 1)]
    return out


def fetch(pairs, arrived):
    copies = [pltpu.make_async_copy(src, dst, arrived.at[n]) for n, (src, dst) in enumerate(pairs)]
    for copy in copies:
        copy.start()
    return copies


def pack_columns(*refs):
    inputs, (fields, near, far), scratch = refs[:7], refs[7:10], refs[12:]
    copies = fetch(zip(inputs, [*scratch[:5], *refs[10:12]]), scratch[5])
    for copy in copies[:5]:
        copy.wait()
    shape = near.shape[1:]
    lane = lanes(shape)
    west = [jnp.zeros(shape, f32) for _ in range(near.shape[0])]
    east = [jnp.zeros(shape, f32) for _ in range(near.shape[0])]
    for i, field in enumerate(tile_fields(*scratch[:5])):
        fields[i] = field
        part, at = divmod(i, PER_LANES)
        at *= HALO
        here = (lane >= at) & (lane < at + HALO)
        west[part] = jnp.where(here, turn(field[:, :BLOCK], at, 1), west[part])
        east[part] = jnp.where(here, turn(field[:, -BLOCK:], at + HALO, 1), east[part])
    for part in range(near.shape[0]):
        near[part], far[part] = sort_swap("lon", east[part], west[part])
    for copy in copies[5:]:
        copy.wait()


def unpack_columns(from_west, from_east, i):
    part, at = divmod(i, PER_LANES)
    at *= HALO
    lane = lanes(from_west[part].shape)
    east = turn(from_east[part], -at, 1)
    west = turn(from_west[part], -at - HALO, 1)
    return jnp.where(lane < HALO, east, jnp.where(lane >= BLOCK - HALO, west, 0.0))


def row_sources(fields, from_west, from_east):
    out = [(fields, (i, slice(None), slice(h * BLOCK, (h + 1) * BLOCK)))
           for i in range(fields.shape[0]) for h in range(fields.shape[2] // BLOCK)]
    for columns in (from_west, from_east):
        out += [(columns, (part,)) for part in range(columns.shape[0])]
    return out


def pack_rows(fields, near_columns, far_columns, sums, near, far, from_west, from_east, same_sums):
    for part in range(from_west.shape[0]):
        from_east[part], from_west[part] = sort_swap("lon", near_columns[part], far_columns[part])
    sources = [ref[at] for ref, at in row_sources(fields, from_west, from_east)]
    half = near.shape[0]
    row = rows((8, BLOCK))
    for i in range(half):
        first = sources[i]
        second = sources[i + half] if i + half < len(sources) else jnp.zeros_like(first)
        to_north = jnp.where(row < HALO, turn(first[-8:], HALO, 0), second[-8:])
        to_south = jnp.where(row < HALO, first[:8], turn(second[:8], HALO, 0))
        near[i], far[i] = sort_swap("lat", to_north, to_south)


def edge_rows(near, far, i):
    half = near.shape[0]
    from_north, from_south = sort_swap("lat", near[i % half], far[i % half])
    if i < half:
        from_south = turn(from_south, HALO, 0)
    else:
        from_north = turn(from_north, HALO, 0)
    return jnp.where(rows(from_north.shape) < HALO, from_north, from_south)


def widen(fields, from_west, from_east, near, far, start, wide):
    count, tile_lat, tile_lon = fields.shape
    halves = tile_lon // BLOCK
    parts = from_west.shape[0]
    corners = [edge_rows(near, far, count * halves + n) for n in range(2 * parts)]
    for i in range(count):
        out = start.at[i] if i < start.shape[0] else wide.at[i - start.shape[0]]
        out[:tile_lat, :tile_lon] = fields[i]
        out[:tile_lat, tile_lon:] = unpack_columns(from_west, from_east, i)
        for h in range(halves):
            out[tile_lat:, h * BLOCK : (h + 1) * BLOCK] = edge_rows(near, far, i * halves + h)
        out[tile_lat:, tile_lon:] = unpack_columns(corners[:parts], corners[parts:], i)


def eastward(x):
    return turn(x, -1, 1)


def westward(x):
    return turn(x, 1, 1)


def northward(x):
    return turn(x, -1, 0)


def southward(x):
    return turn(x, 1, 0)


def adjoint_step(coeffs, read, write, first, last):
    levels = coeffs.shape[1]
    above = coeffs[4, first - 1] * (read(first) - read(first - 1)) if first else None
    for level in range(first, last):
        lam = read(level)
        step_x = eastward(lam) - lam
        step_y = northward(lam) - lam
        out = lam + coeffs[0, level] * step_x + westward(coeffs[1, level] * step_x)
        out = out + coeffs[2, level] * step_y + southward(coeffs[3, level] * step_y)
        if above is not None:
            out = out - above
        if level < levels - 1:
            above = coeffs[4, level] * (read(level + 1) - lam)
            out = out + above
        write(level, out)


def surface_levels(step, levels):
    return min(levels, STEPS - 1 - step)


def run_adjoint(
    fields, from_west, from_east, far, near, blocks, coeffs, start, states, wide, own, sent
):
    levels = coeffs.shape[1]
    tile_lat, tile_lon = fields.shape[1:]
    halves = tile_lon // BLOCK
    widen(fields, from_west, from_east, near, far, start, wide)
    base = 0
    mask0 = None
    for level in range(levels):
        east_d, east_u = wide[base + level], wide[base + levels + level]
        north_d, north_u = wide[base + 2 * levels + level], wide[base + 3 * levels + level]
        mask = (east_d > 0.0).astype(f32)
        mask0 = mask if mask0 is None else mask0
        mask_e, mask_n = eastward(mask), northward(mask)
        east_k, east_v = east_d * mask_e, east_u * mask_e
        north_k, north_v = north_d * mask_n, north_u * mask_n
        coeffs[0, level] = jnp.maximum(east_v, 0.0) + east_k
        coeffs[1, level] = jnp.minimum(east_v, 0.0) - east_k
        coeffs[2, level] = jnp.maximum(north_v, 0.0) + north_k
        coeffs[3, level] = jnp.minimum(north_v, 0.0) - north_k
        coeffs[4, level] = wide[base + 4 * levels + level] if level < levels - 1 else jnp.zeros_like(mask)
        coeffs[5, level] = mask
    copies = []
    for f in range(2):
        surface = start[(2 + f) * levels, :tile_lat, :tile_lon]
        for step in range(STEPS - 1):

            def read(level):
                return states[f, step - 1, level] if step else start[(2 + f) * levels + level]

            def write(level, lam):
                states[f, step, level] = lam

            adjoint_step(coeffs, read, write, 0, surface_levels(step, levels))
            surface = surface + states[f, step, 0, :tile_lat, :tile_lon]
        surface = surface * mask0[:tile_lat, :tile_lon]
        for h in range(halves):
            at = (f * halves + h) * tile_lat
            own[at : at + tile_lat] = surface[:, h * BLOCK : (h + 1) * BLOCK]
        field = pl.ds(f * halves * tile_lat, halves * tile_lat)
        copies += fetch([(own.at[field], blocks.at[k, field]) for k in range(blocks.shape[0])], sent.at[f])
    for copy in copies:
        copy.wait()


def finish_adjoint(coeffs, start, states, adjoint_out, rest):
    levels = coeffs.shape[1]
    tile_lat, tile_lon = adjoint_out.shape[2:]
    for f in range(2):
        for step in range(STEPS):
            done = surface_levels(step, levels)

            def read(level):
                if not step:
                    return start[(2 + f) * levels + level]
                return (states if level < surface_levels(step - 1, levels) else rest)[f, step - 1, level]

            def write(level, lam):
                if step == STEPS - 1:
                    adjoint_out[f, level] = lam[:tile_lat, :tile_lon]
                else:
                    rest[f, step, level] = lam

            adjoint_step(coeffs, read, write, done, levels)


def sum_forcing(received, forcing, near, far):
    tile_lat = forcing.shape[1]
    halves = forcing.shape[2] // BLOCK - 1
    total = received[0]
    for j in range(1, received.shape[0]):
        total = total + received[j]
    lane = lanes((tile_lat, BLOCK))
    upper = total[2 * halves * tile_lat :]
    lower = jnp.where(lane[: tile_lat // 2] < BLOCK // 2, turn(upper, -2 * HALO, 1), turn(upper, 2 * HALO, 1))
    packed = jnp.concatenate([upper, lower], axis=0)
    for f in range(2):
        for h in range(halves):
            at = (f * halves + h) * tile_lat
            forcing[f, :, h * BLOCK : (h + 1) * BLOCK] = total[at : at + tile_lat]
        used = (lane < HALO) | (lane >= BLOCK - HALO)
        if f == 0:
            edge = packed
        else:
            edge = jnp.where(lane < HALO, turn(packed, -HALO, 1), turn(packed, HALO, 1))
        forcing[f, :, halves * BLOCK :] = jnp.where(used, edge, 0.0)
    row = rows((8, forcing.shape[2]))
    to_north = jnp.where(row < HALO, turn(forcing[0, tile_lat - 8 :], HALO, 0), forcing[1, tile_lat - 8 :])
    to_south = jnp.where(row < HALO, forcing[0, :8], turn(forcing[1, :8], HALO, 0))
    near[0], far[0] = sort_swap("lat", to_north, to_south)


def run_forward(coeffs, start, forcing, near, far, final, state):
    levels = coeffs.shape[1]
    tile_lat, tile_lon = final.shape[2:]
    for f in range(2):
        force = jnp.concatenate([forcing[f], edge_rows(near, far, f)], axis=0)
        force = force * coeffs[5, 0]
        for step in range(STEPS):
            above = None
            for level in range(levels):
                read = (lambda n: start[f * levels + n]) if step == 0 else (lambda n: state[(step - 1) % 2, n])
                theta = read(level)
                east_flux = coeffs[0, level] * theta + coeffs[1, level] * eastward(theta)
                north_flux = coeffs[2, level] * theta + coeffs[3, level] * northward(theta)
                out = theta - (east_flux - westward(east_flux)) - (north_flux - southward(north_flux))
                if level < levels - 1:
                    vertical = coeffs[4, level] * (theta - read(level + 1))
                    out = out - vertical
                if above is not None:
                    out = out + above
                above = vertical if level < levels - 1 else None
                if level == 0:
                    out = out + force
                if step == STEPS - 1:
                    final[f, level] = out[:tile_lat, :tile_lon]
                else:
                    state[step % 2, level] = out


def split(x):
    high = x.astype(bf16)
    return high, (x - high.astype(f32)).astype(bf16)


def weight_copy(weights, held, arrived, n):
    own = pl.ds(n * FETCH, FETCH)
    return pltpu.make_async_copy(weights.at[own], held.at[own], arrived.at[n])


def fetch_weights(weights, held, arrived):
    for n in range(held.shape[0] // FETCH):
        weight_copy(weights, held, arrived, n).start()


def held_part(weights, held, arrived):
    def part(r, g, u):
        if u == 0:

            @pl.when(r == 0)
            def _():
                for n in range(GROUP // FETCH):
                    weight_copy(weights, held, arrived, g * (GROUP // FETCH) + n).wait()

        return split(held[g * GROUP + u])

    return part


def one_hot(where):
    return jnp.where(where, 1.0, 0.0).astype(bf16)


def places(slots, blocks):
    return 8 * (-(-2 * slots // (8 * blocks)) + 1)


def round_chunks(slots, blocks):
    return -(-(slots + 7 * blocks) // BLOCK)


def as_row(ids):
    return jnp.concatenate([ids[k : k + 1, :] for k in range(ids.shape[0])], axis=1)


def rank_slots(block_row, blocks):
    slots = block_row.shape[1]
    mine = rows((blocks, slots)) == block_row
    cuts = range(0, slots, BLOCK)
    stacked = jnp.concatenate([one_hot(mine[:, at : at + BLOCK]) for at in cuts], axis=0)
    shape = (BLOCK, 2 * BLOCK)
    counts = jnp.dot(stacked, one_hot(rows(shape) < lanes(shape)), preferred_element_type=f32)
    before, out = jnp.zeros((blocks, BLOCK), f32), []
    for n, at in enumerate(cuts):
        run = counts[n * blocks : (n + 1) * blocks]
        here = jnp.where(mine[:, at : at + BLOCK], run[:, :BLOCK] + before, 0.0)
        out.append(jnp.sum(here, axis=0, keepdims=True))
        before = before + run[:, BLOCK:]
    return jnp.concatenate(out, axis=1), before


def find_slots(r, keys, counts, capacity, columns, lines, starts):
    slots = keys.shape[1]
    blocks = counts.shape[0]
    atm_row, ocean_row, block_row, rank = (keys[n : n + 1] for n in range(4))
    count = jnp.clip(counts - r * capacity, 0.0, capacity)
    tiles = jnp.floor((count + 7.0) * 0.125) * 8.0
    shape = (blocks, blocks)
    first = jnp.dot(one_hot(lanes(shape) < rows(shape)), tiles.astype(bf16), preferred_element_type=f32)
    starts[...] = first.astype(jnp.int32)
    mine = rows((blocks, slots)).astype(f32) == block_row
    own = jnp.where(mine, jnp.concatenate([first] * (slots // BLOCK), axis=1), 0.0)
    place = rank - r * capacity
    here = (place >= 0.0) & (place < capacity)
    place = jnp.where(here, jnp.sum(own, axis=0, keepdims=True) + place, -1.0)
    run = jnp.floor(place * (1.0 / BLOCK))
    low = one_hot(rows((BLOCK, slots)).astype(f32) == place - run * BLOCK)
    size = lines.shape[1]
    in_run = rows((size, slots)).astype(f32) == run
    ocean_high = jnp.floor(ocean_row * (1.0 / BLOCK))
    digits = [atm_row, ocean_high, ocean_row - ocean_high * BLOCK]
    digits = [jnp.where(in_run, digit, 0.0).astype(bf16) for digit in digits]
    across = (((1,), (1,)), ((), ()))
    down = [lax.dot_general(low, digit, across, preferred_element_type=f32) for digit in digits]
    along = [lax.dot_general(digit, low, across, preferred_element_type=f32) for digit in digits]
    columns[0, :, :size], columns[1, :, :size] = down[0], down[1] * BLOCK + down[2] - 1.0
    ocean = along[1] * BLOCK + along[2] - 1.0
    lines[0], lines[1] = jnp.where(ocean < 0.0, -1.0, along[0]), ocean


def couple(part, table, capacity, rounds, prepare, columns, lines, starts, transposed, result, scratch):
    vectors, products, starts_near = scratch
    blocks = starts.shape[0]
    total_rows = vectors.shape[0] - capacity
    width = table.shape[0]
    result[...] = jnp.zeros_like(result)
    products[...] = jnp.zeros_like(products)

    def one_round(r, carry):
        prepare(r)
        first_rows = starts[...]
        for w in range(blocks):
            starts_near[w] = first_rows[w, 0]
        place_hot = []
        for n in range(total_rows // BLOCK):
            gather = jnp.broadcast_to(columns[int(transposed), :, n : n + 1], (BLOCK, BLOCK))
            gather = jnp.concatenate([gather] * (width // BLOCK), axis=1)
            hot = one_hot(gather == lanes((BLOCK, width)).astype(f32))
            vectors[n * BLOCK : (n + 1) * BLOCK] = jnp.dot(hot, table, preferred_element_type=f32)
            put = lines[1 - int(transposed), n : n + 1]
            place_hot.append(one_hot(rows((result.shape[0], BLOCK)).astype(f32) == put))

        def group(g, carry):
            for u in range(GROUP):
                at = pl.ds(pl.multiple_of(starts_near[g * GROUP + u], 8), capacity)
                own = vectors[at]
                left = jnp.concatenate([own[:, n * BLOCK : (n + 1) * BLOCK] for n in range(4)], axis=0)
                high, low = part(r, g, u)
                right = jnp.concatenate([high, low], axis=1 if transposed else 0)
                contract = (((1,), (0 if transposed else 1,)), ((), ()))
                product = lax.dot_general(left.astype(bf16), right, contract, preferred_element_type=f32)
                for f in range(2):
                    high_part = product[f * capacity : (f + 1) * capacity]
                    low_part = product[(f + 2) * capacity : (f + 3) * capacity, :BLOCK]
                    products[at, f * BLOCK : (f + 1) * BLOCK] = (
                        high_part[:, BLOCK:] + low_part
                    ) + high_part[:, :BLOCK]
            return carry

        lax.fori_loop(0, blocks // GROUP, group, 0)
        summed = jnp.dot(
            jnp.concatenate(place_hot, axis=1),
            jnp.concatenate(split(products[:total_rows]), axis=1),
            preferred_element_type=f32,
        )
        result[...] += summed[:, : 2 * BLOCK] + summed[:, 2 * BLOCK :]
        return carry

    lax.fori_loop(0, rounds, one_round, 0)


def slot_keys(ids, tile_lat, keys):
    lon_count, cap = ids.shape[3:]
    ocean, atm_ids, block_ids = (ids[n, 0, 0] for n in range(3))
    order = (ocean & 1) * tile_lat + (ocean >> 1) + rows((lon_count, cap)) * (2 * tile_lat)
    order = jnp.where(ocean >= 0, order, lon_count * 2 * tile_lat) + 1
    for n, part in enumerate((atm_ids, order, block_ids)):
        keys[n : n + 1] = as_row(part.astype(f32))


def weigh(
    atm_near, margins, weights, after, sums, keys, counts, columns, lines, starts, result, *scratch
):
    scratch, (held, arrived) = scratch[:3], scratch[3:]
    fetch_weights(weights, held, arrived)
    lon_count = margins.shape[3]
    blocks = weights.shape[0]
    tile_lat = 2 * sums.shape[1] // 9
    slot_keys(margins, tile_lat, keys)
    rank, count = rank_slots(keys[2:3].astype(jnp.int32), blocks)
    keys[3:4] = rank
    counts[...] = count
    capacity = places(keys.shape[1], blocks)
    rounds = jnp.max(rank).astype(jnp.int32) // capacity + 1
    parts = [split(atm_near[f, 0]) for f in range(2)]
    table = jnp.concatenate([parts[f][n] for n in range(2) for f in range(2)], axis=1)
    part = held_part(weights, held, arrived)

    def prepare(r):
        find_slots((rounds - 1 - r).astype(f32), keys, counts[...], capacity, columns, lines, starts)

    couple(part, table, capacity, rounds, prepare, columns, lines, starts, False, result, scratch)
    lane = lanes((tile_lat, BLOCK))

    def block_sums(k, f, h):
        at = (2 * k + h) * tile_lat
        return result[at : at + tile_lat, f * BLOCK : (f + 1) * BLOCK]

    for n, k in enumerate(group_order(lon_count)):
        edge = jnp.zeros((tile_lat, BLOCK), f32)
        for f in range(2):
            for h in range(2):
                sums[n, (2 * f + h) * tile_lat : (2 * f + h + 1) * tile_lat] = block_sums(k, f, h)
            at = f * HALO
            after = turn(block_sums((k + 1) % lon_count, f, 0), at, 1)
            before = turn(block_sums((k - 1) % lon_count, f, 1), -at, 1)
            edge = jnp.where((lane >= at) & (lane < at + HALO), after, edge)
            end = BLOCK - at
            edge = jnp.where((lane >= end - HALO) & (lane < end), before, edge)
        upper, lower = edge[: tile_lat // 2], edge[tile_lat // 2 :]
        near = lane[: tile_lat // 2]
        lower = jnp.where(near < BLOCK // 2, turn(lower, 2 * HALO, 1), turn(lower, -2 * HALO, 1))
        sums[n, 4 * tile_lat :] = jnp.where((near < 2 * HALO) | (near >= BLOCK - 2 * HALO), upper, lower)


def unweigh(
    gathered, keys, counts, columns_in, lines_in, starts_in, weights, gradient, result, columns, lines, starts, *scratch
):
    scratch, (held, arrived) = scratch[:3], scratch[3:]
    fetch_weights(weights, held, arrived)
    blocks = weights.shape[0]
    lon_count, ocean_blocks = gathered.shape[0], gathered.shape[1] // 2
    order = group_order(lon_count)
    capacity = places(keys.shape[1], blocks)
    rounds = jnp.max(keys[3:4]).astype(jnp.int32) // capacity + 1
    parts = [
        split(
            jnp.concatenate(
                [gathered[order.index(k), f * ocean_blocks : (f + 1) * ocean_blocks] for k in range(lon_count)],
                axis=0,
            )
        )
        for f in range(2)
    ]
    table = jnp.concatenate([parts[f][n] for n in range(2) for f in range(2)], axis=1)

    def prepare(r):
        @pl.when(r == 0)
        def _():
            columns[...] = columns_in[...]
            lines[...] = lines_in[...]
            starts[...] = starts_in[...]

        @pl.when(r > 0)
        def _():
            find_slots(r.astype(f32), keys, counts[...], capacity, columns, lines, starts)

    part = held_part(weights, held, arrived)
    couple(part, table, capacity, rounds, prepare, columns, lines, starts, True, result, scratch)
    for f in range(2):
        gradient[f, 0] = result[:, f * BLOCK : (f + 1) * BLOCK]


def on_device(tracers, cotangent, land_mask, diffusion, velocity, weights, atm_state, margins):
    levels, tile_lat, tile_lon = land_mask.shape
    lon_count = lax.axis_size("lon")
    slots = lon_count * margins.shape[4]
    halves = tile_lon // BLOCK
    count = 9 * levels - 1
    parts = -(-count // PER_LANES)
    inputs = (tracers, cotangent, land_mask, diffusion, velocity)

    def in_vmem(s):
        return pltpu.VMEM(s.shape, s.dtype)

    message = (parts, tile_lat, BLOCK)
    fields, near, far, atm_near, margins_near = call(
        pack_columns,
        [
            (count, tile_lat, tile_lon),
            message,
            message,
            atm_state.shape,
            jax.ShapeDtypeStruct(margins.shape, margins.dtype),
        ],
        [*map(in_vmem, inputs), pltpu.SemaphoreType.DMA((7,))],
        name="pack_columns",
        inputs=7,
        far=range(7),
    )(*inputs, atm_state, margins)
    near_columns, far_columns = swap(near, far, "lon", True)

    blocks_of, atm = weights.shape[0], atm_state.shape[2]
    sum_rows = 2 * halves * tile_lat + tile_lat // 2
    ocean_blocks = lon_count * halves * tile_lat
    chunks = round_chunks(slots, blocks_of)
    held_rows = chunks * BLOCK + places(slots, blocks_of)

    def coupling_scratch(result_rows):
        return [
            pltpu.VMEM((result_rows, 2 * BLOCK), f32),
            pltpu.VMEM((held_rows, 4 * BLOCK), f32),
            pltpu.VMEM((held_rows, 2 * BLOCK), f32),
            pltpu.SMEM((blocks_of,), jnp.int32),
            pltpu.VMEM(weights.shape, f32),
            pltpu.SemaphoreType.DMA((blocks_of // FETCH,)),
        ]

    coupling_flops = 4 * slots * blocks_of * 2 * BLOCK * BLOCK * 2
    found = [
        jax.ShapeDtypeStruct((2, BLOCK, BLOCK), f32),
        jax.ShapeDtypeStruct((2, -(-chunks // 8) * 8, BLOCK), f32),
        jax.ShapeDtypeStruct((blocks_of, BLOCK), jnp.int32),
    ]
    sums, *slot_data = call(
        weigh,
        [(lon_count, sum_rows, BLOCK), (8, slots), (blocks_of, BLOCK), *found],
        coupling_scratch(ocean_blocks),
        coupling_flops,
        name="weigh",
        inputs=4,
        far=(2,),
    )(atm_near, margins_near, weights, far)

    sources = count * halves + 2 * parts
    message = (-(-sources // 2), 8, BLOCK)
    columns = (parts, tile_lat, BLOCK)
    near, far, from_west, from_east, sums = call(
        pack_rows,
        [message, message, columns, columns, sums.shape],
        name="pack_rows",
        inputs=4,
        aliases={3: 4},
    )(fields, near_columns, far_columns, sums)
    received = exchange(sums)
    near_rows, far_rows = swap(near, far, "lat", False)

    wide = (tile_lat + 8, tile_lon + BLOCK)
    own = (2 * halves * tile_lat, BLOCK)
    adjoint_states = (2, STEPS - 1, levels, *wide)
    blocks, coeffs, start, states = call(
        run_adjoint,
        [(lon_count, *own), (6, levels, *wide), (4 * levels, *wide), adjoint_states],
        [
            pltpu.VMEM((count - 4 * levels, *wide), f32),
            pltpu.VMEM(own, f32),
            pltpu.SemaphoreType.DMA((2, lon_count)),
        ],
        name="run_adjoint",
        inputs=5,
        far_outs=(0,),
    )(fields, from_west, from_east, far_rows, near_rows)
    gathered = exchange(blocks)

    message = (1, 8, tile_lon + BLOCK)
    forcing, near, far = call(
        sum_forcing, [(2, tile_lat, tile_lon + BLOCK), message, message], name="sum_forcing", inputs=1
    )(received)
    near_rows, far_rows = swap(near, far, "lat", False)
    (adjoint,) = call(
        finish_adjoint,
        [cotangent.shape],
        [pltpu.VMEM(adjoint_states, f32)],
        name="finish_adjoint",
        inputs=3,
    )(coeffs, start, states)
    (final,) = call(
        run_forward,
        [tracers.shape],
        [pltpu.VMEM((2, levels, *wide), f32)],
        name="run_forward",
        inputs=5,
    )(coeffs, start, forcing, near_rows, far_rows)

    (gradient,) = call(
        unweigh,
        [atm_state.shape],
        [coupling_scratch(atm)[0], *map(in_vmem, found), *coupling_scratch(atm)[1:]],
        coupling_flops,
        name="unweigh",
        inputs=7,
        far=(6,),
    )(gathered, *slot_data, weights)
    return (final, adjoint, gradient)


def solution(mesh):
    return jax.shard_map(
        on_device,
        mesh=mesh,
        in_specs=(
            P(None, None, "lat", "lon"),
            P(None, None, "lat", "lon"),
            P(None, "lat", "lon"),
            P(None, None, "lat", "lon"),
            P(None, None, "lat", "lon"),
            P(),
            P(None, "lat", "lon", None),
            P(None, "lat", "lon", None, None),
        ),
        out_specs=(
            P(None, None, "lat", "lon"),
            P(None, None, "lat", "lon"),
            P(None, "lat", "lon", None),
        ),
        check_vma=False,
    )
```

```python
import jax
import jax.numpy as jnp
from jax import lax
from jax.experimental import pallas as pl
from jax.experimental.pallas import tpu as pltpu
from jax.sharding import PartitionSpec as P

BLOCK = 128
STEPS = 4
HALO = STEPS
PER_LANES = BLOCK // HALO
GROUP = 16
FETCH = 4
f32 = jnp.float32
bf16 = jnp.bfloat16
VMEM_LIMIT = 20 * 1024 * 1024


def call(body, outs, scratch=(), flops=0, name=None, inputs=0, far=(), far_outs=(), aliases=None):
    outs = [s if isinstance(s, jax.ShapeDtypeStruct) else jax.ShapeDtypeStruct(s, f32) for s in outs]
    near = pl.BlockSpec(memory_space=pltpu.VMEM)
    aliases = aliases or {}
    kernel = pl.pallas_call(
        body,
        out_shape=outs,
        in_specs=[
            pl.BlockSpec(memory_space=pl.ANY)
            if n in aliases
            else pl.BlockSpec(memory_space=pltpu.HBM)
            if n in far
            else near
            for n in range(inputs)
        ],
        out_specs=[
            pl.BlockSpec(memory_space=pl.ANY) if n in aliases.values() or n in far_outs else near
            for n in range(len(outs))
        ],
        input_output_aliases=aliases,
        scratch_shapes=list(scratch),
        compiler_params=pltpu.CompilerParams(vmem_limit_bytes=VMEM_LIMIT),
        cost_estimate=pl.CostEstimate(flops=flops, bytes_accessed=1 << 20, transcendentals=0),
        name=name,
    )

    def run(*args):
        return kernel(
            *(pltpu.with_memory_space_constraint(x, pltpu.HBM) if n in far else x for n, x in enumerate(args))
        )

    return run


def lanes(shape):
    return lax.broadcasted_iota(jnp.int32, shape, len(shape) - 1)


def rows(shape):
    return lax.broadcasted_iota(jnp.int32, shape, len(shape) - 2)


def turn(x, shift, axis):
    shift %= x.shape[axis]
    return pltpu.roll(x, shift, axis) if shift else x


def group_order(count):
    half = count // 2
    return [k for n in range(half) for k in (half + n, n)]


def exchange(x):
    order = group_order(x.shape[0])
    return lax.all_to_all(x, "lon", split_axis=0, concat_axis=0, tiled=True, axis_index_groups=[order])


def swap(near, far, axis, wrap):
    count = lax.axis_size(axis)
    pairs = [[], []]
    for i in range(count if wrap else count - 1):
        j = (i + 1) % count
        pairs[i % 2] += [(i, j), (j, i)]
    far = lax.ppermute(far, axis, pairs[1])
    return lax.ppermute(near, axis, pairs[0]), far


def sort_swap(axis, after, before):
    odd = lax.rem(lax.axis_index(axis), 2) == 1
    return jnp.where(odd, before, after), jnp.where(odd, after, before)


def tile_fields(tracers, cotangent, land_mask, diffusion, velocity):
    levels = land_mask.shape[0]
    mask = [land_mask[level].astype(f32) for level in range(levels)]
    out = [tracers[f, level] for f in range(2) for level in range(levels)]
    out += [cotangent[f, level] for f in range(2) for level in range(levels)]
    out += [diffusion[0, level] * mask[level] for level in range(levels)]
    out += [velocity[0, level] * mask[level] for level in range(levels)]
    out += [diffusion[1, level] * mask[level] for level in range(levels)]
    out += [velocity[1, level] * mask[level] for level in range(levels)]
    out += [diffusion[2, level] * mask[level] * mask[level + 1] for level in range(levels - 1)]
    return out


def fetch(pairs, arrived):
    copies = [pltpu.make_async_copy(src, dst, arrived.at[n]) for n, (src, dst) in enumerate(pairs)]
    for copy in copies:
        copy.start()
    return copies


def pack_columns(*refs):
    inputs, (fields, near, far), scratch = refs[:7], refs[7:10], refs[12:]
    copies = fetch(zip(inputs, [*scratch[:5], *refs[10:12]]), scratch[5])
    for copy in copies[:5]:
        copy.wait()
    shape = near.shape[1:]
    lane = lanes(shape)
    west = [jnp.zeros(shape, f32) for _ in range(near.shape[0])]
    east = [jnp.zeros(shape, f32) for _ in range(near.shape[0])]
    for i, field in enumerate(tile_fields(*scratch[:5])):
        fields[i] = field
        part, at = divmod(i, PER_LANES)
        at *= HALO
        here = (lane >= at) & (lane < at + HALO)
        west[part] = jnp.where(here, turn(field[:, :BLOCK], at, 1), west[part])
        east[part] = jnp.where(here, turn(field[:, -BLOCK:], at + HALO, 1), east[part])
    for part in range(near.shape[0]):
        near[part], far[part] = sort_swap("lon", east[part], west[part])
    for copy in copies[5:]:
        copy.wait()


def unpack_columns(from_west, from_east, i):
    part, at = divmod(i, PER_LANES)
    at *= HALO
    lane = lanes(from_west[part].shape)
    east = turn(from_east[part], -at, 1)
    west = turn(from_west[part], -at - HALO, 1)
    return jnp.where(lane < HALO, east, jnp.where(lane >= BLOCK - HALO, west, 0.0))


def row_sources(fields, from_west, from_east):
    out = [(fields, (i, slice(None), slice(h * BLOCK, (h + 1) * BLOCK)))
           for i in range(fields.shape[0]) for h in range(fields.shape[2] // BLOCK)]
    for columns in (from_west, from_east):
        out += [(columns, (part,)) for part in range(columns.shape[0])]
    return out


def pack_rows(fields, near_columns, far_columns, sums, near, far, from_west, from_east, same_sums):
    for part in range(from_west.shape[0]):
        from_east[part], from_west[part] = sort_swap("lon", near_columns[part], far_columns[part])
    sources = [ref[at] for ref, at in row_sources(fields, from_west, from_east)]
    half = near.shape[0]
    row = rows((8, BLOCK))
    for i in range(half):
        first = sources[i]
        second = sources[i + half] if i + half < len(sources) else jnp.zeros_like(first)
        to_north = jnp.where(row < HALO, turn(first[-8:], HALO, 0), second[-8:])
        to_south = jnp.where(row < HALO, first[:8], turn(second[:8], HALO, 0))
        near[i], far[i] = sort_swap("lat", to_north, to_south)


def edge_rows(near, far, i):
    half = near.shape[0]
    from_north, from_south = sort_swap("lat", near[i % half], far[i % half])
    if i < half:
        from_south = turn(from_south, HALO, 0)
    else:
        from_north = turn(from_north, HALO, 0)
    return jnp.where(rows(from_north.shape) < HALO, from_north, from_south)


def widen(fields, from_west, from_east, near, far, start, wide):
    count, tile_lat, tile_lon = fields.shape
    halves = tile_lon // BLOCK
    parts = from_west.shape[0]
    corners = [edge_rows(near, far, count * halves + n) for n in range(2 * parts)]
    for i in range(count):
        out = start.at[i] if i < start.shape[0] else wide.at[i - start.shape[0]]
        out[:tile_lat, :tile_lon] = fields[i]
        out[:tile_lat, tile_lon:] = unpack_columns(from_west, from_east, i)
        for h in range(halves):
            out[tile_lat:, h * BLOCK : (h + 1) * BLOCK] = edge_rows(near, far, i * halves + h)
        out[tile_lat:, tile_lon:] = unpack_columns(corners[:parts], corners[parts:], i)


def eastward(x):
    return turn(x, -1, 1)


def westward(x):
    return turn(x, 1, 1)


def northward(x):
    return turn(x, -1, 0)


def southward(x):
    return turn(x, 1, 0)


def adjoint_step(coeffs, read, write, first, last):
    levels = coeffs.shape[1]
    above = coeffs[4, first - 1] * (read(first) - read(first - 1)) if first else None
    for level in range(first, last):
        lam = read(level)
        step_x = eastward(lam) - lam
        step_y = northward(lam) - lam
        out = lam + coeffs[0, level] * step_x + westward(coeffs[1, level] * step_x)
        out = out + coeffs[2, level] * step_y + southward(coeffs[3, level] * step_y)
        if above is not None:
            out = out - above
        if level < levels - 1:
            above = coeffs[4, level] * (read(level + 1) - lam)
            out = out + above
        write(level, out)


def surface_levels(step, levels):
    return min(levels, STEPS - 1 - step)


def run_adjoint(
    fields, from_west, from_east, far, near, blocks, coeffs, start, states, wide, own, sent
):
    levels = coeffs.shape[1]
    tile_lat, tile_lon = fields.shape[1:]
    halves = tile_lon // BLOCK
    widen(fields, from_west, from_east, near, far, start, wide)
    base = 0
    mask0 = None
    for level in range(levels):
        east_d, east_u = wide[base + level], wide[base + levels + level]
        north_d, north_u = wide[base + 2 * levels + level], wide[base + 3 * levels + level]
        mask = (east_d > 0.0).astype(f32)
        mask0 = mask if mask0 is None else mask0
        mask_e, mask_n = eastward(mask), northward(mask)
        east_k, east_v = east_d * mask_e, east_u * mask_e
        north_k, north_v = north_d * mask_n, north_u * mask_n
        coeffs[0, level] = jnp.maximum(east_v, 0.0) + east_k
        coeffs[1, level] = jnp.minimum(east_v, 0.0) - east_k
        coeffs[2, level] = jnp.maximum(north_v, 0.0) + north_k
        coeffs[3, level] = jnp.minimum(north_v, 0.0) - north_k
        coeffs[4, level] = wide[base + 4 * levels + level] if level < levels - 1 else jnp.zeros_like(mask)
        coeffs[5, level] = mask
    copies = []
    for f in range(2):
        surface = start[(2 + f) * levels, :tile_lat, :tile_lon]
        for step in range(STEPS - 1):

            def read(level):
                return states[f, step - 1, level] if step else start[(2 + f) * levels + level]

            def write(level, lam):
                states[f, step, level] = lam

            adjoint_step(coeffs, read, write, 0, surface_levels(step, levels))
            surface = surface + states[f, step, 0, :tile_lat, :tile_lon]
        surface = surface * mask0[:tile_lat, :tile_lon]
        for h in range(halves):
            at = (f * halves + h) * tile_lat
            own[at : at + tile_lat] = surface[:, h * BLOCK : (h + 1) * BLOCK]
        field = pl.ds(f * halves * tile_lat, halves * tile_lat)
        copies += fetch([(own.at[field], blocks.at[k, field]) for k in range(blocks.shape[0])], sent.at[f])
    for copy in copies:
        copy.wait()


def finish_adjoint(coeffs, start, states, adjoint_out, rest):
    levels = coeffs.shape[1]
    tile_lat, tile_lon = adjoint_out.shape[2:]
    for f in range(2):
        for step in range(STEPS):
            done = surface_levels(step, levels)

            def read(level):
                if not step:
                    return start[(2 + f) * levels + level]
                return (states if level < surface_levels(step - 1, levels) else rest)[f, step - 1, level]

            def write(level, lam):
                if step == STEPS - 1:
                    adjoint_out[f, level] = lam[:tile_lat, :tile_lon]
                else:
                    rest[f, step, level] = lam

            adjoint_step(coeffs, read, write, done, levels)


def sum_forcing(received, forcing, near, far):
    tile_lat = forcing.shape[1]
    halves = forcing.shape[2] // BLOCK - 1
    total = received[0]
    for j in range(1, received.shape[0]):
        total = total + received[j]
    lane = lanes((tile_lat, BLOCK))
    upper = total[2 * halves * tile_lat :]
    lower = jnp.where(lane[: tile_lat // 2] < BLOCK // 2, turn(upper, -2 * HALO, 1), turn(upper, 2 * HALO, 1))
    packed = jnp.concatenate([upper, lower], axis=0)
    for f in range(2):
        for h in range(halves):
            at = (f * halves + h) * tile_lat
            forcing[f, :, h * BLOCK : (h + 1) * BLOCK] = total[at : at + tile_lat]
        used = (lane < HALO) | (lane >= BLOCK - HALO)
        if f == 0:
            edge = packed
        else:
            edge = jnp.where(lane < HALO, turn(packed, -HALO, 1), turn(packed, HALO, 1))
        forcing[f, :, halves * BLOCK :] = jnp.where(used, edge, 0.0)
    row = rows((8, forcing.shape[2]))
    to_north = jnp.where(row < HALO, turn(forcing[0, tile_lat - 8 :], HALO, 0), forcing[1, tile_lat - 8 :])
    to_south = jnp.where(row < HALO, forcing[0, :8], turn(forcing[1, :8], HALO, 0))
    near[0], far[0] = sort_swap("lat", to_north, to_south)


def run_forward(coeffs, start, forcing, near, far, weights, final, weights_near, state, arrived):
    bring = pltpu.make_async_copy(weights.at[: weights_near.shape[0]], weights_near, arrived)
    bring.start()
    levels = coeffs.shape[1]
    tile_lat, tile_lon = final.shape[2:]
    for f in range(2):
        force = jnp.concatenate([forcing[f], edge_rows(near, far, f)], axis=0)
        force = force * coeffs[5, 0]
        for step in range(STEPS):
            above = None
            for level in range(levels):
                read = (lambda n: start[f * levels + n]) if step == 0 else (lambda n: state[(step - 1) % 2, n])
                theta = read(level)
                east_flux = coeffs[0, level] * theta + coeffs[1, level] * eastward(theta)
                north_flux = coeffs[2, level] * theta + coeffs[3, level] * northward(theta)
                out = theta - (east_flux - westward(east_flux)) - (north_flux - southward(north_flux))
                if level < levels - 1:
                    vertical = coeffs[4, level] * (theta - read(level + 1))
                    out = out - vertical
                if above is not None:
                    out = out + above
                above = vertical if level < levels - 1 else None
                if level == 0:
                    out = out + force
                if step == STEPS - 1:
                    final[f, level] = out[:tile_lat, :tile_lon]
                else:
                    state[step % 2, level] = out
    bring.wait()


def split(x):
    high = x.astype(bf16)
    return high, (x - high.astype(f32)).astype(bf16)


def weight_copy(weights, held, arrived, n):
    own = pl.ds(n * FETCH, FETCH)
    return pltpu.make_async_copy(weights.at[own], held.at[own], arrived.at[n])


def fetch_weights(weights, held, arrived, near=None):
    for n in range(held.shape[0] // FETCH):
        source = near if near is not None and (n + 1) * FETCH <= near.shape[0] else weights
        weight_copy(source, held, arrived, n).start()


def held_part(weights, held, arrived):
    def part(r, g, u):
        if u == 0:

            @pl.when(r == 0)
            def _():
                for n in range(GROUP // FETCH):
                    weight_copy(weights, held, arrived, g * (GROUP // FETCH) + n).wait()

        return split(held[g * GROUP + u])

    return part


def one_hot(where):
    return jnp.where(where, 1.0, 0.0).astype(bf16)


def places(slots, blocks):
    return 8 * (-(-2 * slots // (8 * blocks)) + 1)


def round_chunks(slots, blocks):
    return -(-(slots + 7 * blocks) // BLOCK)


def as_row(ids):
    return jnp.concatenate([ids[k : k + 1, :] for k in range(ids.shape[0])], axis=1)


def rank_slots(block_row, blocks):
    slots = block_row.shape[1]
    mine = rows((blocks, slots)) == block_row
    cuts = range(0, slots, BLOCK)
    stacked = jnp.concatenate([one_hot(mine[:, at : at + BLOCK]) for at in cuts], axis=0)
    shape = (BLOCK, 2 * BLOCK)
    counts = jnp.dot(stacked, one_hot(rows(shape) < lanes(shape)), preferred_element_type=f32)
    before, out = jnp.zeros((blocks, BLOCK), f32), []
    for n, at in enumerate(cuts):
        run = counts[n * blocks : (n + 1) * blocks]
        here = jnp.where(mine[:, at : at + BLOCK], run[:, :BLOCK] + before, 0.0)
        out.append(jnp.sum(here, axis=0, keepdims=True))
        before = before + run[:, BLOCK:]
    return jnp.concatenate(out, axis=1), before


def find_slots(r, keys, counts, capacity, columns, lines, starts):
    slots = keys.shape[1]
    blocks = counts.shape[0]
    atm_row, ocean_row, block_row, rank = (keys[n : n + 1] for n in range(4))
    count = jnp.clip(counts - r * capacity, 0.0, capacity)
    tiles = jnp.floor((count + 7.0) * 0.125) * 8.0
    shape = (blocks, blocks)
    first = jnp.dot(one_hot(lanes(shape) < rows(shape)), tiles.astype(bf16), preferred_element_type=f32)
    starts[...] = first.astype(jnp.int32)
    mine = rows((blocks, slots)).astype(f32) == block_row
    own = jnp.where(mine, jnp.concatenate([first] * (slots // BLOCK), axis=1), 0.0)
    place = rank - r * capacity
    here = (place >= 0.0) & (place < capacity)
    place = jnp.where(here, jnp.sum(own, axis=0, keepdims=True) + place, -1.0)
    run = jnp.floor(place * (1.0 / BLOCK))
    low = one_hot(rows((BLOCK, slots)).astype(f32) == place - run * BLOCK)
    size = lines.shape[1]
    in_run = rows((size, slots)).astype(f32) == run
    ocean_high = jnp.floor(ocean_row * (1.0 / BLOCK))
    digits = [atm_row, ocean_high, ocean_row - ocean_high * BLOCK]
    digits = [jnp.where(in_run, digit, 0.0).astype(bf16) for digit in digits]
    across = (((1,), (1,)), ((), ()))
    down = [lax.dot_general(low, digit, across, preferred_element_type=f32) for digit in digits]
    along = [lax.dot_general(digit, low, across, preferred_element_type=f32) for digit in digits]
    columns[0, :, :size], columns[1, :, :size] = down[0], down[1] * BLOCK + down[2] - 1.0
    ocean = along[1] * BLOCK + along[2] - 1.0
    lines[0], lines[1] = jnp.where(ocean < 0.0, -1.0, along[0]), ocean


def couple(part, table, capacity, rounds, prepare, columns, lines, starts, transposed, result, scratch):
    vectors, products, starts_near = scratch
    blocks = starts.shape[0]
    total_rows = vectors.shape[0] - capacity
    width = table.shape[0]
    result[...] = jnp.zeros_like(result)
    products[...] = jnp.zeros_like(products)

    def one_round(r, carry):
        prepare(r)
        first_rows = starts[...]
        for w in range(blocks):
            starts_near[w] = first_rows[w, 0]
        place_hot = []
        for n in range(total_rows // BLOCK):
            gather = jnp.broadcast_to(columns[int(transposed), :, n : n + 1], (BLOCK, BLOCK))
            gather = jnp.concatenate([gather] * (width // BLOCK), axis=1)
            hot = one_hot(gather == lanes((BLOCK, width)).astype(f32))
            vectors[n * BLOCK : (n + 1) * BLOCK] = jnp.dot(hot, table, preferred_element_type=f32)
            put = lines[1 - int(transposed), n : n + 1]
            place_hot.append(one_hot(rows((result.shape[0], BLOCK)).astype(f32) == put))

        def group(g, carry):
            for u in range(GROUP):
                at = pl.ds(pl.multiple_of(starts_near[g * GROUP + u], 8), capacity)
                own = vectors[at]
                left = jnp.concatenate([own[:, n * BLOCK : (n + 1) * BLOCK] for n in range(4)], axis=0)
                high, low = part(r, g, u)
                right = jnp.concatenate([high, low], axis=1 if transposed else 0)
                contract = (((1,), (0 if transposed else 1,)), ((), ()))
                product = lax.dot_general(left.astype(bf16), right, contract, preferred_element_type=f32)
                for f in range(2):
                    high_part = product[f * capacity : (f + 1) * capacity]
                    low_part = product[(f + 2) * capacity : (f + 3) * capacity, :BLOCK]
                    products[at, f * BLOCK : (f + 1) * BLOCK] = (
                        high_part[:, BLOCK:] + low_part
                    ) + high_part[:, :BLOCK]
            return carry

        lax.fori_loop(0, blocks // GROUP, group, 0)
        summed = jnp.dot(
            jnp.concatenate(place_hot, axis=1),
            jnp.concatenate(split(products[:total_rows]), axis=1),
            preferred_element_type=f32,
        )
        result[...] += summed[:, : 2 * BLOCK] + summed[:, 2 * BLOCK :]
        return carry

    lax.fori_loop(0, rounds, one_round, 0)


def slot_keys(ids, tile_lat, keys):
    lon_count, cap = ids.shape[3:]
    ocean, atm_ids, block_ids = (ids[n, 0, 0] for n in range(3))
    order = (ocean & 1) * tile_lat + (ocean >> 1) + rows((lon_count, cap)) * (2 * tile_lat)
    order = jnp.where(ocean >= 0, order, lon_count * 2 * tile_lat) + 1
    for n, part in enumerate((atm_ids, order, block_ids)):
        keys[n : n + 1] = as_row(part.astype(f32))


def weigh(
    atm_near, margins, weights, after, sums, keys, counts, columns, lines, starts, result, *scratch
):
    scratch, (held, arrived) = scratch[:3], scratch[3:]
    fetch_weights(weights, held, arrived)
    lon_count = margins.shape[3]
    blocks = weights.shape[0]
    tile_lat = 2 * sums.shape[1] // 9
    slot_keys(margins, tile_lat, keys)
    rank, count = rank_slots(keys[2:3].astype(jnp.int32), blocks)
    keys[3:4] = rank
    counts[...] = count
    capacity = places(keys.shape[1], blocks)
    rounds = jnp.max(rank).astype(jnp.int32) // capacity + 1
    parts = [split(atm_near[f, 0]) for f in range(2)]
    table = jnp.concatenate([parts[f][n] for n in range(2) for f in range(2)], axis=1)
    part = held_part(weights, held, arrived)

    def prepare(r):
        find_slots((rounds - 1 - r).astype(f32), keys, counts[...], capacity, columns, lines, starts)

    couple(part, table, capacity, rounds, prepare, columns, lines, starts, False, result, scratch)
    lane = lanes((tile_lat, BLOCK))

    def block_sums(k, f, h):
        at = (2 * k + h) * tile_lat
        return result[at : at + tile_lat, f * BLOCK : (f + 1) * BLOCK]

    for n, k in enumerate(group_order(lon_count)):
        edge = jnp.zeros((tile_lat, BLOCK), f32)
        for f in range(2):
            for h in range(2):
                sums[n, (2 * f + h) * tile_lat : (2 * f + h + 1) * tile_lat] = block_sums(k, f, h)
            at = f * HALO
            after = turn(block_sums((k + 1) % lon_count, f, 0), at, 1)
            before = turn(block_sums((k - 1) % lon_count, f, 1), -at, 1)
            edge = jnp.where((lane >= at) & (lane < at + HALO), after, edge)
            end = BLOCK - at
            edge = jnp.where((lane >= end - HALO) & (lane < end), before, edge)
        upper, lower = edge[: tile_lat // 2], edge[tile_lat // 2 :]
        near = lane[: tile_lat // 2]
        lower = jnp.where(near < BLOCK // 2, turn(lower, 2 * HALO, 1), turn(lower, -2 * HALO, 1))
        sums[n, 4 * tile_lat :] = jnp.where((near < 2 * HALO) | (near >= BLOCK - 2 * HALO), upper, lower)


def unweigh(
    gathered, keys, counts, columns_in, lines_in, starts_in, weights_near, weights, gradient, result, columns, lines, starts, *scratch
):
    scratch, (held, arrived) = scratch[:3], scratch[3:]
    fetch_weights(weights, held, arrived, weights_near)
    blocks = weights.shape[0]
    lon_count, ocean_blocks = gathered.shape[0], gathered.shape[1] // 2
    order = group_order(lon_count)
    capacity = places(keys.shape[1], blocks)
    rounds = jnp.max(keys[3:4]).astype(jnp.int32) // capacity + 1
    parts = [
        split(
            jnp.concatenate(
                [gathered[order.index(k), f * ocean_blocks : (f + 1) * ocean_blocks] for k in range(lon_count)],
                axis=0,
            )
        )
        for f in range(2)
    ]
    table = jnp.concatenate([parts[f][n] for n in range(2) for f in range(2)], axis=1)

    def prepare(r):
        @pl.when(r == 0)
        def _():
            columns[...] = columns_in[...]
            lines[...] = lines_in[...]
            starts[...] = starts_in[...]

        @pl.when(r > 0)
        def _():
            find_slots(r.astype(f32), keys, counts[...], capacity, columns, lines, starts)

    part = held_part(weights, held, arrived)
    couple(part, table, capacity, rounds, prepare, columns, lines, starts, True, result, scratch)
    for f in range(2):
        gradient[f, 0] = result[:, f * BLOCK : (f + 1) * BLOCK]


def on_device(tracers, cotangent, land_mask, diffusion, velocity, weights, atm_state, margins):
    levels, tile_lat, tile_lon = land_mask.shape
    lon_count = lax.axis_size("lon")
    slots = lon_count * margins.shape[4]
    halves = tile_lon // BLOCK
    count = 9 * levels - 1
    parts = -(-count // PER_LANES)
    inputs = (tracers, cotangent, land_mask, diffusion, velocity)

    def in_vmem(s):
        return pltpu.VMEM(s.shape, s.dtype)

    message = (parts, tile_lat, BLOCK)
    fields, near, far, atm_near, margins_near = call(
        pack_columns,
        [
            (count, tile_lat, tile_lon),
            message,
            message,
            atm_state.shape,
            jax.ShapeDtypeStruct(margins.shape, margins.dtype),
        ],
        [*map(in_vmem, inputs), pltpu.SemaphoreType.DMA((7,))],
        name="pack_columns",
        inputs=7,
        far=range(7),
    )(*inputs, atm_state, margins)
    near_columns, far_columns = swap(near, far, "lon", True)

    blocks_of, atm = weights.shape[0], atm_state.shape[2]
    sum_rows = 2 * halves * tile_lat + tile_lat // 2
    ocean_blocks = lon_count * halves * tile_lat
    chunks = round_chunks(slots, blocks_of)
    held_rows = chunks * BLOCK + places(slots, blocks_of)

    def coupling_scratch(result_rows):
        return [
            pltpu.VMEM((result_rows, 2 * BLOCK), f32),
            pltpu.VMEM((held_rows, 4 * BLOCK), f32),
            pltpu.VMEM((held_rows, 2 * BLOCK), f32),
            pltpu.SMEM((blocks_of,), jnp.int32),
            pltpu.VMEM(weights.shape, f32),
            pltpu.SemaphoreType.DMA((blocks_of // FETCH,)),
        ]

    coupling_flops = 4 * slots * blocks_of * 2 * BLOCK * BLOCK * 2
    found = [
        jax.ShapeDtypeStruct((2, BLOCK, BLOCK), f32),
        jax.ShapeDtypeStruct((2, -(-chunks // 8) * 8, BLOCK), f32),
        jax.ShapeDtypeStruct((blocks_of, BLOCK), jnp.int32),
    ]
    sums, *slot_data = call(
        weigh,
        [(lon_count, sum_rows, BLOCK), (8, slots), (blocks_of, BLOCK), *found],
        coupling_scratch(ocean_blocks),
        coupling_flops,
        name="weigh",
        inputs=4,
        far=(2,),
    )(atm_near, margins_near, weights, far)

    sources = count * halves + 2 * parts
    message = (-(-sources // 2), 8, BLOCK)
    columns = (parts, tile_lat, BLOCK)
    near, far, from_west, from_east, sums = call(
        pack_rows,
        [message, message, columns, columns, sums.shape],
        name="pack_rows",
        inputs=4,
        aliases={3: 4},
    )(fields, near_columns, far_columns, sums)
    received = exchange(sums)
    near_rows, far_rows = swap(near, far, "lat", False)

    wide = (tile_lat + 8, tile_lon + BLOCK)
    own = (2 * halves * tile_lat, BLOCK)
    adjoint_states = (2, STEPS - 1, levels, *wide)
    blocks, coeffs, start, states = call(
        run_adjoint,
        [(lon_count, *own), (6, levels, *wide), (4 * levels, *wide), adjoint_states],
        [
            pltpu.VMEM((count - 4 * levels, *wide), f32),
            pltpu.VMEM(own, f32),
            pltpu.SemaphoreType.DMA((2, lon_count)),
        ],
        name="run_adjoint",
        inputs=5,
        far_outs=(0,),
    )(fields, from_west, from_east, far_rows, near_rows)
    gathered = exchange(blocks)

    message = (1, 8, tile_lon + BLOCK)
    forcing, near, far = call(
        sum_forcing, [(2, tile_lat, tile_lon + BLOCK), message, message], name="sum_forcing", inputs=1
    )(received)
    near_rows, far_rows = swap(near, far, "lat", False)
    (adjoint,) = call(
        finish_adjoint,
        [cotangent.shape],
        [pltpu.VMEM(adjoint_states, f32)],
        name="finish_adjoint",
        inputs=3,
    )(coeffs, start, states)
    final, weights_near = call(
        run_forward,
        [tracers.shape, (blocks_of // 2, BLOCK, BLOCK)],
        [pltpu.VMEM((2, levels, *wide), f32), pltpu.SemaphoreType.DMA],
        name="run_forward",
        inputs=6,
        far=(5,),
    )(coeffs, start, forcing, near_rows, far_rows, weights)

    (gradient,) = call(
        unweigh,
        [atm_state.shape],
        [coupling_scratch(atm)[0], *map(in_vmem, found), *coupling_scratch(atm)[1:]],
        coupling_flops,
        name="unweigh",
        inputs=8,
        far=(7,),
    )(gathered, *slot_data, weights_near, weights)
    return (final, adjoint, gradient)


def solution(mesh):
    return jax.shard_map(
        on_device,
        mesh=mesh,
        in_specs=(
            P(None, None, "lat", "lon"),
            P(None, None, "lat", "lon"),
            P(None, "lat", "lon"),
            P(None, None, "lat", "lon"),
            P(None, None, "lat", "lon"),
            P(),
            P(None, "lat", "lon", None),
            P(None, "lat", "lon", None, None),
        ),
        out_specs=(
            P(None, None, "lat", "lon"),
            P(None, None, "lat", "lon"),
            P(None, "lat", "lon", None),
        ),
        check_vma=False,
    )
```

```python
import jax
import jax.numpy as jnp
from jax import lax
from jax.experimental import pallas as pl
from jax.experimental.pallas import tpu as pltpu
from jax.sharding import PartitionSpec as P

BLOCK = 128
STEPS = 4
HALO = STEPS
PER_LANES = BLOCK // HALO
GROUP = 16
FETCH = 4
f32 = jnp.float32
bf16 = jnp.bfloat16
VMEM_LIMIT = 20 * 1024 * 1024


def call(body, outs, scratch=(), flops=0, name=None, inputs=0, far=(), far_outs=(), aliases=None):
    outs = [s if isinstance(s, jax.ShapeDtypeStruct) else jax.ShapeDtypeStruct(s, f32) for s in outs]
    near = pl.BlockSpec(memory_space=pltpu.VMEM)
    aliases = aliases or {}
    kernel = pl.pallas_call(
        body,
        out_shape=outs,
        in_specs=[
            pl.BlockSpec(memory_space=pl.ANY)
            if n in aliases
            else pl.BlockSpec(memory_space=pltpu.HBM)
            if n in far
            else near
            for n in range(inputs)
        ],
        out_specs=[
            pl.BlockSpec(memory_space=pl.ANY) if n in aliases.values() or n in far_outs else near
            for n in range(len(outs))
        ],
        input_output_aliases=aliases,
        scratch_shapes=list(scratch),
        compiler_params=pltpu.CompilerParams(vmem_limit_bytes=VMEM_LIMIT),
        cost_estimate=pl.CostEstimate(flops=flops, bytes_accessed=1 << 20, transcendentals=0),
        name=name,
    )

    def run(*args):
        return kernel(
            *(pltpu.with_memory_space_constraint(x, pltpu.HBM) if n in far else x for n, x in enumerate(args))
        )

    return run


def lanes(shape):
    return lax.broadcasted_iota(jnp.int32, shape, len(shape) - 1)


def rows(shape):
    return lax.broadcasted_iota(jnp.int32, shape, len(shape) - 2)


def turn(x, shift, axis):
    shift %= x.shape[axis]
    return pltpu.roll(x, shift, axis) if shift else x


def group_order(count):
    half = count // 2
    return [k for n in range(half) for k in (half + n, n)]


def exchange(x):
    order = group_order(x.shape[0])
    return lax.all_to_all(x, "lon", split_axis=0, concat_axis=0, tiled=True, axis_index_groups=[order])


def swap(near, far, axis, wrap):
    count = lax.axis_size(axis)
    pairs = [[], []]
    for i in range(count if wrap else count - 1):
        j = (i + 1) % count
        pairs[i % 2] += [(i, j), (j, i)]
    far = lax.ppermute(far, axis, pairs[1])
    return lax.ppermute(near, axis, pairs[0]), far


def sort_swap(axis, after, before):
    odd = lax.rem(lax.axis_index(axis), 2) == 1
    return jnp.where(odd, before, after), jnp.where(odd, after, before)


def tile_fields(tracers, cotangent, land_mask, diffusion, velocity):
    levels = land_mask.shape[0]
    mask = [land_mask[level].astype(f32) for level in range(levels)]
    out = [tracers[f, level] for f in range(2) for level in range(levels)]
    out += [cotangent[f, level] for f in range(2) for level in range(levels)]
    out += [diffusion[0, level] * mask[level] for level in range(levels)]
    out += [velocity[0, level] * mask[level] for level in range(levels)]
    out += [diffusion[1, level] * mask[level] for level in range(levels)]
    out += [velocity[1, level] * mask[level] for level in range(levels)]
    out += [diffusion[2, level] * mask[level] * mask[level + 1] for level in range(levels - 1)]
    return out


def fetch(pairs, arrived):
    copies = [pltpu.make_async_copy(src, dst, arrived.at[n]) for n, (src, dst) in enumerate(pairs)]
    for copy in copies:
        copy.start()
    return copies


def pack_columns(*refs):
    inputs, (fields, near, far), scratch = refs[:7], refs[7:10], refs[12:]
    copies = fetch(zip(inputs, [*scratch[:5], *refs[10:12]]), scratch[5])
    for copy in copies[:5]:
        copy.wait()
    shape = near.shape[1:]
    lane = lanes(shape)
    west = [jnp.zeros(shape, f32) for _ in range(near.shape[0])]
    east = [jnp.zeros(shape, f32) for _ in range(near.shape[0])]
    for i, field in enumerate(tile_fields(*scratch[:5])):
        fields[i] = field
        part, at = divmod(i, PER_LANES)
        at *= HALO
        here = (lane >= at) & (lane < at + HALO)
        west[part] = jnp.where(here, turn(field[:, :BLOCK], at, 1), west[part])
        east[part] = jnp.where(here, turn(field[:, -BLOCK:], at + HALO, 1), east[part])
    for part in range(near.shape[0]):
        near[part], far[part] = sort_swap("lon", east[part], west[part])
    for copy in copies[5:]:
        copy.wait()


def unpack_columns(from_west, from_east, i):
    part, at = divmod(i, PER_LANES)
    at *= HALO
    lane = lanes(from_west[part].shape)
    east = turn(from_east[part], -at, 1)
    west = turn(from_west[part], -at - HALO, 1)
    return jnp.where(lane < HALO, east, jnp.where(lane >= BLOCK - HALO, west, 0.0))


def row_sources(fields, from_west, from_east):
    out = [(fields, (i, slice(None), slice(h * BLOCK, (h + 1) * BLOCK)))
           for i in range(fields.shape[0]) for h in range(fields.shape[2] // BLOCK)]
    for columns in (from_west, from_east):
        out += [(columns, (part,)) for part in range(columns.shape[0])]
    return out


def pack_rows(fields, near_columns, far_columns, sums, near, far, from_west, from_east, same_sums):
    for part in range(from_west.shape[0]):
        from_east[part], from_west[part] = sort_swap("lon", near_columns[part], far_columns[part])
    sources = [ref[at] for ref, at in row_sources(fields, from_west, from_east)]
    half = near.shape[0]
    row = rows((8, BLOCK))
    for i in range(half):
        first = sources[i]
        second = sources[i + half] if i + half < len(sources) else jnp.zeros_like(first)
        to_north = jnp.where(row < HALO, turn(first[-8:], HALO, 0), second[-8:])
        to_south = jnp.where(row < HALO, first[:8], turn(second[:8], HALO, 0))
        near[i], far[i] = sort_swap("lat", to_north, to_south)


def edge_rows(near, far, i):
    half = near.shape[0]
    from_north, from_south = sort_swap("lat", near[i % half], far[i % half])
    if i < half:
        from_south = turn(from_south, HALO, 0)
    else:
        from_north = turn(from_north, HALO, 0)
    return jnp.where(rows(from_north.shape) < HALO, from_north, from_south)


def widen(fields, from_west, from_east, near, far, start, wide):
    count, tile_lat, tile_lon = fields.shape
    halves = tile_lon // BLOCK
    parts = from_west.shape[0]
    corners = [edge_rows(near, far, count * halves + n) for n in range(2 * parts)]
    for i in range(count):
        out = start.at[i] if i < start.shape[0] else wide.at[i - start.shape[0]]
        out[:tile_lat, :tile_lon] = fields[i]
        out[:tile_lat, tile_lon:] = unpack_columns(from_west, from_east, i)
        for h in range(halves):
            out[tile_lat:, h * BLOCK : (h + 1) * BLOCK] = edge_rows(near, far, i * halves + h)
        out[tile_lat:, tile_lon:] = unpack_columns(corners[:parts], corners[parts:], i)


def eastward(x):
    return turn(x, -1, 1)


def westward(x):
    return turn(x, 1, 1)


def northward(x):
    return turn(x, -1, 0)


def southward(x):
    return turn(x, 1, 0)


def adjoint_step(coeffs, read, write, first, last):
    levels = coeffs.shape[1]
    above = coeffs[4, first - 1] * (read(first) - read(first - 1)) if first else None
    for level in range(first, last):
        lam = read(level)
        step_x = eastward(lam) - lam
        step_y = northward(lam) - lam
        out = lam + coeffs[0, level] * step_x + westward(coeffs[1, level] * step_x)
        out = out + coeffs[2, level] * step_y + southward(coeffs[3, level] * step_y)
        if above is not None:
            out = out - above
        if level < levels - 1:
            above = coeffs[4, level] * (read(level + 1) - lam)
            out = out + above
        write(level, out)


def surface_levels(step, levels):
    return min(levels, STEPS - 1 - step)


def run_adjoint(
    fields, from_west, from_east, far, near, blocks, coeffs, start, states, wide, own, sent
):
    levels = coeffs.shape[1]
    tile_lat, tile_lon = fields.shape[1:]
    halves = tile_lon // BLOCK
    widen(fields, from_west, from_east, near, far, start, wide)
    base = 0
    mask0 = None
    for level in range(levels):
        east_d, east_u = wide[base + level], wide[base + levels + level]
        north_d, north_u = wide[base + 2 * levels + level], wide[base + 3 * levels + level]
        mask = (east_d > 0.0).astype(f32)
        mask0 = mask if mask0 is None else mask0
        mask_e, mask_n = eastward(mask), northward(mask)
        east_k, east_v = east_d * mask_e, east_u * mask_e
        north_k, north_v = north_d * mask_n, north_u * mask_n
        coeffs[0, level] = jnp.maximum(east_v, 0.0) + east_k
        coeffs[1, level] = jnp.minimum(east_v, 0.0) - east_k
        coeffs[2, level] = jnp.maximum(north_v, 0.0) + north_k
        coeffs[3, level] = jnp.minimum(north_v, 0.0) - north_k
        coeffs[4, level] = wide[base + 4 * levels + level] if level < levels - 1 else jnp.zeros_like(mask)
        coeffs[5, level] = mask
    copies = []
    for f in range(2):
        surface = start[(2 + f) * levels, :tile_lat, :tile_lon]
        for step in range(STEPS - 1):

            def read(level):
                return states[f, step - 1, level] if step else start[(2 + f) * levels + level]

            def write(level, lam):
                states[f, step, level] = lam

            adjoint_step(coeffs, read, write, 0, surface_levels(step, levels))
            surface = surface + states[f, step, 0, :tile_lat, :tile_lon]
        surface = surface * mask0[:tile_lat, :tile_lon]
        for h in range(halves):
            at = (f * halves + h) * tile_lat
            own[at : at + tile_lat] = surface[:, h * BLOCK : (h + 1) * BLOCK]
        field = pl.ds(f * halves * tile_lat, halves * tile_lat)
        copies += fetch([(own.at[field], blocks.at[k, field]) for k in range(blocks.shape[0])], sent.at[f])
    for copy in copies:
        copy.wait()


def finish_adjoint(coeffs, start, states, adjoint_out, rest):
    levels = coeffs.shape[1]
    tile_lat, tile_lon = adjoint_out.shape[2:]
    for f in range(2):
        for step in range(STEPS):
            done = surface_levels(step, levels)

            def read(level):
                if not step:
                    return start[(2 + f) * levels + level]
                return (states if level < surface_levels(step - 1, levels) else rest)[f, step - 1, level]

            def write(level, lam):
                if step == STEPS - 1:
                    adjoint_out[f, level] = lam[:tile_lat, :tile_lon]
                else:
                    rest[f, step, level] = lam

            adjoint_step(coeffs, read, write, done, levels)


def sum_forcing(received, forcing, near, far):
    tile_lat = forcing.shape[1]
    halves = forcing.shape[2] // BLOCK - 1
    total = received[0]
    for j in range(1, received.shape[0]):
        total = total + received[j]
    lane = lanes((tile_lat, BLOCK))
    upper = total[2 * halves * tile_lat :]
    lower = jnp.where(lane[: tile_lat // 2] < BLOCK // 2, turn(upper, -2 * HALO, 1), turn(upper, 2 * HALO, 1))
    packed = jnp.concatenate([upper, lower], axis=0)
    for f in range(2):
        for h in range(halves):
            at = (f * halves + h) * tile_lat
            forcing[f, :, h * BLOCK : (h + 1) * BLOCK] = total[at : at + tile_lat]
        used = (lane < HALO) | (lane >= BLOCK - HALO)
        if f == 0:
            edge = packed
        else:
            edge = jnp.where(lane < HALO, turn(packed, -HALO, 1), turn(packed, HALO, 1))
        forcing[f, :, halves * BLOCK :] = jnp.where(used, edge, 0.0)
    row = rows((8, forcing.shape[2]))
    to_north = jnp.where(row < HALO, turn(forcing[0, tile_lat - 8 :], HALO, 0), forcing[1, tile_lat - 8 :])
    to_south = jnp.where(row < HALO, forcing[0, :8], turn(forcing[1, :8], HALO, 0))
    near[0], far[0] = sort_swap("lat", to_north, to_south)


def run_forward(coeffs, start, forcing, near, far, weights, final, weights_near, state, arrived):
    fetch_weights(weights, weights_near, arrived)
    levels = coeffs.shape[1]
    tile_lat, tile_lon = final.shape[2:]
    for f in range(2):
        force = jnp.concatenate([forcing[f], edge_rows(near, far, f)], axis=0)
        force = force * coeffs[5, 0]
        for step in range(STEPS):
            above = None
            for level in range(levels):
                read = (lambda n: start[f * levels + n]) if step == 0 else (lambda n: state[(step - 1) % 2, n])
                theta = read(level)
                east_flux = coeffs[0, level] * theta + coeffs[1, level] * eastward(theta)
                north_flux = coeffs[2, level] * theta + coeffs[3, level] * northward(theta)
                out = theta - (east_flux - westward(east_flux)) - (north_flux - southward(north_flux))
                if level < levels - 1:
                    vertical = coeffs[4, level] * (theta - read(level + 1))
                    out = out - vertical
                if above is not None:
                    out = out + above
                above = vertical if level < levels - 1 else None
                if level == 0:
                    out = out + force
                if step == STEPS - 1:
                    final[f, level] = out[:tile_lat, :tile_lon]
                else:
                    state[step % 2, level] = out
    for n in range(weights_near.shape[0] // FETCH):
        weight_copy(weights, weights_near, arrived, n).wait()


def split(x):
    high = x.astype(bf16)
    return high, (x - high.astype(f32)).astype(bf16)


def weight_copy(weights, held, arrived, n):
    own = pl.ds(n * FETCH, FETCH)
    return pltpu.make_async_copy(weights.at[own], held.at[own], arrived.at[n])


def fetch_weights(weights, held, arrived, near=None):
    for n in range(held.shape[0] // FETCH):
        source = near if near is not None and (n + 1) * FETCH <= near.shape[0] else weights
        weight_copy(source, held, arrived, n).start()


def held_part(weights, held, arrived):
    def part(r, g, u):
        if u == 0:

            @pl.when(r == 0)
            def _():
                for n in range(GROUP // FETCH):
                    weight_copy(weights, held, arrived, g * (GROUP // FETCH) + n).wait()

        return split(held[g * GROUP + u])

    return part


def one_hot(where):
    return jnp.where(where, 1.0, 0.0).astype(bf16)


def places(slots, blocks):
    return 8 * (-(-2 * slots // (8 * blocks)) + 1)


def round_chunks(slots, blocks):
    return -(-(slots + 7 * blocks) // BLOCK)


def as_row(ids):
    return jnp.concatenate([ids[k : k + 1, :] for k in range(ids.shape[0])], axis=1)


def rank_slots(block_row, blocks):
    slots = block_row.shape[1]
    mine = rows((blocks, slots)) == block_row
    cuts = range(0, slots, BLOCK)
    stacked = jnp.concatenate([one_hot(mine[:, at : at + BLOCK]) for at in cuts], axis=0)
    shape = (BLOCK, 2 * BLOCK)
    counts = jnp.dot(stacked, one_hot(rows(shape) < lanes(shape)), preferred_element_type=f32)
    before, out = jnp.zeros((blocks, BLOCK), f32), []
    for n, at in enumerate(cuts):
        run = counts[n * blocks : (n + 1) * blocks]
        here = jnp.where(mine[:, at : at + BLOCK], run[:, :BLOCK] + before, 0.0)
        out.append(jnp.sum(here, axis=0, keepdims=True))
        before = before + run[:, BLOCK:]
    return jnp.concatenate(out, axis=1), before


def find_slots(r, keys, counts, capacity, columns, lines, starts):
    slots = keys.shape[1]
    blocks = counts.shape[0]
    atm_row, ocean_row, block_row, rank = (keys[n : n + 1] for n in range(4))
    count = jnp.clip(counts - r * capacity, 0.0, capacity)
    tiles = jnp.floor((count + 7.0) * 0.125) * 8.0
    shape = (blocks, blocks)
    first = jnp.dot(one_hot(lanes(shape) < rows(shape)), tiles.astype(bf16), preferred_element_type=f32)
    starts[...] = first.astype(jnp.int32)
    mine = rows((blocks, slots)).astype(f32) == block_row
    own = jnp.where(mine, jnp.concatenate([first] * (slots // BLOCK), axis=1), 0.0)
    place = rank - r * capacity
    here = (place >= 0.0) & (place < capacity)
    place = jnp.where(here, jnp.sum(own, axis=0, keepdims=True) + place, -1.0)
    run = jnp.floor(place * (1.0 / BLOCK))
    low = one_hot(rows((BLOCK, slots)).astype(f32) == place - run * BLOCK)
    size = lines.shape[1]
    in_run = rows((size, slots)).astype(f32) == run
    ocean_high = jnp.floor(ocean_row * (1.0 / BLOCK))
    digits = [atm_row, ocean_high, ocean_row - ocean_high * BLOCK]
    digits = [jnp.where(in_run, digit, 0.0).astype(bf16) for digit in digits]
    across = (((1,), (1,)), ((), ()))
    down = [lax.dot_general(low, digit, across, preferred_element_type=f32) for digit in digits]
    along = [lax.dot_general(digit, low, across, preferred_element_type=f32) for digit in digits]
    columns[0, :, :size], columns[1, :, :size] = down[0], down[1] * BLOCK + down[2] - 1.0
    ocean = along[1] * BLOCK + along[2] - 1.0
    lines[0], lines[1] = jnp.where(ocean < 0.0, -1.0, along[0]), ocean


def couple(part, table, capacity, rounds, prepare, columns, lines, starts, transposed, result, scratch):
    vectors, products, starts_near = scratch
    blocks = starts.shape[0]
    total_rows = vectors.shape[0] - capacity
    width = table.shape[0]
    result[...] = jnp.zeros_like(result)
    products[...] = jnp.zeros_like(products)

    def one_round(r, carry):
        prepare(r)
        first_rows = starts[...]
        for w in range(blocks):
            starts_near[w] = first_rows[w, 0]
        place_hot = []
        for n in range(total_rows // BLOCK):
            gather = jnp.broadcast_to(columns[int(transposed), :, n : n + 1], (BLOCK, BLOCK))
            gather = jnp.concatenate([gather] * (width // BLOCK), axis=1)
            hot = one_hot(gather == lanes((BLOCK, width)).astype(f32))
            vectors[n * BLOCK : (n + 1) * BLOCK] = jnp.dot(hot, table, preferred_element_type=f32)
            put = lines[1 - int(transposed), n : n + 1]
            place_hot.append(one_hot(rows((result.shape[0], BLOCK)).astype(f32) == put))

        def group(g, carry):
            for u in range(GROUP):
                at = pl.ds(pl.multiple_of(starts_near[g * GROUP + u], 8), capacity)
                own = vectors[at]
                left = jnp.concatenate([own[:, n * BLOCK : (n + 1) * BLOCK] for n in range(4)], axis=0)
                high, low = part(r, g, u)
                right = jnp.concatenate([high, low], axis=1 if transposed else 0)
                contract = (((1,), (0 if transposed else 1,)), ((), ()))
                product = lax.dot_general(left.astype(bf16), right, contract, preferred_element_type=f32)
                for f in range(2):
                    high_part = product[f * capacity : (f + 1) * capacity]
                    low_part = product[(f + 2) * capacity : (f + 3) * capacity, :BLOCK]
                    products[at, f * BLOCK : (f + 1) * BLOCK] = (
                        high_part[:, BLOCK:] + low_part
                    ) + high_part[:, :BLOCK]
            return carry

        lax.fori_loop(0, blocks // GROUP, group, 0)
        summed = jnp.dot(
            jnp.concatenate(place_hot, axis=1),
            jnp.concatenate(split(products[:total_rows]), axis=1),
            preferred_element_type=f32,
        )
        result[...] += summed[:, : 2 * BLOCK] + summed[:, 2 * BLOCK :]
        return carry

    lax.fori_loop(0, rounds, one_round, 0)


def slot_keys(ids, tile_lat, keys):
    lon_count, cap = ids.shape[3:]
    ocean, atm_ids, block_ids = (ids[n, 0, 0] for n in range(3))
    order = (ocean & 1) * tile_lat + (ocean >> 1) + rows((lon_count, cap)) * (2 * tile_lat)
    order = jnp.where(ocean >= 0, order, lon_count * 2 * tile_lat) + 1
    for n, part in enumerate((atm_ids, order, block_ids)):
        keys[n : n + 1] = as_row(part.astype(f32))


def weigh(
    atm_near, margins, weights, after, sums, keys, counts, columns, lines, starts, result, *scratch
):
    scratch, (held, arrived) = scratch[:3], scratch[3:]
    fetch_weights(weights, held, arrived)
    lon_count = margins.shape[3]
    blocks = weights.shape[0]
    tile_lat = 2 * sums.shape[1] // 9
    slot_keys(margins, tile_lat, keys)
    rank, count = rank_slots(keys[2:3].astype(jnp.int32), blocks)
    keys[3:4] = rank
    counts[...] = count
    capacity = places(keys.shape[1], blocks)
    rounds = jnp.max(rank).astype(jnp.int32) // capacity + 1
    parts = [split(atm_near[f, 0]) for f in range(2)]
    table = jnp.concatenate([parts[f][n] for n in range(2) for f in range(2)], axis=1)
    part = held_part(weights, held, arrived)

    def prepare(r):
        find_slots((rounds - 1 - r).astype(f32), keys, counts[...], capacity, columns, lines, starts)

    couple(part, table, capacity, rounds, prepare, columns, lines, starts, False, result, scratch)
    lane = lanes((tile_lat, BLOCK))

    def block_sums(k, f, h):
        at = (2 * k + h) * tile_lat
        return result[at : at + tile_lat, f * BLOCK : (f + 1) * BLOCK]

    for n, k in enumerate(group_order(lon_count)):
        edge = jnp.zeros((tile_lat, BLOCK), f32)
        for f in range(2):
            for h in range(2):
                sums[n, (2 * f + h) * tile_lat : (2 * f + h + 1) * tile_lat] = block_sums(k, f, h)
            at = f * HALO
            after = turn(block_sums((k + 1) % lon_count, f, 0), at, 1)
            before = turn(block_sums((k - 1) % lon_count, f, 1), -at, 1)
            edge = jnp.where((lane >= at) & (lane < at + HALO), after, edge)
            end = BLOCK - at
            edge = jnp.where((lane >= end - HALO) & (lane < end), before, edge)
        upper, lower = edge[: tile_lat // 2], edge[tile_lat // 2 :]
        near = lane[: tile_lat // 2]
        lower = jnp.where(near < BLOCK // 2, turn(lower, 2 * HALO, 1), turn(lower, -2 * HALO, 1))
        sums[n, 4 * tile_lat :] = jnp.where((near < 2 * HALO) | (near >= BLOCK - 2 * HALO), upper, lower)


def unweigh(
    gathered, keys, counts, columns_in, lines_in, starts_in, weights_near, weights, gradient, result, columns, lines, starts, *scratch
):
    scratch, (held, arrived) = scratch[:3], scratch[3:]
    fetch_weights(weights, held, arrived, weights_near)
    blocks = weights.shape[0]
    lon_count, ocean_blocks = gathered.shape[0], gathered.shape[1] // 2
    order = group_order(lon_count)
    capacity = places(keys.shape[1], blocks)
    rounds = jnp.max(keys[3:4]).astype(jnp.int32) // capacity + 1
    parts = [
        split(
            jnp.concatenate(
                [gathered[order.index(k), f * ocean_blocks : (f + 1) * ocean_blocks] for k in range(lon_count)],
                axis=0,
            )
        )
        for f in range(2)
    ]
    table = jnp.concatenate([parts[f][n] for n in range(2) for f in range(2)], axis=1)

    def prepare(r):
        @pl.when(r == 0)
        def _():
            columns[...] = columns_in[...]
            lines[...] = lines_in[...]
            starts[...] = starts_in[...]

        @pl.when(r > 0)
        def _():
            find_slots(r.astype(f32), keys, counts[...], capacity, columns, lines, starts)

    part = held_part(weights, held, arrived)
    couple(part, table, capacity, rounds, prepare, columns, lines, starts, True, result, scratch)
    for f in range(2):
        gradient[f, 0] = result[:, f * BLOCK : (f + 1) * BLOCK]


def on_device(tracers, cotangent, land_mask, diffusion, velocity, weights, atm_state, margins):
    levels, tile_lat, tile_lon = land_mask.shape
    lon_count = lax.axis_size("lon")
    slots = lon_count * margins.shape[4]
    halves = tile_lon // BLOCK
    count = 9 * levels - 1
    parts = -(-count // PER_LANES)
    inputs = (tracers, cotangent, land_mask, diffusion, velocity)

    def in_vmem(s):
        return pltpu.VMEM(s.shape, s.dtype)

    message = (parts, tile_lat, BLOCK)
    fields, near, far, atm_near, margins_near = call(
        pack_columns,
        [
            (count, tile_lat, tile_lon),
            message,
            message,
            atm_state.shape,
            jax.ShapeDtypeStruct(margins.shape, margins.dtype),
        ],
        [*map(in_vmem, inputs), pltpu.SemaphoreType.DMA((7,))],
        name="pack_columns",
        inputs=7,
        far=range(7),
    )(*inputs, atm_state, margins)
    near_columns, far_columns = swap(near, far, "lon", True)

    blocks_of, atm = weights.shape[0], atm_state.shape[2]
    sum_rows = 2 * halves * tile_lat + tile_lat // 2
    ocean_blocks = lon_count * halves * tile_lat
    chunks = round_chunks(slots, blocks_of)
    held_rows = chunks * BLOCK + places(slots, blocks_of)

    def coupling_scratch(result_rows):
        return [
            pltpu.VMEM((result_rows, 2 * BLOCK), f32),
            pltpu.VMEM((held_rows, 4 * BLOCK), f32),
            pltpu.VMEM((held_rows, 2 * BLOCK), f32),
            pltpu.SMEM((blocks_of,), jnp.int32),
            pltpu.VMEM(weights.shape, f32),
            pltpu.SemaphoreType.DMA((blocks_of // FETCH,)),
        ]

    coupling_flops = 4 * slots * blocks_of * 2 * BLOCK * BLOCK * 2
    found = [
        jax.ShapeDtypeStruct((2, BLOCK, BLOCK), f32),
        jax.ShapeDtypeStruct((2, -(-chunks // 8) * 8, BLOCK), f32),
        jax.ShapeDtypeStruct((blocks_of, BLOCK), jnp.int32),
    ]
    sums, *slot_data = call(
        weigh,
        [(lon_count, sum_rows, BLOCK), (8, slots), (blocks_of, BLOCK), *found],
        coupling_scratch(ocean_blocks),
        coupling_flops,
        name="weigh",
        inputs=4,
        far=(2,),
    )(atm_near, margins_near, weights, far)

    sources = count * halves + 2 * parts
    message = (-(-sources // 2), 8, BLOCK)
    columns = (parts, tile_lat, BLOCK)
    near, far, from_west, from_east, sums = call(
        pack_rows,
        [message, message, columns, columns, sums.shape],
        name="pack_rows",
        inputs=4,
        aliases={3: 4},
    )(fields, near_columns, far_columns, sums)
    received = exchange(sums)
    near_rows, far_rows = swap(near, far, "lat", False)

    wide = (tile_lat + 8, tile_lon + BLOCK)
    own = (2 * halves * tile_lat, BLOCK)
    adjoint_states = (2, STEPS - 1, levels, *wide)
    blocks, coeffs, start, states = call(
        run_adjoint,
        [(lon_count, *own), (6, levels, *wide), (4 * levels, *wide), adjoint_states],
        [
            pltpu.VMEM((count - 4 * levels, *wide), f32),
            pltpu.VMEM(own, f32),
            pltpu.SemaphoreType.DMA((2, lon_count)),
        ],
        name="run_adjoint",
        inputs=5,
        far_outs=(0,),
    )(fields, from_west, from_east, far_rows, near_rows)
    gathered = exchange(blocks)

    message = (1, 8, tile_lon + BLOCK)
    forcing, near, far = call(
        sum_forcing, [(2, tile_lat, tile_lon + BLOCK), message, message], name="sum_forcing", inputs=1
    )(received)
    near_rows, far_rows = swap(near, far, "lat", False)
    (adjoint,) = call(
        finish_adjoint,
        [cotangent.shape],
        [pltpu.VMEM(adjoint_states, f32)],
        name="finish_adjoint",
        inputs=3,
    )(coeffs, start, states)
    final, weights_near = call(
        run_forward,
        [tracers.shape, (blocks_of // 2, BLOCK, BLOCK)],
        [pltpu.VMEM((2, levels, *wide), f32), pltpu.SemaphoreType.DMA((blocks_of // 2 // FETCH,))],
        name="run_forward",
        inputs=6,
        far=(5,),
    )(coeffs, start, forcing, near_rows, far_rows, weights)

    (gradient,) = call(
        unweigh,
        [atm_state.shape],
        [coupling_scratch(atm)[0], *map(in_vmem, found), *coupling_scratch(atm)[1:]],
        coupling_flops,
        name="unweigh",
        inputs=8,
        far=(7,),
    )(gathered, *slot_data, weights_near, weights)
    return (final, adjoint, gradient)


def solution(mesh):
    return jax.shard_map(
        on_device,
        mesh=mesh,
        in_specs=(
            P(None, None, "lat", "lon"),
            P(None, None, "lat", "lon"),
            P(None, "lat", "lon"),
            P(None, None, "lat", "lon"),
            P(None, None, "lat", "lon"),
            P(),
            P(None, "lat", "lon", None),
            P(None, "lat", "lon", None, None),
        ),
        out_specs=(
            P(None, None, "lat", "lon"),
            P(None, None, "lat", "lon"),
            P(None, "lat", "lon", None),
        ),
        check_vma=False,
    )
```

```python
import jax
import jax.numpy as jnp
from jax import lax
from jax.experimental import pallas as pl
from jax.experimental.pallas import tpu as pltpu
from jax.sharding import PartitionSpec as P

BLOCK = 128
STEPS = 4
HALO = STEPS
PER_LANES = BLOCK // HALO
GROUP = 16
FETCH = 4
f32 = jnp.float32
bf16 = jnp.bfloat16
VMEM_LIMIT = 20 * 1024 * 1024


def call(body, outs, scratch=(), flops=0, name=None, inputs=0, far=(), far_outs=(), aliases=None):
    outs = [s if isinstance(s, jax.ShapeDtypeStruct) else jax.ShapeDtypeStruct(s, f32) for s in outs]
    near = pl.BlockSpec(memory_space=pltpu.VMEM)
    aliases = aliases or {}
    kernel = pl.pallas_call(
        body,
        out_shape=outs,
        in_specs=[
            pl.BlockSpec(memory_space=pl.ANY)
            if n in aliases
            else pl.BlockSpec(memory_space=pltpu.HBM)
            if n in far
            else near
            for n in range(inputs)
        ],
        out_specs=[
            pl.BlockSpec(memory_space=pl.ANY) if n in aliases.values() or n in far_outs else near
            for n in range(len(outs))
        ],
        input_output_aliases=aliases,
        scratch_shapes=list(scratch),
        compiler_params=pltpu.CompilerParams(vmem_limit_bytes=VMEM_LIMIT),
        cost_estimate=pl.CostEstimate(flops=flops, bytes_accessed=1 << 20, transcendentals=0),
        name=name,
    )

    def run(*args):
        return kernel(
            *(pltpu.with_memory_space_constraint(x, pltpu.HBM) if n in far else x for n, x in enumerate(args))
        )

    return run


def lanes(shape):
    return lax.broadcasted_iota(jnp.int32, shape, len(shape) - 1)


def rows(shape):
    return lax.broadcasted_iota(jnp.int32, shape, len(shape) - 2)


def turn(x, shift, axis):
    shift %= x.shape[axis]
    return pltpu.roll(x, shift, axis) if shift else x


def group_order(count):
    half = count // 2
    return [k for n in range(half) for k in (half + n, n)]


def exchange(x):
    order = group_order(x.shape[0])
    return lax.all_to_all(x, "lon", split_axis=0, concat_axis=0, tiled=True, axis_index_groups=[order])


def swap(near, far, axis, wrap):
    count = lax.axis_size(axis)
    pairs = [[], []]
    for i in range(count if wrap else count - 1):
        j = (i + 1) % count
        pairs[i % 2] += [(i, j), (j, i)]
    far = lax.ppermute(far, axis, pairs[1])
    return lax.ppermute(near, axis, pairs[0]), far


def sort_swap(axis, after, before):
    odd = lax.rem(lax.axis_index(axis), 2) == 1
    return jnp.where(odd, before, after), jnp.where(odd, after, before)


def tile_fields(tracers, cotangent, land_mask, diffusion, velocity):
    levels = land_mask.shape[0]
    mask = [land_mask[level].astype(f32) for level in range(levels)]
    out = [tracers[f, level] for f in range(2) for level in range(levels)]
    out += [cotangent[f, level] for f in range(2) for level in range(levels)]
    out += [diffusion[0, level] * mask[level] for level in range(levels)]
    out += [velocity[0, level] * mask[level] for level in range(levels)]
    out += [diffusion[1, level] * mask[level] for level in range(levels)]
    out += [velocity[1, level] * mask[level] for level in range(levels)]
    out += [diffusion[2, level] * mask[level] * mask[level + 1] for level in range(levels - 1)]
    return out


def fetch(pairs, arrived):
    copies = [pltpu.make_async_copy(src, dst, arrived.at[n]) for n, (src, dst) in enumerate(pairs)]
    for copy in copies:
        copy.start()
    return copies


def pack_columns(*refs):
    inputs, (fields, near, far), scratch = refs[:7], refs[7:10], refs[12:]
    copies = fetch(zip(inputs, [*scratch[:5], *refs[10:12]]), scratch[5])
    for copy in copies[:5]:
        copy.wait()
    shape = near.shape[1:]
    lane = lanes(shape)
    west = [jnp.zeros(shape, f32) for _ in range(near.shape[0])]
    east = [jnp.zeros(shape, f32) for _ in range(near.shape[0])]
    for i, field in enumerate(tile_fields(*scratch[:5])):
        fields[i] = field
        part, at = divmod(i, PER_LANES)
        at *= HALO
        here = (lane >= at) & (lane < at + HALO)
        west[part] = jnp.where(here, turn(field[:, :BLOCK], at, 1), west[part])
        east[part] = jnp.where(here, turn(field[:, -BLOCK:], at + HALO, 1), east[part])
    for part in range(near.shape[0]):
        near[part], far[part] = sort_swap("lon", east[part], west[part])
    for copy in copies[5:]:
        copy.wait()


def unpack_columns(from_west, from_east, i):
    part, at = divmod(i, PER_LANES)
    at *= HALO
    lane = lanes(from_west[part].shape)
    east = turn(from_east[part], -at, 1)
    west = turn(from_west[part], -at - HALO, 1)
    return jnp.where(lane < HALO, east, jnp.where(lane >= BLOCK - HALO, west, 0.0))


def row_sources(fields, from_west, from_east):
    out = [(fields, (i, slice(None), slice(h * BLOCK, (h + 1) * BLOCK)))
           for i in range(fields.shape[0]) for h in range(fields.shape[2] // BLOCK)]
    for columns in (from_west, from_east):
        out += [(columns, (part,)) for part in range(columns.shape[0])]
    return out


def pack_rows(fields, near_columns, far_columns, sums, near, far, from_west, from_east, same_sums):
    for part in range(from_west.shape[0]):
        from_east[part], from_west[part] = sort_swap("lon", near_columns[part], far_columns[part])
    sources = [ref[at] for ref, at in row_sources(fields, from_west, from_east)]
    half = near.shape[0]
    row = rows((8, BLOCK))
    for i in range(half):
        first = sources[i]
        second = sources[i + half] if i + half < len(sources) else jnp.zeros_like(first)
        to_north = jnp.where(row < HALO, turn(first[-8:], HALO, 0), second[-8:])
        to_south = jnp.where(row < HALO, first[:8], turn(second[:8], HALO, 0))
        near[i], far[i] = sort_swap("lat", to_north, to_south)


def edge_rows(near, far, i):
    half = near.shape[0]
    from_north, from_south = sort_swap("lat", near[i % half], far[i % half])
    if i < half:
        from_south = turn(from_south, HALO, 0)
    else:
        from_north = turn(from_north, HALO, 0)
    return jnp.where(rows(from_north.shape) < HALO, from_north, from_south)


def widen(fields, from_west, from_east, near, far, start, wide):
    count, tile_lat, tile_lon = fields.shape
    halves = tile_lon // BLOCK
    parts = from_west.shape[0]
    corners = [edge_rows(near, far, count * halves + n) for n in range(2 * parts)]
    for i in range(count):
        out = start.at[i] if i < start.shape[0] else wide.at[i - start.shape[0]]
        out[:tile_lat, :tile_lon] = fields[i]
        out[:tile_lat, tile_lon:] = unpack_columns(from_west, from_east, i)
        for h in range(halves):
            out[tile_lat:, h * BLOCK : (h + 1) * BLOCK] = edge_rows(near, far, i * halves + h)
        out[tile_lat:, tile_lon:] = unpack_columns(corners[:parts], corners[parts:], i)


def eastward(x):
    return turn(x, -1, 1)


def westward(x):
    return turn(x, 1, 1)


def northward(x):
    return turn(x, -1, 0)


def southward(x):
    return turn(x, 1, 0)


def adjoint_step(coeffs, read, write, first, last):
    levels = coeffs.shape[1]
    above = coeffs[4, first - 1] * (read(first) - read(first - 1)) if first else None
    for level in range(first, last):
        lam = read(level)
        step_x = eastward(lam) - lam
        step_y = northward(lam) - lam
        out = lam + coeffs[0, level] * step_x + westward(coeffs[1, level] * step_x)
        out = out + coeffs[2, level] * step_y + southward(coeffs[3, level] * step_y)
        if above is not None:
            out = out - above
        if level < levels - 1:
            above = coeffs[4, level] * (read(level + 1) - lam)
            out = out + above
        write(level, out)


def surface_levels(step, levels):
    return min(levels, STEPS - 1 - step)


def run_adjoint(
    fields, from_west, from_east, far, near, blocks, coeffs, start, states, wide, own, sent
):
    levels = coeffs.shape[1]
    tile_lat, tile_lon = fields.shape[1:]
    halves = tile_lon // BLOCK
    widen(fields, from_west, from_east, near, far, start, wide)
    base = 0
    mask0 = None
    for level in range(levels):
        east_d, east_u = wide[base + level], wide[base + levels + level]
        north_d, north_u = wide[base + 2 * levels + level], wide[base + 3 * levels + level]
        mask = (east_d > 0.0).astype(f32)
        mask0 = mask if mask0 is None else mask0
        mask_e, mask_n = eastward(mask), northward(mask)
        east_k, east_v = east_d * mask_e, east_u * mask_e
        north_k, north_v = north_d * mask_n, north_u * mask_n
        coeffs[0, level] = jnp.maximum(east_v, 0.0) + east_k
        coeffs[1, level] = jnp.minimum(east_v, 0.0) - east_k
        coeffs[2, level] = jnp.maximum(north_v, 0.0) + north_k
        coeffs[3, level] = jnp.minimum(north_v, 0.0) - north_k
        coeffs[4, level] = wide[base + 4 * levels + level] if level < levels - 1 else jnp.zeros_like(mask)
        coeffs[5, level] = mask
    copies = []
    for f in range(2):
        surface = start[(2 + f) * levels, :tile_lat, :tile_lon]
        for step in range(STEPS - 1):

            def read(level):
                return states[f, step - 1, level] if step else start[(2 + f) * levels + level]

            def write(level, lam):
                states[f, step, level] = lam

            adjoint_step(coeffs, read, write, 0, surface_levels(step, levels))
            surface = surface + states[f, step, 0, :tile_lat, :tile_lon]
        surface = surface * mask0[:tile_lat, :tile_lon]
        for h in range(halves):
            at = (f * halves + h) * tile_lat
            own[at : at + tile_lat] = surface[:, h * BLOCK : (h + 1) * BLOCK]
        field = pl.ds(f * halves * tile_lat, halves * tile_lat)
        copies += fetch([(own.at[field], blocks.at[k, field]) for k in range(blocks.shape[0])], sent.at[f])
    for copy in copies:
        copy.wait()


def finish_adjoint(coeffs, start, states, weights, adjoint_out, weights_near, rest, arrived):
    bring = pltpu.make_async_copy(weights.at[: weights_near.shape[0]], weights_near, arrived)
    bring.start()
    levels = coeffs.shape[1]
    tile_lat, tile_lon = adjoint_out.shape[2:]
    for f in range(2):
        for step in range(STEPS):
            done = surface_levels(step, levels)

            def read(level):
                if not step:
                    return start[(2 + f) * levels + level]
                return (states if level < surface_levels(step - 1, levels) else rest)[f, step - 1, level]

            def write(level, lam):
                if step == STEPS - 1:
                    adjoint_out[f, level] = lam[:tile_lat, :tile_lon]
                else:
                    rest[f, step, level] = lam

            adjoint_step(coeffs, read, write, done, levels)
    bring.wait()


def sum_forcing(received, forcing, near, far):
    tile_lat = forcing.shape[1]
    halves = forcing.shape[2] // BLOCK - 1
    total = received[0]
    for j in range(1, received.shape[0]):
        total = total + received[j]
    lane = lanes((tile_lat, BLOCK))
    upper = total[2 * halves * tile_lat :]
    lower = jnp.where(lane[: tile_lat // 2] < BLOCK // 2, turn(upper, -2 * HALO, 1), turn(upper, 2 * HALO, 1))
    packed = jnp.concatenate([upper, lower], axis=0)
    for f in range(2):
        for h in range(halves):
            at = (f * halves + h) * tile_lat
            forcing[f, :, h * BLOCK : (h + 1) * BLOCK] = total[at : at + tile_lat]
        used = (lane < HALO) | (lane >= BLOCK - HALO)
        if f == 0:
            edge = packed
        else:
            edge = jnp.where(lane < HALO, turn(packed, -HALO, 1), turn(packed, HALO, 1))
        forcing[f, :, halves * BLOCK :] = jnp.where(used, edge, 0.0)
    row = rows((8, forcing.shape[2]))
    to_north = jnp.where(row < HALO, turn(forcing[0, tile_lat - 8 :], HALO, 0), forcing[1, tile_lat - 8 :])
    to_south = jnp.where(row < HALO, forcing[0, :8], turn(forcing[1, :8], HALO, 0))
    near[0], far[0] = sort_swap("lat", to_north, to_south)


def run_forward(coeffs, start, forcing, near, far, final, state):
    levels = coeffs.shape[1]
    tile_lat, tile_lon = final.shape[2:]
    for f in range(2):
        force = jnp.concatenate([forcing[f], edge_rows(near, far, f)], axis=0)
        force = force * coeffs[5, 0]
        for step in range(STEPS):
            above = None
            for level in range(levels):
                read = (lambda n: start[f * levels + n]) if step == 0 else (lambda n: state[(step - 1) % 2, n])
                theta = read(level)
                east_flux = coeffs[0, level] * theta + coeffs[1, level] * eastward(theta)
                north_flux = coeffs[2, level] * theta + coeffs[3, level] * northward(theta)
                out = theta - (east_flux - westward(east_flux)) - (north_flux - southward(north_flux))
                if level < levels - 1:
                    vertical = coeffs[4, level] * (theta - read(level + 1))
                    out = out - vertical
                if above is not None:
                    out = out + above
                above = vertical if level < levels - 1 else None
                if level == 0:
                    out = out + force
                if step == STEPS - 1:
                    final[f, level] = out[:tile_lat, :tile_lon]
                else:
                    state[step % 2, level] = out


def split(x):
    high = x.astype(bf16)
    return high, (x - high.astype(f32)).astype(bf16)


def weight_copy(weights, held, arrived, n):
    own = pl.ds(n * FETCH, FETCH)
    return pltpu.make_async_copy(weights.at[own], held.at[own], arrived.at[n])


def fetch_weights(weights, held, arrived, near=None):
    for n in range(held.shape[0] // FETCH):
        source = near if near is not None and (n + 1) * FETCH <= near.shape[0] else weights
        weight_copy(source, held, arrived, n).start()


def held_part(weights, held, arrived):
    def part(r, g, u):
        if u == 0:

            @pl.when(r == 0)
            def _():
                for n in range(GROUP // FETCH):
                    weight_copy(weights, held, arrived, g * (GROUP // FETCH) + n).wait()

        return split(held[g * GROUP + u])

    return part


def one_hot(where):
    return jnp.where(where, 1.0, 0.0).astype(bf16)


def places(slots, blocks):
    return 8 * (-(-2 * slots // (8 * blocks)) + 1)


def round_chunks(slots, blocks):
    return -(-(slots + 7 * blocks) // BLOCK)


def as_row(ids):
    return jnp.concatenate([ids[k : k + 1, :] for k in range(ids.shape[0])], axis=1)


def rank_slots(block_row, blocks):
    slots = block_row.shape[1]
    mine = rows((blocks, slots)) == block_row
    cuts = range(0, slots, BLOCK)
    stacked = jnp.concatenate([one_hot(mine[:, at : at + BLOCK]) for at in cuts], axis=0)
    shape = (BLOCK, 2 * BLOCK)
    counts = jnp.dot(stacked, one_hot(rows(shape) < lanes(shape)), preferred_element_type=f32)
    before, out = jnp.zeros((blocks, BLOCK), f32), []
    for n, at in enumerate(cuts):
        run = counts[n * blocks : (n + 1) * blocks]
        here = jnp.where(mine[:, at : at + BLOCK], run[:, :BLOCK] + before, 0.0)
        out.append(jnp.sum(here, axis=0, keepdims=True))
        before = before + run[:, BLOCK:]
    return jnp.concatenate(out, axis=1), before


def find_slots(r, keys, counts, capacity, columns, lines, starts):
    slots = keys.shape[1]
    blocks = counts.shape[0]
    atm_row, ocean_row, block_row, rank = (keys[n : n + 1] for n in range(4))
    count = jnp.clip(counts - r * capacity, 0.0, capacity)
    tiles = jnp.floor((count + 7.0) * 0.125) * 8.0
    shape = (blocks, blocks)
    first = jnp.dot(one_hot(lanes(shape) < rows(shape)), tiles.astype(bf16), preferred_element_type=f32)
    starts[...] = first.astype(jnp.int32)
    mine = rows((blocks, slots)).astype(f32) == block_row
    own = jnp.where(mine, jnp.concatenate([first] * (slots // BLOCK), axis=1), 0.0)
    place = rank - r * capacity
    here = (place >= 0.0) & (place < capacity)
    place = jnp.where(here, jnp.sum(own, axis=0, keepdims=True) + place, -1.0)
    run = jnp.floor(place * (1.0 / BLOCK))
    low = one_hot(rows((BLOCK, slots)).astype(f32) == place - run * BLOCK)
    size = lines.shape[1]
    in_run = rows((size, slots)).astype(f32) == run
    ocean_high = jnp.floor(ocean_row * (1.0 / BLOCK))
    digits = [atm_row, ocean_high, ocean_row - ocean_high * BLOCK]
    digits = [jnp.where(in_run, digit, 0.0).astype(bf16) for digit in digits]
    across = (((1,), (1,)), ((), ()))
    down = [lax.dot_general(low, digit, across, preferred_element_type=f32) for digit in digits]
    along = [lax.dot_general(digit, low, across, preferred_element_type=f32) for digit in digits]
    columns[0, :, :size], columns[1, :, :size] = down[0], down[1] * BLOCK + down[2] - 1.0
    ocean = along[1] * BLOCK + along[2] - 1.0
    lines[0], lines[1] = jnp.where(ocean < 0.0, -1.0, along[0]), ocean


def couple(part, table, capacity, rounds, prepare, columns, lines, starts, transposed, result, scratch):
    vectors, products, starts_near = scratch
    blocks = starts.shape[0]
    total_rows = vectors.shape[0] - capacity
    width = table.shape[0]
    result[...] = jnp.zeros_like(result)
    products[...] = jnp.zeros_like(products)

    def one_round(r, carry):
        prepare(r)
        first_rows = starts[...]
        for w in range(blocks):
            starts_near[w] = first_rows[w, 0]
        place_hot = []
        for n in range(total_rows // BLOCK):
            gather = jnp.broadcast_to(columns[int(transposed), :, n : n + 1], (BLOCK, BLOCK))
            gather = jnp.concatenate([gather] * (width // BLOCK), axis=1)
            hot = one_hot(gather == lanes((BLOCK, width)).astype(f32))
            vectors[n * BLOCK : (n + 1) * BLOCK] = jnp.dot(hot, table, preferred_element_type=f32)
            put = lines[1 - int(transposed), n : n + 1]
            place_hot.append(one_hot(rows((result.shape[0], BLOCK)).astype(f32) == put))

        def group(g, carry):
            for u in range(GROUP):
                at = pl.ds(pl.multiple_of(starts_near[g * GROUP + u], 8), capacity)
                own = vectors[at]
                left = jnp.concatenate([own[:, n * BLOCK : (n + 1) * BLOCK] for n in range(4)], axis=0)
                high, low = part(r, g, u)
                right = jnp.concatenate([high, low], axis=1 if transposed else 0)
                contract = (((1,), (0 if transposed else 1,)), ((), ()))
                product = lax.dot_general(left.astype(bf16), right, contract, preferred_element_type=f32)
                for f in range(2):
                    high_part = product[f * capacity : (f + 1) * capacity]
                    low_part = product[(f + 2) * capacity : (f + 3) * capacity, :BLOCK]
                    products[at, f * BLOCK : (f + 1) * BLOCK] = (
                        high_part[:, BLOCK:] + low_part
                    ) + high_part[:, :BLOCK]
            return carry

        lax.fori_loop(0, blocks // GROUP, group, 0)
        summed = jnp.dot(
            jnp.concatenate(place_hot, axis=1),
            jnp.concatenate(split(products[:total_rows]), axis=1),
            preferred_element_type=f32,
        )
        result[...] += summed[:, : 2 * BLOCK] + summed[:, 2 * BLOCK :]
        return carry

    lax.fori_loop(0, rounds, one_round, 0)


def slot_keys(ids, tile_lat, keys):
    lon_count, cap = ids.shape[3:]
    ocean, atm_ids, block_ids = (ids[n, 0, 0] for n in range(3))
    order = (ocean & 1) * tile_lat + (ocean >> 1) + rows((lon_count, cap)) * (2 * tile_lat)
    order = jnp.where(ocean >= 0, order, lon_count * 2 * tile_lat) + 1
    for n, part in enumerate((atm_ids, order, block_ids)):
        keys[n : n + 1] = as_row(part.astype(f32))


def weigh(
    atm_near, margins, weights, after, sums, keys, counts, columns, lines, starts, result, *scratch
):
    scratch, (held, arrived) = scratch[:3], scratch[3:]
    fetch_weights(weights, held, arrived)
    lon_count = margins.shape[3]
    blocks = weights.shape[0]
    tile_lat = 2 * sums.shape[1] // 9
    slot_keys(margins, tile_lat, keys)
    rank, count = rank_slots(keys[2:3].astype(jnp.int32), blocks)
    keys[3:4] = rank
    counts[...] = count
    capacity = places(keys.shape[1], blocks)
    rounds = jnp.max(rank).astype(jnp.int32) // capacity + 1
    parts = [split(atm_near[f, 0]) for f in range(2)]
    table = jnp.concatenate([parts[f][n] for n in range(2) for f in range(2)], axis=1)
    part = held_part(weights, held, arrived)

    def prepare(r):
        find_slots((rounds - 1 - r).astype(f32), keys, counts[...], capacity, columns, lines, starts)

    couple(part, table, capacity, rounds, prepare, columns, lines, starts, False, result, scratch)
    lane = lanes((tile_lat, BLOCK))

    def block_sums(k, f, h):
        at = (2 * k + h) * tile_lat
        return result[at : at + tile_lat, f * BLOCK : (f + 1) * BLOCK]

    for n, k in enumerate(group_order(lon_count)):
        edge = jnp.zeros((tile_lat, BLOCK), f32)
        for f in range(2):
            for h in range(2):
                sums[n, (2 * f + h) * tile_lat : (2 * f + h + 1) * tile_lat] = block_sums(k, f, h)
            at = f * HALO
            after = turn(block_sums((k + 1) % lon_count, f, 0), at, 1)
            before = turn(block_sums((k - 1) % lon_count, f, 1), -at, 1)
            edge = jnp.where((lane >= at) & (lane < at + HALO), after, edge)
            end = BLOCK - at
            edge = jnp.where((lane >= end - HALO) & (lane < end), before, edge)
        upper, lower = edge[: tile_lat // 2], edge[tile_lat // 2 :]
        near = lane[: tile_lat // 2]
        lower = jnp.where(near < BLOCK // 2, turn(lower, 2 * HALO, 1), turn(lower, -2 * HALO, 1))
        sums[n, 4 * tile_lat :] = jnp.where((near < 2 * HALO) | (near >= BLOCK - 2 * HALO), upper, lower)


def unweigh(
    gathered, keys, counts, columns_in, lines_in, starts_in, weights_near, weights, gradient, result, columns, lines, starts, *scratch
):
    scratch, (held, arrived) = scratch[:3], scratch[3:]
    fetch_weights(weights, held, arrived, weights_near)
    blocks = weights.shape[0]
    lon_count, ocean_blocks = gathered.shape[0], gathered.shape[1] // 2
    order = group_order(lon_count)
    capacity = places(keys.shape[1], blocks)
    rounds = jnp.max(keys[3:4]).astype(jnp.int32) // capacity + 1
    parts = [
        split(
            jnp.concatenate(
                [gathered[order.index(k), f * ocean_blocks : (f + 1) * ocean_blocks] for k in range(lon_count)],
                axis=0,
            )
        )
        for f in range(2)
    ]
    table = jnp.concatenate([parts[f][n] for n in range(2) for f in range(2)], axis=1)

    def prepare(r):
        @pl.when(r == 0)
        def _():
            columns[...] = columns_in[...]
            lines[...] = lines_in[...]
            starts[...] = starts_in[...]

        @pl.when(r > 0)
        def _():
            find_slots(r.astype(f32), keys, counts[...], capacity, columns, lines, starts)

    part = held_part(weights, held, arrived)
    couple(part, table, capacity, rounds, prepare, columns, lines, starts, True, result, scratch)
    for f in range(2):
        gradient[f, 0] = result[:, f * BLOCK : (f + 1) * BLOCK]


def on_device(tracers, cotangent, land_mask, diffusion, velocity, weights, atm_state, margins):
    levels, tile_lat, tile_lon = land_mask.shape
    lon_count = lax.axis_size("lon")
    slots = lon_count * margins.shape[4]
    halves = tile_lon // BLOCK
    count = 9 * levels - 1
    parts = -(-count // PER_LANES)
    inputs = (tracers, cotangent, land_mask, diffusion, velocity)

    def in_vmem(s):
        return pltpu.VMEM(s.shape, s.dtype)

    message = (parts, tile_lat, BLOCK)
    fields, near, far, atm_near, margins_near = call(
        pack_columns,
        [
            (count, tile_lat, tile_lon),
            message,
            message,
            atm_state.shape,
            jax.ShapeDtypeStruct(margins.shape, margins.dtype),
        ],
        [*map(in_vmem, inputs), pltpu.SemaphoreType.DMA((7,))],
        name="pack_columns",
        inputs=7,
        far=range(7),
    )(*inputs, atm_state, margins)
    near_columns, far_columns = swap(near, far, "lon", True)

    blocks_of, atm = weights.shape[0], atm_state.shape[2]
    sum_rows = 2 * halves * tile_lat + tile_lat // 2
    ocean_blocks = lon_count * halves * tile_lat
    chunks = round_chunks(slots, blocks_of)
    held_rows = chunks * BLOCK + places(slots, blocks_of)

    def coupling_scratch(result_rows):
        return [
            pltpu.VMEM((result_rows, 2 * BLOCK), f32),
            pltpu.VMEM((held_rows, 4 * BLOCK), f32),
            pltpu.VMEM((held_rows, 2 * BLOCK), f32),
            pltpu.SMEM((blocks_of,), jnp.int32),
            pltpu.VMEM(weights.shape, f32),
            pltpu.SemaphoreType.DMA((blocks_of // FETCH,)),
        ]

    coupling_flops = 4 * slots * blocks_of * 2 * BLOCK * BLOCK * 2
    found = [
        jax.ShapeDtypeStruct((2, BLOCK, BLOCK), f32),
        jax.ShapeDtypeStruct((2, -(-chunks // 8) * 8, BLOCK), f32),
        jax.ShapeDtypeStruct((blocks_of, BLOCK), jnp.int32),
    ]
    sums, *slot_data = call(
        weigh,
        [(lon_count, sum_rows, BLOCK), (8, slots), (blocks_of, BLOCK), *found],
        coupling_scratch(ocean_blocks),
        coupling_flops,
        name="weigh",
        inputs=4,
        far=(2,),
    )(atm_near, margins_near, weights, far)

    sources = count * halves + 2 * parts
    message = (-(-sources // 2), 8, BLOCK)
    columns = (parts, tile_lat, BLOCK)
    near, far, from_west, from_east, sums = call(
        pack_rows,
        [message, message, columns, columns, sums.shape],
        name="pack_rows",
        inputs=4,
        aliases={3: 4},
    )(fields, near_columns, far_columns, sums)
    received = exchange(sums)
    near_rows, far_rows = swap(near, far, "lat", False)

    wide = (tile_lat + 8, tile_lon + BLOCK)
    own = (2 * halves * tile_lat, BLOCK)
    adjoint_states = (2, STEPS - 1, levels, *wide)
    blocks, coeffs, start, states = call(
        run_adjoint,
        [(lon_count, *own), (6, levels, *wide), (4 * levels, *wide), adjoint_states],
        [
            pltpu.VMEM((count - 4 * levels, *wide), f32),
            pltpu.VMEM(own, f32),
            pltpu.SemaphoreType.DMA((2, lon_count)),
        ],
        name="run_adjoint",
        inputs=5,
        far_outs=(0,),
    )(fields, from_west, from_east, far_rows, near_rows)
    gathered = exchange(blocks)

    message = (1, 8, tile_lon + BLOCK)
    forcing, near, far = call(
        sum_forcing, [(2, tile_lat, tile_lon + BLOCK), message, message], name="sum_forcing", inputs=1
    )(received)
    near_rows, far_rows = swap(near, far, "lat", False)
    adjoint, weights_near = call(
        finish_adjoint,
        [cotangent.shape, (blocks_of // 2, BLOCK, BLOCK)],
        [pltpu.VMEM(adjoint_states, f32), pltpu.SemaphoreType.DMA],
        name="finish_adjoint",
        inputs=4,
        far=(3,),
    )(coeffs, start, states, weights)
    (final,) = call(
        run_forward,
        [tracers.shape],
        [pltpu.VMEM((2, levels, *wide), f32)],
        name="run_forward",
        inputs=5,
    )(coeffs, start, forcing, near_rows, far_rows)

    (gradient,) = call(
        unweigh,
        [atm_state.shape],
        [coupling_scratch(atm)[0], *map(in_vmem, found), *coupling_scratch(atm)[1:]],
        coupling_flops,
        name="unweigh",
        inputs=8,
        far=(7,),
    )(gathered, *slot_data, weights_near, weights)
    return (final, adjoint, gradient)


def solution(mesh):
    return jax.shard_map(
        on_device,
        mesh=mesh,
        in_specs=(
            P(None, None, "lat", "lon"),
            P(None, None, "lat", "lon"),
            P(None, "lat", "lon"),
            P(None, None, "lat", "lon"),
            P(None, None, "lat", "lon"),
            P(),
            P(None, "lat", "lon", None),
            P(None, "lat", "lon", None, None),
        ),
        out_specs=(
            P(None, None, "lat", "lon"),
            P(None, None, "lat", "lon"),
            P(None, "lat", "lon", None),
        ),
        check_vma=False,
    )
```

```python
import jax
import jax.numpy as jnp
from jax import lax
from jax.experimental import pallas as pl
from jax.experimental.pallas import tpu as pltpu
from jax.sharding import PartitionSpec as P

BLOCK = 128
STEPS = 4
HALO = STEPS
PER_LANES = BLOCK // HALO
GROUP = 16
FETCH = 4
f32 = jnp.float32
bf16 = jnp.bfloat16
VMEM_LIMIT = 20 * 1024 * 1024


def call(body, outs, scratch=(), flops=0, name=None, inputs=0, far=(), far_outs=(), aliases=None):
    outs = [s if isinstance(s, jax.ShapeDtypeStruct) else jax.ShapeDtypeStruct(s, f32) for s in outs]
    near = pl.BlockSpec(memory_space=pltpu.VMEM)
    aliases = aliases or {}
    kernel = pl.pallas_call(
        body,
        out_shape=outs,
        in_specs=[
            pl.BlockSpec(memory_space=pl.ANY)
            if n in aliases
            else pl.BlockSpec(memory_space=pltpu.HBM)
            if n in far
            else near
            for n in range(inputs)
        ],
        out_specs=[
            pl.BlockSpec(memory_space=pl.ANY) if n in aliases.values() or n in far_outs else near
            for n in range(len(outs))
        ],
        input_output_aliases=aliases,
        scratch_shapes=list(scratch),
        compiler_params=pltpu.CompilerParams(vmem_limit_bytes=VMEM_LIMIT),
        cost_estimate=pl.CostEstimate(flops=flops, bytes_accessed=1 << 20, transcendentals=0),
        name=name,
    )

    def run(*args):
        return kernel(
            *(pltpu.with_memory_space_constraint(x, pltpu.HBM) if n in far else x for n, x in enumerate(args))
        )

    return run


def lanes(shape):
    return lax.broadcasted_iota(jnp.int32, shape, len(shape) - 1)


def rows(shape):
    return lax.broadcasted_iota(jnp.int32, shape, len(shape) - 2)


def turn(x, shift, axis):
    shift %= x.shape[axis]
    return pltpu.roll(x, shift, axis) if shift else x


def group_order(count):
    half = count // 2
    return [k for n in range(half) for k in (half + n, n)]


def exchange(x):
    order = group_order(x.shape[0])
    return lax.all_to_all(x, "lon", split_axis=0, concat_axis=0, tiled=True, axis_index_groups=[order])


def swap(near, far, axis, wrap):
    count = lax.axis_size(axis)
    pairs = [[], []]
    for i in range(count if wrap else count - 1):
        j = (i + 1) % count
        pairs[i % 2] += [(i, j), (j, i)]
    far = lax.ppermute(far, axis, pairs[1])
    return lax.ppermute(near, axis, pairs[0]), far


def sort_swap(axis, after, before):
    odd = lax.rem(lax.axis_index(axis), 2) == 1
    return jnp.where(odd, before, after), jnp.where(odd, after, before)


def tile_fields(tracers, cotangent, land_mask, diffusion, velocity):
    levels = land_mask.shape[0]
    mask = [land_mask[level].astype(f32) for level in range(levels)]
    out = [tracers[f, level] for f in range(2) for level in range(levels)]
    out += [cotangent[f, level] for f in range(2) for level in range(levels)]
    out += [diffusion[0, level] * mask[level] for level in range(levels)]
    out += [velocity[0, level] * mask[level] for level in range(levels)]
    out += [diffusion[1, level] * mask[level] for level in range(levels)]
    out += [velocity[1, level] * mask[level] for level in range(levels)]
    out += [diffusion[2, level] * mask[level] * mask[level + 1] for level in range(levels - 1)]
    return out


def fetch(pairs, arrived):
    copies = [pltpu.make_async_copy(src, dst, arrived.at[n]) for n, (src, dst) in enumerate(pairs)]
    for copy in copies:
        copy.start()
    return copies


def pack_columns(*refs):
    inputs, (fields, near, far), scratch = refs[:7], refs[7:10], refs[12:]
    copies = fetch(zip(inputs, [*scratch[:5], *refs[10:12]]), scratch[5])
    for copy in copies[:5]:
        copy.wait()
    shape = near.shape[1:]
    lane = lanes(shape)
    west = [jnp.zeros(shape, f32) for _ in range(near.shape[0])]
    east = [jnp.zeros(shape, f32) for _ in range(near.shape[0])]
    for i, field in enumerate(tile_fields(*scratch[:5])):
        fields[i] = field
        part, at = divmod(i, PER_LANES)
        at *= HALO
        here = (lane >= at) & (lane < at + HALO)
        west[part] = jnp.where(here, turn(field[:, :BLOCK], at, 1), west[part])
        east[part] = jnp.where(here, turn(field[:, -BLOCK:], at + HALO, 1), east[part])
    for part in range(near.shape[0]):
        near[part], far[part] = sort_swap("lon", east[part], west[part])
    for copy in copies[5:]:
        copy.wait()


def unpack_columns(from_west, from_east, i):
    part, at = divmod(i, PER_LANES)
    at *= HALO
    lane = lanes(from_west[part].shape)
    east = turn(from_east[part], -at, 1)
    west = turn(from_west[part], -at - HALO, 1)
    return jnp.where(lane < HALO, east, jnp.where(lane >= BLOCK - HALO, west, 0.0))


def row_sources(fields, from_west, from_east):
    out = [(fields, (i, slice(None), slice(h * BLOCK, (h + 1) * BLOCK)))
           for i in range(fields.shape[0]) for h in range(fields.shape[2] // BLOCK)]
    for columns in (from_west, from_east):
        out += [(columns, (part,)) for part in range(columns.shape[0])]
    return out


def pack_rows(fields, near_columns, far_columns, sums, near, far, from_west, from_east, same_sums):
    for part in range(from_west.shape[0]):
        from_east[part], from_west[part] = sort_swap("lon", near_columns[part], far_columns[part])
    sources = [ref[at] for ref, at in row_sources(fields, from_west, from_east)]
    half = near.shape[0]
    row = rows((8, BLOCK))
    for i in range(half):
        first = sources[i]
        second = sources[i + half] if i + half < len(sources) else jnp.zeros_like(first)
        to_north = jnp.where(row < HALO, turn(first[-8:], HALO, 0), second[-8:])
        to_south = jnp.where(row < HALO, first[:8], turn(second[:8], HALO, 0))
        near[i], far[i] = sort_swap("lat", to_north, to_south)


def edge_rows(near, far, i):
    half = near.shape[0]
    from_north, from_south = sort_swap("lat", near[i % half], far[i % half])
    if i < half:
        from_south = turn(from_south, HALO, 0)
    else:
        from_north = turn(from_north, HALO, 0)
    return jnp.where(rows(from_north.shape) < HALO, from_north, from_south)


def widen(fields, from_west, from_east, near, far, start, wide):
    count, tile_lat, tile_lon = fields.shape
    halves = tile_lon // BLOCK
    parts = from_west.shape[0]
    corners = [edge_rows(near, far, count * halves + n) for n in range(2 * parts)]
    for i in range(count):
        out = start.at[i] if i < start.shape[0] else wide.at[i - start.shape[0]]
        out[:tile_lat, :tile_lon] = fields[i]
        out[:tile_lat, tile_lon:] = unpack_columns(from_west, from_east, i)
        for h in range(halves):
            out[tile_lat:, h * BLOCK : (h + 1) * BLOCK] = edge_rows(near, far, i * halves + h)
        out[tile_lat:, tile_lon:] = unpack_columns(corners[:parts], corners[parts:], i)


def eastward(x):
    return turn(x, -1, 1)


def westward(x):
    return turn(x, 1, 1)


def northward(x):
    return turn(x, -1, 0)


def southward(x):
    return turn(x, 1, 0)


def adjoint_step(coeffs, read, write, first, last):
    levels = coeffs.shape[1]
    above = coeffs[4, first - 1] * (read(first) - read(first - 1)) if first else None
    for level in range(first, last):
        lam = read(level)
        step_x = eastward(lam) - lam
        step_y = northward(lam) - lam
        out = lam + coeffs[0, level] * step_x + westward(coeffs[1, level] * step_x)
        out = out + coeffs[2, level] * step_y + southward(coeffs[3, level] * step_y)
        if above is not None:
            out = out - above
        if level < levels - 1:
            above = coeffs[4, level] * (read(level + 1) - lam)
            out = out + above
        write(level, out)


def surface_levels(step, levels):
    return min(levels, STEPS - 1 - step)


def run_adjoint(
    fields, from_west, from_east, far, near, blocks, coeffs, start, states, wide, own, sent
):
    levels = coeffs.shape[1]
    tile_lat, tile_lon = fields.shape[1:]
    halves = tile_lon // BLOCK
    widen(fields, from_west, from_east, near, far, start, wide)
    base = 0
    mask0 = None
    for level in range(levels):
        east_d, east_u = wide[base + level], wide[base + levels + level]
        north_d, north_u = wide[base + 2 * levels + level], wide[base + 3 * levels + level]
        mask = (east_d > 0.0).astype(f32)
        mask0 = mask if mask0 is None else mask0
        mask_e, mask_n = eastward(mask), northward(mask)
        east_k, east_v = east_d * mask_e, east_u * mask_e
        north_k, north_v = north_d * mask_n, north_u * mask_n
        coeffs[0, level] = jnp.maximum(east_v, 0.0) + east_k
        coeffs[1, level] = jnp.minimum(east_v, 0.0) - east_k
        coeffs[2, level] = jnp.maximum(north_v, 0.0) + north_k
        coeffs[3, level] = jnp.minimum(north_v, 0.0) - north_k
        coeffs[4, level] = wide[base + 4 * levels + level] if level < levels - 1 else jnp.zeros_like(mask)
        coeffs[5, level] = mask
    copies = []
    for f in range(2):
        surface = start[(2 + f) * levels, :tile_lat, :tile_lon]
        for step in range(STEPS - 1):

            def read(level):
                return states[f, step - 1, level] if step else start[(2 + f) * levels + level]

            def write(level, lam):
                states[f, step, level] = lam

            adjoint_step(coeffs, read, write, 0, surface_levels(step, levels))
            surface = surface + states[f, step, 0, :tile_lat, :tile_lon]
        surface = surface * mask0[:tile_lat, :tile_lon]
        for h in range(halves):
            at = (f * halves + h) * tile_lat
            own[at : at + tile_lat] = surface[:, h * BLOCK : (h + 1) * BLOCK]
        field = pl.ds(f * halves * tile_lat, halves * tile_lat)
        copies += fetch([(own.at[field], blocks.at[k, field]) for k in range(blocks.shape[0])], sent.at[f])
    for copy in copies:
        copy.wait()


def finish_adjoint(coeffs, start, states, adjoint_out, rest):
    levels = coeffs.shape[1]
    tile_lat, tile_lon = adjoint_out.shape[2:]
    for f in range(2):
        for step in range(STEPS):
            done = surface_levels(step, levels)

            def read(level):
                if not step:
                    return start[(2 + f) * levels + level]
                return (states if level < surface_levels(step - 1, levels) else rest)[f, step - 1, level]

            def write(level, lam):
                if step == STEPS - 1:
                    adjoint_out[f, level] = lam[:tile_lat, :tile_lon]
                else:
                    rest[f, step, level] = lam

            adjoint_step(coeffs, read, write, done, levels)


def sum_forcing(received, forcing, near, far):
    tile_lat = forcing.shape[1]
    halves = forcing.shape[2] // BLOCK - 1
    total = received[0]
    for j in range(1, received.shape[0]):
        total = total + received[j]
    lane = lanes((tile_lat, BLOCK))
    upper = total[2 * halves * tile_lat :]
    lower = jnp.where(lane[: tile_lat // 2] < BLOCK // 2, turn(upper, -2 * HALO, 1), turn(upper, 2 * HALO, 1))
    packed = jnp.concatenate([upper, lower], axis=0)
    for f in range(2):
        for h in range(halves):
            at = (f * halves + h) * tile_lat
            forcing[f, :, h * BLOCK : (h + 1) * BLOCK] = total[at : at + tile_lat]
        used = (lane < HALO) | (lane >= BLOCK - HALO)
        if f == 0:
            edge = packed
        else:
            edge = jnp.where(lane < HALO, turn(packed, -HALO, 1), turn(packed, HALO, 1))
        forcing[f, :, halves * BLOCK :] = jnp.where(used, edge, 0.0)
    row = rows((8, forcing.shape[2]))
    to_north = jnp.where(row < HALO, turn(forcing[0, tile_lat - 8 :], HALO, 0), forcing[1, tile_lat - 8 :])
    to_south = jnp.where(row < HALO, forcing[0, :8], turn(forcing[1, :8], HALO, 0))
    near[0], far[0] = sort_swap("lat", to_north, to_south)


def run_forward(coeffs, start, forcing, near, far, weights, final, weights_near, state, arrived):
    bring = pltpu.make_async_copy(weights.at[: weights_near.shape[0]], weights_near, arrived)
    bring.start()
    levels = coeffs.shape[1]
    tile_lat, tile_lon = final.shape[2:]
    for f in range(2):
        force = jnp.concatenate([forcing[f], edge_rows(near, far, f)], axis=0)
        force = force * coeffs[5, 0]
        for step in range(STEPS):
            above = None
            for level in range(levels):
                read = (lambda n: start[f * levels + n]) if step == 0 else (lambda n: state[(step - 1) % 2, n])
                theta = read(level)
                east_flux = coeffs[0, level] * theta + coeffs[1, level] * eastward(theta)
                north_flux = coeffs[2, level] * theta + coeffs[3, level] * northward(theta)
                out = theta - (east_flux - westward(east_flux)) - (north_flux - southward(north_flux))
                if level < levels - 1:
                    vertical = coeffs[4, level] * (theta - read(level + 1))
                    out = out - vertical
                if above is not None:
                    out = out + above
                above = vertical if level < levels - 1 else None
                if level == 0:
                    out = out + force
                if step == STEPS - 1:
                    final[f, level] = out[:tile_lat, :tile_lon]
                else:
                    state[step % 2, level] = out
    bring.wait()


def split(x):
    high = x.astype(bf16)
    return high, (x - high.astype(f32)).astype(bf16)


def weight_copy(weights, held, arrived, n):
    own = pl.ds(n * FETCH, FETCH)
    return pltpu.make_async_copy(weights.at[own], held.at[own], arrived.at[n])


def fetch_weights(weights, held, arrived, near=None):
    for n in range(held.shape[0] // FETCH):
        source = near if near is not None and (n + 1) * FETCH <= near.shape[0] else weights
        weight_copy(source, held, arrived, n).start()


def held_part(weights, held, arrived):
    def part(r, g, u):
        if u == 0:

            @pl.when(r == 0)
            def _():
                for n in range(GROUP // FETCH):
                    weight_copy(weights, held, arrived, g * (GROUP // FETCH) + n).wait()

        return split(held[g * GROUP + u])

    return part


def one_hot(where):
    return jnp.where(where, 1.0, 0.0).astype(bf16)


def places(slots, blocks):
    return 8 * (-(-2 * slots // (8 * blocks)) + 1)


def round_chunks(slots, blocks):
    return -(-(slots + 7 * blocks) // BLOCK)


def as_row(ids):
    return jnp.concatenate([ids[k : k + 1, :] for k in range(ids.shape[0])], axis=1)


def rank_slots(block_row, blocks):
    slots = block_row.shape[1]
    mine = rows((blocks, slots)) == block_row
    cuts = range(0, slots, BLOCK)
    stacked = jnp.concatenate([one_hot(mine[:, at : at + BLOCK]) for at in cuts], axis=0)
    shape = (BLOCK, 2 * BLOCK)
    counts = jnp.dot(stacked, one_hot(rows(shape) < lanes(shape)), preferred_element_type=f32)
    before, out = jnp.zeros((blocks, BLOCK), f32), []
    for n, at in enumerate(cuts):
        run = counts[n * blocks : (n + 1) * blocks]
        here = jnp.where(mine[:, at : at + BLOCK], run[:, :BLOCK] + before, 0.0)
        out.append(jnp.sum(here, axis=0, keepdims=True))
        before = before + run[:, BLOCK:]
    return jnp.concatenate(out, axis=1), before


def find_slots(r, keys, counts, capacity, columns, lines, starts):
    slots = keys.shape[1]
    blocks = counts.shape[0]
    atm_row, ocean_row, block_row, rank = (keys[n : n + 1] for n in range(4))
    count = jnp.clip(counts - r * capacity, 0.0, capacity)
    tiles = jnp.floor((count + 7.0) * 0.125) * 8.0
    shape = (blocks, blocks)
    first = jnp.dot(one_hot(lanes(shape) < rows(shape)), tiles.astype(bf16), preferred_element_type=f32)
    starts[...] = first.astype(jnp.int32)
    mine = rows((blocks, slots)).astype(f32) == block_row
    own = jnp.where(mine, jnp.concatenate([first] * (slots // BLOCK), axis=1), 0.0)
    place = rank - r * capacity
    here = (place >= 0.0) & (place < capacity)
    place = jnp.where(here, jnp.sum(own, axis=0, keepdims=True) + place, -1.0)
    run = jnp.floor(place * (1.0 / BLOCK))
    low = one_hot(rows((BLOCK, slots)).astype(f32) == place - run * BLOCK)
    size = lines.shape[1]
    in_run = rows((size, slots)).astype(f32) == run
    ocean_high = jnp.floor(ocean_row * (1.0 / BLOCK))
    digits = [atm_row, ocean_high, ocean_row - ocean_high * BLOCK]
    digits = [jnp.where(in_run, digit, 0.0).astype(bf16) for digit in digits]
    across = (((1,), (1,)), ((), ()))
    down = [lax.dot_general(low, digit, across, preferred_element_type=f32) for digit in digits]
    along = [lax.dot_general(digit, low, across, preferred_element_type=f32) for digit in digits]
    columns[0, :, :size], columns[1, :, :size] = down[0], down[1] * BLOCK + down[2] - 1.0
    ocean = along[1] * BLOCK + along[2] - 1.0
    lines[0], lines[1] = jnp.where(ocean < 0.0, -1.0, along[0]), ocean


def couple(part, table, capacity, rounds, prepare, columns, lines, starts, transposed, result, scratch):
    vectors, products, starts_near = scratch
    blocks = starts.shape[0]
    total_rows = vectors.shape[0] - capacity
    width = table.shape[0]
    result[...] = jnp.zeros_like(result)
    products[...] = jnp.zeros_like(products)

    def one_round(r, carry):
        prepare(r)
        first_rows = starts[...]
        for w in range(blocks):
            starts_near[w] = first_rows[w, 0]
        place_hot = []
        for n in range(total_rows // BLOCK):
            gather = jnp.broadcast_to(columns[int(transposed), :, n : n + 1], (BLOCK, BLOCK))
            gather = jnp.concatenate([gather] * (width // BLOCK), axis=1)
            hot = one_hot(gather == lanes((BLOCK, width)).astype(f32))
            vectors[n * BLOCK : (n + 1) * BLOCK] = jnp.dot(hot, table, preferred_element_type=f32)
            put = lines[1 - int(transposed), n : n + 1]
            place_hot.append(one_hot(rows((result.shape[0], BLOCK)).astype(f32) == put))

        def group(g, carry):
            for u in range(GROUP):
                at = pl.ds(pl.multiple_of(starts_near[g * GROUP + u], 8), capacity)
                own = vectors[at]
                left = jnp.concatenate([own[:, n * BLOCK : (n + 1) * BLOCK] for n in range(4)], axis=0)
                high, low = part(r, g, u)
                right = jnp.concatenate([high, low], axis=1 if transposed else 0)
                contract = (((1,), (0 if transposed else 1,)), ((), ()))
                product = lax.dot_general(left.astype(bf16), right, contract, preferred_element_type=f32)
                for f in range(2):
                    high_part = product[f * capacity : (f + 1) * capacity]
                    low_part = product[(f + 2) * capacity : (f + 3) * capacity, :BLOCK]
                    products[at, f * BLOCK : (f + 1) * BLOCK] = (
                        high_part[:, BLOCK:] + low_part
                    ) + high_part[:, :BLOCK]
            return carry

        lax.fori_loop(0, blocks // GROUP, group, 0)
        summed = jnp.dot(
            jnp.concatenate(place_hot, axis=1),
            jnp.concatenate(split(products[:total_rows]), axis=1),
            preferred_element_type=f32,
        )
        result[...] += summed[:, : 2 * BLOCK] + summed[:, 2 * BLOCK :]
        return carry

    lax.fori_loop(0, rounds, one_round, 0)


def slot_keys(ids, tile_lat, keys):
    lon_count, cap = ids.shape[3:]
    ocean, atm_ids, block_ids = (ids[n, 0, 0] for n in range(3))
    order = (ocean & 1) * tile_lat + (ocean >> 1) + rows((lon_count, cap)) * (2 * tile_lat)
    order = jnp.where(ocean >= 0, order, lon_count * 2 * tile_lat) + 1
    for n, part in enumerate((atm_ids, order, block_ids)):
        keys[n : n + 1] = as_row(part.astype(f32))


def weigh(
    atm_near, margins, weights, after, sums, keys, counts, columns, lines, starts, result, *scratch
):
    scratch, (held, arrived) = scratch[:3], scratch[3:]
    fetch_weights(weights, held, arrived)
    lon_count = margins.shape[3]
    blocks = weights.shape[0]
    tile_lat = 2 * sums.shape[1] // 9
    slot_keys(margins, tile_lat, keys)
    rank, count = rank_slots(keys[2:3].astype(jnp.int32), blocks)
    keys[3:4] = rank
    counts[...] = count
    capacity = places(keys.shape[1], blocks)
    rounds = jnp.max(rank).astype(jnp.int32) // capacity + 1
    parts = [split(atm_near[f, 0]) for f in range(2)]
    table = jnp.concatenate([parts[f][n] for n in range(2) for f in range(2)], axis=1)
    part = held_part(weights, held, arrived)

    def prepare(r):
        find_slots((rounds - 1 - r).astype(f32), keys, counts[...], capacity, columns, lines, starts)

    couple(part, table, capacity, rounds, prepare, columns, lines, starts, False, result, scratch)
    lane = lanes((tile_lat, BLOCK))

    def block_sums(k, f, h):
        at = (2 * k + h) * tile_lat
        return result[at : at + tile_lat, f * BLOCK : (f + 1) * BLOCK]

    for n, k in enumerate(group_order(lon_count)):
        edge = jnp.zeros((tile_lat, BLOCK), f32)
        for f in range(2):
            for h in range(2):
                sums[n, (2 * f + h) * tile_lat : (2 * f + h + 1) * tile_lat] = block_sums(k, f, h)
            at = f * HALO
            after = turn(block_sums((k + 1) % lon_count, f, 0), at, 1)
            before = turn(block_sums((k - 1) % lon_count, f, 1), -at, 1)
            edge = jnp.where((lane >= at) & (lane < at + HALO), after, edge)
            end = BLOCK - at
            edge = jnp.where((lane >= end - HALO) & (lane < end), before, edge)
        upper, lower = edge[: tile_lat // 2], edge[tile_lat // 2 :]
        near = lane[: tile_lat // 2]
        lower = jnp.where(near < BLOCK // 2, turn(lower, 2 * HALO, 1), turn(lower, -2 * HALO, 1))
        sums[n, 4 * tile_lat :] = jnp.where((near < 2 * HALO) | (near >= BLOCK - 2 * HALO), upper, lower)


def unweigh(
    gathered, keys, counts, columns_in, lines_in, starts_in, weights_near, weights, gradient, result, columns, lines, starts, *scratch
):
    scratch, (held, arrived) = scratch[:3], scratch[3:]
    fetch_weights(weights, held, arrived, weights_near)
    blocks = weights.shape[0]
    lon_count, ocean_blocks = gathered.shape[0], gathered.shape[1] // 2
    order = group_order(lon_count)
    capacity = places(keys.shape[1], blocks)
    rounds = jnp.max(keys[3:4]).astype(jnp.int32) // capacity + 1
    parts = [
        split(
            jnp.concatenate(
                [gathered[order.index(k), f * ocean_blocks : (f + 1) * ocean_blocks] for k in range(lon_count)],
                axis=0,
            )
        )
        for f in range(2)
    ]
    table = jnp.concatenate([parts[f][n] for n in range(2) for f in range(2)], axis=1)

    def prepare(r):
        @pl.when(r == 0)
        def _():
            columns[...] = columns_in[...]
            lines[...] = lines_in[...]
            starts[...] = starts_in[...]

        @pl.when(r > 0)
        def _():
            find_slots(r.astype(f32), keys, counts[...], capacity, columns, lines, starts)

    part = held_part(weights, held, arrived)
    couple(part, table, capacity, rounds, prepare, columns, lines, starts, True, result, scratch)
    for f in range(2):
        gradient[f, 0] = result[:, f * BLOCK : (f + 1) * BLOCK]


def on_device(tracers, cotangent, land_mask, diffusion, velocity, weights, atm_state, margins):
    levels, tile_lat, tile_lon = land_mask.shape
    lon_count = lax.axis_size("lon")
    slots = lon_count * margins.shape[4]
    halves = tile_lon // BLOCK
    count = 9 * levels - 1
    parts = -(-count // PER_LANES)
    inputs = (tracers, cotangent, land_mask, diffusion, velocity)

    def in_vmem(s):
        return pltpu.VMEM(s.shape, s.dtype)

    message = (parts, tile_lat, BLOCK)
    fields, near, far, atm_near, margins_near = call(
        pack_columns,
        [
            (count, tile_lat, tile_lon),
            message,
            message,
            atm_state.shape,
            jax.ShapeDtypeStruct(margins.shape, margins.dtype),
        ],
        [*map(in_vmem, inputs), pltpu.SemaphoreType.DMA((7,))],
        name="pack_columns",
        inputs=7,
        far=range(7),
    )(*inputs, atm_state, margins)
    near_columns, far_columns = swap(near, far, "lon", True)

    blocks_of, atm = weights.shape[0], atm_state.shape[2]
    sum_rows = 2 * halves * tile_lat + tile_lat // 2
    ocean_blocks = lon_count * halves * tile_lat
    chunks = round_chunks(slots, blocks_of)
    held_rows = chunks * BLOCK + places(slots, blocks_of)

    def coupling_scratch(result_rows):
        return [
            pltpu.VMEM((result_rows, 2 * BLOCK), f32),
            pltpu.VMEM((held_rows, 4 * BLOCK), f32),
            pltpu.VMEM((held_rows, 2 * BLOCK), f32),
            pltpu.SMEM((blocks_of,), jnp.int32),
            pltpu.VMEM(weights.shape, f32),
            pltpu.SemaphoreType.DMA((blocks_of // FETCH,)),
        ]

    coupling_flops = 4 * slots * blocks_of * 2 * BLOCK * BLOCK * 2
    found = [
        jax.ShapeDtypeStruct((2, BLOCK, BLOCK), f32),
        jax.ShapeDtypeStruct((2, -(-chunks // 8) * 8, BLOCK), f32),
        jax.ShapeDtypeStruct((blocks_of, BLOCK), jnp.int32),
    ]
    sums, *slot_data = call(
        weigh,
        [(lon_count, sum_rows, BLOCK), (8, slots), (blocks_of, BLOCK), *found],
        coupling_scratch(ocean_blocks),
        coupling_flops,
        name="weigh",
        inputs=4,
        far=(2,),
    )(atm_near, margins_near, weights, far)

    sources = count * halves + 2 * parts
    message = (-(-sources // 2), 8, BLOCK)
    columns = (parts, tile_lat, BLOCK)
    near, far, from_west, from_east, sums = call(
        pack_rows,
        [message, message, columns, columns, sums.shape],
        name="pack_rows",
        inputs=4,
        aliases={3: 4},
    )(fields, near_columns, far_columns, sums)
    received = exchange(sums)
    near_rows, far_rows = swap(near, far, "lat", False)

    wide = (tile_lat + 8, tile_lon + BLOCK)
    own = (2 * halves * tile_lat, BLOCK)
    adjoint_states = (2, STEPS - 1, levels, *wide)
    blocks, coeffs, start, states = call(
        run_adjoint,
        [(lon_count, *own), (6, levels, *wide), (4 * levels, *wide), adjoint_states],
        [
            pltpu.VMEM((count - 4 * levels, *wide), f32),
            pltpu.VMEM(own, f32),
            pltpu.SemaphoreType.DMA((2, lon_count)),
        ],
        name="run_adjoint",
        inputs=5,
        far_outs=(0,),
    )(fields, from_west, from_east, far_rows, near_rows)
    gathered = exchange(blocks)

    message = (1, 8, tile_lon + BLOCK)
    forcing, near, far = call(
        sum_forcing, [(2, tile_lat, tile_lon + BLOCK), message, message], name="sum_forcing", inputs=1
    )(received)
    near_rows, far_rows = swap(near, far, "lat", False)
    (adjoint,) = call(
        finish_adjoint,
        [cotangent.shape],
        [pltpu.VMEM(adjoint_states, f32)],
        name="finish_adjoint",
        inputs=3,
    )(coeffs, start, states)
    final, weights_near = call(
        run_forward,
        [tracers.shape, (blocks_of // 4, BLOCK, BLOCK)],
        [pltpu.VMEM((2, levels, *wide), f32), pltpu.SemaphoreType.DMA],
        name="run_forward",
        inputs=6,
        far=(5,),
    )(coeffs, start, forcing, near_rows, far_rows, weights)

    (gradient,) = call(
        unweigh,
        [atm_state.shape],
        [coupling_scratch(atm)[0], *map(in_vmem, found), *coupling_scratch(atm)[1:]],
        coupling_flops,
        name="unweigh",
        inputs=8,
        far=(7,),
    )(gathered, *slot_data, weights_near, weights)
    return (final, adjoint, gradient)


def solution(mesh):
    return jax.shard_map(
        on_device,
        mesh=mesh,
        in_specs=(
            P(None, None, "lat", "lon"),
            P(None, None, "lat", "lon"),
            P(None, "lat", "lon"),
            P(None, None, "lat", "lon"),
            P(None, None, "lat", "lon"),
            P(),
            P(None, "lat", "lon", None),
            P(None, "lat", "lon", None, None),
        ),
        out_specs=(
            P(None, None, "lat", "lon"),
            P(None, None, "lat", "lon"),
            P(None, "lat", "lon", None),
        ),
        check_vma=False,
    )
```
